32 devices in a mesh: ctx: 8 (over y, x, core), shard: 4 (over z).
Axes of the slice: x: 2, y: 2, z: 4, core: 2. Of those that a mesh axis runs over, the one named last changes fastest.
Arguments:
- hidden_in: bfloat16 [8, 4096, 768], P('shard', 'ctx'), may hold values from -6 to 6
- cotangent: bfloat16 [8, 4096, 768], P('shard', 'ctx'), may hold values from -6 to 6
- qkv_weight: bfloat16 [768, 1152], P('shard'), may hold values from -0.21875 to 0.21875
- conv_depth: bfloat16 [9, 768], P(None, 'shard'), may hold values from -2 to 2
- conv_point: bfloat16 [768, 384], P('shard'), may hold values from -0.21875 to 0.21875
- span_weight: bfloat16 [384, 54], P('shard'), may hold values from -0.3125 to 0.3125
- conv_value: bfloat16 [768, 384], P('shard'), may hold values from -0.21875 to 0.21875
- dense_attn: bfloat16 [384, 768], P('shard'), may hold values from -6 to 6
- dense_conv: bfloat16 [384, 768], P('shard'), may hold values from -0.5 to 0.5
- attn_norm_gain: bfloat16 [768], P('shard'), may hold values from 0.5 to 1.5
- attn_norm_bias: bfloat16 [768], P('shard'), may hold values from -1.25 to 1.25
- ffn_inner: bfloat16 [2, 384, 1536], P(None, 'shard'), may hold values from -0.3125 to 0.3125
- ffn_outer: bfloat16 [2, 1536, 384], P(None, 'shard'), may hold values from -0.15625 to 0.15625
- out_norm_gain: bfloat16 [768], P('shard'), may hold values from 0.5 to 1.5
- out_norm_bias: bfloat16 [768], P('shard'), may hold values from -1.25 to 1.25
Outputs:
- layer_out: bfloat16 [8, 4096, 768], P('shard', 'ctx')
- grad_in: float32 [8, 4096, 768], P('shard', 'ctx')
- grad_qkv: float32 [768, 1152], P('shard')
- grad_depth: float32 [9, 768], P(None, 'shard')
- grad_point: float32 [768, 384], P('shard')
- grad_span: float32 [384, 54], P('shard')
- grad_conv_value: float32 [768, 384], P('shard')
- grad_dense_attn: float32 [384, 768], P('shard')
- grad_dense_conv: float32 [384, 768], P('shard')
- grad_attn_gain: float32 [768], P('shard')
- grad_attn_bias: float32 [768], P('shard')
- grad_ffn_inner: float32 [2, 384, 1536], P(None, 'shard')
- grad_ffn_outer: float32 [2, 1536, 384], P(None, 'shard')
- grad_out_gain: float32 [768], P('shard')
- grad_out_bias: float32 [768], P('shard')
The draws below stay inside these ranges and needn't reach their ends.
All inputs are finite; a program needn't handle non-finite values.
Results may differ from the reference program's by a relative error of at most 0.025.
Values may be sent and summed in bfloat16 or wider, within the bound.
A program may use at most 192 MiB of HBM per device.

```python
import math
from functools import partial
import jax
import jax.numpy as jnp
from jax import lax

D = 768
HEADS = 6
HEAD = 64
FF = 3072
GROUPS = 2
KERNEL = 9
SEQ_LEN = 4096
SEQS = 8


def level_of(stream_key, extent, pieces, smallest, top_value):
    def one(dim, parts):
        heights = jax.random.uniform(jax.random.fold_in(jax.random.fold_in(stream_key, 6), dim), (parts,), jnp.float32, smallest / len(pieces), top_value / len(pieces))
        return jnp.repeat(jnp.exp(heights), extent[dim] // parts).reshape((-1,) + (1,) * (len(extent) - dim - 1))

    level = one(*pieces[0])
    for cut in pieces[1:]:
        level = level * one(*cut)
    return level


def gaussian(rng, shape, deviation, bound, shards=(), dtype=jnp.bfloat16):
    drawn = jax.random.normal(rng, shape, jnp.float32) * deviation
    if len(shards) > 0:
        drawn = level_of(rng, shape, shards, -0.22, 0.18) * drawn
    return jnp.clip(drawn, min=-bound, max=bound).astype(dtype)


def setup_inputs(seed: int = 0) -> dict:
    keys = jax.random.split(jax.random.key(seed), 16)
    hidden_in = gaussian(keys[0], (SEQS, SEQ_LEN, D), 1.0, 6.0, ((0, 4), (1, 8)))
    cotangent = gaussian(keys[1], (SEQS, SEQ_LEN, D), 1.0, 6.0, ((0, 4), (1, 8)))
    qkv_weight = gaussian(keys[2], (D, 3 * HEADS * HEAD), D ** -0.5, 0.21875, ((0, 4),))
    conv_depth = gaussian(keys[3], (KERNEL, D), KERNEL ** -0.5, 2.0, ((1, 4),))
    conv_point = gaussian(keys[4], (D, HEADS * HEAD), D ** -0.5, 0.21875, ((0, 4),))
    span_weight = gaussian(keys[5], (HEADS * HEAD, HEADS * KERNEL), (HEADS * HEAD) ** -0.5, 0.3125, ((0, 4),))
    conv_value = gaussian(keys[6], (D, HEADS * HEAD), D ** -0.5, 0.21875, ((0, 4),))
    dense_attn = gaussian(keys[7], (HEADS * HEAD, D), 1 ** -0.5, 6.0, ((0, 4),))
    dense_conv = gaussian(keys[8], (HEADS * HEAD, D), (HEADS * HEAD // 3) ** -0.5, 0.5, ((0, 4),))
    attn_norm_gain = jnp.clip(1.0 + 0.1 * jax.random.normal(keys[9], (D,), jnp.float32), 0.5, 1.5).astype(jnp.bfloat16)
    attn_norm_bias = gaussian(keys[10], (D,), 0.2, 1.25, ((0, 4),))
    ffn_inner = gaussian(keys[11], (GROUPS, D // GROUPS, FF // GROUPS), (D // GROUPS) ** -0.5, 0.3125, ((1, 4),))
    ffn_outer = gaussian(keys[12], (GROUPS, FF // GROUPS, D // GROUPS), (FF // GROUPS) ** -0.5, 0.15625, ((1, 4),))
    out_norm_gain = jnp.clip(1.0 + 0.1 * jax.random.normal(keys[13], (D,), jnp.float32), 0.5, 1.5).astype(jnp.bfloat16)
    out_norm_bias = gaussian(keys[14], (D,), 0.2, 1.25, ((0, 4),))
    return {"hidden_in": hidden_in, "cotangent": cotangent, "qkv_weight": qkv_weight, "conv_depth": conv_depth, "conv_point": conv_point, "span_weight": span_weight, "conv_value": conv_value, "dense_attn": dense_attn, "dense_conv": dense_conv, "attn_norm_gain": attn_norm_gain, "attn_norm_bias": attn_norm_bias, "ffn_inner": ffn_inner, "ffn_outer": ffn_outer, "out_norm_gain": out_norm_gain, "out_norm_bias": out_norm_bias}


@jax.custom_vjp
def low(v):
    return lax.optimization_barrier(v.astype(jnp.bfloat16)).astype(jnp.float32)

@jax.custom_vjp
def low_back(v):
    return v

def low_keep(v):
    return (low(v), None)

def low_pass(kept, grad):
    return (grad,)

def back_keep(v):
    return (v, None)

def back_low(kept, grad):
    return (low(grad),)
low.defvjp(low_keep, low_pass)
low_back.defvjp(back_keep, back_low)
highest = lax.Precision.HIGHEST
norm_eps = 1e-12

def layer_norm(hidden, norm_gain, norm_bias):
    center = hidden - lax.optimization_barrier(jnp.mean(hidden, axis=-1, keepdims=True))
    return center * lax.rsqrt(lax.optimization_barrier(jnp.mean(center * center, axis=-1, keepdims=True)) + norm_eps) * norm_gain + norm_bias

def attend_block(query_block, keys_heads, values_heads):
    score_scale = 1.0 / math.sqrt(HEAD)
    scores = low_back(jnp.einsum('qhe,khe->hqk', query_block, keys_heads, precision=highest) * score_scale)
    score_top = lax.optimization_barrier(jnp.max(scores, axis=-1, keepdims=True))
    exp_scores = jnp.exp(scores - score_top)
    attend = low(exp_scores / lax.optimization_barrier(jnp.sum(exp_scores, axis=-1, keepdims=True)))
    return jnp.einsum('hqk,khe->qhe', attend, values_heads, precision=highest)

def forward(seq_rows, qkv_weight, conv_depth, conv_point, span_weight, conv_value, dense_attn, dense_conv, attn_norm_gain, attn_norm_bias, ffn_inner, ffn_outer, out_norm_gain, out_norm_bias):
    attn_width = HEADS * HEAD
    half_kernel = KERNEL // 2
    mixed_qkv = jnp.dot(seq_rows, qkv_weight, precision=highest)
    queries = low_back(low(mixed_qkv[:, :attn_width]))
    keys_all = low_back(low(mixed_qkv[:, attn_width:2 * attn_width]))
    values_all = low_back(low(mixed_qkv[:, 2 * attn_width:]))
    block_rows = math.gcd(SEQ_LEN, 512)
    query_blocks = queries.reshape(SEQ_LEN // block_rows, block_rows, HEADS, HEAD)
    keys_heads = keys_all.reshape(SEQ_LEN, HEADS, HEAD)
    values_heads = values_all.reshape(SEQ_LEN, HEADS, HEAD)
    attend_one = jax.checkpoint(partial(attend_block, keys_heads=keys_heads, values_heads=values_heads))
    context = lax.map(attend_one, query_blocks).reshape(SEQ_LEN, attn_width)
    padded = jnp.pad(seq_rows, ((half_kernel, half_kernel), (0, 0)))
    spread = padded[0:SEQ_LEN] * conv_depth[0]
    for offset in range(1, KERNEL):
        spread = spread + padded[offset:offset + SEQ_LEN] * conv_depth[offset]
    key_conv = low_back(jnp.dot(low(spread), conv_point, precision=highest))
    span_mix = low(key_conv * queries)
    logits = low_back(jnp.dot(span_mix, span_weight, precision=highest)).reshape(SEQ_LEN, HEADS, KERNEL)
    logit_top = lax.optimization_barrier(jnp.max(logits, axis=-1, keepdims=True))
    exp_logits = jnp.exp(logits - logit_top)
    kernel_soft = exp_logits / lax.optimization_barrier(jnp.sum(exp_logits, axis=-1, keepdims=True))
    conv_values = low_back(jnp.dot(seq_rows, conv_value, precision=highest))
    value_pad = jnp.pad(conv_values, ((half_kernel, half_kernel), (0, 0))).reshape(SEQ_LEN + 2 * half_kernel, HEADS, HEAD)
    conv_res = kernel_soft[:, :, 0:1] * value_pad[0:SEQ_LEN]
    for offset in range(1, KERNEL):
        conv_res = conv_res + kernel_soft[:, :, offset:offset + 1] * value_pad[offset:offset + SEQ_LEN]
    dense_sum = low_back(jnp.dot(low_back(low(context)), dense_attn, precision=highest) + jnp.dot(low(conv_res.reshape(SEQ_LEN, attn_width)), dense_conv, precision=highest))
    hidden_one = layer_norm(dense_sum + seq_rows, attn_norm_gain, attn_norm_bias)
    grouped = low(hidden_one).reshape(SEQ_LEN, GROUPS, D // GROUPS)
    inner_act = low_back(jnp.einsum('tgi,gio->tgo', grouped, ffn_inner, precision=highest))
    active = low(jax.nn.gelu(inner_act, approximate=False))
    outer_sum = low_back(jnp.einsum('tgo,goi->tgi', active, ffn_outer, precision=highest)).reshape(SEQ_LEN, D)
    return layer_norm(outer_sum + hidden_one, out_norm_gain, out_norm_bias)

def reference(hidden_in, cotangent, qkv_weight, conv_depth, conv_point, span_weight, conv_value, dense_attn, dense_conv, attn_norm_gain, attn_norm_bias, ffn_inner, ffn_outer, out_norm_gain, out_norm_bias):
    weights = (qkv_weight.astype(jnp.float32), conv_depth.astype(jnp.float32), conv_point.astype(jnp.float32), span_weight.astype(jnp.float32), conv_value.astype(jnp.float32), dense_attn.astype(jnp.float32), dense_conv.astype(jnp.float32), attn_norm_gain.astype(jnp.float32), attn_norm_bias.astype(jnp.float32), ffn_inner.astype(jnp.float32), ffn_outer.astype(jnp.float32), out_norm_gain.astype(jnp.float32), out_norm_bias.astype(jnp.float32))

    def one_sequence(totals, pair_rows):
        seq_rows, seq_cot = pair_rows
        result, pull_back = jax.vjp(forward, seq_rows.astype(jnp.float32), *weights)
        seq_grads = pull_back(seq_cot.astype(jnp.float32))
        totals = tuple((total_now + grad_now for total_now, grad_now in zip(totals, seq_grads[1:])))
        return (totals, (result.astype(jnp.bfloat16), seq_grads[0]))
    start_totals = tuple((jnp.zeros(weight_now.shape, jnp.float32) for weight_now in weights))
    totals, outputs = lax.scan(one_sequence, start_totals, (hidden_in, cotangent))
    layer_out, grad_in = outputs
    grad_qkv, grad_depth, grad_point, grad_span, grad_conv_value, grad_dense_attn, grad_dense_conv, grad_attn_gain, grad_attn_bias, grad_ffn_inner, grad_ffn_outer, grad_out_gain, grad_out_bias = totals
    return (layer_out, grad_in, grad_qkv, grad_depth, grad_point, grad_span, grad_conv_value, grad_dense_attn, grad_dense_conv, grad_attn_gain, grad_attn_bias, grad_ffn_inner, grad_ffn_outer, grad_out_gain, grad_out_bias)
```

```python
import functools
from functools import partial
import math

import jax
import jax.numpy as jnp
from jax import lax
from jax.experimental import pallas as pl
from jax.experimental.pallas import tpu as pltpu
from jax.sharding import PartitionSpec as P

D = 768
HEADS = 6
HEAD = 64
GROUPS = 2
KERNEL = 9


norm_eps = 1e-12


def with_halo(block, sides, width):
    for axis, dim in sides:
        count = lax.axis_size(axis)
        forward = [(i, i + 1) for i in range(count - 1)]
        backward = [(target, source) for source, target in forward]
        low = lax.ppermute(
            lax.slice_in_dim(block, block.shape[dim] - width, None, axis=dim), axis, forward
        )
        high = lax.ppermute(lax.slice_in_dim(block, 0, width, axis=dim), axis, backward)
        block = jnp.concatenate([low, block, high], axis=dim)
    return block


def layer_norm(hidden, norm_gain, norm_bias):
    center = hidden - jnp.mean(hidden, axis=-1, keepdims=True)
    inv_std = lax.rsqrt(jnp.mean(center * center, axis=-1, keepdims=True) + norm_eps)
    normed = center * inv_std
    return (normed * norm_gain + norm_bias, normed, inv_std)


def norm_back(normed, inv_std, norm_gain, d_result):
    d_gain = jnp.sum(d_result * normed, axis=(0, 1))
    d_shift = jnp.sum(d_result, axis=(0, 1))
    d_scaled = d_result * norm_gain
    d_hidden = inv_std * (
        d_scaled
        - jnp.mean(d_scaled, axis=-1, keepdims=True)
        - normed * jnp.mean(d_scaled * normed, axis=-1, keepdims=True)
    )
    return (d_hidden, d_gain, d_shift)


def four_heads(values):
    return values.reshape(values.shape[0], values.shape[1], HEADS, HEAD)


BF = jnp.bfloat16
F32 = jnp.float32
MESH_ID = pl.DeviceIdType.MESH
NT = (((1,), (1,)), ((), ()))
NN = (((1,), (0,)), ((), ()))
EXP2_SCALE = math.log2(math.e) / math.sqrt(HEAD)
TRIPLE = 3
QUADS = 4
CHUNK = 128


def dot(a, b, dims):
    return lax.dot_general(a, b, dims, preferred_element_type=F32)


def swap_halves(packed):
    return jnp.concatenate([packed[:, HEAD:], packed[:, :HEAD]], axis=1)


def low_lanes():
    return lax.broadcasted_iota(jnp.int32, (1, 2 * HEAD), 1) < HEAD


def remote(src, dst, send, recv, target):
    return pltpu.make_async_remote_copy(
        src_ref=src, dst_ref=dst, send_sem=send, recv_sem=recv,
        device_id=target, device_id_type=MESH_ID,
    )


def greet(peers):
    barrier = pltpu.get_barrier_semaphore()
    for peer in peers:
        pl.semaphore_signal(barrier, inc=1, device_id=peer, device_id_type=MESH_ID)
    pl.semaphore_wait(barrier, len(peers))


def attend_forward_kernel(
    members, kv_in, q_in, kv_all, q_all, out_all, lse, ctx_out,
    out_send, kv_s, kv_r, q_s, q_r, f_s, f_r, o_s, o_r, local,
):
    rows = kv_in.shape[2]
    half = rows // 2
    me = lax.axis_index("ctx")
    shard = lax.axis_index("shard")
    quad, sub = me // members, me % members

    def peer(step):
        return ((quad + step) % QUADS * members + sub, shard)

    def sibling(step):
        return (quad * members + (sub + step) % members, shard)

    greet([peer(k) for k in range(1, QUADS)] + [sibling(m) for m in range(1, members)])

    def kv_copy(h, k):
        return remote(
            kv_in.at[(quad + k) % QUADS, h], kv_all.at[h, quad, sub], kv_s.at[h, k], kv_r.at[h, k], peer(k)
        )

    def q_copy(h, k):
        return remote(
            q_in.at[(quad + k) % QUADS, h], q_all.at[h, quad], q_s.at[h, k], q_r.at[h, k], peer(k)
        )

    def forward_copy(h, m):
        return remote(
            kv_all.at[h, :, sub], kv_all.at[h, :, sub], f_s.at[h, m], f_r.at[h, m], sibling(m)
        )

    def out_copy(h, i, k):
        return remote(
            out_send.at[h, i], ctx_out.at[quad, h], o_s.at[h, i], o_r.at[h, i], peer(k)
        )

    own_kv = pltpu.make_async_copy(kv_in.at[quad], kv_all.at[:, quad, sub], local.at[0])
    own_q = pltpu.make_async_copy(q_in.at[quad], q_all.at[:, quad], local.at[1])
    own_kv.start()
    own_q.start()
    for h in range(TRIPLE):
        for k in range(1, QUADS):
            kv_copy(h, k).start()
            q_copy(h, k).start()
    own_kv.wait()
    own_q.wait()

    def receive(h):
        for k in range(1, QUADS):
            kv_copy(h, k).wait_recv()
            q_copy(h, k).wait_recv()
        for m in range(1, members):
            forward_copy(h, m).start()

    receive(0)
    is_low = low_lanes()

    def block(step, carry):
        h, i = step // QUADS, step % QUADS
        k = (i + 1) % QUADS
        source = (quad + k) % QUADS

        @pl.when(i == 0)
        def _():
            for m in range(1, members):
                forward_copy(h, m).wait_recv()

        keys = kv_all[h].reshape(QUADS * members * rows, 2 * HEAD)

        def rows_turn(r, inner):
            at = pl.multiple_of(r * CHUNK, CHUNK)
            packed = q_all[h, source, pl.ds(at, CHUNK), :]
            outs = []
            stats = []
            for part in range(2):
                q = jnp.where(is_low, packed if part == 0 else swap_halves(packed), jnp.zeros_like(packed))
                scores = dot(q, keys, NT)
                top = jnp.max(scores, axis=1, keepdims=True)
                probs = jnp.exp2((scores - top) * EXP2_SCALE)
                total = jnp.sum(probs, axis=1, keepdims=True)
                outs.append(dot(probs.astype(BF), keys, NN) / total)
                stats.append(top * EXP2_SCALE + jnp.log2(total))
            both = jnp.where(is_low, swap_halves(outs[0]), outs[1])
            out_all[h, source, pl.ds(at, CHUNK), :] = both
            out_send[h, i, pl.ds(at, CHUNK), :] = both.astype(BF)
            for part in range(2):
                lse[h, source, part, r] = jnp.broadcast_to(stats[part], (CHUNK, CHUNK)).T[0:8, :]
            return inner

        lax.fori_loop(0, half // CHUNK, rows_turn, 0)

        @pl.when(k != 0)
        def _():
            out_copy(h, i, k).start()

        @pl.when(k == 0)
        def _():
            own = pltpu.make_async_copy(out_send.at[h, i], ctx_out.at[quad, h], local.at[0])
            own.start()
            own.wait()

        @pl.when((i == 2) & (h < TRIPLE - 1))
        def _():
            receive(h + 1)

        return carry

    lax.fori_loop(0, TRIPLE * QUADS, block, 0)
    for h in range(TRIPLE):
        for k in range(1, QUADS):
            out_copy(h, k - 1, k).wait()
            kv_copy(h, k).wait_send()
            q_copy(h, k).wait_send()
        for m in range(1, members):
            forward_copy(h, m).wait_send()


def attend_forward(kv, q, members):
    rows = kv.shape[2]
    half = rows // 2
    vm = pl.BlockSpec(memory_space=pltpu.VMEM)
    anywhere = pl.BlockSpec(memory_space=pl.ANY)
    dma = pltpu.SemaphoreType.DMA
    total = TRIPLE * QUADS * rows * QUADS * members * rows
    return pl.pallas_call(
        functools.partial(attend_forward_kernel, members),
        in_specs=[anywhere, anywhere],
        out_specs=[vm, vm, vm, vm, anywhere],
        out_shape=[
            jax.ShapeDtypeStruct((TRIPLE, QUADS, members, rows, 2 * HEAD), BF),
            jax.ShapeDtypeStruct((TRIPLE, QUADS, half, 2 * HEAD), BF),
            jax.ShapeDtypeStruct((TRIPLE, QUADS, half, 2 * HEAD), F32),
            jax.ShapeDtypeStruct((TRIPLE, QUADS, 2, half // CHUNK, 8, CHUNK), F32),
            jax.ShapeDtypeStruct((QUADS, TRIPLE, half, 2 * HEAD), BF),
        ],
        scratch_shapes=[
            pltpu.VMEM((TRIPLE, QUADS, half, 2 * HEAD), BF),
            dma((TRIPLE, QUADS)), dma((TRIPLE, QUADS)), dma((TRIPLE, QUADS)), dma((TRIPLE, QUADS)),
            dma((TRIPLE, members)), dma((TRIPLE, members)), dma((TRIPLE, QUADS)), dma((TRIPLE, QUADS)),
            dma((2,)),
        ],
        compiler_params=pltpu.CompilerParams(
            collective_id=1, has_side_effects=True, vmem_limit_bytes=56 * 2**20
        ),
        cost_estimate=pl.CostEstimate(flops=total * 256, bytes_accessed=8 * 2**20, transcendentals=total),
    )(kv, q)


def attend_backward_kernel(
    members, d_in, kv_all, q_all, out_all, lse, dq_out, dkv_out,
    d_all, q_zero, d_zero, stat, delta, dq_sum, dkv_sum, own_part, sib_send, sib_recv, dkv_send, dq_send,
    d_s, d_r, p_s, p_r, k_s, k_r, g_s, g_r, local,
):
    rows = kv_all.shape[3]
    half = rows // 2
    me = lax.axis_index("ctx")
    shard = lax.axis_index("shard")
    quad, sub = me // members, me % members
    steps = TRIPLE * QUADS

    def peer(step):
        return ((quad + step) % QUADS * members + sub, shard)

    def sibling(step):
        return (quad * members + (sub + step) % members, shard)

    greet([peer(k) for k in range(1, QUADS)] + [sibling(m) for m in range(1, members)])

    def d_copy(h, k):
        return remote(
            d_in.at[(quad + k) % QUADS, h], d_all.at[h, quad], d_s.at[h, k], d_r.at[h, k], peer(k)
        )

    def part_copy(step, m):
        return remote(
            sib_send.at[step % 2, m], sib_recv.at[step, m], p_s.at[step, m], p_r.at[step, m], sibling(m)
        )

    def dkv_copy(h, i, k):
        return remote(
            dkv_send.at[h, i], dkv_out.at[quad, h], k_s.at[h, i], k_r.at[h, i], peer(k)
        )

    def dq_copy(h, k):
        return remote(
            dq_send.at[h, (quad + k) % QUADS], dq_out.at[quad, h], g_s.at[h, k], g_r.at[h, k], peer(k)
        )

    own = pltpu.make_async_copy(d_in.at[quad], d_all.at[:, quad], local.at[0])
    own.start()
    for h in range(TRIPLE):
        for k in range(1, QUADS):
            d_copy(h, k).start()
    own.wait()
    is_low = low_lanes()

    def finish(step):
        h, i = step // QUADS, step % QUADS
        k = (i + 1) % QUADS
        total = own_part[step % 2]
        for m in range(1, members):
            part_copy(step, m).wait_recv()
            total = total + sib_recv[step, m].astype(F32)
        dkv_send[h, i] = total.astype(BF)

        @pl.when(k != 0)
        def _():
            dkv_copy(h, i, k).start()

        @pl.when(k == 0)
        def _():
            own = pltpu.make_async_copy(dkv_send.at[h, i], dkv_out.at[quad, h], local.at[0])
            own.start()
            own.wait()

    def block(step, carry):
        h, i = step // QUADS, step % QUADS
        k = (i + 1) % QUADS
        source = (quad + k) % QUADS

        @pl.when(i == 0)
        def _():
            for j in range(1, QUADS):
                d_copy(h, j).wait_recv()

            def prepare(b, inner):
                q = q_all[h, b]
                d = d_all[h, b]
                zero = jnp.zeros_like(q)
                q_zero[b, 0:half] = jnp.where(is_low, q, zero)
                q_zero[b, half:rows] = jnp.where(is_low, swap_halves(q), zero)
                d_zero[b, 0:half] = jnp.where(is_low, zero, swap_halves(d))
                d_zero[b, half:rows] = jnp.where(is_low, zero, d)
                both = (out_all[h, b] * d.astype(F32)).T
                delta[b, :, 0:half] = jnp.broadcast_to(jnp.sum(both[0:HEAD], axis=0, keepdims=True), (8, half))
                delta[b, :, half:rows] = jnp.broadcast_to(jnp.sum(both[HEAD:], axis=0, keepdims=True), (8, half))
                for part in range(2):
                    for r in range(half // CHUNK):
                        at = part * half + r * CHUNK
                        stat[b, :, at : at + CHUNK] = lse[h, b, part, r]
                dq_sum[b] = jnp.zeros((HEAD, rows), F32)
                return inner

            lax.fori_loop(0, QUADS, prepare, 0)

        keys = kv_all[h, source].reshape(members * rows, 2 * HEAD)
        keys_turned = keys.T[0:HEAD]
        dkv_sum[...] = jnp.zeros_like(dkv_sum)

        def queries_turn(b, inner):
            qz = q_zero[b]
            dz = d_zero[b]
            probs = jnp.exp2(dot(keys, qz, NT) * EXP2_SCALE - stat[b, 0:1, :])
            d_probs = dot(keys, dz, NT)
            d_scores = (probs * (d_probs - delta[b, 0:1, :])).astype(BF)
            dkv_sum[...] += dot(d_scores, qz, NN) * (1.0 / math.sqrt(HEAD)) + dot(probs.astype(BF), dz, NN)
            dq_sum[b] += dot(keys_turned, d_scores, NN)
            return inner

        lax.fori_loop(0, QUADS, queries_turn, 0)

        @pl.when(step > 0)
        def _():
            finish(step - 1)

        own_part[step % 2] = dkv_sum[pl.ds(pl.multiple_of(sub * rows, rows), rows), :]
        for m in range(1, members):
            @pl.when(step > 1)
            def _():
                part_copy(step - 2, m).wait_send()
            target = (sub + m) % members
            sib_send[step % 2, m] = dkv_sum[pl.ds(pl.multiple_of(target * rows, rows), rows), :].astype(BF)
            part_copy(step, m).start()

        @pl.when(i == QUADS - 1)
        def _():
            def give(b, inner):
                turned = dq_sum[b] * (1.0 / math.sqrt(HEAD))
                dq_send[h, b] = jnp.concatenate([turned[:, 0:half], turned[:, half:rows]], axis=0).T.astype(BF)
                return inner

            lax.fori_loop(0, QUADS, give, 0)
            for j in range(1, QUADS):
                dq_copy(h, j).start()
            mine = pltpu.make_async_copy(dq_send.at[h, quad], dq_out.at[quad, h], local.at[0])
            mine.start()
            mine.wait()

        return carry

    lax.fori_loop(0, steps, block, 0)
    finish(steps - 1)
    for m in range(1, members):
        part_copy(steps - 2, m).wait_send()
        part_copy(steps - 1, m).wait_send()
    for h in range(TRIPLE):
        for k in range(1, QUADS):
            d_copy(h, k).wait_send()
            dkv_copy(h, k - 1, k).wait()
            dq_copy(h, k).wait()


def attend_backward(d_context, kv_all, q_all, out_all, lse, members):
    rows = kv_all.shape[3]
    half = rows // 2
    steps = TRIPLE * QUADS
    vm = pl.BlockSpec(memory_space=pltpu.VMEM)
    anywhere = pl.BlockSpec(memory_space=pl.ANY)
    dma = pltpu.SemaphoreType.DMA
    total = TRIPLE * QUADS * rows * QUADS * members * rows
    return pl.pallas_call(
        functools.partial(attend_backward_kernel, members),
        in_specs=[anywhere, vm, vm, vm, vm],
        out_specs=[anywhere, anywhere],
        out_shape=[
            jax.ShapeDtypeStruct((QUADS, TRIPLE, half, 2 * HEAD), BF),
            jax.ShapeDtypeStruct((QUADS, TRIPLE, rows, 2 * HEAD), BF),
        ],
        scratch_shapes=[
            pltpu.VMEM((TRIPLE, QUADS, half, 2 * HEAD), BF),
            pltpu.VMEM((QUADS, rows, 2 * HEAD), BF),
            pltpu.VMEM((QUADS, rows, 2 * HEAD), BF),
            pltpu.VMEM((QUADS, 8, rows), F32),
            pltpu.VMEM((QUADS, 8, rows), F32),
            pltpu.VMEM((QUADS, HEAD, rows), F32),
            pltpu.VMEM((members * rows, 2 * HEAD), F32),
            pltpu.VMEM((2, rows, 2 * HEAD), F32),
            pltpu.VMEM((2, members, rows, 2 * HEAD), BF),
            pltpu.VMEM((steps, members, rows, 2 * HEAD), BF),
            pltpu.VMEM((TRIPLE, QUADS, rows, 2 * HEAD), BF),
            pltpu.VMEM((TRIPLE, QUADS, half, 2 * HEAD), BF),
            dma((TRIPLE, QUADS)), dma((TRIPLE, QUADS)),
            dma((steps, members)), dma((steps, members)),
            dma((TRIPLE, QUADS)), dma((TRIPLE, QUADS)), dma((TRIPLE, QUADS)), dma((TRIPLE, QUADS)),
            dma((2,)),
        ],
        compiler_params=pltpu.CompilerParams(
            collective_id=2, has_side_effects=True, vmem_limit_bytes=56 * 2**20
        ),
        cost_estimate=pl.CostEstimate(flops=total * 640, bytes_accessed=8 * 2**20, transcendentals=total),
    )(d_context, kv_all, q_all, out_all, lse)


def pack_heads(values):
    seqs, rows, _ = values.shape
    split = values.reshape(seqs, 2, rows // 2, HEADS, HEAD)
    return split.transpose(0, 3, 2, 1, 4).reshape(QUADS, TRIPLE, rows // 2, 2 * HEAD)


def unpack_heads(packed, seqs):
    half = packed.shape[2]
    split = packed.reshape(seqs, HEADS, half, 2, HEAD)
    return split.transpose(0, 3, 2, 1, 4).reshape(seqs, 2 * half, HEADS * HEAD)


def shards(
    hidden_in,
    cotangent,
    qkv_weight,
    conv_depth,
    conv_point,
    span_weight,
    conv_value,
    dense_attn,
    dense_conv,
    attn_norm_gain,
    attn_norm_bias,
    ffn_inner,
    ffn_outer,
    out_norm_gain,
    out_norm_bias,
):
    attn_width = HEADS * HEAD
    half_kernel = KERNEL // 2
    seq_count, local_rows, model_width = hidden_in.shape
    gathered = (
        lax.all_gather(qkv_weight, "shard", axis=0, tiled=True),
        lax.all_gather(conv_depth, "shard", axis=1, tiled=True),
        lax.all_gather(conv_point, "shard", axis=0, tiled=True),
        lax.all_gather(span_weight, "shard", axis=0, tiled=True),
        lax.all_gather(conv_value, "shard", axis=0, tiled=True),
        lax.all_gather(dense_attn, "shard", axis=0, tiled=True),
        lax.all_gather(dense_conv, "shard", axis=0, tiled=True),
        lax.all_gather(attn_norm_gain, "shard", axis=0, tiled=True),
        lax.all_gather(attn_norm_bias, "shard", axis=0, tiled=True),
        lax.all_gather(ffn_inner, "shard", axis=1, tiled=True),
        lax.all_gather(ffn_outer, "shard", axis=1, tiled=True),
        lax.all_gather(out_norm_gain, "shard", axis=0, tiled=True),
        lax.all_gather(out_norm_bias, "shard", axis=0, tiled=True),
    )
    (
        full_qkv,
        full_depth,
        full_point,
        full_span,
        full_value,
        full_dense_attn,
        full_dense_conv,
        attn_gain_full,
        attn_bias_full,
        full_inner,
        full_outer,
        out_gain_full,
        out_bias_full,
    ) = gathered
    rows_ext = with_halo(hidden_in, (("ctx", 1),), half_kernel)
    mixed_qkv = jnp.einsum("sti,io->sto", hidden_in, full_qkv, preferred_element_type=jnp.float32)
    query_low = mixed_qkv[..., :attn_width].astype(jnp.bfloat16)
    pair_low = mixed_qkv[..., attn_width:].astype(jnp.bfloat16)
    members = lax.axis_size("ctx") // QUADS
    pair = pair_low.reshape(seq_count, local_rows, 2, HEADS, HEAD).transpose(0, 3, 1, 2, 4)
    pair = pair.reshape(QUADS, TRIPLE, local_rows, 2 * HEAD)
    kv_all, q_all, out_all, lse, context_packed = attend_forward(pair, pack_heads(query_low), members)
    context_low = unpack_heads(context_packed, seq_count)
    depth_fwd = full_depth.astype(jnp.float32)
    spread = rows_ext[:, 0:local_rows].astype(jnp.float32) * depth_fwd[0]
    for offset in range(1, KERNEL):
        spread = (
            spread
            + rows_ext[:, offset : offset + local_rows].astype(jnp.float32) * depth_fwd[offset]
        )
    spread_low = spread.astype(jnp.bfloat16)
    key_conv = jnp.einsum("sti,ia->sta", spread_low, full_point, preferred_element_type=jnp.float32)
    query_f32 = query_low.astype(jnp.float32)
    span_mix = (key_conv * query_f32).astype(jnp.bfloat16)
    logits = jnp.einsum("sta,ak->stk", span_mix, full_span, preferred_element_type=jnp.float32)
    logits = logits.reshape(seq_count, local_rows, HEADS, KERNEL)
    logit_top = jnp.max(logits, axis=-1, keepdims=True)
    exp_logits = jnp.exp(logits - logit_top)
    kernel_soft = exp_logits / jnp.sum(exp_logits, axis=-1, keepdims=True)
    value_ext = jnp.einsum("sti,ia->sta", rows_ext, full_value, preferred_element_type=jnp.float32)
    value_ext = four_heads(value_ext)
    conv_res = kernel_soft[..., 0:1] * value_ext[:, 0:local_rows]
    for offset in range(1, KERNEL):
        conv_res = (
            conv_res
            + kernel_soft[..., offset : offset + 1] * value_ext[:, offset : offset + local_rows]
        )
    conv_low = conv_res.reshape(seq_count, local_rows, attn_width).astype(jnp.bfloat16)
    dense_sum = jnp.einsum(
        "sta,ai->sti", context_low, full_dense_attn, preferred_element_type=jnp.float32
    ) + jnp.einsum("sta,ai->sti", conv_low, full_dense_conv, preferred_element_type=jnp.float32)
    hidden_one, normed_one, inv_one = layer_norm(
        dense_sum + hidden_in.astype(jnp.float32),
        attn_gain_full.astype(jnp.float32),
        attn_bias_full.astype(jnp.float32),
    )
    hidden_low = hidden_one.astype(jnp.bfloat16).reshape(seq_count, local_rows, GROUPS, D // GROUPS)
    inner_act = jnp.einsum(
        "stgi,gio->stgo", hidden_low, full_inner, preferred_element_type=jnp.float32
    )
    active, gelu_pull = jax.vjp(partial(jax.nn.gelu, approximate=False), inner_act)
    active_low = active.astype(jnp.bfloat16)
    outer_sum = jnp.einsum(
        "stgo,goi->stgi", active_low, full_outer, preferred_element_type=jnp.float32
    )
    outer_sum = outer_sum.reshape(seq_count, local_rows, model_width)
    layer_f32, normed_two, inv_two = layer_norm(
        outer_sum + hidden_one, out_gain_full.astype(jnp.float32), out_bias_full.astype(jnp.float32)
    )
    layer_out = layer_f32.astype(jnp.bfloat16)
    d_second, grad_out_gain, grad_out_bias = norm_back(
        normed_two, inv_two, out_gain_full.astype(jnp.float32), cotangent.astype(jnp.float32)
    )
    d_outer_low = d_second.astype(jnp.bfloat16).reshape(seq_count, local_rows, GROUPS, D // GROUPS)
    grad_ffn_outer = jnp.einsum(
        "stgo,stgi->goi", active_low, d_outer_low, preferred_element_type=jnp.float32
    )
    d_active = jnp.einsum(
        "stgi,goi->stgo", d_outer_low, full_outer, preferred_element_type=jnp.float32
    )
    d_inner_low = gelu_pull(d_active)[0].astype(jnp.bfloat16)
    grad_ffn_inner = jnp.einsum(
        "stgi,stgo->gio", hidden_low, d_inner_low, preferred_element_type=jnp.float32
    )
    d_hidden = jnp.einsum(
        "stgo,gio->stgi", d_inner_low, full_inner, preferred_element_type=jnp.float32
    )
    d_hidden = d_hidden.reshape(seq_count, local_rows, model_width) + d_second
    d_first, grad_attn_gain, grad_attn_bias = norm_back(
        normed_one, inv_one, attn_gain_full.astype(jnp.float32), d_hidden
    )
    d_dense_low = d_first.astype(jnp.bfloat16)
    grad_dense_attn = jnp.einsum(
        "sta,sti->ai", context_low, d_dense_low, preferred_element_type=jnp.float32
    )
    grad_dense_conv = jnp.einsum(
        "sta,sti->ai", conv_low, d_dense_low, preferred_element_type=jnp.float32
    )
    d_context_low = jnp.einsum(
        "sti,ai->sta", d_dense_low, full_dense_attn, preferred_element_type=jnp.float32
    ).astype(jnp.bfloat16)
    d_conv_res = four_heads(
        jnp.einsum("sti,ai->sta", d_dense_low, full_dense_conv, preferred_element_type=jnp.float32)
    )
    d_kernel = jnp.concatenate(
        [
            jnp.sum(d_conv_res * value_ext[:, offset : offset + local_rows], axis=-1, keepdims=True)
            for offset in range(KERNEL)
        ],
        axis=-1,
    )
    d_logits = kernel_soft * (d_kernel - jnp.sum(d_kernel * kernel_soft, axis=-1, keepdims=True))
    d_logits_low = d_logits.reshape(seq_count, local_rows, HEADS * KERNEL).astype(jnp.bfloat16)
    grad_span = jnp.einsum(
        "sta,stk->ak", span_mix, d_logits_low, preferred_element_type=jnp.float32
    )
    d_mix = jnp.einsum("stk,ak->sta", d_logits_low, full_span, preferred_element_type=jnp.float32)
    d_key_low = (d_mix * query_f32).astype(jnp.bfloat16)
    d_query_conv = d_mix * key_conv
    grad_point = jnp.einsum(
        "sti,sta->ia", spread_low, d_key_low, preferred_element_type=jnp.float32
    )
    d_spread = jnp.einsum("sta,ia->sti", d_key_low, full_point, preferred_element_type=jnp.float32)
    grad_depth = jnp.stack(
        [
            jnp.sum(
                d_spread * rows_ext[:, offset : offset + local_rows].astype(jnp.float32),
                axis=(0, 1),
            )
            for offset in range(KERNEL)
        ],
        axis=0,
    )
    ext_rows = local_rows + 2 * half_kernel
    d_rows_ext = jnp.zeros((seq_count, ext_rows, model_width), jnp.float32)
    d_value_ext = jnp.zeros((seq_count, ext_rows, HEADS, HEAD), jnp.float32)
    for offset in range(KERNEL):
        d_rows_ext = d_rows_ext + jnp.pad(
            d_spread * depth_fwd[offset], ((0, 0), (offset, 2 * half_kernel - offset), (0, 0))
        )
        d_value_ext = d_value_ext + jnp.pad(
            kernel_soft[..., offset : offset + 1] * d_conv_res,
            ((0, 0), (offset, 2 * half_kernel - offset), (0, 0), (0, 0)),
        )
    grad_ext = jnp.concatenate(
        [d_value_ext.reshape(seq_count, ext_rows, attn_width), d_rows_ext], axis=-1
    )
    edge_rims = jnp.concatenate(
        [grad_ext[:, :half_kernel], grad_ext[:, ext_rows - half_kernel :]], axis=1
    )
    edge_sums = with_halo(edge_rims.astype(jnp.bfloat16), (("ctx", 1),), half_kernel).astype(
        edge_rims.dtype
    )
    own_rows = grad_ext[:, half_kernel : half_kernel + local_rows]
    own_rows = jnp.concatenate(
        [
            own_rows[:, :half_kernel] + edge_sums[:, :half_kernel],
            own_rows[:, half_kernel : local_rows - half_kernel],
            own_rows[:, local_rows - half_kernel :] + edge_sums[:, 3 * half_kernel :],
        ],
        axis=1,
    )
    d_value_low = own_rows[..., :attn_width].astype(jnp.bfloat16)
    d_rows_conv = own_rows[..., attn_width:]
    grad_conv_value = jnp.einsum(
        "sti,sta->ia", hidden_in, d_value_low, preferred_element_type=jnp.float32
    )
    dq_packed, dkv = attend_backward(pack_heads(d_context_low), kv_all, q_all, out_all, lse, members)
    d_query_attn = unpack_heads(dq_packed, seq_count).astype(jnp.float32)
    d_pair = dkv.reshape(seq_count, HEADS, local_rows, 2, HEAD).transpose(0, 2, 3, 1, 4)
    d_pair = d_pair.reshape(seq_count, local_rows, 2 * attn_width)
    d_query_low = (d_query_attn + d_query_conv).astype(jnp.bfloat16)
    d_all_low = jnp.concatenate([d_query_low, d_pair.astype(jnp.bfloat16)], axis=-1)
    grad_qkv = jnp.einsum("sti,sto->io", hidden_in, d_all_low, preferred_element_type=jnp.float32)
    grad_in = (
        d_first
        + jnp.einsum("sto,io->sti", d_all_low, full_qkv, preferred_element_type=jnp.float32)
        + jnp.einsum("sta,ia->sti", d_value_low, full_value, preferred_element_type=jnp.float32)
        + d_rows_conv
    )
    shared = (
        lax.psum_scatter(
            grad_qkv.astype(jnp.bfloat16), "shard", scatter_dimension=0, tiled=True
        ).astype(jnp.float32),
        lax.psum_scatter(
            grad_depth.astype(jnp.bfloat16), "shard", scatter_dimension=1, tiled=True
        ).astype(jnp.float32),
        lax.psum_scatter(
            grad_point.astype(jnp.bfloat16), "shard", scatter_dimension=0, tiled=True
        ).astype(jnp.float32),
        lax.psum_scatter(
            grad_span.astype(jnp.bfloat16), "shard", scatter_dimension=0, tiled=True
        ).astype(jnp.float32),
        lax.psum_scatter(
            grad_conv_value.astype(jnp.bfloat16), "shard", scatter_dimension=0, tiled=True
        ).astype(jnp.float32),
        lax.psum_scatter(
            grad_dense_attn.astype(jnp.bfloat16), "shard", scatter_dimension=0, tiled=True
        ).astype(jnp.float32),
        lax.psum_scatter(
            grad_dense_conv.astype(jnp.bfloat16), "shard", scatter_dimension=0, tiled=True
        ).astype(jnp.float32),
        lax.psum_scatter(
            grad_attn_gain.astype(jnp.bfloat16), "shard", scatter_dimension=0, tiled=True
        ).astype(jnp.float32),
        lax.psum_scatter(
            grad_attn_bias.astype(jnp.bfloat16), "shard", scatter_dimension=0, tiled=True
        ).astype(jnp.float32),
        lax.psum_scatter(
            grad_ffn_inner.astype(jnp.bfloat16), "shard", scatter_dimension=1, tiled=True
        ).astype(jnp.float32),
        lax.psum_scatter(
            grad_ffn_outer.astype(jnp.bfloat16), "shard", scatter_dimension=1, tiled=True
        ).astype(jnp.float32),
        lax.psum_scatter(
            grad_out_gain.astype(jnp.bfloat16), "shard", scatter_dimension=0, tiled=True
        ).astype(jnp.float32),
        lax.psum_scatter(
            grad_out_bias.astype(jnp.bfloat16), "shard", scatter_dimension=0, tiled=True
        ).astype(jnp.float32),
    )
    summed = (
        lax.psum(shared[0].astype(jnp.bfloat16), "ctx").astype(jnp.float32),
        lax.psum(shared[1].astype(jnp.bfloat16), "ctx").astype(jnp.float32),
        lax.psum(shared[2].astype(jnp.bfloat16), "ctx").astype(jnp.float32),
        lax.psum(shared[3].astype(jnp.bfloat16), "ctx").astype(jnp.float32),
        lax.psum(shared[4].astype(jnp.bfloat16), "ctx").astype(jnp.float32),
        lax.psum(shared[5].astype(jnp.bfloat16), "ctx").astype(jnp.float32),
        lax.psum(shared[6].astype(jnp.bfloat16), "ctx").astype(jnp.float32),
        lax.psum(shared[7].astype(jnp.bfloat16), "ctx").astype(jnp.float32),
        lax.psum(shared[8].astype(jnp.bfloat16), "ctx").astype(jnp.float32),
        lax.psum(shared[9].astype(jnp.bfloat16), "ctx").astype(jnp.float32),
        lax.psum(shared[10].astype(jnp.bfloat16), "ctx").astype(jnp.float32),
        lax.psum(shared[11].astype(jnp.bfloat16), "ctx").astype(jnp.float32),
        lax.psum(shared[12].astype(jnp.bfloat16), "ctx").astype(jnp.float32),
    )
    result_grads = tuple(summed)
    return (layer_out, grad_in) + result_grads


def solution(mesh):
    return jax.shard_map(
        shards,
        mesh=mesh,
        in_specs=(
            P("shard", "ctx", None),
            P("shard", "ctx", None),
            P("shard", None),
            P(None, "shard"),
            P("shard", None),
            P("shard", None),
            P("shard", None),
            P("shard", None),
            P("shard", None),
            P("shard"),
            P("shard"),
            P(None, "shard", None),
            P(None, "shard", None),
            P("shard"),
            P("shard"),
        ),
        out_specs=(
            P("shard", "ctx", None),
            P("shard", "ctx", None),
            P("shard", None),
            P(None, "shard"),
            P("shard", None),
            P("shard", None),
            P("shard", None),
            P("shard", None),
            P("shard", None),
            P("shard"),
            P("shard"),
            P(None, "shard", None),
            P(None, "shard", None),
            P("shard"),
            P("shard"),
        ),
        check_vma=False,
    )
```

```python
import functools
from functools import partial
import math

import jax
import jax.numpy as jnp
from jax import lax
from jax.experimental import pallas as pl
from jax.experimental.pallas import tpu as pltpu
from jax.sharding import PartitionSpec as P

D = 768
HEADS = 6
HEAD = 64
GROUPS = 2
KERNEL = 9


norm_eps = 1e-12


def with_halo(block, sides, width):
    for axis, dim in sides:
        count = lax.axis_size(axis)
        forward = [(i, i + 1) for i in range(count - 1)]
        backward = [(target, source) for source, target in forward]
        low = lax.ppermute(
            lax.slice_in_dim(block, block.shape[dim] - width, None, axis=dim), axis, forward
        )
        high = lax.ppermute(lax.slice_in_dim(block, 0, width, axis=dim), axis, backward)
        block = jnp.concatenate([low, block, high], axis=dim)
    return block


def layer_norm(hidden, norm_gain, norm_bias):
    center = hidden - jnp.mean(hidden, axis=-1, keepdims=True)
    inv_std = lax.rsqrt(jnp.mean(center * center, axis=-1, keepdims=True) + norm_eps)
    normed = center * inv_std
    return (normed * norm_gain + norm_bias, normed, inv_std)


def norm_back(normed, inv_std, norm_gain, d_result):
    d_gain = jnp.sum(d_result * normed, axis=(0, 1))
    d_shift = jnp.sum(d_result, axis=(0, 1))
    d_scaled = d_result * norm_gain
    d_hidden = inv_std * (
        d_scaled
        - jnp.mean(d_scaled, axis=-1, keepdims=True)
        - normed * jnp.mean(d_scaled * normed, axis=-1, keepdims=True)
    )
    return (d_hidden, d_gain, d_shift)


def four_heads(values):
    return values.reshape(values.shape[0], values.shape[1], HEADS, HEAD)


BF = jnp.bfloat16
F32 = jnp.float32
MESH_ID = pl.DeviceIdType.MESH
NT = (((1,), (1,)), ((), ()))
NN = (((1,), (0,)), ((), ()))
EXP2_SCALE = math.log2(math.e) / math.sqrt(HEAD)
TRIPLE = 3
QUADS = 4
CHUNK = 128


def dot(a, b, dims):
    return lax.dot_general(a, b, dims, preferred_element_type=F32)


def swap_halves(packed):
    return jnp.concatenate([packed[:, HEAD:], packed[:, :HEAD]], axis=1)


def low_lanes():
    return lax.broadcasted_iota(jnp.int32, (1, 2 * HEAD), 1) < HEAD


def remote(src, dst, send, recv, target):
    return pltpu.make_async_remote_copy(
        src_ref=src, dst_ref=dst, send_sem=send, recv_sem=recv,
        device_id=target, device_id_type=MESH_ID,
    )


def greet(peers):
    barrier = pltpu.get_barrier_semaphore()
    for peer in peers:
        pl.semaphore_signal(barrier, inc=1, device_id=peer, device_id_type=MESH_ID)
    pl.semaphore_wait(barrier, len(peers))


class Place:
    def __init__(self, members, shards):
        self.members, self.shards = members, shards
        self.me = lax.axis_index("ctx")
        self.z = lax.axis_index("shard")
        self.quad, self.sub = self.me // members, self.me % members

    def peer(self, step):
        return ((self.quad + step) % QUADS * self.members + self.sub, self.z)

    def sibling(self, step):
        return (self.quad * self.members + (self.sub + step) % self.members, self.z)

    def behind(self, step):
        return (self.quad + QUADS - step) % QUADS

    def along(self, step):
        return (self.me, (self.z + step) % self.shards)

    def z_behind(self, step):
        return (self.z + self.shards - step) % self.shards

    def greet(self, with_shard):
        peers = [self.peer(k) for k in range(1, QUADS)]
        peers += [self.sibling(m) for m in range(1, self.members)]
        if with_shard:
            peers += [self.along(d) for d in range(1, self.shards)]
        greet(peers)


class Pieces:
    def __init__(self, place, rows, columns, col_split):
        count = QUADS * place.members
        self.place, self.rows, self.col_split = place, rows, col_split
        self.piece_rows = rows // (count // col_split)
        self.piece_cols = columns // col_split

    def at(self, ref, z, quad, sub):
        index = quad * self.place.members + sub
        top = pl.multiple_of(z * self.rows + index // self.col_split * self.piece_rows, 16)
        left = pl.multiple_of(index % self.col_split * self.piece_cols, 128)
        return ref.at[pl.ds(top, self.piece_rows), pl.ds(left, self.piece_cols)]


def fits(rows, columns, members, col_split):
    count = QUADS * members
    if count % col_split:
        return False
    row_split = count // col_split
    return rows % (16 * row_split) == 0 and columns % (128 * col_split) == 0


class Gather:
    def __init__(self, place, shard_ref, full_ref, col_split, sems):
        self.place, self.shard_ref, self.full_ref = place, shard_ref, full_ref
        rows, columns = shard_ref.shape
        self.rows = rows
        self.pieces = Pieces(place, rows, columns, col_split)
        self.z_s, self.z_r, self.q_s, self.q_r, self.f_s, self.f_r, self.local = sems

    @staticmethod
    def semaphores(members, shards):
        dma = pltpu.SemaphoreType.DMA
        return [
            dma((shards,)), dma((shards,)), dma((shards, QUADS)), dma((shards, QUADS)),
            dma((shards, QUADS, members)), dma((shards, QUADS, members)), dma((1,)),
        ]

    def z_copy(self, d):
        p = self.place
        return remote(
            self.pieces.at(self.shard_ref, 0, p.quad, p.sub), self.pieces.at(self.full_ref, p.z, p.quad, p.sub),
            self.z_s.at[d], self.z_r.at[d], p.along(d),
        )

    def q_copy(self, d, k):
        p = self.place
        block = self.pieces.at(self.full_ref, p.z_behind(d), p.quad, p.sub)
        return remote(block, block, self.q_s.at[d, k], self.q_r.at[d, k], p.peer(k))

    def f_copy(self, d, k, m):
        p = self.place
        block = self.pieces.at(self.full_ref, p.z_behind(d), p.behind(k), p.sub)
        return remote(block, block, self.f_s.at[d, k, m], self.f_r.at[d, k, m], p.sibling(m))

    def own_copy(self):
        top = pl.multiple_of(self.place.z * self.rows, 16)
        return pltpu.make_async_copy(
            self.shard_ref, self.full_ref.at[pl.ds(top, self.rows), :], self.local.at[0]
        )

    def start(self):
        for d in range(1, self.place.shards):
            self.z_copy(d).start()
        self.own_copy().start()

    def relay(self):
        for d in range(1, self.place.shards):
            self.z_copy(d).wait_recv()
            for k in range(1, QUADS):
                self.q_copy(d, k).start()
            for m in range(1, self.place.members):
                self.f_copy(d, 0, m).start()

    def share(self):
        for d in range(1, self.place.shards):
            for k in range(1, QUADS):
                self.q_copy(d, k).wait_recv()
                for m in range(1, self.place.members):
                    self.f_copy(d, k, m).start()

    def end(self):
        for d in range(1, self.place.shards):
            self.z_copy(d).wait_send()
            for k in range(QUADS):
                if k:
                    self.q_copy(d, k).wait_send()
                for m in range(1, self.place.members):
                    self.f_copy(d, k, m).wait()
        self.own_copy().wait()


class Reduce:
    def __init__(self, place, part_ref, out_ref, col_split, scratch):
        self.place, self.part_ref, self.out_ref = place, part_ref, out_ref
        self.piece_rows, self.piece_cols = part_ref.shape[3:]
        rows, columns = out_ref.shape
        self.pieces = Pieces(place, rows, columns, col_split)
        (
            self.half, self.half_in, self.quad_in, self.block, self.z_in, self.last,
            self.h_s, self.h_r, self.q_s, self.q_r, self.z_s, self.z_r, self.a_s, self.a_r, self.f_s, self.f_r, self.local,
        ) = scratch

    @staticmethod
    def scratch(members, shards, rows, columns):
        dma = pltpu.SemaphoreType.DMA
        return [
            pltpu.VMEM((shards, QUADS, rows, columns), BF),
            pltpu.VMEM((members, shards, QUADS, rows, columns), BF),
            pltpu.VMEM((QUADS, shards, rows, columns), BF),
            pltpu.VMEM((shards, rows, columns), BF),
            pltpu.VMEM((shards, rows, columns), BF),
            pltpu.VMEM((rows, columns), BF),
            dma((members,)), dma((members,)), dma((QUADS,)), dma((QUADS,)), dma((shards,)), dma((shards,)),
            dma((QUADS,)), dma((QUADS,)), dma((QUADS, members)), dma((QUADS, members)), dma((1,)),
        ]

    def h_copy(self, m):
        p = self.place
        return remote(
            self.part_ref.at[(p.sub + m) % p.members], self.half_in.at[m], self.h_s.at[m], self.h_r.at[m], p.sibling(m)
        )

    def q_copy(self, k):
        p = self.place
        return remote(
            self.half.at[:, (p.quad + k) % QUADS], self.quad_in.at[k], self.q_s.at[k], self.q_r.at[k], p.peer(k)
        )

    def z_copy(self, d):
        p = self.place
        return remote(
            self.block.at[(p.z + d) % p.shards], self.z_in.at[d], self.z_s.at[d], self.z_r.at[d], p.along(d)
        )

    def a_copy(self, k):
        p = self.place
        return remote(
            self.last, self.pieces.at(self.out_ref, 0, p.quad, p.sub), self.a_s.at[k], self.a_r.at[k], p.peer(k)
        )

    def f_copy(self, k, m):
        p = self.place
        block = self.pieces.at(self.out_ref, 0, p.behind(k), p.sub)
        return remote(block, block, self.f_s.at[k, m], self.f_r.at[k, m], p.sibling(m))

    def own_copy(self):
        p = self.place
        return pltpu.make_async_copy(
            self.last, self.pieces.at(self.out_ref, 0, p.quad, p.sub), self.local.at[0]
        )

    def start(self):
        for m in range(1, self.place.members):
            self.h_copy(m).start()

    def to_quads(self):
        for m in range(1, self.place.members):
            self.h_copy(m).wait_recv()

        def turn(i, carry):
            z, q = i // QUADS, i % QUADS
            total = self.part_ref[self.place.sub, z, q].astype(F32)
            for m in range(1, self.place.members):
                total = total + self.half_in[m, z, q].astype(F32)
            self.half[z, q] = total.astype(BF)
            return carry

        lax.fori_loop(0, self.place.shards * QUADS, turn, 0)
        for k in range(1, QUADS):
            self.q_copy(k).start()

    def to_shards(self):
        for k in range(1, QUADS):
            self.q_copy(k).wait_recv()

        def turn(z, carry):
            total = self.half[z, self.place.quad].astype(F32)
            for k in range(1, QUADS):
                total = total + self.quad_in[k, z].astype(F32)
            self.block[z] = total.astype(BF)
            return carry

        lax.fori_loop(0, self.place.shards, turn, 0)
        for d in range(1, self.place.shards):
            self.z_copy(d).start()

    def give(self):
        total = self.block[self.place.z].astype(F32)
        for d in range(1, self.place.shards):
            self.z_copy(d).wait_recv()
            total = total + self.z_in[d].astype(F32)
        self.last[...] = total.astype(BF)
        for k in range(1, QUADS):
            self.a_copy(k).start()
        self.own_copy().start()
        self.own_copy().wait()
        for m in range(1, self.place.members):
            self.f_copy(0, m).start()

    def share(self):
        for k in range(1, QUADS):
            self.a_copy(k).wait_recv()
            for m in range(1, self.place.members):
                self.f_copy(k, m).start()

    def end(self):
        for m in range(1, self.place.members):
            self.h_copy(m).wait_send()
        for k in range(1, QUADS):
            self.q_copy(k).wait_send()
            self.a_copy(k).wait_send()
        for d in range(1, self.place.shards):
            self.z_copy(d).wait_send()
        for k in range(QUADS):
            for m in range(1, self.place.members):
                self.f_copy(k, m).wait()


def cut(part, members, shards, col_split):
    count = QUADS * members
    row_split = count // col_split
    piece_rows = part.shape[0] // (shards * row_split)
    piece_cols = part.shape[1] // col_split
    split = part.astype(BF).reshape(shards, row_split, piece_rows, col_split, piece_cols)
    split = split.transpose(0, 1, 3, 2, 4).reshape(shards, QUADS, members, piece_rows, piece_cols)
    return split.transpose(2, 0, 1, 3, 4)


def gather_kernel(members, shards, split, shard_ref, full_ref, *sems):
    place = Place(members, shards)
    place.greet(True)
    one = Gather(place, shard_ref, full_ref, split, sems)
    one.start()
    one.relay()
    one.share()
    one.end()


def gather_weight(block, members, shards, split, number):
    anywhere = pl.BlockSpec(memory_space=pl.ANY)
    return pl.pallas_call(
        functools.partial(gather_kernel, members, shards, split),
        in_specs=[anywhere],
        out_specs=anywhere,
        out_shape=jax.ShapeDtypeStruct((shards * block.shape[0], block.shape[1]), BF),
        scratch_shapes=Gather.semaphores(members, shards),
        compiler_params=pltpu.CompilerParams(collective_id=number, has_side_effects=True),
    )(block)


def reduce_kernel(members, shards, split, part_ref, out_ref, *scratch):
    place = Place(members, shards)
    place.greet(True)
    one = Reduce(place, part_ref, out_ref, split, scratch)
    one.start()
    one.to_quads()
    one.to_shards()
    one.give()
    one.share()
    one.end()


def reduce_weight(part, members, shards, split, number):
    pieces = cut(part, members, shards, split)
    rows = part.shape[0] // shards
    return pl.pallas_call(
        functools.partial(reduce_kernel, members, shards, split),
        in_specs=[pl.BlockSpec(memory_space=pltpu.VMEM)],
        out_specs=pl.BlockSpec(memory_space=pl.ANY),
        out_shape=jax.ShapeDtypeStruct((rows, part.shape[1]), BF),
        scratch_shapes=Reduce.scratch(members, shards, *pieces.shape[3:]),
        compiler_params=pltpu.CompilerParams(
            collective_id=number, has_side_effects=True, vmem_limit_bytes=56 * 2**20
        ),
    )(pieces)


def attend_forward_kernel(members, shards, splits, *refs):
    count = len(splits)
    kv_in, q_in, *blocks = refs[: 2 + count]
    kv_all, q_all, out_all, lse, ctx_out, *fulls = refs[2 + count : 7 + 2 * count]
    out_send, kv_s, kv_r, q_s, q_r, f_s, f_r, o_s, o_r, local, *sems = refs[7 + 2 * count :]
    rows = kv_in.shape[2]
    half = rows // 2
    place = Place(members, shards)
    quad, sub, peer, sibling = place.quad, place.sub, place.peer, place.sibling
    place.greet(bool(splits))

    def kv_copy(h, k):
        return remote(
            kv_in.at[(quad + k) % QUADS, h], kv_all.at[h, quad, sub], kv_s.at[h, k], kv_r.at[h, k], peer(k)
        )

    def q_copy(h, k):
        return remote(
            q_in.at[(quad + k) % QUADS, h], q_all.at[h, quad], q_s.at[h, k], q_r.at[h, k], peer(k)
        )

    def forward_copy(h, m):
        return remote(
            kv_all.at[h, :, sub], kv_all.at[h, :, sub], f_s.at[h, m], f_r.at[h, m], sibling(m)
        )

    def out_copy(h, i, k):
        return remote(
            out_send.at[h, i], ctx_out.at[quad, h], o_s.at[h, i], o_r.at[h, i], peer(k)
        )

    own_kv = pltpu.make_async_copy(kv_in.at[quad], kv_all.at[:, quad, sub], local.at[0])
    own_q = pltpu.make_async_copy(q_in.at[quad], q_all.at[:, quad], local.at[1])
    own_kv.start()
    own_q.start()
    gathers = [
        Gather(place, block, full, split, sems[7 * j : 7 * j + 7])
        for j, (block, full, split) in enumerate(zip(blocks, fulls, splits))
    ]
    for gather in gathers:
        gather.start()
    for h in range(TRIPLE):
        for k in range(1, QUADS):
            kv_copy(h, k).start()
            q_copy(h, k).start()
    own_kv.wait()
    own_q.wait()

    def receive(h):
        for k in range(1, QUADS):
            kv_copy(h, k).wait_recv()
            q_copy(h, k).wait_recv()
        for m in range(1, members):
            forward_copy(h, m).start()

    receive(0)
    is_low = low_lanes()

    def block(step, carry):
        h, i = step // QUADS, step % QUADS
        k = (i + 1) % QUADS
        source = (quad + k) % QUADS

        @pl.when(i == 0)
        def _():
            for m in range(1, members):
                forward_copy(h, m).wait_recv()

        keys = kv_all[h].reshape(QUADS * members * rows, 2 * HEAD)

        def rows_turn(r, inner):
            at = pl.multiple_of(r * CHUNK, CHUNK)
            packed = q_all[h, source, pl.ds(at, CHUNK), :]
            outs = []
            stats = []
            for part in range(2):
                q = jnp.where(is_low, packed if part == 0 else swap_halves(packed), jnp.zeros_like(packed))
                scores = dot(q, keys, NT)
                top = jnp.max(scores, axis=1, keepdims=True)
                probs = jnp.exp2((scores - top) * EXP2_SCALE)
                total = jnp.sum(probs, axis=1, keepdims=True)
                outs.append(dot(probs.astype(BF), keys, NN) / total)
                stats.append(top * EXP2_SCALE + jnp.log2(total))
            both = jnp.where(is_low, swap_halves(outs[0]), outs[1])
            out_all[h, source, pl.ds(at, CHUNK), :] = both
            out_send[h, i, pl.ds(at, CHUNK), :] = both.astype(BF)
            for part in range(2):
                lse[h, source, part, r] = jnp.broadcast_to(stats[part], (CHUNK, CHUNK)).T[0:8, :]
            return inner

        lax.fori_loop(0, half // CHUNK, rows_turn, 0)

        @pl.when(k != 0)
        def _():
            out_copy(h, i, k).start()

        @pl.when(k == 0)
        def _():
            own = pltpu.make_async_copy(out_send.at[h, i], ctx_out.at[quad, h], local.at[0])
            own.start()
            own.wait()

        @pl.when((i == 2) & (h < TRIPLE - 1))
        def _():
            receive(h + 1)

        if gathers:

            @pl.when(step == 4)
            def _():
                for gather in gathers:
                    gather.relay()

            @pl.when(step == TRIPLE * QUADS - 1)
            def _():
                for gather in gathers:
                    gather.share()

        return carry

    lax.fori_loop(0, TRIPLE * QUADS, block, 0)
    for gather in gathers:
        gather.end()
    for h in range(TRIPLE):
        for k in range(1, QUADS):
            out_copy(h, k - 1, k).wait()
            kv_copy(h, k).wait_send()
            q_copy(h, k).wait_send()
        for m in range(1, members):
            forward_copy(h, m).wait_send()


def attend_forward(kv, q, members, shards, blocks, splits):
    rows = kv.shape[2]
    half = rows // 2
    vm = pl.BlockSpec(memory_space=pltpu.VMEM)
    anywhere = pl.BlockSpec(memory_space=pl.ANY)
    dma = pltpu.SemaphoreType.DMA
    total = TRIPLE * QUADS * rows * QUADS * members * rows
    return pl.pallas_call(
        functools.partial(attend_forward_kernel, members, shards, splits),
        in_specs=[anywhere, anywhere] + [anywhere] * len(blocks),
        out_specs=[vm, vm, vm, vm, anywhere] + [anywhere] * len(blocks),
        out_shape=[
            jax.ShapeDtypeStruct((TRIPLE, QUADS, members, rows, 2 * HEAD), BF),
            jax.ShapeDtypeStruct((TRIPLE, QUADS, half, 2 * HEAD), BF),
            jax.ShapeDtypeStruct((TRIPLE, QUADS, half, 2 * HEAD), F32),
            jax.ShapeDtypeStruct((TRIPLE, QUADS, 2, half // CHUNK, 8, CHUNK), F32),
            jax.ShapeDtypeStruct((QUADS, TRIPLE, half, 2 * HEAD), BF),
        ]
        + [jax.ShapeDtypeStruct((shards * block.shape[0], block.shape[1]), BF) for block in blocks],
        scratch_shapes=[
            pltpu.VMEM((TRIPLE, QUADS, half, 2 * HEAD), BF),
            dma((TRIPLE, QUADS)), dma((TRIPLE, QUADS)), dma((TRIPLE, QUADS)), dma((TRIPLE, QUADS)),
            dma((TRIPLE, members)), dma((TRIPLE, members)), dma((TRIPLE, QUADS)), dma((TRIPLE, QUADS)),
            dma((2,)),
        ]
        + Gather.semaphores(members, shards) * len(blocks),
        compiler_params=pltpu.CompilerParams(
            collective_id=1, has_side_effects=True, vmem_limit_bytes=56 * 2**20
        ),
        cost_estimate=pl.CostEstimate(flops=total * 256, bytes_accessed=8 * 2**20, transcendentals=total),
    )(kv, q, *blocks)


def attend_backward_kernel(members, shards, splits, *refs):
    count = len(splits)
    d_in, kv_all, q_all, out_all, lse, *parts = refs[: 5 + count]
    dq_out, dkv_out, *sums = refs[5 + count : 7 + 2 * count]
    (
        d_all, q_zero, d_zero, stat, delta, dq_sum, dkv_sum, own_part, sib_send, sib_recv, dkv_send, dq_send,
        d_s, d_r, p_s, p_r, k_s, k_r, g_s, g_r, local, *scratch,
    ) = refs[7 + 2 * count :]
    rows = kv_all.shape[3]
    half = rows // 2
    steps = TRIPLE * QUADS
    place = Place(members, shards)
    quad, sub, peer, sibling = place.quad, place.sub, place.peer, place.sibling
    place.greet(bool(splits))
    reduces = [
        Reduce(place, one, total, split, scratch[17 * j : 17 * j + 17])
        for j, (one, total, split) in enumerate(zip(parts, sums, splits))
    ]

    def d_copy(h, k):
        return remote(
            d_in.at[(quad + k) % QUADS, h], d_all.at[h, quad], d_s.at[h, k], d_r.at[h, k], peer(k)
        )

    def part_copy(step, m):
        return remote(
            sib_send.at[step % 2, m], sib_recv.at[step, m], p_s.at[step, m], p_r.at[step, m], sibling(m)
        )

    def dkv_copy(h, i, k):
        return remote(
            dkv_send.at[h, i], dkv_out.at[quad, h], k_s.at[h, i], k_r.at[h, i], peer(k)
        )

    def dq_copy(h, k):
        return remote(
            dq_send.at[h, (quad + k) % QUADS], dq_out.at[quad, h], g_s.at[h, k], g_r.at[h, k], peer(k)
        )

    own = pltpu.make_async_copy(d_in.at[quad], d_all.at[:, quad], local.at[0])
    own.start()
    for h in range(TRIPLE):
        for k in range(1, QUADS):
            d_copy(h, k).start()
    for one in reduces:
        one.start()
    own.wait()
    is_low = low_lanes()

    def finish(step):
        h, i = step // QUADS, step % QUADS
        k = (i + 1) % QUADS
        total = own_part[step % 2]
        for m in range(1, members):
            part_copy(step, m).wait_recv()
            total = total + sib_recv[step, m].astype(F32)
        dkv_send[h, i] = total.astype(BF)

        @pl.when(k != 0)
        def _():
            dkv_copy(h, i, k).start()

        @pl.when(k == 0)
        def _():
            own = pltpu.make_async_copy(dkv_send.at[h, i], dkv_out.at[quad, h], local.at[0])
            own.start()
            own.wait()

    def block(step, carry):
        h, i = step // QUADS, step % QUADS
        k = (i + 1) % QUADS
        source = (quad + k) % QUADS

        @pl.when(i == 0)
        def _():
            for j in range(1, QUADS):
                d_copy(h, j).wait_recv()

            def prepare(b, inner):
                q = q_all[h, b]
                d = d_all[h, b]
                zero = jnp.zeros_like(q)
                q_zero[b, 0:half] = jnp.where(is_low, q, zero)
                q_zero[b, half:rows] = jnp.where(is_low, swap_halves(q), zero)
                d_zero[b, 0:half] = jnp.where(is_low, zero, swap_halves(d))
                d_zero[b, half:rows] = jnp.where(is_low, zero, d)
                both = (out_all[h, b] * d.astype(F32)).T
                delta[b, :, 0:half] = jnp.broadcast_to(jnp.sum(both[0:HEAD], axis=0, keepdims=True), (8, half))
                delta[b, :, half:rows] = jnp.broadcast_to(jnp.sum(both[HEAD:], axis=0, keepdims=True), (8, half))
                for part in range(2):
                    for r in range(half // CHUNK):
                        at = part * half + r * CHUNK
                        stat[b, :, at : at + CHUNK] = lse[h, b, part, r]
                dq_sum[b] = jnp.zeros((HEAD, rows), F32)
                return inner

            lax.fori_loop(0, QUADS, prepare, 0)

        keys = kv_all[h, source].reshape(members * rows, 2 * HEAD)
        keys_turned = keys.T[0:HEAD]
        dkv_sum[...] = jnp.zeros_like(dkv_sum)

        def queries_turn(b, inner):
            qz = q_zero[b]
            dz = d_zero[b]
            probs = jnp.exp2(dot(keys, qz, NT) * EXP2_SCALE - stat[b, 0:1, :])
            d_probs = dot(keys, dz, NT)
            d_scores = (probs * (d_probs - delta[b, 0:1, :])).astype(BF)
            dkv_sum[...] += dot(d_scores, qz, NN) * (1.0 / math.sqrt(HEAD)) + dot(probs.astype(BF), dz, NN)
            dq_sum[b] += dot(keys_turned, d_scores, NN)
            return inner

        lax.fori_loop(0, QUADS, queries_turn, 0)

        @pl.when(step > 0)
        def _():
            finish(step - 1)

        own_part[step % 2] = dkv_sum[pl.ds(pl.multiple_of(sub * rows, rows), rows), :]
        for m in range(1, members):
            @pl.when(step > 1)
            def _():
                part_copy(step - 2, m).wait_send()
            target = (sub + m) % members
            sib_send[step % 2, m] = dkv_sum[pl.ds(pl.multiple_of(target * rows, rows), rows), :].astype(BF)
            part_copy(step, m).start()

        @pl.when(i == QUADS - 1)
        def _():
            def give(b, inner):
                turned = dq_sum[b] * (1.0 / math.sqrt(HEAD))
                dq_send[h, b] = jnp.concatenate([turned[:, 0:half], turned[:, half:rows]], axis=0).T.astype(BF)
                return inner

            lax.fori_loop(0, QUADS, give, 0)
            for j in range(1, QUADS):
                dq_copy(h, j).start()
            mine = pltpu.make_async_copy(dq_send.at[h, quad], dq_out.at[quad, h], local.at[0])
            mine.start()
            mine.wait()

        for j, one in enumerate(reduces):
            for at, stage in ((j, one.to_quads), (j + 4, one.to_shards), (j + 6, one.give), (j + 8, one.share)):

                @pl.when(step == at)
                def _(stage=stage):
                    stage()

        return carry

    lax.fori_loop(0, steps, block, 0)
    finish(steps - 1)
    for m in range(1, members):
        part_copy(steps - 2, m).wait_send()
        part_copy(steps - 1, m).wait_send()
    for h in range(TRIPLE):
        for k in range(1, QUADS):
            d_copy(h, k).wait_send()
            dkv_copy(h, k - 1, k).wait()
            dq_copy(h, k).wait()
    for one in reduces:
        one.end()


def attend_backward(d_context, kv_all, q_all, out_all, lse, members, shards, parts, splits):
    rows = kv_all.shape[3]
    half = rows // 2
    steps = TRIPLE * QUADS
    vm = pl.BlockSpec(memory_space=pltpu.VMEM)
    anywhere = pl.BlockSpec(memory_space=pl.ANY)
    dma = pltpu.SemaphoreType.DMA
    total = TRIPLE * QUADS * rows * QUADS * members * rows
    return pl.pallas_call(
        functools.partial(attend_backward_kernel, members, shards, splits),
        in_specs=[anywhere, vm, vm, vm, vm] + [vm] * len(parts),
        out_specs=[anywhere, anywhere] + [anywhere] * len(parts),
        out_shape=[
            jax.ShapeDtypeStruct((QUADS, TRIPLE, half, 2 * HEAD), BF),
            jax.ShapeDtypeStruct((QUADS, TRIPLE, rows, 2 * HEAD), BF),
        ]
        + [jax.ShapeDtypeStruct(shape, BF) for _, shape in parts],
        scratch_shapes=[
            pltpu.VMEM((TRIPLE, QUADS, half, 2 * HEAD), BF),
            pltpu.VMEM((QUADS, rows, 2 * HEAD), BF),
            pltpu.VMEM((QUADS, rows, 2 * HEAD), BF),
            pltpu.VMEM((QUADS, 8, rows), F32),
            pltpu.VMEM((QUADS, 8, rows), F32),
            pltpu.VMEM((QUADS, HEAD, rows), F32),
            pltpu.VMEM((members * rows, 2 * HEAD), F32),
            pltpu.VMEM((2, rows, 2 * HEAD), F32),
            pltpu.VMEM((2, members, rows, 2 * HEAD), BF),
            pltpu.VMEM((steps, members, rows, 2 * HEAD), BF),
            pltpu.VMEM((TRIPLE, QUADS, rows, 2 * HEAD), BF),
            pltpu.VMEM((TRIPLE, QUADS, half, 2 * HEAD), BF),
            dma((TRIPLE, QUADS)), dma((TRIPLE, QUADS)),
            dma((steps, members)), dma((steps, members)),
            dma((TRIPLE, QUADS)), dma((TRIPLE, QUADS)), dma((TRIPLE, QUADS)), dma((TRIPLE, QUADS)),
            dma((2,)),
        ]
        + sum((Reduce.scratch(members, shards, *one.shape[3:]) for one, _ in parts), []),
        compiler_params=pltpu.CompilerParams(
            collective_id=2, has_side_effects=True, vmem_limit_bytes=56 * 2**20
        ),
        cost_estimate=pl.CostEstimate(flops=total * 640, bytes_accessed=8 * 2**20, transcendentals=total),
    )(d_context, kv_all, q_all, out_all, lse, *[one for one, _ in parts])


def pack_heads(values):
    seqs, rows, _ = values.shape
    split = values.reshape(seqs, 2, rows // 2, HEADS, HEAD)
    return split.transpose(0, 3, 2, 1, 4).reshape(QUADS, TRIPLE, rows // 2, 2 * HEAD)


def unpack_heads(packed, seqs):
    half = packed.shape[2]
    split = packed.reshape(seqs, HEADS, half, 2, HEAD)
    return split.transpose(0, 3, 2, 1, 4).reshape(seqs, 2 * half, HEADS * HEAD)


SPLITS = (2, 4, 1)


def shards(
    hidden_in,
    cotangent,
    qkv_weight,
    conv_depth,
    conv_point,
    span_weight,
    conv_value,
    dense_attn,
    dense_conv,
    attn_norm_gain,
    attn_norm_bias,
    ffn_inner,
    ffn_outer,
    out_norm_gain,
    out_norm_bias,
):
    attn_width = HEADS * HEAD
    half_kernel = KERNEL // 2
    seq_count, local_rows, model_width = hidden_in.shape
    members = lax.axis_size("ctx") // QUADS
    shard_count = lax.axis_size("shard")
    width_rows = model_width // shard_count
    head_rows = attn_width // shard_count
    small = jnp.concatenate(
        [
            jnp.pad(span_weight, ((0, width_rows - head_rows), (0, 64 - HEADS * KERNEL))),
            conv_depth.T,
            jnp.stack([attn_norm_gain, attn_norm_bias, out_norm_gain, out_norm_bias], axis=1),
            jnp.zeros((width_rows, 128 - 64 - KERNEL - 4), jnp.bfloat16),
        ],
        axis=1,
    )
    first_block = jnp.concatenate([qkv_weight, conv_value, conv_point, small], axis=1)
    second_block = jnp.concatenate([dense_attn, dense_conv, ffn_inner[0], ffn_inner[1]], axis=1)
    third_block = jnp.concatenate([ffn_outer[0], ffn_outer[1]], axis=1)
    shapes = (first_block.shape, second_block.shape, third_block.shape)
    by_kernel = all(fits(*shape, members, split) for shape, split in zip(shapes, SPLITS))
    if by_kernel:
        first = gather_weight(first_block, members, shard_count, SPLITS[0], 3)
    else:
        first = lax.all_gather(first_block, "shard", axis=0, tiled=True)
        second = lax.all_gather(second_block, "shard", axis=0, tiled=True)
        third = lax.all_gather(third_block, "shard", axis=0, tiled=True)
    full_qkv = first[:, : 3 * attn_width]
    full_value = first[:, 3 * attn_width : 4 * attn_width]
    full_point = first[:, 4 * attn_width : 5 * attn_width]
    full_small = first[:, 5 * attn_width :]
    full_span = full_small.reshape(shard_count, width_rows, 128)[:, :head_rows, : HEADS * KERNEL]
    full_span = full_span.reshape(attn_width, HEADS * KERNEL)
    full_depth = full_small[:, 64 : 64 + KERNEL].T
    attn_gain_full, attn_bias_full, out_gain_full, out_bias_full = full_small[:, 64 + KERNEL : 68 + KERNEL].T
    rows_ext = with_halo(hidden_in, (("ctx", 1),), half_kernel)
    mixed_qkv = jnp.einsum("sti,io->sto", hidden_in, full_qkv, preferred_element_type=jnp.float32)
    query_low = mixed_qkv[..., :attn_width].astype(jnp.bfloat16)
    pair_low = mixed_qkv[..., attn_width:].astype(jnp.bfloat16)
    pair = pair_low.reshape(seq_count, local_rows, 2, HEADS, HEAD).transpose(0, 3, 1, 2, 4)
    pair = pair.reshape(QUADS, TRIPLE, local_rows, 2 * HEAD)
    kv_all, q_all, out_all, lse, context_packed, *gathered = attend_forward(
        pair, pack_heads(query_low), members, shard_count,
        (second_block, third_block) if by_kernel else (), SPLITS[1:] if by_kernel else (),
    )
    if by_kernel:
        second, third = gathered
    full_dense_attn = second[:, :model_width]
    full_dense_conv = second[:, model_width : 2 * model_width]
    full_inner = second[:, 2 * model_width :].reshape(D // GROUPS, GROUPS, -1).transpose(1, 0, 2)
    full_outer = third.reshape(-1, GROUPS, D // GROUPS).transpose(1, 0, 2)
    context_low = unpack_heads(context_packed, seq_count)
    depth_fwd = full_depth.astype(jnp.float32)
    spread = rows_ext[:, 0:local_rows].astype(jnp.float32) * depth_fwd[0]
    for offset in range(1, KERNEL):
        spread = (
            spread
            + rows_ext[:, offset : offset + local_rows].astype(jnp.float32) * depth_fwd[offset]
        )
    spread_low = spread.astype(jnp.bfloat16)
    key_conv = jnp.einsum("sti,ia->sta", spread_low, full_point, preferred_element_type=jnp.float32)
    query_f32 = query_low.astype(jnp.float32)
    span_mix = (key_conv * query_f32).astype(jnp.bfloat16)
    logits = jnp.einsum("sta,ak->stk", span_mix, full_span, preferred_element_type=jnp.float32)
    logits = logits.reshape(seq_count, local_rows, HEADS, KERNEL)
    logit_top = jnp.max(logits, axis=-1, keepdims=True)
    exp_logits = jnp.exp(logits - logit_top)
    kernel_soft = exp_logits / jnp.sum(exp_logits, axis=-1, keepdims=True)
    value_ext = jnp.einsum("sti,ia->sta", rows_ext, full_value, preferred_element_type=jnp.float32)
    value_ext = four_heads(value_ext)
    conv_res = kernel_soft[..., 0:1] * value_ext[:, 0:local_rows]
    for offset in range(1, KERNEL):
        conv_res = (
            conv_res
            + kernel_soft[..., offset : offset + 1] * value_ext[:, offset : offset + local_rows]
        )
    conv_low = conv_res.reshape(seq_count, local_rows, attn_width).astype(jnp.bfloat16)
    dense_sum = jnp.einsum(
        "sta,ai->sti", context_low, full_dense_attn, preferred_element_type=jnp.float32
    ) + jnp.einsum("sta,ai->sti", conv_low, full_dense_conv, preferred_element_type=jnp.float32)
    hidden_one, normed_one, inv_one = layer_norm(
        dense_sum + hidden_in.astype(jnp.float32),
        attn_gain_full.astype(jnp.float32),
        attn_bias_full.astype(jnp.float32),
    )
    hidden_low = hidden_one.astype(jnp.bfloat16).reshape(seq_count, local_rows, GROUPS, D // GROUPS)
    inner_act = jnp.einsum(
        "stgi,gio->stgo", hidden_low, full_inner, preferred_element_type=jnp.float32
    )
    active, gelu_pull = jax.vjp(partial(jax.nn.gelu, approximate=False), inner_act)
    active_low = active.astype(jnp.bfloat16)
    outer_sum = jnp.einsum(
        "stgo,goi->stgi", active_low, full_outer, preferred_element_type=jnp.float32
    )
    outer_sum = outer_sum.reshape(seq_count, local_rows, model_width)
    layer_f32, normed_two, inv_two = layer_norm(
        outer_sum + hidden_one, out_gain_full.astype(jnp.float32), out_bias_full.astype(jnp.float32)
    )
    layer_out = layer_f32.astype(jnp.bfloat16)
    d_second, grad_out_gain, grad_out_bias = norm_back(
        normed_two, inv_two, out_gain_full.astype(jnp.float32), cotangent.astype(jnp.float32)
    )
    d_outer_low = d_second.astype(jnp.bfloat16).reshape(seq_count, local_rows, GROUPS, D // GROUPS)
    grad_ffn_outer = jnp.einsum(
        "stgo,stgi->goi", active_low, d_outer_low, preferred_element_type=jnp.float32
    )
    d_active = jnp.einsum(
        "stgi,goi->stgo", d_outer_low, full_outer, preferred_element_type=jnp.float32
    )
    d_inner_low = gelu_pull(d_active)[0].astype(jnp.bfloat16)
    grad_ffn_inner = jnp.einsum(
        "stgi,stgo->gio", hidden_low, d_inner_low, preferred_element_type=jnp.float32
    )
    d_hidden = jnp.einsum(
        "stgo,gio->stgi", d_inner_low, full_inner, preferred_element_type=jnp.float32
    )
    d_hidden = d_hidden.reshape(seq_count, local_rows, model_width) + d_second
    d_first, grad_attn_gain, grad_attn_bias = norm_back(
        normed_one, inv_one, attn_gain_full.astype(jnp.float32), d_hidden
    )
    d_dense_low = d_first.astype(jnp.bfloat16)
    grad_dense_attn = jnp.einsum(
        "sta,sti->ai", context_low, d_dense_low, preferred_element_type=jnp.float32
    )
    grad_dense_conv = jnp.einsum(
        "sta,sti->ai", conv_low, d_dense_low, preferred_element_type=jnp.float32
    )
    d_context_low = jnp.einsum(
        "sti,ai->sta", d_dense_low, full_dense_attn, preferred_element_type=jnp.float32
    ).astype(jnp.bfloat16)
    d_conv_res = four_heads(
        jnp.einsum("sti,ai->sta", d_dense_low, full_dense_conv, preferred_element_type=jnp.float32)
    )
    d_kernel = jnp.concatenate(
        [
            jnp.sum(d_conv_res * value_ext[:, offset : offset + local_rows], axis=-1, keepdims=True)
            for offset in range(KERNEL)
        ],
        axis=-1,
    )
    d_logits = kernel_soft * (d_kernel - jnp.sum(d_kernel * kernel_soft, axis=-1, keepdims=True))
    d_logits_low = d_logits.reshape(seq_count, local_rows, HEADS * KERNEL).astype(jnp.bfloat16)
    grad_span = jnp.einsum(
        "sta,stk->ak", span_mix, d_logits_low, preferred_element_type=jnp.float32
    )
    d_mix = jnp.einsum("stk,ak->sta", d_logits_low, full_span, preferred_element_type=jnp.float32)
    d_key_low = (d_mix * query_f32).astype(jnp.bfloat16)
    d_query_conv = d_mix * key_conv
    grad_point = jnp.einsum(
        "sti,sta->ia", spread_low, d_key_low, preferred_element_type=jnp.float32
    )
    d_spread = jnp.einsum("sta,ia->sti", d_key_low, full_point, preferred_element_type=jnp.float32)
    grad_depth = jnp.stack(
        [
            jnp.sum(
                d_spread * rows_ext[:, offset : offset + local_rows].astype(jnp.float32),
                axis=(0, 1),
            )
            for offset in range(KERNEL)
        ],
        axis=0,
    )
    ext_rows = local_rows + 2 * half_kernel
    d_rows_ext = jnp.zeros((seq_count, ext_rows, model_width), jnp.float32)
    d_value_ext = jnp.zeros((seq_count, ext_rows, HEADS, HEAD), jnp.float32)
    for offset in range(KERNEL):
        d_rows_ext = d_rows_ext + jnp.pad(
            d_spread * depth_fwd[offset], ((0, 0), (offset, 2 * half_kernel - offset), (0, 0))
        )
        d_value_ext = d_value_ext + jnp.pad(
            kernel_soft[..., offset : offset + 1] * d_conv_res,
            ((0, 0), (offset, 2 * half_kernel - offset), (0, 0), (0, 0)),
        )
    grad_ext = jnp.concatenate(
        [d_value_ext.reshape(seq_count, ext_rows, attn_width), d_rows_ext], axis=-1
    )
    edge_rims = jnp.concatenate(
        [grad_ext[:, :half_kernel], grad_ext[:, ext_rows - half_kernel :]], axis=1
    )
    edge_sums = with_halo(edge_rims.astype(jnp.bfloat16), (("ctx", 1),), half_kernel).astype(
        edge_rims.dtype
    )
    own_rows = grad_ext[:, half_kernel : half_kernel + local_rows]
    own_rows = jnp.concatenate(
        [
            own_rows[:, :half_kernel] + edge_sums[:, :half_kernel],
            own_rows[:, half_kernel : local_rows - half_kernel],
            own_rows[:, local_rows - half_kernel :] + edge_sums[:, 3 * half_kernel :],
        ],
        axis=1,
    )
    d_value_low = own_rows[..., :attn_width].astype(jnp.bfloat16)
    d_rows_conv = own_rows[..., attn_width:]
    grad_conv_value = jnp.einsum(
        "sti,sta->ia", hidden_in, d_value_low, preferred_element_type=jnp.float32
    )
    def spread_rows(part, rows):
        split = part.reshape(shard_count, rows, part.shape[1])
        return jnp.pad(split, ((0, 0), (0, width_rows - rows), (0, 0))).reshape(model_width, -1)

    middle = jnp.concatenate(
        [
            grad_conv_value,
            grad_point,
            spread_rows(grad_span, head_rows),
            jnp.zeros((model_width, 64 - HEADS * KERNEL), jnp.float32),
            grad_depth.T,
            jnp.stack([grad_attn_gain, grad_attn_bias, grad_out_gain, grad_out_bias], axis=1),
            jnp.zeros((model_width, 256 - 64 - KERNEL - 4), jnp.float32),
        ],
        axis=1,
    )
    second_part = jnp.concatenate([grad_dense_attn, grad_dense_conv, grad_ffn_inner[0], grad_ffn_inner[1]], axis=1)
    third_part = jnp.concatenate([grad_ffn_outer[0], grad_ffn_outer[1]], axis=1)
    parts = ()
    part_splits = ()
    if by_kernel:
        whole_parts = (third_part, second_part, middle)
        part_splits = (SPLITS[2], SPLITS[1], SPLITS[0])
        parts = tuple(
            (cut(one, members, shard_count, split), (one.shape[0] // shard_count, one.shape[1]))
            for one, split in zip(whole_parts, part_splits)
        )
    dq_packed, dkv, *reduced = attend_backward(
        pack_heads(d_context_low), kv_all, q_all, out_all, lse, members, shard_count, parts, part_splits
    )
    d_query_attn = unpack_heads(dq_packed, seq_count).astype(jnp.float32)
    d_pair = dkv.reshape(seq_count, HEADS, local_rows, 2, HEAD).transpose(0, 2, 3, 1, 4)
    d_pair = d_pair.reshape(seq_count, local_rows, 2 * attn_width)
    d_query_low = (d_query_attn + d_query_conv).astype(jnp.bfloat16)
    d_all_low = jnp.concatenate([d_query_low, d_pair.astype(jnp.bfloat16)], axis=-1)
    grad_qkv = jnp.einsum("sti,sto->io", hidden_in, d_all_low, preferred_element_type=jnp.float32)
    grad_in = (
        d_first
        + jnp.einsum("sto,io->sti", d_all_low, full_qkv, preferred_element_type=jnp.float32)
        + jnp.einsum("sta,ia->sti", d_value_low, full_value, preferred_element_type=jnp.float32)
        + d_rows_conv
    )
    first_part = jnp.pad(grad_qkv, ((0, 0), (0, 128)))
    if by_kernel:
        third_sum, second_sum, middle_sum = reduced
        first_sum = reduce_weight(first_part, members, shard_count, SPLITS[0], 4)
    else:
        first_sum, second_sum, third_sum, middle_sum = (
            lax.psum(lax.psum_scatter(one.astype(BF), "shard", scatter_dimension=0, tiled=True), "ctx")
            for one in (first_part, second_part, third_part, middle)
        )
    first_sum, second_sum, third_sum, middle_sum = (
        one.astype(F32) for one in (first_sum, second_sum, third_sum, middle_sum)
    )
    edge = 2 * attn_width
    norms = middle_sum[:, edge + 64 + KERNEL : edge + 68 + KERNEL].T
    summed = (
        first_sum[:, : 3 * attn_width],
        middle_sum[:, edge + 64 : edge + 64 + KERNEL].T,
        middle_sum[:, attn_width:edge],
        middle_sum[:head_rows, edge : edge + HEADS * KERNEL],
        middle_sum[:, :attn_width],
        second_sum[:, :model_width],
        second_sum[:, model_width : 2 * model_width],
        norms[0],
        norms[1],
        second_sum[:, 2 * model_width :].reshape(head_rows, GROUPS, -1).transpose(1, 0, 2),
        third_sum.reshape(-1, GROUPS, D // GROUPS).transpose(1, 0, 2),
        norms[2],
        norms[3],
    )
    result_grads = tuple(summed)
    return (layer_out, grad_in) + result_grads


def solution(mesh):
    return jax.shard_map(
        shards,
        mesh=mesh,
        in_specs=(
            P("shard", "ctx", None),
            P("shard", "ctx", None),
            P("shard", None),
            P(None, "shard"),
            P("shard", None),
            P("shard", None),
            P("shard", None),
            P("shard", None),
            P("shard", None),
            P("shard"),
            P("shard"),
            P(None, "shard", None),
            P(None, "shard", None),
            P("shard"),
            P("shard"),
        ),
        out_specs=(
            P("shard", "ctx", None),
            P("shard", "ctx", None),
            P("shard", None),
            P(None, "shard"),
            P("shard", None),
            P("shard", None),
            P("shard", None),
            P("shard", None),
            P("shard", None),
            P("shard"),
            P("shard"),
            P(None, "shard", None),
            P(None, "shard", None),
            P("shard"),
            P("shard"),
        ),
        check_vma=False,
    )
```

```python
import functools
import math

import jax
import jax.numpy as jnp
from jax import lax
from jax.experimental import pallas as pl
from jax.experimental.pallas import tpu as pltpu
from jax.sharding import PartitionSpec as P

D = 768
HEADS = 6
HEAD = 64
GROUPS = 2
KERNEL = 9


norm_eps = 1e-12


BF = jnp.bfloat16
F32 = jnp.float32
MESH_ID = pl.DeviceIdType.MESH
NT = (((1,), (1,)), ((), ()))
NN = (((1,), (0,)), ((), ()))
EXP2_SCALE = math.log2(math.e) / math.sqrt(HEAD)
TRIPLE = 3
QUADS = 4
CHUNK = 128


def dot(a, b, dims):
    return lax.dot_general(a, b, dims, preferred_element_type=F32)


def swap_halves(packed):
    return jnp.concatenate([packed[:, HEAD:], packed[:, :HEAD]], axis=1)


def low_lanes():
    return lax.broadcasted_iota(jnp.int32, (1, 2 * HEAD), 1) < HEAD


def remote(src, dst, send, recv, target):
    return pltpu.make_async_remote_copy(
        src_ref=src, dst_ref=dst, send_sem=send, recv_sem=recv,
        device_id=target, device_id_type=MESH_ID,
    )


def greet(peers):
    barrier = pltpu.get_barrier_semaphore()
    for peer in peers:
        pl.semaphore_signal(barrier, inc=1, device_id=peer, device_id_type=MESH_ID)
    pl.semaphore_wait(barrier, len(peers))


class Place:
    def __init__(self, members, shards):
        self.members, self.shards = members, shards
        self.me = lax.axis_index("ctx")
        self.z = lax.axis_index("shard")
        self.quad, self.sub = self.me // members, self.me % members

    def peer(self, step):
        return ((self.quad + step) % QUADS * self.members + self.sub, self.z)

    def sibling(self, step):
        return (self.quad * self.members + (self.sub + step) % self.members, self.z)

    def behind(self, step):
        return (self.quad + QUADS - step) % QUADS

    def along(self, step):
        return (self.me, (self.z + step) % self.shards)

    def z_behind(self, step):
        return (self.z + self.shards - step) % self.shards

    def greet(self, with_shard):
        peers = [self.peer(k) for k in range(1, QUADS)]
        peers += [self.sibling(m) for m in range(1, self.members)]
        if with_shard:
            peers += [self.along(d) for d in range(1, self.shards)]
        greet(peers)


class Pieces:
    def __init__(self, place, rows, columns, col_split):
        count = QUADS * place.members
        self.place, self.rows, self.col_split = place, rows, col_split
        self.piece_rows = rows // (count // col_split)
        self.piece_cols = columns // col_split

    def at(self, ref, z, quad, sub):
        index = quad * self.place.members + sub
        top = pl.multiple_of(z * self.rows + index // self.col_split * self.piece_rows, 16)
        left = pl.multiple_of(index % self.col_split * self.piece_cols, 128)
        return ref.at[pl.ds(top, self.piece_rows), pl.ds(left, self.piece_cols)]


def fits(rows, columns, members, col_split):
    count = QUADS * members
    if count % col_split:
        return False
    row_split = count // col_split
    return rows % (16 * row_split) == 0 and columns % (128 * col_split) == 0


class Gather:
    def __init__(self, place, shard_ref, full_ref, col_split, sems):
        self.place, self.shard_ref, self.full_ref = place, shard_ref, full_ref
        rows, columns = shard_ref.shape
        self.rows = rows
        self.pieces = Pieces(place, rows, columns, col_split)
        self.z_s, self.z_r, self.q_s, self.q_r, self.f_s, self.f_r, self.local = sems

    @staticmethod
    def semaphores(members, shards):
        dma = pltpu.SemaphoreType.DMA
        return [
            dma((shards,)), dma((shards,)), dma((shards, QUADS)), dma((shards, QUADS)),
            dma((shards, QUADS, members)), dma((shards, QUADS, members)), dma((1,)),
        ]

    def z_copy(self, d):
        p = self.place
        return remote(
            self.pieces.at(self.shard_ref, 0, p.quad, p.sub), self.pieces.at(self.full_ref, p.z, p.quad, p.sub),
            self.z_s.at[d], self.z_r.at[d], p.along(d),
        )

    def q_copy(self, d, k):
        p = self.place
        block = self.pieces.at(self.full_ref, p.z_behind(d), p.quad, p.sub)
        return remote(block, block, self.q_s.at[d, k], self.q_r.at[d, k], p.peer(k))

    def f_copy(self, d, k, m):
        p = self.place
        block = self.pieces.at(self.full_ref, p.z_behind(d), p.behind(k), p.sub)
        return remote(block, block, self.f_s.at[d, k, m], self.f_r.at[d, k, m], p.sibling(m))

    def own_copy(self):
        top = pl.multiple_of(self.place.z * self.rows, 16)
        return pltpu.make_async_copy(
            self.shard_ref, self.full_ref.at[pl.ds(top, self.rows), :], self.local.at[0]
        )

    def start(self):
        for d in range(1, self.place.shards):
            self.z_copy(d).start()
        self.own_copy().start()

    def relay(self):
        for d in range(1, self.place.shards):
            self.z_copy(d).wait_recv()
            for k in range(1, QUADS):
                self.q_copy(d, k).start()
            for m in range(1, self.place.members):
                self.f_copy(d, 0, m).start()

    def share(self):
        for d in range(1, self.place.shards):
            for k in range(1, QUADS):
                self.q_copy(d, k).wait_recv()
                for m in range(1, self.place.members):
                    self.f_copy(d, k, m).start()

    def end(self):
        for d in range(1, self.place.shards):
            self.z_copy(d).wait_send()
            for k in range(QUADS):
                if k:
                    self.q_copy(d, k).wait_send()
                for m in range(1, self.place.members):
                    self.f_copy(d, k, m).wait()
        self.own_copy().wait()


class Reduce:
    def __init__(self, place, part_ref, out_ref, col_split, scratch):
        self.place, self.part_ref, self.out_ref = place, part_ref, out_ref
        self.piece_rows, self.piece_cols = part_ref.shape[3:]
        rows, columns = out_ref.shape
        self.pieces = Pieces(place, rows, columns, col_split)
        (
            self.half, self.half_in, self.quad_in, self.block, self.z_in, self.last,
            self.h_s, self.h_r, self.q_s, self.q_r, self.z_s, self.z_r, self.a_s, self.a_r, self.f_s, self.f_r, self.local,
        ) = scratch

    @staticmethod
    def scratch(members, shards, rows, columns):
        dma = pltpu.SemaphoreType.DMA
        return [
            pltpu.VMEM((shards, QUADS, rows, columns), BF),
            pltpu.VMEM((members, shards, QUADS, rows, columns), BF),
            pltpu.VMEM((QUADS, shards, rows, columns), BF),
            pltpu.VMEM((shards, rows, columns), BF),
            pltpu.VMEM((shards, rows, columns), BF),
            pltpu.VMEM((rows, columns), BF),
            dma((members,)), dma((members,)), dma((QUADS,)), dma((QUADS,)), dma((shards,)), dma((shards,)),
            dma((QUADS,)), dma((QUADS,)), dma((QUADS, members)), dma((QUADS, members)), dma((1,)),
        ]

    def h_copy(self, m):
        p = self.place
        return remote(
            self.part_ref.at[(p.sub + m) % p.members], self.half_in.at[m], self.h_s.at[m], self.h_r.at[m], p.sibling(m)
        )

    def q_copy(self, k):
        p = self.place
        return remote(
            self.half.at[:, (p.quad + k) % QUADS], self.quad_in.at[k], self.q_s.at[k], self.q_r.at[k], p.peer(k)
        )

    def z_copy(self, d):
        p = self.place
        return remote(
            self.block.at[(p.z + d) % p.shards], self.z_in.at[d], self.z_s.at[d], self.z_r.at[d], p.along(d)
        )

    def a_copy(self, k):
        p = self.place
        return remote(
            self.last, self.pieces.at(self.out_ref, 0, p.quad, p.sub), self.a_s.at[k], self.a_r.at[k], p.peer(k)
        )

    def f_copy(self, k, m):
        p = self.place
        block = self.pieces.at(self.out_ref, 0, p.behind(k), p.sub)
        return remote(block, block, self.f_s.at[k, m], self.f_r.at[k, m], p.sibling(m))

    def own_copy(self):
        p = self.place
        return pltpu.make_async_copy(
            self.last, self.pieces.at(self.out_ref, 0, p.quad, p.sub), self.local.at[0]
        )

    def start(self):
        for m in range(1, self.place.members):
            self.h_copy(m).start()

    def to_quads(self):
        for m in range(1, self.place.members):
            self.h_copy(m).wait_recv()

        def turn(i, carry):
            z, q = i // QUADS, i % QUADS
            total = self.part_ref[self.place.sub, z, q].astype(F32)
            for m in range(1, self.place.members):
                total = total + self.half_in[m, z, q].astype(F32)
            self.half[z, q] = total.astype(BF)
            return carry

        lax.fori_loop(0, self.place.shards * QUADS, turn, 0)
        for k in range(1, QUADS):
            self.q_copy(k).start()

    def to_shards(self):
        for k in range(1, QUADS):
            self.q_copy(k).wait_recv()

        def turn(z, carry):
            total = self.half[z, self.place.quad].astype(F32)
            for k in range(1, QUADS):
                total = total + self.quad_in[k, z].astype(F32)
            self.block[z] = total.astype(BF)
            return carry

        lax.fori_loop(0, self.place.shards, turn, 0)
        for d in range(1, self.place.shards):
            self.z_copy(d).start()

    def give(self):
        total = self.block[self.place.z].astype(F32)
        for d in range(1, self.place.shards):
            self.z_copy(d).wait_recv()
            total = total + self.z_in[d].astype(F32)
        self.last[...] = total.astype(BF)
        for k in range(1, QUADS):
            self.a_copy(k).start()
        self.own_copy().start()
        self.own_copy().wait()
        for m in range(1, self.place.members):
            self.f_copy(0, m).start()

    def share(self):
        for k in range(1, QUADS):
            self.a_copy(k).wait_recv()
            for m in range(1, self.place.members):
                self.f_copy(k, m).start()

    def end(self):
        for m in range(1, self.place.members):
            self.h_copy(m).wait_send()
        for k in range(1, QUADS):
            self.q_copy(k).wait_send()
            self.a_copy(k).wait_send()
        for d in range(1, self.place.shards):
            self.z_copy(d).wait_send()
        for k in range(QUADS):
            for m in range(1, self.place.members):
                self.f_copy(k, m).wait()


def gather_kernel(members, shards, split, shard_ref, full_ref, *sems):
    place = Place(members, shards)
    place.greet(True)
    one = Gather(place, shard_ref, full_ref, split, sems)
    one.start()
    one.relay()
    one.share()
    one.end()


def gather_weight(block, members, shards, split, number):
    anywhere = pl.BlockSpec(memory_space=pl.ANY)
    return pl.pallas_call(
        functools.partial(gather_kernel, members, shards, split),
        in_specs=[anywhere],
        out_specs=anywhere,
        out_shape=jax.ShapeDtypeStruct((shards * block.shape[0], block.shape[1]), BF),
        scratch_shapes=Gather.semaphores(members, shards),
        compiler_params=pltpu.CompilerParams(collective_id=number, has_side_effects=True),
    )(block)


def attend_forward_kernel(members, shards, splits, *refs):
    count = len(splits)
    kv_in, q_in, *blocks = refs[: 2 + count]
    kv_all, q_all, out_all, lse, ctx_out, *fulls = refs[2 + count : 7 + 2 * count]
    out_send, kv_s, kv_r, q_s, q_r, f_s, f_r, o_s, o_r, local, *sems = refs[7 + 2 * count :]
    rows = kv_in.shape[2]
    half = rows // 2
    place = Place(members, shards)
    quad, sub, peer, sibling = place.quad, place.sub, place.peer, place.sibling
    place.greet(bool(splits))

    def kv_copy(h, k):
        return remote(
            kv_in.at[(quad + k) % QUADS, h], kv_all.at[h, quad, sub], kv_s.at[h, k], kv_r.at[h, k], peer(k)
        )

    def q_copy(h, k):
        return remote(
            q_in.at[(quad + k) % QUADS, h], q_all.at[h, quad], q_s.at[h, k], q_r.at[h, k], peer(k)
        )

    def forward_copy(h, m):
        return remote(
            kv_all.at[h, :, sub], kv_all.at[h, :, sub], f_s.at[h, m], f_r.at[h, m], sibling(m)
        )

    def out_copy(h, i, k):
        return remote(
            out_send.at[h, i], ctx_out.at[quad, h], o_s.at[h, i], o_r.at[h, i], peer(k)
        )

    own_kv = pltpu.make_async_copy(kv_in.at[quad], kv_all.at[:, quad, sub], local.at[0])
    own_q = pltpu.make_async_copy(q_in.at[quad], q_all.at[:, quad], local.at[1])
    own_kv.start()
    own_q.start()
    gathers = [
        Gather(place, block, full, split, sems[7 * j : 7 * j + 7])
        for j, (block, full, split) in enumerate(zip(blocks, fulls, splits))
    ]
    for gather in gathers:
        gather.start()
    for h in range(TRIPLE):
        for k in range(1, QUADS):
            kv_copy(h, k).start()
            q_copy(h, k).start()
    own_kv.wait()
    own_q.wait()

    def receive(h):
        for k in range(1, QUADS):
            kv_copy(h, k).wait_recv()
            q_copy(h, k).wait_recv()
        for m in range(1, members):
            forward_copy(h, m).start()

    receive(0)
    is_low = low_lanes()

    def block(step, carry):
        h, i = step // QUADS, step % QUADS
        k = (i + 1) % QUADS
        source = (quad + k) % QUADS

        @pl.when(i == 0)
        def _():
            for m in range(1, members):
                forward_copy(h, m).wait_recv()

        keys = kv_all[h].reshape(QUADS * members * rows, 2 * HEAD)

        def rows_turn(r, inner):
            at = pl.multiple_of(r * CHUNK, CHUNK)
            packed = q_all[h, source, pl.ds(at, CHUNK), :]
            outs = []
            stats = []
            for part in range(2):
                q = jnp.where(is_low, packed if part == 0 else swap_halves(packed), jnp.zeros_like(packed))
                scores = dot(q, keys, NT)
                top = jnp.max(scores, axis=1, keepdims=True)
                probs = jnp.exp2((scores - top) * EXP2_SCALE)
                total = jnp.sum(probs, axis=1, keepdims=True)
                outs.append(dot(probs.astype(BF), keys, NN) / total)
                stats.append(top * EXP2_SCALE + jnp.log2(total))
            both = jnp.where(is_low, swap_halves(outs[0]), outs[1])
            out_all[h, source, pl.ds(at, CHUNK), :] = both
            out_send[h, i, pl.ds(at, CHUNK), :] = both.astype(BF)
            for part in range(2):
                lse[h, source, part, r] = jnp.broadcast_to(stats[part], (CHUNK, CHUNK)).T[0:8, :]
            return inner

        lax.fori_loop(0, half // CHUNK, rows_turn, 0)

        @pl.when(k != 0)
        def _():
            out_copy(h, i, k).start()

        @pl.when(k == 0)
        def _():
            own = pltpu.make_async_copy(out_send.at[h, i], ctx_out.at[quad, h], local.at[0])
            own.start()
            own.wait()

        @pl.when((i == 2) & (h < TRIPLE - 1))
        def _():
            receive(h + 1)

        if gathers:

            @pl.when(step == 4)
            def _():
                for gather in gathers:
                    gather.relay()

            @pl.when(step == TRIPLE * QUADS - 1)
            def _():
                for gather in gathers:
                    gather.share()

        return carry

    lax.fori_loop(0, TRIPLE * QUADS, block, 0)
    for gather in gathers:
        gather.end()
    for h in range(TRIPLE):
        for k in range(1, QUADS):
            out_copy(h, k - 1, k).wait()
            kv_copy(h, k).wait_send()
            q_copy(h, k).wait_send()
        for m in range(1, members):
            forward_copy(h, m).wait_send()


def attend_forward(kv, q, members, shards, blocks, splits):
    rows = kv.shape[2]
    half = rows // 2
    vm = pl.BlockSpec(memory_space=pltpu.VMEM)
    anywhere = pl.BlockSpec(memory_space=pl.ANY)
    dma = pltpu.SemaphoreType.DMA
    total = TRIPLE * QUADS * rows * QUADS * members * rows
    return pl.pallas_call(
        functools.partial(attend_forward_kernel, members, shards, splits),
        in_specs=[anywhere, anywhere] + [anywhere] * len(blocks),
        out_specs=[vm, vm, vm, vm, anywhere] + [anywhere] * len(blocks),
        out_shape=[
            jax.ShapeDtypeStruct((TRIPLE, QUADS, members, rows, 2 * HEAD), BF),
            jax.ShapeDtypeStruct((TRIPLE, QUADS, half, 2 * HEAD), BF),
            jax.ShapeDtypeStruct((TRIPLE, QUADS, half, 2 * HEAD), F32),
            jax.ShapeDtypeStruct((TRIPLE, QUADS, 2, half // CHUNK, 8, CHUNK), F32),
            jax.ShapeDtypeStruct((QUADS, TRIPLE, half, 2 * HEAD), BF),
        ]
        + [jax.ShapeDtypeStruct((shards * block.shape[0], block.shape[1]), BF) for block in blocks],
        scratch_shapes=[
            pltpu.VMEM((TRIPLE, QUADS, half, 2 * HEAD), BF),
            dma((TRIPLE, QUADS)), dma((TRIPLE, QUADS)), dma((TRIPLE, QUADS)), dma((TRIPLE, QUADS)),
            dma((TRIPLE, members)), dma((TRIPLE, members)), dma((TRIPLE, QUADS)), dma((TRIPLE, QUADS)),
            dma((2,)),
        ]
        + Gather.semaphores(members, shards) * len(blocks),
        compiler_params=pltpu.CompilerParams(
            collective_id=1, has_side_effects=True, vmem_limit_bytes=56 * 2**20
        ),
        cost_estimate=pl.CostEstimate(flops=total * 256, bytes_accessed=8 * 2**20, transcendentals=total),
    )(kv, q, *blocks)


def attend_backward_kernel(members, shards, splits, *refs):
    count = len(splits)
    d_in, kv_all, q_all, out_all, lse, *parts = refs[: 5 + count]
    dq_out, dkv_out, *sums = refs[5 + count : 7 + 2 * count]
    (
        d_all, q_zero, d_zero, stat, delta, dq_sum, dkv_sum, own_part, sib_send, sib_recv, dkv_send, dq_send,
        d_s, d_r, p_s, p_r, k_s, k_r, g_s, g_r, local, *scratch,
    ) = refs[7 + 2 * count :]
    rows = kv_all.shape[3]
    half = rows // 2
    steps = TRIPLE * QUADS
    place = Place(members, shards)
    quad, sub, peer, sibling = place.quad, place.sub, place.peer, place.sibling
    place.greet(bool(splits))
    reduces = [
        Reduce(place, one, total, split, scratch[17 * j : 17 * j + 17])
        for j, (one, total, split) in enumerate(zip(parts, sums, splits))
    ]

    def d_copy(h, k):
        return remote(
            d_in.at[(quad + k) % QUADS, h], d_all.at[h, quad], d_s.at[h, k], d_r.at[h, k], peer(k)
        )

    def part_copy(step, m):
        return remote(
            sib_send.at[step % 2, m], sib_recv.at[step, m], p_s.at[step, m], p_r.at[step, m], sibling(m)
        )

    def dkv_copy(h, i, k):
        return remote(
            dkv_send.at[h, i], dkv_out.at[quad, h], k_s.at[h, i], k_r.at[h, i], peer(k)
        )

    def dq_copy(h, k):
        return remote(
            dq_send.at[h, (quad + k) % QUADS], dq_out.at[quad, h], g_s.at[h, k], g_r.at[h, k], peer(k)
        )

    own = pltpu.make_async_copy(d_in.at[quad], d_all.at[:, quad], local.at[0])
    own.start()
    for h in range(TRIPLE):
        for k in range(1, QUADS):
            d_copy(h, k).start()
    for one in reduces:
        one.start()
    own.wait()
    is_low = low_lanes()

    def finish(step):
        h, i = step // QUADS, step % QUADS
        k = (i + 1) % QUADS
        total = own_part[step % 2]
        for m in range(1, members):
            part_copy(step, m).wait_recv()
            total = total + sib_recv[step, m].astype(F32)
        dkv_send[h, i] = total.astype(BF)

        @pl.when(k != 0)
        def _():
            dkv_copy(h, i, k).start()

        @pl.when(k == 0)
        def _():
            own = pltpu.make_async_copy(dkv_send.at[h, i], dkv_out.at[quad, h], local.at[0])
            own.start()
            own.wait()

    def block(step, carry):
        h, i = step // QUADS, step % QUADS
        k = (i + 1) % QUADS
        source = (quad + k) % QUADS

        @pl.when(i == 0)
        def _():
            for j in range(1, QUADS):
                d_copy(h, j).wait_recv()

            def prepare(b, inner):
                q = q_all[h, b]
                d = d_all[h, b]
                zero = jnp.zeros_like(q)
                q_zero[b, 0:half] = jnp.where(is_low, q, zero)
                q_zero[b, half:rows] = jnp.where(is_low, swap_halves(q), zero)
                d_zero[b, 0:half] = jnp.where(is_low, zero, swap_halves(d))
                d_zero[b, half:rows] = jnp.where(is_low, zero, d)
                both = (out_all[h, b] * d.astype(F32)).T
                delta[b, :, 0:half] = jnp.broadcast_to(jnp.sum(both[0:HEAD], axis=0, keepdims=True), (8, half))
                delta[b, :, half:rows] = jnp.broadcast_to(jnp.sum(both[HEAD:], axis=0, keepdims=True), (8, half))
                for part in range(2):
                    for r in range(half // CHUNK):
                        at = part * half + r * CHUNK
                        stat[b, :, at : at + CHUNK] = lse[h, b, part, r]
                dq_sum[b] = jnp.zeros((HEAD, rows), F32)
                return inner

            lax.fori_loop(0, QUADS, prepare, 0)

        keys = kv_all[h, source].reshape(members * rows, 2 * HEAD)
        keys_turned = keys.T[0:HEAD]
        dkv_sum[...] = jnp.zeros_like(dkv_sum)

        def queries_turn(b, inner):
            qz = q_zero[b]
            dz = d_zero[b]
            probs = jnp.exp2(dot(keys, qz, NT) * EXP2_SCALE - stat[b, 0:1, :])
            d_probs = dot(keys, dz, NT)
            d_scores = (probs * (d_probs - delta[b, 0:1, :])).astype(BF)
            dkv_sum[...] += dot(d_scores, qz, NN) * (1.0 / math.sqrt(HEAD)) + dot(probs.astype(BF), dz, NN)
            dq_sum[b] += dot(keys_turned, d_scores, NN)
            return inner

        lax.fori_loop(0, QUADS, queries_turn, 0)

        @pl.when(step > 0)
        def _():
            finish(step - 1)

        own_part[step % 2] = dkv_sum[pl.ds(pl.multiple_of(sub * rows, rows), rows), :]
        for m in range(1, members):
            @pl.when(step > 1)
            def _():
                part_copy(step - 2, m).wait_send()
            target = (sub + m) % members
            sib_send[step % 2, m] = dkv_sum[pl.ds(pl.multiple_of(target * rows, rows), rows), :].astype(BF)
            part_copy(step, m).start()

        @pl.when(i == QUADS - 1)
        def _():
            def give(b, inner):
                turned = dq_sum[b] * (1.0 / math.sqrt(HEAD))
                dq_send[h, b] = jnp.concatenate([turned[:, 0:half], turned[:, half:rows]], axis=0).T.astype(BF)
                return inner

            lax.fori_loop(0, QUADS, give, 0)
            for j in range(1, QUADS):
                dq_copy(h, j).start()
            mine = pltpu.make_async_copy(dq_send.at[h, quad], dq_out.at[quad, h], local.at[0])
            mine.start()
            mine.wait()

        for j, one in enumerate(reduces):
            for at, stage in ((j, one.to_quads), (j + 4, one.to_shards), (j + 6, one.give), (j + 8, one.share)):

                @pl.when(step == at)
                def _(stage=stage):
                    stage()

        return carry

    lax.fori_loop(0, steps, block, 0)
    finish(steps - 1)
    for m in range(1, members):
        part_copy(steps - 2, m).wait_send()
        part_copy(steps - 1, m).wait_send()
    for h in range(TRIPLE):
        for k in range(1, QUADS):
            d_copy(h, k).wait_send()
            dkv_copy(h, k - 1, k).wait()
            dq_copy(h, k).wait()
    for one in reduces:
        one.end()


def attend_backward(d_context, kv_all, q_all, out_all, lse, members, shards, parts, splits):
    rows = kv_all.shape[3]
    half = rows // 2
    steps = TRIPLE * QUADS
    vm = pl.BlockSpec(memory_space=pltpu.VMEM)
    anywhere = pl.BlockSpec(memory_space=pl.ANY)
    dma = pltpu.SemaphoreType.DMA
    total = TRIPLE * QUADS * rows * QUADS * members * rows
    return pl.pallas_call(
        functools.partial(attend_backward_kernel, members, shards, splits),
        in_specs=[anywhere, vm, vm, vm, vm] + [vm] * len(parts),
        out_specs=[anywhere, anywhere] + [anywhere] * len(parts),
        out_shape=[
            jax.ShapeDtypeStruct((QUADS, TRIPLE, half, 2 * HEAD), BF),
            jax.ShapeDtypeStruct((QUADS, TRIPLE, rows, 2 * HEAD), BF),
        ]
        + [jax.ShapeDtypeStruct(shape, BF) for _, shape in parts],
        scratch_shapes=[
            pltpu.VMEM((TRIPLE, QUADS, half, 2 * HEAD), BF),
            pltpu.VMEM((QUADS, rows, 2 * HEAD), BF),
            pltpu.VMEM((QUADS, rows, 2 * HEAD), BF),
            pltpu.VMEM((QUADS, 8, rows), F32),
            pltpu.VMEM((QUADS, 8, rows), F32),
            pltpu.VMEM((QUADS, HEAD, rows), F32),
            pltpu.VMEM((members * rows, 2 * HEAD), F32),
            pltpu.VMEM((2, rows, 2 * HEAD), F32),
            pltpu.VMEM((2, members, rows, 2 * HEAD), BF),
            pltpu.VMEM((steps, members, rows, 2 * HEAD), BF),
            pltpu.VMEM((TRIPLE, QUADS, rows, 2 * HEAD), BF),
            pltpu.VMEM((TRIPLE, QUADS, half, 2 * HEAD), BF),
            dma((TRIPLE, QUADS)), dma((TRIPLE, QUADS)),
            dma((steps, members)), dma((steps, members)),
            dma((TRIPLE, QUADS)), dma((TRIPLE, QUADS)), dma((TRIPLE, QUADS)), dma((TRIPLE, QUADS)),
            dma((2,)),
        ]
        + sum((Reduce.scratch(members, shards, *one.shape[3:]) for one, _ in parts), []),
        compiler_params=pltpu.CompilerParams(
            collective_id=2, has_side_effects=True, vmem_limit_bytes=56 * 2**20
        ),
        cost_estimate=pl.CostEstimate(flops=total * 640, bytes_accessed=8 * 2**20, transcendentals=total),
    )(d_context, kv_all, q_all, out_all, lse, *[one for one, _ in parts])


RIM = 16
TILE = 128
SMALL = 128
TN = (((0,), (0,)), ((), ()))


def moved(value, by):
    rows = value.shape[0]
    return value if by % rows == 0 else pltpu.roll(value, (-by) % rows, 0)


def head_columns(tap, wide_first):
    shape = (SMALL, HEADS * HEAD) if wide_first else (HEADS * HEAD, SMALL)
    narrow = lax.broadcasted_iota(jnp.int32, shape, 0 if wide_first else 1)
    wide = lax.broadcasted_iota(jnp.int32, shape, 1 if wide_first else 0)
    if wide_first:
        same = narrow == wide // HEAD * KERNEL + tap
    else:
        same = (narrow * HEAD == (wide * KERNEL + tap * HEAD)) & (wide % HEAD == 0)
    return jnp.where(same, 1.0, 0.0).astype(BF)


def norm_rows(value):
    center = value - jnp.mean(value, axis=-1, keepdims=True)
    inv_std = lax.rsqrt(jnp.mean(center * center, axis=-1, keepdims=True) + norm_eps)
    return center * inv_std, inv_std


def norm_rows_back(normed, inv_std, d_scaled):
    return inv_std * (
        d_scaled
        - jnp.mean(d_scaled, axis=-1, keepdims=True)
        - normed * jnp.mean(d_scaled * normed, axis=-1, keepdims=True)
    )


def fold(value):
    return jnp.sum(value.reshape(value.shape[0] // 8, 8, value.shape[1]), axis=0)


def gelu_both(value):
    size = jnp.abs(value)
    turn = 1.0 / (1.0 + (0.3275911 / math.sqrt(2.0)) * size)
    bell = jnp.exp2(value * value * (-0.5 * math.log2(math.e)))
    poly = ((((1.061405429 * turn - 1.453152027) * turn + 1.421413741) * turn - 0.284496736) * turn + 0.254829592) * turn
    tail = 0.5 * poly * bell
    below = jnp.where(value < 0.0, tail, 1.0 - tail)
    return value * below, below + value * bell * (1.0 / math.sqrt(2.0 * math.pi))


def project_body(hidden, first, kv_out, q_packed, q_out):
    seqs, rows, _ = hidden.shape
    half = rows // 2
    width = HEADS * HEAD
    is_low = low_lanes()

    def turn(step, carry):
        s, r = step // (half // TILE), step % (half // TILE)
        tops = (pl.multiple_of(r * TILE, TILE), pl.multiple_of(half + r * TILE, TILE))
        rows_in = jnp.concatenate([hidden[s, pl.ds(top, TILE), :] for top in tops], axis=0)
        mixed = dot(rows_in, first[:, : 3 * width], NN).astype(BF)
        for part, top in enumerate(tops):
            block = mixed[part * TILE : part * TILE + TILE]
            q_out[s, pl.ds(top, TILE), :] = block[:, :width]
            for h in range(HEADS):
                at = width + 2 * HEAD * h
                kv_out[s * 2 + h // TRIPLE, h % TRIPLE, pl.ds(top, TILE), :] = block[:, at : at + 2 * HEAD]
        for h in range(HEADS):
            at = h // 2 * 2 * HEAD
            upper = mixed[:TILE, at : at + 2 * HEAD]
            lower = mixed[TILE:, at : at + 2 * HEAD]
            if h % 2:
                packed = jnp.where(is_low, swap_halves(upper), lower)
            else:
                packed = jnp.where(is_low, upper, swap_halves(lower))
            q_packed[s * 2 + h // TRIPLE, h % TRIPLE, pl.ds(tops[0], TILE), :] = packed
        return carry

    lax.fori_loop(0, seqs * half // TILE, turn, 0)


def conv_forward_body(
    hidden, low_rim, high_rim, first, span_in, q_out, spread_out, key_out, mix_out, soft_out, value_out, conv_out,
    ext, span_wide, small_turned,
):
    seqs, rows, model = hidden.shape
    width = HEADS * HEAD
    point_at = 4 * width
    value_at = 3 * width
    small_turned[...] = first[:, 5 * width :].astype(F32).T
    depth = small_turned[64 : 64 + 16, :]
    for tap in range(KERNEL):
        span_wide[:, tap * width : tap * width + width] = dot(span_in[...], head_columns(tap, True), NN).astype(BF)

    for s in range(seqs):
        low, high = low_rim[s], high_rim[s]
        ext[0:RIM] = low.astype(F32)
        ext[RIM : RIM + rows] = hidden[s].astype(F32)
        ext[RIM + rows : rows + 2 * RIM] = high.astype(F32)
        value = first[:, value_at : value_at + width]
        value_out[s, 0:RIM] = dot(low, value, NN)
        value_out[s, RIM : RIM + rows] = dot(hidden[s], value, NN)
        value_out[s, RIM + rows : rows + 2 * RIM] = dot(high, value, NN)

        def turn(r, carry):
            top = pl.multiple_of(r * TILE, TILE)
            around = ext[pl.ds(top, TILE + 2 * RIM), :]
            spread = jnp.zeros((TILE, model), F32)
            for tap in range(KERNEL):
                spread = spread + moved(around, tap - KERNEL // 2)[RIM : RIM + TILE] * depth[tap : tap + 1]
            spread_low = spread.astype(BF)
            spread_out[s, pl.ds(top, TILE), :] = spread_low
            key_conv = dot(spread_low, first[:, point_at : point_at + width], NN)
            key_out[s, pl.ds(top, TILE), :] = key_conv
            mix = (key_conv * q_out[s, pl.ds(top, TILE), :].astype(F32)).astype(BF)
            mix_out[s, pl.ds(top, TILE), :] = mix
            logits = [dot(mix, span_wide[:, tap * width : tap * width + width], NN) for tap in range(KERNEL)]
            peak = functools.reduce(jnp.maximum, logits)
            powers = [jnp.exp(one - peak) for one in logits]
            scale = 1.0 / sum(powers[1:], powers[0])
            values = value_out[s, pl.ds(top, TILE + 2 * RIM), :]
            result = jnp.zeros((TILE, width), F32)
            for tap in range(KERNEL):
                soft = powers[tap] * scale
                soft_out[tap, s, pl.ds(top, TILE), :] = soft.astype(BF)
                result = result + soft * moved(values, tap - KERNEL // 2)[RIM : RIM + TILE]
            conv_out[s, pl.ds(top, TILE), :] = result.astype(BF)
            return carry

        lax.fori_loop(0, rows // TILE, turn, 0)


def front_kernel(
    hidden, low_rim, high_rim, first, span, kv_out, q_packed, q_out, spread_out, key_out, mix_out, soft_out, value_out, conv_out, small_turned,
    ext, span_wide,
):
    project_body(hidden, first, kv_out, q_packed, q_out)
    conv_forward_body(
        hidden, low_rim, high_rim, first, span, q_out, spread_out, key_out, mix_out, soft_out, value_out, conv_out,
        ext, span_wide, small_turned,
    )


def front(hidden, low_rim, high_rim, first, span):
    seqs, rows, model = hidden.shape
    width = HEADS * HEAD
    shape = jax.ShapeDtypeStruct
    return pl.pallas_call(
        front_kernel,
        out_shape=[
            shape((QUADS, TRIPLE, rows, 2 * HEAD), BF),
            shape((QUADS, TRIPLE, rows // 2, 2 * HEAD), BF),
            shape((seqs, rows, width), BF),
            shape((seqs, rows, model), BF),
            shape((seqs, rows, width), F32),
            shape((seqs, rows, width), BF),
            shape((KERNEL, seqs, rows, width), BF),
            shape((seqs, rows + 2 * RIM, width), F32),
            shape((seqs, rows, width), BF),
            shape((SMALL, model), F32),
        ],
        scratch_shapes=[
            pltpu.VMEM((rows + 2 * RIM, model), F32),
            pltpu.VMEM((width, KERNEL * width), BF),
        ],
        compiler_params=pltpu.CompilerParams(vmem_limit_bytes=56 * 2**20),
    )(hidden, low_rim, high_rim, first, span)


def middle_kernel(
    by_kernel, shards, members,
    context, conv, hidden, cotangent, second, third, small_turned,
    layer_out, d_first_out, d_context_out, d_conv_out, second_part, third_part, norm_sums,
    context_low, hidden_low, active_all, d_outer_all, d_inner_all, d_dense_all, d_context_all,
):
    seqs, rows, model = hidden.shape
    half = rows // 2
    width = HEADS * HEAD
    group = model // GROUPS
    units = third.shape[0]
    is_low = low_lanes()
    gains = small_turned[64 + KERNEL : 64 + KERNEL + 4, :]
    attn_gain, attn_bias, out_gain, out_bias = (gains[j : j + 1] for j in range(4))
    norm_sums[...] = jnp.zeros_like(norm_sums)

    def turn(step, carry):
        s, p = step // 2, step % 2
        top = pl.multiple_of(p * half, half)
        at = pl.ds(top, half)
        every = pl.ds(pl.multiple_of(step * half, half), half)
        pairs = []
        for j in range(HEADS // 2):
            a = context[s * 2 + 2 * j // TRIPLE, 2 * j % TRIPLE]
            b = context[s * 2 + (2 * j + 1) // TRIPLE, (2 * j + 1) % TRIPLE]
            upper = jnp.where(is_low, a, swap_halves(b))
            lower = jnp.where(is_low, swap_halves(a), b)
            pairs.append(jnp.where(p == 0, upper, lower))
        low = jnp.concatenate(pairs, axis=1)
        context_low[every] = low
        dense = dot(low, second[:, :model], NN) + dot(conv[s, at], second[:, model : 2 * model], NN)
        normed_one, inv_one = norm_rows(dense + hidden[s, at].astype(F32))
        hidden_one = normed_one * attn_gain + attn_bias
        one_low = hidden_one.astype(BF)
        hidden_low[every] = one_low
        outers = []
        slopes = []
        for g in range(GROUPS):
            edge = 2 * model + g * units
            inner = dot(one_low[:, g * group : g * group + group], second[:, edge : edge + units], NN)
            active, slope = gelu_both(inner)
            active = active.astype(BF)
            active_all[every, g * units : g * units + units] = active
            slopes.append(slope)
            outers.append(dot(active, third[:, g * group : g * group + group], NN))
        normed_two, inv_two = norm_rows(jnp.concatenate(outers, axis=1) + hidden_one)
        layer_out[s, at] = (normed_two * out_gain + out_bias).astype(BF)
        d_result = cotangent[s, at].astype(F32)
        norm_sums[2] += fold(d_result * normed_two)
        norm_sums[3] += fold(d_result)
        d_second = norm_rows_back(normed_two, inv_two, d_result * out_gain)
        d_outer = d_second.astype(BF)
        d_outer_all[every] = d_outer
        backs = []
        for g in range(GROUPS):
            edge = 2 * model + g * units
            d_active = dot(d_outer[:, g * group : g * group + group], third[:, g * group : g * group + group], NT)
            d_inner = (d_active * slopes[g]).astype(BF)
            d_inner_all[every, g * units : g * units + units] = d_inner
            backs.append(dot(d_inner, second[:, edge : edge + units], NT))
        d_hidden = jnp.concatenate(backs, axis=1) + d_second
        norm_sums[0] += fold(d_hidden * normed_one)
        norm_sums[1] += fold(d_hidden)
        d_first = norm_rows_back(normed_one, inv_one, d_hidden * attn_gain)
        d_first_out[s, at] = d_first
        d_dense = d_first.astype(BF)
        d_dense_all[every] = d_dense
        d_context_all[every] = dot(d_dense, second[:, :model], NT).astype(BF)
        d_conv_out[s, at] = dot(d_dense, second[:, model : 2 * model], NT)
        return carry

    lax.fori_loop(0, seqs * 2, turn, 0)
    for s in range(seqs):
        for h in range(HEADS):
            at = h // 2 * 2 * HEAD
            upper = d_context_all[s * rows : s * rows + half, at : at + 2 * HEAD]
            lower = d_context_all[s * rows + half : s * rows + rows, at : at + 2 * HEAD]
            if h % 2:
                packed = jnp.where(is_low, swap_halves(upper), lower)
            else:
                packed = jnp.where(is_low, upper, swap_halves(lower))
            d_context_out[s * 2 + h // TRIPLE, h % TRIPLE] = packed
    for g in range(GROUPS):
        for z in range(shards):
            block = units // shards
            part = dot(
                active_all[:, g * units + z * block : g * units + z * block + block],
                d_outer_all[:, g * group : g * group + group], TN,
            ).astype(BF)
            if by_kernel:
                piece = block // (QUADS * members)
                for q in range(QUADS):
                    for c in range(members):
                        row = (q * members + c) * piece
                        third_part[c, z, q, :, g * group : g * group + group] = part[row : row + piece]
            else:
                third_part[z * block : z * block + block, g * group : g * group + group] = part

    def columns(left, right):
        found = []
        for start, size, rows_in, columns_in in (
            (0, model, context_low[...], d_dense_all),
            (model, model, None, d_dense_all),
            (2 * model, units, hidden_low[:, :group], d_inner_all.at[:, :units]),
            (2 * model + units, units, hidden_low[:, group:], d_inner_all.at[:, units:]),
        ):
            a, b = max(left, start), min(right, start + size)
            if a < b:
                if rows_in is None:
                    rows_in = conv[...].reshape(seqs * rows, width)
                found.append(dot(rows_in, columns_in[:, a - start : b - start], TN).astype(BF))
        return jnp.concatenate(found, axis=1) if len(found) > 1 else found[0]

    wide = second.shape[1] // 4
    for j in range(4):
        part = columns(j * wide, j * wide + wide)
        if by_kernel:
            block = width // shards
            piece = block // 2
            for z in range(shards):
                for r in range(2):
                    row = z * block + r * piece
                    second_part[j % members, z, r * 2 + j // members] = part[row : row + piece]
        else:
            second_part[:, j * wide : j * wide + wide] = part


def middle(context, conv, hidden, cotangent, second, third, small_turned, by_kernel, shards, members):
    seqs, rows, model = hidden.shape
    width = HEADS * HEAD
    units = third.shape[0]
    tokens = seqs * rows
    shape = jax.ShapeDtypeStruct
    if by_kernel:
        parts = [
            shape((members, shards, QUADS, width // shards // 2, second.shape[1] // 4), BF),
            shape((members, shards, QUADS, units // shards // (QUADS * members), model), BF),
        ]
    else:
        parts = [shape(second.shape, BF), shape(third.shape, BF)]
    return pl.pallas_call(
        functools.partial(middle_kernel, by_kernel, shards, members),
        out_shape=[
            shape((seqs, rows, model), BF),
            shape((seqs, rows, model), F32),
            shape((QUADS, TRIPLE, rows // 2, 2 * HEAD), BF),
            shape((seqs, rows, width), F32),
            *parts,
            shape((4, 8, model), F32),
        ],
        scratch_shapes=[
            pltpu.VMEM((tokens, width), BF),
            pltpu.VMEM((tokens, model), BF),
            pltpu.VMEM((tokens, GROUPS * units), BF),
            pltpu.VMEM((tokens, model), BF),
            pltpu.VMEM((tokens, GROUPS * units), BF),
            pltpu.VMEM((tokens, model), BF),
            pltpu.VMEM((tokens, width), BF),
        ],
        compiler_params=pltpu.CompilerParams(vmem_limit_bytes=60 * 2**20),
    )(context, conv, hidden, cotangent, second, third, small_turned)


def conv_back_kernel(
    by_kernel, shards, members,
    hidden, low_rim, high_rim, first, span, small_turned, d_conv, q_out, spread, key_conv, mix, soft, value, d_first, norm_sums,
    grad_rows, low_edge, high_edge, dq_conv, part_out,
    ext, d_value, d_rows, slim_all, d_key_all, depth_sums, ext_low,
):
    seqs, rows, model = hidden.shape
    width = HEADS * HEAD
    value_at, point_at = 3 * width, 4 * width
    depth = small_turned[64 : 64 + 16, :]
    pair = lax.broadcasted_iota(jnp.int32, (4 * HEAD, 2 * HEAD), 0) // HEAD % 2
    same = pair == lax.broadcasted_iota(jnp.int32, (4 * HEAD, 2 * HEAD), 1) // HEAD
    group_sum = jnp.where(same, 1.0, 0.0).astype(BF)
    depth_sums[...] = jnp.zeros_like(depth_sums)
    long = rows + 2 * RIM
    for s in range(seqs):
        ext[0:RIM] = low_rim[s].astype(F32)
        ext[RIM : RIM + rows] = hidden[s].astype(F32)
        ext[RIM + rows : long] = high_rim[s].astype(F32)
        ext_low[s * long : s * long + RIM] = low_rim[s]
        ext_low[s * long + RIM : s * long + RIM + rows] = hidden[s]
        ext_low[s * long + RIM + rows : s * long + long] = high_rim[s]
        d_value[...] = jnp.zeros_like(d_value)
        d_rows[...] = jnp.zeros_like(d_rows)

        def turn(r, carry):
            top = pl.multiple_of(r * TILE, TILE)
            here = pl.ds(top, TILE)
            there = pl.ds(top, TILE + 2 * RIM)
            every = pl.ds(pl.multiple_of(s * rows + r * TILE, TILE), TILE)
            d_res = d_conv[s, here, :]
            values = value[s, there, :]
            softs = []
            d_kernels = []
            rim = jnp.zeros((RIM, width), F32)
            d_values = jnp.zeros((TILE + 2 * RIM, width), F32)
            total = jnp.zeros((TILE, width), F32)
            for tap in range(KERNEL):
                one = soft[tap, s, here, :].astype(F32)
                softs.append(one)
                weighted = jnp.concatenate([rim, one * d_res, rim], axis=0)
                d_values = d_values + moved(weighted, KERNEL // 2 - tap)
                product = d_res * moved(values, tap - KERNEL // 2)[RIM : RIM + TILE]
                high = product.astype(BF)
                rest = (product - high.astype(F32)).astype(BF)
                sums = []
                for at in range(0, width, 2 * HEAD):
                    both = jnp.concatenate([high[:, at : at + 2 * HEAD], rest[:, at : at + 2 * HEAD]], axis=1)
                    sums.append(dot(both, group_sum, NN))
                d_kernel = jnp.concatenate(sums, axis=1)
                d_kernels.append(d_kernel)
                total = total + d_kernel * one
            d_value[there, :] += d_values
            slim = jnp.zeros((TILE, SMALL), F32)
            for tap in range(KERNEL):
                d_logits = (softs[tap] * (d_kernels[tap] - total)).astype(BF)
                slim = slim + dot(d_logits, head_columns(tap, False), NN)
            slim = slim.astype(BF)
            slim_all[every] = slim
            d_mix = dot(slim, span[...], NT)
            dq_conv[s, here, :] = d_mix * key_conv[s, here, :]
            d_key = (d_mix * q_out[s, here, :].astype(F32)).astype(BF)
            d_key_all[every] = d_key
            d_spread = dot(d_key, first[:, point_at : point_at + width], NT)
            around = ext[there, :]
            wide_rim = jnp.zeros((RIM, model), F32)
            padded = jnp.concatenate([wide_rim, d_spread, wide_rim], axis=0)
            back = jnp.zeros((TILE + 2 * RIM, model), F32)
            for tap in range(KERNEL):
                depth_sums[tap] += fold(d_spread * moved(around, tap - KERNEL // 2)[RIM : RIM + TILE])
                back = back + moved(padded, KERNEL // 2 - tap) * depth[tap : tap + 1]
            d_rows[there, :] += back
            return carry

        lax.fori_loop(0, rows // TILE, turn, 0)
        value_low = d_value[...].astype(BF)
        value_part = dot(ext_low[s * long : s * long + long], value_low, TN)
        if s == 0:
            grad_value = value_part
        else:
            grad_value = grad_value + value_part
        all_rows = dot(value_low, first[:, value_at : value_at + width], NT) + d_rows[...]
        grad_rows[s] = all_rows[RIM : RIM + rows] + d_first[s]
        low_edge[s] = all_rows[0:RIM].astype(BF)
        high_edge[s] = all_rows[RIM + rows :].astype(BF)

    grad_point = dot(spread[...].reshape(seqs * rows, model), d_key_all[...], TN)
    grad_span = dot(mix[...].reshape(seqs * rows, width), slim_all[...], TN)
    lines = [jnp.zeros((64, model), F32)]
    lines += [jnp.sum(depth_sums[tap], axis=0, keepdims=True) for tap in range(KERNEL)]
    lines += [jnp.sum(norm_sums[j], axis=0, keepdims=True) for j in range(4)]
    lines += [jnp.zeros((SMALL - 64 - KERNEL - 4, model), F32)]
    block, head_block = model // shards, width // shards
    slots = []
    for z in range(shards):
        slots += [grad_span[z * head_block : z * head_block + head_block], jnp.zeros((block - head_block, SMALL), F32)]
    small = jnp.concatenate(lines, axis=0).T + jnp.concatenate(slots, axis=0)
    whole = jnp.concatenate([grad_value, grad_point, small, jnp.zeros((model, SMALL), F32)], axis=1).astype(BF)
    if by_kernel:
        piece = block // QUADS
        wide = whole.shape[1] // members
        for z in range(shards):
            for q in range(QUADS):
                row = z * block + q * piece
                for c in range(members):
                    part_out[c, z, q] = whole[row : row + piece, c * wide : c * wide + wide]
    else:
        part_out[...] = whole


def conv_back(by_kernel, shards, members, *arrays):
    hidden = arrays[0]
    seqs, rows, model = hidden.shape
    width = HEADS * HEAD
    long = rows + 2 * RIM
    columns = 2 * width + 2 * SMALL
    shape = jax.ShapeDtypeStruct
    if by_kernel:
        part = shape((members, shards, QUADS, model // shards // QUADS, columns // members), BF)
    else:
        part = shape((model, columns), BF)
    return pl.pallas_call(
        functools.partial(conv_back_kernel, by_kernel, shards, members),
        out_shape=[
            shape((seqs, rows, model), F32),
            shape((seqs, RIM, model), BF),
            shape((seqs, RIM, model), BF),
            shape((seqs, rows, width), F32),
            part,
        ],
        scratch_shapes=[
            pltpu.VMEM((long, model), F32),
            pltpu.VMEM((long, width), F32),
            pltpu.VMEM((long, model), F32),
            pltpu.VMEM((seqs * rows, SMALL), BF),
            pltpu.VMEM((seqs * rows, width), BF),
            pltpu.VMEM((KERNEL, 8, model), F32),
            pltpu.VMEM((seqs * long, model), BF),
        ],
        compiler_params=pltpu.CompilerParams(vmem_limit_bytes=60 * 2**20),
    )(*arrays)


def tail_kernel(by_kernel, shards, members, *refs):
    hidden, first, dq_in, dkv_in, dq_conv, grad_rows, low_edge, high_edge, grad_in, out, d_all, *scratch = refs
    seqs, rows, model = hidden.shape
    half = rows // 2
    width = HEADS * HEAD
    is_low = low_lanes()
    if by_kernel:
        part, *scratch = scratch
        place = Place(members, shards)
        place.greet(True)
        one = Reduce(place, part, out, 2, scratch)
    for s in range(seqs):
        for j in range(HEADS // 2):
            a = dq_in[s * 2 + 2 * j // TRIPLE, 2 * j % TRIPLE].astype(F32)
            b = dq_in[s * 2 + (2 * j + 1) // TRIPLE, (2 * j + 1) % TRIPLE].astype(F32)
            at = j * 2 * HEAD
            upper = jnp.where(is_low, a, swap_halves(b)) + dq_conv[s, 0:half, at : at + 2 * HEAD]
            lower = jnp.where(is_low, swap_halves(a), b) + dq_conv[s, half:rows, at : at + 2 * HEAD]
            d_all[s * rows : s * rows + half, at : at + 2 * HEAD] = upper.astype(BF)
            d_all[s * rows + half : s * rows + rows, at : at + 2 * HEAD] = lower.astype(BF)
        for h in range(HEADS):
            at = width + h * 2 * HEAD
            d_all[s * rows : s * rows + rows, at : at + 2 * HEAD] = dkv_in[s * 2 + h // TRIPLE, h % TRIPLE]
    tokens = hidden[...].reshape(seqs * rows, model)
    if by_kernel:
        block = model // shards
        piece = block // QUADS
        wide = part.shape[4]
        for c in range(members):
            left, right = c * wide, min(c * wide + wide, 3 * width)
            value = dot(tokens, d_all[:, left:right], TN).astype(BF)
            for z in range(shards):
                for q in range(QUADS):
                    row = z * block + q * piece
                    part[c, z, q, :, 0 : right - left] = value[row : row + piece]
                    if right - left < wide:
                        part[c, z, q, :, right - left : wide] = jnp.zeros((piece, wide - right + left), BF)
        one.start()
    else:
        out[:, : 3 * width] = dot(tokens, d_all[...], TN).astype(BF)
        out[:, 3 * width :] = jnp.zeros((model, out.shape[1] - 3 * width), BF)

    def rows_turn(s):
        total = grad_rows[s] + dot(d_all[s * rows : s * rows + rows], first[:, : 3 * width], NT)
        grad_in[s] = total
        grad_in[s, 0:RIM] = total[0:RIM] + low_edge[s].astype(F32)
        grad_in[s, rows - RIM : rows] = total[rows - RIM : rows] + high_edge[s].astype(F32)

    if by_kernel:
        one.to_quads()
    for s in range(seqs):
        rows_turn(s)
    if by_kernel:
        one.to_shards()
        one.give()
        one.share()
        one.end()


def tail(by_kernel, shards, members, *arrays):
    hidden = arrays[0]
    seqs, rows, model = hidden.shape
    width = HEADS * HEAD
    columns = 3 * width + SMALL
    shape = jax.ShapeDtypeStruct
    scratch = [pltpu.VMEM((seqs * rows, 3 * width), BF)]
    if by_kernel:
        piece = (model // shards // QUADS, columns // members)
        scratch += [pltpu.VMEM((members, shards, QUADS, *piece), BF)] + Reduce.scratch(members, shards, *piece)
        params = pltpu.CompilerParams(collective_id=4, has_side_effects=True, vmem_limit_bytes=56 * 2**20)
    else:
        params = pltpu.CompilerParams(vmem_limit_bytes=56 * 2**20)
    vm = pl.BlockSpec(memory_space=pltpu.VMEM)
    return pl.pallas_call(
        functools.partial(tail_kernel, by_kernel, shards, members),
        in_specs=[vm] * len(arrays),
        out_specs=[vm, pl.BlockSpec(memory_space=pl.ANY) if by_kernel else vm],
        out_shape=[
            shape((seqs, rows, model), F32),
            shape((model // shards if by_kernel else model, columns), BF),
        ],
        scratch_shapes=scratch,
        compiler_params=params,
    )(*arrays)


SPLITS = (2, 4, 1)


def shards(
    hidden_in,
    cotangent,
    qkv_weight,
    conv_depth,
    conv_point,
    span_weight,
    conv_value,
    dense_attn,
    dense_conv,
    attn_norm_gain,
    attn_norm_bias,
    ffn_inner,
    ffn_outer,
    out_norm_gain,
    out_norm_bias,
):
    attn_width = HEADS * HEAD
    seq_count, local_rows, model_width = hidden_in.shape
    ctx_count = lax.axis_size("ctx")
    members = ctx_count // QUADS
    shard_count = lax.axis_size("shard")
    width_rows = model_width // shard_count
    head_rows = attn_width // shard_count
    forward = [(i, i + 1) for i in range(ctx_count - 1)]
    backward = [(i + 1, i) for i in range(ctx_count - 1)]
    low_rim = lax.ppermute(hidden_in[:, local_rows - RIM :], "ctx", forward)
    high_rim = lax.ppermute(hidden_in[:, :RIM], "ctx", backward)
    small = jnp.concatenate(
        [
            jnp.pad(span_weight, ((0, width_rows - head_rows), (0, 64 - HEADS * KERNEL))),
            conv_depth.T,
            jnp.stack([attn_norm_gain, attn_norm_bias, out_norm_gain, out_norm_bias], axis=1),
            jnp.zeros((width_rows, SMALL - 64 - KERNEL - 4), BF),
        ],
        axis=1,
    )
    pairs = qkv_weight[:, attn_width:].reshape(width_rows, 2, HEADS, HEAD).transpose(0, 2, 1, 3)
    first_block = jnp.concatenate(
        [qkv_weight[:, :attn_width], pairs.reshape(width_rows, -1), conv_value, conv_point, small], axis=1
    )
    second_block = jnp.concatenate([dense_attn, dense_conv, ffn_inner[0], ffn_inner[1]], axis=1)
    third_block = jnp.concatenate([ffn_outer[0], ffn_outer[1]], axis=1)
    shapes = (first_block.shape, second_block.shape, third_block.shape)
    by_kernel = members == 2 and all(fits(*shape, members, split) for shape, split in zip(shapes, SPLITS))
    if by_kernel:
        first = gather_weight(first_block, members, shard_count, SPLITS[0], 3)
    else:
        first = lax.all_gather(first_block, "shard", axis=0, tiled=True)
        second = lax.all_gather(second_block, "shard", axis=0, tiled=True)
        third = lax.all_gather(third_block, "shard", axis=0, tiled=True)
    span = first[:, 5 * attn_width :].reshape(shard_count, width_rows, SMALL)[:, :head_rows]
    span = span.reshape(attn_width, SMALL)
    kv, q_packed, q_low, spread, key_conv, span_mix, kernel_soft, value_ext, conv_low, small_turned = front(
        hidden_in, low_rim, high_rim, first, span
    )
    kv_all, q_all, out_all, lse, context, *gathered = attend_forward(
        kv, q_packed, members, shard_count,
        (second_block, third_block) if by_kernel else (), SPLITS[1:] if by_kernel else (),
    )
    if by_kernel:
        second, third = gathered
    layer_out, d_first, d_context, d_conv, second_part, third_part, norm_sums = middle(
        context, conv_low, hidden_in, cotangent, second, third, small_turned, by_kernel, shard_count, members
    )
    grad_rows, low_edge, high_edge, dq_conv, middle_part = conv_back(
        by_kernel, shard_count, members,
        hidden_in, low_rim, high_rim, first, span, small_turned, d_conv, q_low, spread, key_conv, span_mix,
        kernel_soft, value_ext, d_first, norm_sums,
    )
    low_in = lax.ppermute(high_edge, "ctx", forward)
    high_in = lax.ppermute(low_edge, "ctx", backward)
    parts = ()
    part_splits = ()
    middle_width = 2 * attn_width + 2 * SMALL
    if by_kernel:
        parts = (
            (third_part, third_block.shape),
            (second_part, second_block.shape),
            (middle_part, (width_rows, middle_width)),
        )
        part_splits = (SPLITS[2], SPLITS[1], SPLITS[0])
    dq_packed, dkv, *reduced = attend_backward(
        d_context, kv_all, q_all, out_all, lse, members, shard_count, parts, part_splits
    )
    grad_in, first_sum = tail(
        by_kernel, shard_count, members,
        hidden_in, first, dq_packed, dkv, dq_conv, grad_rows, low_in, high_in,
    )
    if by_kernel:
        third_sum, second_sum, middle_sum = reduced
    else:
        first_sum, second_sum, third_sum, middle_sum = (
            lax.psum(lax.psum_scatter(one, "shard", scatter_dimension=0, tiled=True), "ctx")
            for one in (first_sum, second_part, third_part, middle_part)
        )
    first_sum, second_sum, third_sum, middle_sum = (
        one.astype(F32) for one in (first_sum, second_sum, third_sum, middle_sum)
    )
    edge = 2 * attn_width
    norms = middle_sum[:, edge + 64 + KERNEL : edge + 68 + KERNEL].T
    pair_sum = first_sum[:, attn_width : 3 * attn_width].reshape(width_rows, HEADS, 2, HEAD).transpose(0, 2, 1, 3)
    result_grads = (
        jnp.concatenate([first_sum[:, :attn_width], pair_sum.reshape(width_rows, -1)], axis=1),
        middle_sum[:, edge + 64 : edge + 64 + KERNEL].T,
        middle_sum[:, attn_width:edge],
        middle_sum[:head_rows, edge : edge + HEADS * KERNEL],
        middle_sum[:, :attn_width],
        second_sum[:, :model_width],
        second_sum[:, model_width : 2 * model_width],
        norms[0],
        norms[1],
        second_sum[:, 2 * model_width :].reshape(head_rows, GROUPS, -1).transpose(1, 0, 2),
        third_sum.reshape(-1, GROUPS, D // GROUPS).transpose(1, 0, 2),
        norms[2],
        norms[3],
    )
    return (layer_out, grad_in) + result_grads


def solution(mesh):
    return jax.shard_map(
        shards,
        mesh=mesh,
        in_specs=(
            P("shard", "ctx", None),
            P("shard", "ctx", None),
            P("shard", None),
            P(None, "shard"),
            P("shard", None),
            P("shard", None),
            P("shard", None),
            P("shard", None),
            P("shard", None),
            P("shard"),
            P("shard"),
            P(None, "shard", None),
            P(None, "shard", None),
            P("shard"),
            P("shard"),
        ),
        out_specs=(
            P("shard", "ctx", None),
            P("shard", "ctx", None),
            P("shard", None),
            P(None, "shard"),
            P("shard", None),
            P("shard", None),
            P("shard", None),
            P("shard", None),
            P("shard", None),
            P("shard"),
            P("shard"),
            P(None, "shard", None),
            P(None, "shard", None),
            P("shard"),
            P("shard"),
        ),
        check_vma=False,
    )
```

```python
import functools
import math

import jax
import jax.numpy as jnp
from jax import lax
from jax.experimental import pallas as pl
from jax.experimental.pallas import tpu as pltpu
from jax.sharding import PartitionSpec as P

D = 768
HEADS = 6
HEAD = 64
GROUPS = 2
KERNEL = 9


norm_eps = 1e-12


BF = jnp.bfloat16
F32 = jnp.float32
MESH_ID = pl.DeviceIdType.MESH
NT = (((1,), (1,)), ((), ()))
NN = (((1,), (0,)), ((), ()))
EXP2_SCALE = math.log2(math.e) / math.sqrt(HEAD)
TRIPLE = 3
QUADS = 4
CHUNK = 128


def dot(a, b, dims):
    return lax.dot_general(a, b, dims, preferred_element_type=F32)


def swap_halves(packed):
    return jnp.concatenate([packed[:, HEAD:], packed[:, :HEAD]], axis=1)


def low_lanes():
    return lax.broadcasted_iota(jnp.int32, (1, 2 * HEAD), 1) < HEAD


def remote(src, dst, send, recv, target):
    return pltpu.make_async_remote_copy(
        src_ref=src, dst_ref=dst, send_sem=send, recv_sem=recv,
        device_id=target, device_id_type=MESH_ID,
    )


def greet(peers):
    barrier = pltpu.get_barrier_semaphore()
    for peer in peers:
        pl.semaphore_signal(barrier, inc=1, device_id=peer, device_id_type=MESH_ID)
    pl.semaphore_wait(barrier, len(peers))


class Place:
    def __init__(self, members, shards):
        self.members, self.shards = members, shards
        self.me = lax.axis_index("ctx")
        self.z = lax.axis_index("shard")
        self.quad, self.sub = self.me // members, self.me % members

    def peer(self, step):
        return ((self.quad + step) % QUADS * self.members + self.sub, self.z)

    def sibling(self, step):
        return (self.quad * self.members + (self.sub + step) % self.members, self.z)

    def behind(self, step):
        return (self.quad + QUADS - step) % QUADS

    def along(self, step):
        return (self.me, (self.z + step) % self.shards)

    def z_behind(self, step):
        return (self.z + self.shards - step) % self.shards

    def greet(self, with_shard, more=()):
        peers = [self.peer(k) for k in range(1, QUADS)]
        peers += [self.sibling(m) for m in range(1, self.members)]
        if with_shard:
            peers += [self.along(d) for d in range(1, self.shards)]
        greet(peers + list(more))


class Pieces:
    def __init__(self, place, rows, columns, col_split):
        count = QUADS * place.members
        self.place, self.rows, self.col_split = place, rows, col_split
        self.piece_rows = rows // (count // col_split)
        self.piece_cols = columns // col_split

    def at(self, ref, z, quad, sub):
        index = quad * self.place.members + sub
        top = pl.multiple_of(z * self.rows + index // self.col_split * self.piece_rows, 16)
        left = pl.multiple_of(index % self.col_split * self.piece_cols, 128)
        return ref.at[pl.ds(top, self.piece_rows), pl.ds(left, self.piece_cols)]


def fits(rows, columns, members, col_split):
    count = QUADS * members
    if count % col_split:
        return False
    row_split = count // col_split
    return rows % (16 * row_split) == 0 and columns % (128 * col_split) == 0


class Gather:
    def __init__(self, place, shard_ref, full_ref, col_split, sems):
        self.place, self.shard_ref, self.full_ref = place, shard_ref, full_ref
        rows, columns = shard_ref.shape
        self.rows = rows
        self.pieces = Pieces(place, rows, columns, col_split)
        self.z_s, self.z_r, self.q_s, self.q_r, self.f_s, self.f_r, self.local = sems

    @staticmethod
    def semaphores(members, shards):
        dma = pltpu.SemaphoreType.DMA
        return [
            dma((shards,)), dma((shards,)), dma((shards, QUADS)), dma((shards, QUADS)),
            dma((shards, QUADS, members)), dma((shards, QUADS, members)), dma((1,)),
        ]

    def z_copy(self, d):
        p = self.place
        return remote(
            self.pieces.at(self.shard_ref, 0, p.quad, p.sub), self.pieces.at(self.full_ref, p.z, p.quad, p.sub),
            self.z_s.at[d], self.z_r.at[d], p.along(d),
        )

    def q_copy(self, d, k):
        p = self.place
        block = self.pieces.at(self.full_ref, p.z_behind(d), p.quad, p.sub)
        return remote(block, block, self.q_s.at[d, k], self.q_r.at[d, k], p.peer(k))

    def f_copy(self, d, k, m):
        p = self.place
        block = self.pieces.at(self.full_ref, p.z_behind(d), p.behind(k), p.sub)
        return remote(block, block, self.f_s.at[d, k, m], self.f_r.at[d, k, m], p.sibling(m))

    def own_copy(self):
        top = pl.multiple_of(self.place.z * self.rows, 16)
        return pltpu.make_async_copy(
            self.shard_ref, self.full_ref.at[pl.ds(top, self.rows), :], self.local.at[0]
        )

    def start(self):
        for d in range(1, self.place.shards):
            self.z_copy(d).start()
        self.own_copy().start()

    def relay(self):
        for d in range(1, self.place.shards):
            self.z_copy(d).wait_recv()
            for k in range(1, QUADS):
                self.q_copy(d, k).start()
            for m in range(1, self.place.members):
                self.f_copy(d, 0, m).start()

    def share(self):
        for d in range(1, self.place.shards):
            for k in range(1, QUADS):
                self.q_copy(d, k).wait_recv()
                for m in range(1, self.place.members):
                    self.f_copy(d, k, m).start()

    def end(self):
        for d in range(1, self.place.shards):
            self.z_copy(d).wait_send()
            for k in range(QUADS):
                if k:
                    self.q_copy(d, k).wait_send()
                for m in range(1, self.place.members):
                    self.f_copy(d, k, m).wait()
        self.own_copy().wait()


class Reduce:
    def __init__(self, place, part_ref, out_ref, col_split, scratch):
        self.place, self.part_ref, self.out_ref = place, part_ref, out_ref
        self.piece_rows, self.piece_cols = part_ref.shape[3:]
        rows, columns = out_ref.shape
        self.pieces = Pieces(place, rows, columns, col_split)
        (
            self.half, self.half_in, self.quad_in, self.block, self.z_in, self.last,
            self.h_s, self.h_r, self.q_s, self.q_r, self.z_s, self.z_r, self.a_s, self.a_r, self.f_s, self.f_r, self.local,
        ) = scratch

    @staticmethod
    def scratch(members, shards, rows, columns):
        dma = pltpu.SemaphoreType.DMA
        return [
            pltpu.VMEM((shards, QUADS, rows, columns), BF),
            pltpu.VMEM((members, shards, QUADS, rows, columns), BF),
            pltpu.VMEM((QUADS, shards, rows, columns), BF),
            pltpu.VMEM((shards, rows, columns), BF),
            pltpu.VMEM((shards, rows, columns), BF),
            pltpu.VMEM((rows, columns), BF),
            dma((members,)), dma((members,)), dma((QUADS,)), dma((QUADS,)), dma((shards,)), dma((shards,)),
            dma((QUADS,)), dma((QUADS,)), dma((QUADS, members)), dma((QUADS, members)), dma((1,)),
        ]

    def h_copy(self, m):
        p = self.place
        return remote(
            self.part_ref.at[(p.sub + m) % p.members], self.half_in.at[m], self.h_s.at[m], self.h_r.at[m], p.sibling(m)
        )

    def q_copy(self, k):
        p = self.place
        return remote(
            self.half.at[:, (p.quad + k) % QUADS], self.quad_in.at[k], self.q_s.at[k], self.q_r.at[k], p.peer(k)
        )

    def z_copy(self, d):
        p = self.place
        return remote(
            self.block.at[(p.z + d) % p.shards], self.z_in.at[d], self.z_s.at[d], self.z_r.at[d], p.along(d)
        )

    def a_copy(self, k):
        p = self.place
        return remote(
            self.last, self.pieces.at(self.out_ref, 0, p.quad, p.sub), self.a_s.at[k], self.a_r.at[k], p.peer(k)
        )

    def f_copy(self, k, m):
        p = self.place
        block = self.pieces.at(self.out_ref, 0, p.behind(k), p.sub)
        return remote(block, block, self.f_s.at[k, m], self.f_r.at[k, m], p.sibling(m))

    def own_copy(self):
        p = self.place
        return pltpu.make_async_copy(
            self.last, self.pieces.at(self.out_ref, 0, p.quad, p.sub), self.local.at[0]
        )

    def start(self):
        for m in range(1, self.place.members):
            self.h_copy(m).start()

    def to_quads(self):
        for m in range(1, self.place.members):
            self.h_copy(m).wait_recv()

        def turn(i, carry):
            z, q = i // QUADS, i % QUADS
            total = self.part_ref[self.place.sub, z, q].astype(F32)
            for m in range(1, self.place.members):
                total = total + self.half_in[m, z, q].astype(F32)
            self.half[z, q] = total.astype(BF)
            return carry

        lax.fori_loop(0, self.place.shards * QUADS, turn, 0)
        for k in range(1, QUADS):
            self.q_copy(k).start()

    def to_shards(self):
        for k in range(1, QUADS):
            self.q_copy(k).wait_recv()

        def turn(z, carry):
            total = self.half[z, self.place.quad].astype(F32)
            for k in range(1, QUADS):
                total = total + self.quad_in[k, z].astype(F32)
            self.block[z] = total.astype(BF)
            return carry

        lax.fori_loop(0, self.place.shards, turn, 0)
        for d in range(1, self.place.shards):
            self.z_copy(d).start()

    def give(self):
        total = self.block[self.place.z].astype(F32)
        for d in range(1, self.place.shards):
            self.z_copy(d).wait_recv()
            total = total + self.z_in[d].astype(F32)
        self.last[...] = total.astype(BF)
        for k in range(1, QUADS):
            self.a_copy(k).start()
        self.own_copy().start()
        self.own_copy().wait()
        for m in range(1, self.place.members):
            self.f_copy(0, m).start()

    def share(self):
        for k in range(1, QUADS):
            self.a_copy(k).wait_recv()
            for m in range(1, self.place.members):
                self.f_copy(k, m).start()

    def end(self):
        for m in range(1, self.place.members):
            self.h_copy(m).wait_send()
        for k in range(1, QUADS):
            self.q_copy(k).wait_send()
            self.a_copy(k).wait_send()
        for d in range(1, self.place.shards):
            self.z_copy(d).wait_send()
        for k in range(QUADS):
            for m in range(1, self.place.members):
                self.f_copy(k, m).wait()


def attend_backward_kernel(members, shards, splits, *refs):
    count = len(splits)
    d_in, kv_all, q_all, out_all, lse, *parts = refs[: 5 + count]
    dq_out, dkv_out, *sums = refs[5 + count : 7 + 2 * count]
    (
        d_all, q_zero, d_zero, stat, delta, dq_sum, dkv_sum, own_part, sib_send, sib_recv, dkv_send, dq_send,
        d_s, d_r, p_s, p_r, k_s, k_r, g_s, g_r, local, *scratch,
    ) = refs[7 + 2 * count :]
    rows = kv_all.shape[3]
    half = rows // 2
    steps = TRIPLE * QUADS
    place = Place(members, shards)
    quad, sub, peer, sibling = place.quad, place.sub, place.peer, place.sibling
    place.greet(bool(splits))
    reduces = [
        Reduce(place, one, total, split, scratch[17 * j : 17 * j + 17])
        for j, (one, total, split) in enumerate(zip(parts, sums, splits))
    ]

    def d_copy(h, k):
        return remote(
            d_in.at[(quad + k) % QUADS, h], d_all.at[h, quad], d_s.at[h, k], d_r.at[h, k], peer(k)
        )

    def part_copy(step, m):
        return remote(
            sib_send.at[step % 2, m], sib_recv.at[step, m], p_s.at[step, m], p_r.at[step, m], sibling(m)
        )

    def dkv_copy(h, i, k):
        return remote(
            dkv_send.at[h, i], dkv_out.at[quad, h], k_s.at[h, i], k_r.at[h, i], peer(k)
        )

    def dq_copy(h, k):
        return remote(
            dq_send.at[h, (quad + k) % QUADS], dq_out.at[quad, h], g_s.at[h, k], g_r.at[h, k], peer(k)
        )

    own = pltpu.make_async_copy(d_in.at[quad], d_all.at[:, quad], local.at[0])
    own.start()
    for h in range(TRIPLE):
        for k in range(1, QUADS):
            d_copy(h, k).start()
    for one in reduces:
        one.start()
    own.wait()
    is_low = low_lanes()

    def finish(step):
        h, i = step // QUADS, step % QUADS
        k = (i + 1) % QUADS
        total = own_part[step % 2]
        for m in range(1, members):
            part_copy(step, m).wait_recv()
            total = total + sib_recv[step, m].astype(F32)
        dkv_send[h, i] = total.astype(BF)

        @pl.when(k != 0)
        def _():
            dkv_copy(h, i, k).start()

        @pl.when(k == 0)
        def _():
            own = pltpu.make_async_copy(dkv_send.at[h, i], dkv_out.at[quad, h], local.at[0])
            own.start()
            own.wait()

    def block(step, carry):
        h, i = step // QUADS, step % QUADS
        k = (i + 1) % QUADS
        source = (quad + k) % QUADS

        @pl.when(i == 0)
        def _():
            for j in range(1, QUADS):
                d_copy(h, j).wait_recv()

            def prepare(b, inner):
                q = q_all[h, b]
                d = d_all[h, b]
                zero = jnp.zeros_like(q)
                q_zero[b, 0:half] = jnp.where(is_low, q, zero)
                q_zero[b, half:rows] = jnp.where(is_low, swap_halves(q), zero)
                d_zero[b, 0:half] = jnp.where(is_low, zero, swap_halves(d))
                d_zero[b, half:rows] = jnp.where(is_low, zero, d)
                both = (out_all[h, b] * d.astype(F32)).T
                delta[b, :, 0:half] = jnp.broadcast_to(jnp.sum(both[0:HEAD], axis=0, keepdims=True), (8, half))
                delta[b, :, half:rows] = jnp.broadcast_to(jnp.sum(both[HEAD:], axis=0, keepdims=True), (8, half))
                for part in range(2):
                    for r in range(half // CHUNK):
                        at = part * half + r * CHUNK
                        stat[b, :, at : at + CHUNK] = lse[h, b, part, r]
                dq_sum[b] = jnp.zeros((HEAD, rows), F32)
                return inner

            lax.fori_loop(0, QUADS, prepare, 0)

        keys = kv_all[h, source].reshape(members * rows, 2 * HEAD)
        keys_turned = keys.T[0:HEAD]
        dkv_sum[...] = jnp.zeros_like(dkv_sum)

        def queries_turn(b, inner):
            qz = q_zero[b]
            dz = d_zero[b]
            probs = jnp.exp2(dot(keys, qz, NT) * EXP2_SCALE - stat[b, 0:1, :])
            d_probs = dot(keys, dz, NT)
            d_scores = (probs * (d_probs - delta[b, 0:1, :])).astype(BF)
            dkv_sum[...] += dot(d_scores, qz, NN) * (1.0 / math.sqrt(HEAD)) + dot(probs.astype(BF), dz, NN)
            dq_sum[b] += dot(keys_turned, d_scores, NN)
            return inner

        lax.fori_loop(0, QUADS, queries_turn, 0)

        @pl.when(step > 0)
        def _():
            finish(step - 1)

        own_part[step % 2] = dkv_sum[pl.ds(pl.multiple_of(sub * rows, rows), rows), :]
        for m in range(1, members):
            @pl.when(step > 1)
            def _():
                part_copy(step - 2, m).wait_send()
            target = (sub + m) % members
            sib_send[step % 2, m] = dkv_sum[pl.ds(pl.multiple_of(target * rows, rows), rows), :].astype(BF)
            part_copy(step, m).start()

        @pl.when(i == QUADS - 1)
        def _():
            def give(b, inner):
                turned = dq_sum[b] * (1.0 / math.sqrt(HEAD))
                dq_send[h, b] = jnp.concatenate([turned[:, 0:half], turned[:, half:rows]], axis=0).T.astype(BF)
                return inner

            lax.fori_loop(0, QUADS, give, 0)
            for j in range(1, QUADS):
                dq_copy(h, j).start()
            mine = pltpu.make_async_copy(dq_send.at[h, quad], dq_out.at[quad, h], local.at[0])
            mine.start()
            mine.wait()

        for j, one in enumerate(reduces):
            for at, stage in ((j, one.to_quads), (j + 4, one.to_shards), (j + 6, one.give), (j + 8, one.share)):

                @pl.when(step == at)
                def _(stage=stage):
                    stage()

        return carry

    lax.fori_loop(0, steps, block, 0)
    finish(steps - 1)
    for m in range(1, members):
        part_copy(steps - 2, m).wait_send()
        part_copy(steps - 1, m).wait_send()
    for h in range(TRIPLE):
        for k in range(1, QUADS):
            d_copy(h, k).wait_send()
            dkv_copy(h, k - 1, k).wait()
            dq_copy(h, k).wait()
    for one in reduces:
        one.end()


def attend_backward(d_context, kv_all, q_all, out_all, lse, members, shards, parts, splits):
    rows = kv_all.shape[3]
    half = rows // 2
    steps = TRIPLE * QUADS
    vm = pl.BlockSpec(memory_space=pltpu.VMEM)
    anywhere = pl.BlockSpec(memory_space=pl.ANY)
    dma = pltpu.SemaphoreType.DMA
    total = TRIPLE * QUADS * rows * QUADS * members * rows
    return pl.pallas_call(
        functools.partial(attend_backward_kernel, members, shards, splits),
        in_specs=[anywhere, vm, vm, vm, vm] + [vm] * len(parts),
        out_specs=[anywhere, anywhere] + [anywhere] * len(parts),
        out_shape=[
            jax.ShapeDtypeStruct((QUADS, TRIPLE, half, 2 * HEAD), BF),
            jax.ShapeDtypeStruct((QUADS, TRIPLE, rows, 2 * HEAD), BF),
        ]
        + [jax.ShapeDtypeStruct(shape, BF) for _, shape in parts],
        scratch_shapes=[
            pltpu.VMEM((TRIPLE, QUADS, half, 2 * HEAD), BF),
            pltpu.VMEM((QUADS, rows, 2 * HEAD), BF),
            pltpu.VMEM((QUADS, rows, 2 * HEAD), BF),
            pltpu.VMEM((QUADS, 8, rows), F32),
            pltpu.VMEM((QUADS, 8, rows), F32),
            pltpu.VMEM((QUADS, HEAD, rows), F32),
            pltpu.VMEM((members * rows, 2 * HEAD), F32),
            pltpu.VMEM((2, rows, 2 * HEAD), F32),
            pltpu.VMEM((2, members, rows, 2 * HEAD), BF),
            pltpu.VMEM((steps, members, rows, 2 * HEAD), BF),
            pltpu.VMEM((TRIPLE, QUADS, rows, 2 * HEAD), BF),
            pltpu.VMEM((TRIPLE, QUADS, half, 2 * HEAD), BF),
            dma((TRIPLE, QUADS)), dma((TRIPLE, QUADS)),
            dma((steps, members)), dma((steps, members)),
            dma((TRIPLE, QUADS)), dma((TRIPLE, QUADS)), dma((TRIPLE, QUADS)), dma((TRIPLE, QUADS)),
            dma((2,)),
        ]
        + sum((Reduce.scratch(members, shards, *one.shape[3:]) for one, _ in parts), []),
        compiler_params=pltpu.CompilerParams(
            collective_id=2, has_side_effects=True, vmem_limit_bytes=56 * 2**20
        ),
        cost_estimate=pl.CostEstimate(flops=total * 640, bytes_accessed=8 * 2**20, transcendentals=total),
    )(d_context, kv_all, q_all, out_all, lse, *[one for one, _ in parts])


RIM = 16
TILE = 128
SMALL = 128
TN = (((0,), (0,)), ((), ()))


def moved(value, by):
    rows = value.shape[0]
    return value if by % rows == 0 else pltpu.roll(value, (-by) % rows, 0)


def head_columns(tap, wide_first):
    shape = (SMALL, HEADS * HEAD) if wide_first else (HEADS * HEAD, SMALL)
    narrow = lax.broadcasted_iota(jnp.int32, shape, 0 if wide_first else 1)
    wide = lax.broadcasted_iota(jnp.int32, shape, 1 if wide_first else 0)
    if wide_first:
        same = narrow == wide // HEAD * KERNEL + tap
    else:
        same = (narrow * HEAD == (wide * KERNEL + tap * HEAD)) & (wide % HEAD == 0)
    return jnp.where(same, 1.0, 0.0).astype(BF)


def norm_rows(value):
    center = value - jnp.mean(value, axis=-1, keepdims=True)
    inv_std = lax.rsqrt(jnp.mean(center * center, axis=-1, keepdims=True) + norm_eps)
    return center * inv_std, inv_std


def norm_rows_back(normed, inv_std, d_scaled):
    return inv_std * (
        d_scaled
        - jnp.mean(d_scaled, axis=-1, keepdims=True)
        - normed * jnp.mean(d_scaled * normed, axis=-1, keepdims=True)
    )


def fold(value):
    return jnp.sum(value.reshape(value.shape[0] // 8, 8, value.shape[1]), axis=0)


def gelu_both(value):
    size = jnp.abs(value)
    turn = 1.0 / (1.0 + (0.3275911 / math.sqrt(2.0)) * size)
    bell = jnp.exp2(value * value * (-0.5 * math.log2(math.e)))
    poly = ((((1.061405429 * turn - 1.453152027) * turn + 1.421413741) * turn - 0.284496736) * turn + 0.254829592) * turn
    tail = 0.5 * poly * bell
    below = jnp.where(value < 0.0, tail, 1.0 - tail)
    return value * below, below + value * bell * (1.0 / math.sqrt(2.0 * math.pi))


def project_body(hidden, qkv, kv_out, q_packed, q_out):
    seqs, rows, _ = hidden.shape
    half = rows // 2
    width = HEADS * HEAD
    is_low = low_lanes()

    def turn(step, carry):
        s, r = step // (half // TILE), step % (half // TILE)
        tops = (pl.multiple_of(r * TILE, TILE), pl.multiple_of(half + r * TILE, TILE))
        rows_in = jnp.concatenate([hidden[s, pl.ds(top, TILE), :] for top in tops], axis=0)
        mixed = dot(rows_in, qkv[:, : 3 * width], NN).astype(BF)
        for part, top in enumerate(tops):
            block = mixed[part * TILE : part * TILE + TILE]
            q_out[s, pl.ds(top, TILE), :] = block[:, :width]
            for h in range(HEADS):
                at = width + 2 * HEAD * h
                kv_out[s * 2 + h // TRIPLE, h % TRIPLE, pl.ds(top, TILE), :] = block[:, at : at + 2 * HEAD]
        for h in range(HEADS):
            at = h // 2 * 2 * HEAD
            upper = mixed[:TILE, at : at + 2 * HEAD]
            lower = mixed[TILE:, at : at + 2 * HEAD]
            if h % 2:
                packed = jnp.where(is_low, swap_halves(upper), lower)
            else:
                packed = jnp.where(is_low, upper, swap_halves(lower))
            q_packed[s * 2 + h // TRIPLE, h % TRIPLE, pl.ds(tops[0], TILE), :] = packed
        return carry

    lax.fori_loop(0, seqs * half // TILE, turn, 0)


def conv_forward_body(
    s, hidden, low_rim, high_rim, rest, q_out, spread_out, key_out, mix_out, soft_out, value_out, conv_out,
    small_turned, span_wide, ext, soft_tile, soft_sem,
):
    seqs, rows, model = hidden.shape
    width = HEADS * HEAD
    tiles = rows // TILE
    depth = small_turned[64 : 64 + 16, :]
    low, high = low_rim[s], high_rim[s]
    ext[0:RIM] = low.astype(F32)
    ext[RIM : RIM + rows] = hidden[s].astype(F32)
    ext[RIM + rows : rows + 2 * RIM] = high.astype(F32)
    value = rest[:, 0:width]
    value_out[s, 0:RIM] = dot(low, value, NN)
    value_out[s, RIM : RIM + rows] = dot(hidden[s], value, NN)
    value_out[s, RIM + rows : rows + 2 * RIM] = dot(high, value, NN)

    def soft_copy(number):
        return pltpu.make_async_copy(soft_tile.at[number % 2], soft_out.at[number], soft_sem.at[number % 2])

    def turn(r, carry):
        number = s * tiles + r
        top = pl.multiple_of(r * TILE, TILE)
        around = ext[pl.ds(top, TILE + 2 * RIM), :]
        spread = jnp.zeros((TILE, model), F32)
        for tap in range(KERNEL):
            spread = spread + moved(around, tap - KERNEL // 2)[RIM : RIM + TILE] * depth[tap : tap + 1]
        spread_low = spread.astype(BF)
        spread_out[s, pl.ds(top, TILE), :] = spread_low
        key_conv = dot(spread_low, rest[:, width : 2 * width], NN)
        key_out[s, pl.ds(top, TILE), :] = key_conv
        mix = (key_conv * q_out[s, pl.ds(top, TILE), :].astype(F32)).astype(BF)
        mix_out[s, pl.ds(top, TILE), :] = mix
        logits = [dot(mix, span_wide[:, tap * width : tap * width + width], NN) for tap in range(KERNEL)]
        peak = functools.reduce(jnp.maximum, logits)
        powers = [jnp.exp(one - peak) for one in logits]
        scale = 1.0 / sum(powers[1:], powers[0])
        values = value_out[s, pl.ds(top, TILE + 2 * RIM), :]

        @pl.when(number > 1)
        def _():
            soft_copy(number - 2).wait()

        result = jnp.zeros((TILE, width), F32)
        for tap in range(KERNEL):
            soft = powers[tap] * scale
            soft_tile[number % 2, tap] = soft.astype(BF)
            result = result + soft * moved(values, tap - KERNEL // 2)[RIM : RIM + TILE]
        conv_out[s, pl.ds(top, TILE), :] = result.astype(BF)
        soft_copy(number).start()
        return carry

    lax.fori_loop(0, tiles, turn, 0)
    if s == seqs - 1:
        soft_copy(seqs * tiles - 2).wait()
        soft_copy(seqs * tiles - 1).wait()


def front_kernel(by_kernel, members, shards, splits, *refs):
    if by_kernel:
        hidden, qkv_block, rest_block, second_block, third_block, *refs = refs
        blocks = (qkv_block, rest_block, second_block, third_block)
    else:
        hidden, qkv, rest, span, *refs = refs
    (
        kv_all, q_all, out_all, lse, ctx_out, q_out, spread_out, key_out, mix_out, soft_out, value_out, conv_out,
        small_turned, low_rim, high_rim, *refs,
    ) = refs
    if by_kernel:
        qkv, rest, span, second, third, *refs = refs
    (
        kv_in, q_in, out_send, ext, span_wide, soft_tile,
        kv_s, kv_r, q_s, q_r, f_s, f_r, o_s, o_r, e_s, e_r, soft_sem, local, *sems,
    ) = refs
    seqs, rows, model = hidden.shape
    half = rows // 2
    width = HEADS * HEAD
    place = Place(members, shards)
    quad, sub, peer, sibling = place.quad, place.sub, place.peer, place.sibling
    count = QUADS * members
    after = ((place.me + 1) % count, place.z)
    before = ((place.me + count - 1) % count, place.z)
    place.greet(by_kernel, [after, before])
    gathers = []
    if by_kernel:
        gathers = [
            Gather(place, block, full, split, sems[7 * j : 7 * j + 7])
            for j, (block, full, split) in enumerate(zip(blocks, (qkv, rest, second, third), splits))
        ]
        gathers[0].start()
        gathers[1].start()
    rims = (
        remote(hidden.at[:, rows - RIM : rows, :], low_rim, e_s.at[0], e_r.at[0], after),
        remote(hidden.at[:, 0:RIM, :], high_rim, e_s.at[1], e_r.at[1], before),
    )
    for rim in rims:
        rim.start()
    if by_kernel:
        gathers[0].relay()
        gathers[1].relay()
        gathers[2].start()
        gathers[3].start()
        gathers[0].share()
        gathers[0].end()
    project_body(hidden, qkv, kv_in, q_in, q_out)

    def kv_copy(h, k):
        return remote(
            kv_in.at[(quad + k) % QUADS, h], kv_all.at[h, quad, sub], kv_s.at[h, k], kv_r.at[h, k], peer(k)
        )

    def q_copy(h, k):
        return remote(
            q_in.at[(quad + k) % QUADS, h], q_all.at[h, quad], q_s.at[h, k], q_r.at[h, k], peer(k)
        )

    def forward_copy(h, m):
        return remote(
            kv_all.at[h, :, sub], kv_all.at[h, :, sub], f_s.at[h, m], f_r.at[h, m], sibling(m)
        )

    def out_copy(h, i, k):
        return remote(
            out_send.at[h, i], ctx_out.at[quad, h], o_s.at[h, i], o_r.at[h, i], peer(k)
        )

    def receive(h):
        for k in range(1, QUADS):
            kv_copy(h, k).wait_recv()
            q_copy(h, k).wait_recv()
        for m in range(1, members):
            forward_copy(h, m).start()

    own_kv = pltpu.make_async_copy(kv_in.at[quad], kv_all.at[:, quad, sub], local.at[0])
    own_q = pltpu.make_async_copy(q_in.at[quad], q_all.at[:, quad], local.at[1])
    own_kv.start()
    own_q.start()
    for h in range(TRIPLE):
        for k in range(1, QUADS):
            kv_copy(h, k).start()
            q_copy(h, k).start()
    for rim in rims:
        rim.wait()

    @pl.when(place.me == 0)
    def _():
        low_rim[...] = jnp.zeros_like(low_rim)

    @pl.when(place.me == count - 1)
    def _():
        high_rim[...] = jnp.zeros_like(high_rim)

    if by_kernel:
        gathers[1].share()
        gathers[1].end()
        block, head_block = model // shards, width // shards
        for z in range(shards):
            span[z * head_block : z * head_block + head_block] = rest[
                z * block : z * block + head_block, 2 * width : 2 * width + SMALL
            ]
    small_turned[...] = rest[:, 2 * width : 2 * width + SMALL].astype(F32).T
    for tap in range(KERNEL):
        span_wide[:, tap * width : tap * width + width] = dot(span[...], head_columns(tap, True), NN).astype(BF)
    own_kv.wait()
    own_q.wait()
    for s in range(seqs):
        conv_forward_body(
            s, hidden, low_rim, high_rim, rest, q_out, spread_out, key_out, mix_out, soft_out, value_out, conv_out,
            small_turned, span_wide, ext, soft_tile, soft_sem,
        )
        receive(s)
    is_low = low_lanes()

    def block(step, carry):
        h, i = step // QUADS, step % QUADS
        k = (i + 1) % QUADS
        source = (quad + k) % QUADS

        @pl.when(i == 0)
        def _():
            for m in range(1, members):
                forward_copy(h, m).wait_recv()

        keys = kv_all[h].reshape(QUADS * members * rows, 2 * HEAD)

        def rows_turn(r, inner):
            at = pl.multiple_of(r * CHUNK, CHUNK)
            packed = q_all[h, source, pl.ds(at, CHUNK), :]
            outs = []
            stats = []
            for part in range(2):
                q = jnp.where(is_low, packed if part == 0 else swap_halves(packed), jnp.zeros_like(packed))
                scores = dot(q, keys, NT)
                top = jnp.max(scores, axis=1, keepdims=True)
                probs = jnp.exp2((scores - top) * EXP2_SCALE)
                total = jnp.sum(probs, axis=1, keepdims=True)
                outs.append(dot(probs.astype(BF), keys, NN) / total)
                stats.append(top * EXP2_SCALE + jnp.log2(total))
            both = jnp.where(is_low, swap_halves(outs[0]), outs[1])
            out_all[h, source, pl.ds(at, CHUNK), :] = both
            out_send[h, i, pl.ds(at, CHUNK), :] = both.astype(BF)
            for part in range(2):
                lse[h, source, part, r] = jnp.broadcast_to(stats[part], (CHUNK, CHUNK)).T[0:8, :]
            return inner

        lax.fori_loop(0, half // CHUNK, rows_turn, 0)

        @pl.when(k != 0)
        def _():
            out_copy(h, i, k).start()

        @pl.when(k == 0)
        def _():
            own = pltpu.make_async_copy(out_send.at[h, i], ctx_out.at[quad, h], local.at[0])
            own.start()
            own.wait()

        for j in range(seqs, TRIPLE):

            @pl.when(step == (j - seqs) * QUADS + 2)
            def _(j=j):
                receive(j)

        if by_kernel:

            @pl.when(step == 1)
            def _():
                for gather in gathers[2:]:
                    gather.relay()

            @pl.when(step == TRIPLE * QUADS - 2)
            def _():
                for gather in gathers[2:]:
                    gather.share()

        return carry

    lax.fori_loop(0, TRIPLE * QUADS, block, 0)
    for gather in gathers[2:]:
        gather.end()
    for h in range(TRIPLE):
        for k in range(1, QUADS):
            out_copy(h, k - 1, k).wait()
            kv_copy(h, k).wait_send()
            q_copy(h, k).wait_send()
        for m in range(1, members):
            forward_copy(h, m).wait_send()


def front(by_kernel, members, shards, hidden, *arrays):
    seqs, rows, model = hidden.shape
    half = rows // 2
    width = HEADS * HEAD
    vm = pl.BlockSpec(memory_space=pltpu.VMEM)
    anywhere = pl.BlockSpec(memory_space=pl.ANY)
    dma = pltpu.SemaphoreType.DMA
    shape = jax.ShapeDtypeStruct
    splits = SPLITS if by_kernel else ()
    gathered = []
    if by_kernel:
        qkv, rest, second, third = (shape((shards * one.shape[0], one.shape[1]), BF) for one in arrays)
        gathered = [(vm, qkv), (vm, rest), (vm, shape((width, SMALL), BF)), (anywhere, second), (anywhere, third)]
    total = TRIPLE * QUADS * rows * QUADS * members * rows
    return pl.pallas_call(
        functools.partial(front_kernel, by_kernel, members, shards, splits),
        in_specs=[vm] + [anywhere if by_kernel else vm] * len(arrays),
        out_specs=[vm, vm, vm, vm, anywhere, vm, vm, vm, vm, anywhere, vm, vm, vm, vm, vm] + [one for one, _ in gathered],
        out_shape=[
            shape((TRIPLE, QUADS, members, rows, 2 * HEAD), BF),
            shape((TRIPLE, QUADS, half, 2 * HEAD), BF),
            shape((TRIPLE, QUADS, half, 2 * HEAD), F32),
            shape((TRIPLE, QUADS, 2, half // CHUNK, 8, CHUNK), F32),
            shape((QUADS, TRIPLE, half, 2 * HEAD), BF),
            shape((seqs, rows, width), BF),
            shape((seqs, rows, model), BF),
            shape((seqs, rows, width), F32),
            shape((seqs, rows, width), BF),
            shape((seqs * rows // TILE, KERNEL, TILE, width), BF),
            shape((seqs, rows + 2 * RIM, width), F32),
            shape((seqs, rows, width), BF),
            shape((SMALL, model), F32),
            shape((seqs, RIM, model), BF),
            shape((seqs, RIM, model), BF),
        ]
        + [one for _, one in gathered],
        scratch_shapes=[
            pltpu.VMEM((QUADS, TRIPLE, rows, 2 * HEAD), BF),
            pltpu.VMEM((QUADS, TRIPLE, half, 2 * HEAD), BF),
            pltpu.VMEM((TRIPLE, QUADS, half, 2 * HEAD), BF),
            pltpu.VMEM((rows + 2 * RIM, model), F32),
            pltpu.VMEM((width, KERNEL * width), BF),
            pltpu.VMEM((2, KERNEL, TILE, width), BF),
            dma((TRIPLE, QUADS)), dma((TRIPLE, QUADS)), dma((TRIPLE, QUADS)), dma((TRIPLE, QUADS)),
            dma((TRIPLE, members)), dma((TRIPLE, members)), dma((TRIPLE, QUADS)), dma((TRIPLE, QUADS)),
            dma((2,)), dma((2,)), dma((2,)), dma((2,)),
        ]
        + Gather.semaphores(members, shards) * len(splits),
        compiler_params=pltpu.CompilerParams(
            collective_id=1, has_side_effects=True, vmem_limit_bytes=60 * 2**20
        ),
        cost_estimate=pl.CostEstimate(flops=total * 256, bytes_accessed=8 * 2**20, transcendentals=total),
    )(hidden, *arrays)


def middle_kernel(
    by_kernel, shards, members,
    context, conv, hidden, cotangent, second, third, small_turned,
    layer_out, d_first_out, d_context_out, d_conv_out, second_part, third_part, norm_sums,
    context_low, hidden_low, active_all, d_outer_all, d_inner_all, d_dense_all, d_context_all,
):
    seqs, rows, model = hidden.shape
    half = rows // 2
    width = HEADS * HEAD
    group = model // GROUPS
    units = third.shape[0]
    is_low = low_lanes()
    gains = small_turned[64 + KERNEL : 64 + KERNEL + 4, :]
    attn_gain, attn_bias, out_gain, out_bias = (gains[j : j + 1] for j in range(4))
    norm_sums[...] = jnp.zeros_like(norm_sums)

    def turn(step, carry):
        s, p = step // 2, step % 2
        top = pl.multiple_of(p * half, half)
        at = pl.ds(top, half)
        every = pl.ds(pl.multiple_of(step * half, half), half)
        pairs = []
        for j in range(HEADS // 2):
            a = context[s * 2 + 2 * j // TRIPLE, 2 * j % TRIPLE]
            b = context[s * 2 + (2 * j + 1) // TRIPLE, (2 * j + 1) % TRIPLE]
            upper = jnp.where(is_low, a, swap_halves(b))
            lower = jnp.where(is_low, swap_halves(a), b)
            pairs.append(jnp.where(p == 0, upper, lower))
        low = jnp.concatenate(pairs, axis=1)
        context_low[every] = low
        dense = dot(low, second[:, :model], NN) + dot(conv[s, at], second[:, model : 2 * model], NN)
        normed_one, inv_one = norm_rows(dense + hidden[s, at].astype(F32))
        hidden_one = normed_one * attn_gain + attn_bias
        one_low = hidden_one.astype(BF)
        hidden_low[every] = one_low
        outers = []
        slopes = []
        for g in range(GROUPS):
            edge = 2 * model + g * units
            inner = dot(one_low[:, g * group : g * group + group], second[:, edge : edge + units], NN)
            active, slope = gelu_both(inner)
            active = active.astype(BF)
            active_all[every, g * units : g * units + units] = active
            slopes.append(slope)
            outers.append(dot(active, third[:, g * group : g * group + group], NN))
        normed_two, inv_two = norm_rows(jnp.concatenate(outers, axis=1) + hidden_one)
        layer_out[s, at] = (normed_two * out_gain + out_bias).astype(BF)
        d_result = cotangent[s, at].astype(F32)
        norm_sums[2] += fold(d_result * normed_two)
        norm_sums[3] += fold(d_result)
        d_second = norm_rows_back(normed_two, inv_two, d_result * out_gain)
        d_outer = d_second.astype(BF)
        d_outer_all[every] = d_outer
        backs = []
        for g in range(GROUPS):
            edge = 2 * model + g * units
            d_active = dot(d_outer[:, g * group : g * group + group], third[:, g * group : g * group + group], NT)
            d_inner = (d_active * slopes[g]).astype(BF)
            d_inner_all[every, g * units : g * units + units] = d_inner
            backs.append(dot(d_inner, second[:, edge : edge + units], NT))
        d_hidden = jnp.concatenate(backs, axis=1) + d_second
        norm_sums[0] += fold(d_hidden * normed_one)
        norm_sums[1] += fold(d_hidden)
        d_first = norm_rows_back(normed_one, inv_one, d_hidden * attn_gain)
        d_first_out[s, at] = d_first
        d_dense = d_first.astype(BF)
        d_dense_all[every] = d_dense
        d_context_all[every] = dot(d_dense, second[:, :model], NT).astype(BF)
        d_conv_out[s, at] = dot(d_dense, second[:, model : 2 * model], NT)
        return carry

    lax.fori_loop(0, seqs * 2, turn, 0)
    for s in range(seqs):
        for h in range(HEADS):
            at = h // 2 * 2 * HEAD
            upper = d_context_all[s * rows : s * rows + half, at : at + 2 * HEAD]
            lower = d_context_all[s * rows + half : s * rows + rows, at : at + 2 * HEAD]
            if h % 2:
                packed = jnp.where(is_low, swap_halves(upper), lower)
            else:
                packed = jnp.where(is_low, upper, swap_halves(lower))
            d_context_out[s * 2 + h // TRIPLE, h % TRIPLE] = packed
    for g in range(GROUPS):
        for z in range(shards):
            block = units // shards
            part = dot(
                active_all[:, g * units + z * block : g * units + z * block + block],
                d_outer_all[:, g * group : g * group + group], TN,
            ).astype(BF)
            if by_kernel:
                piece = block // (QUADS * members)
                for q in range(QUADS):
                    for c in range(members):
                        row = (q * members + c) * piece
                        third_part[c, z, q, :, g * group : g * group + group] = part[row : row + piece]
            else:
                third_part[z * block : z * block + block, g * group : g * group + group] = part

    def columns(left, right):
        found = []
        for start, size, rows_in, columns_in in (
            (0, model, context_low[...], d_dense_all),
            (model, model, None, d_dense_all),
            (2 * model, units, hidden_low[:, :group], d_inner_all.at[:, :units]),
            (2 * model + units, units, hidden_low[:, group:], d_inner_all.at[:, units:]),
        ):
            a, b = max(left, start), min(right, start + size)
            if a < b:
                if rows_in is None:
                    rows_in = conv[...].reshape(seqs * rows, width)
                found.append(dot(rows_in, columns_in[:, a - start : b - start], TN).astype(BF))
        return jnp.concatenate(found, axis=1) if len(found) > 1 else found[0]

    wide = second.shape[1] // 4
    for j in range(4):
        part = columns(j * wide, j * wide + wide)
        if by_kernel:
            block = width // shards
            piece = block // 2
            for z in range(shards):
                for r in range(2):
                    row = z * block + r * piece
                    second_part[j % members, z, r * 2 + j // members] = part[row : row + piece]
        else:
            second_part[:, j * wide : j * wide + wide] = part


def middle(context, conv, hidden, cotangent, second, third, small_turned, by_kernel, shards, members):
    seqs, rows, model = hidden.shape
    width = HEADS * HEAD
    units = third.shape[0]
    tokens = seqs * rows
    shape = jax.ShapeDtypeStruct
    if by_kernel:
        parts = [
            shape((members, shards, QUADS, width // shards // 2, second.shape[1] // 4), BF),
            shape((members, shards, QUADS, units // shards // (QUADS * members), model), BF),
        ]
    else:
        parts = [shape(second.shape, BF), shape(third.shape, BF)]
    return pl.pallas_call(
        functools.partial(middle_kernel, by_kernel, shards, members),
        out_shape=[
            shape((seqs, rows, model), BF),
            shape((seqs, rows, model), F32),
            shape((QUADS, TRIPLE, rows // 2, 2 * HEAD), BF),
            shape((seqs, rows, width), F32),
            *parts,
            shape((4, 8, model), F32),
        ],
        scratch_shapes=[
            pltpu.VMEM((tokens, width), BF),
            pltpu.VMEM((tokens, model), BF),
            pltpu.VMEM((tokens, GROUPS * units), BF),
            pltpu.VMEM((tokens, model), BF),
            pltpu.VMEM((tokens, GROUPS * units), BF),
            pltpu.VMEM((tokens, model), BF),
            pltpu.VMEM((tokens, width), BF),
        ],
        compiler_params=pltpu.CompilerParams(vmem_limit_bytes=60 * 2**20),
    )(context, conv, hidden, cotangent, second, third, small_turned)


def conv_back_kernel(
    by_kernel, shards, members,
    hidden, low_rim, high_rim, rest, span, small_turned, d_conv, q_out, spread, key_conv, mix, soft, value, d_first, norm_sums,
    grad_rows, low_edge, high_edge, dq_conv, part_out,
    ext, d_value, d_rows, slim_all, d_key_all, depth_sums, ext_low,
):
    seqs, rows, model = hidden.shape
    width = HEADS * HEAD
    value_at, point_at = 0, width
    depth = small_turned[64 : 64 + 16, :]
    pair = lax.broadcasted_iota(jnp.int32, (4 * HEAD, 2 * HEAD), 0) // HEAD % 2
    same = pair == lax.broadcasted_iota(jnp.int32, (4 * HEAD, 2 * HEAD), 1) // HEAD
    group_sum = jnp.where(same, 1.0, 0.0).astype(BF)
    depth_sums[...] = jnp.zeros_like(depth_sums)
    long = rows + 2 * RIM
    for s in range(seqs):
        ext[0:RIM] = low_rim[s].astype(F32)
        ext[RIM : RIM + rows] = hidden[s].astype(F32)
        ext[RIM + rows : long] = high_rim[s].astype(F32)
        ext_low[s * long : s * long + RIM] = low_rim[s]
        ext_low[s * long + RIM : s * long + RIM + rows] = hidden[s]
        ext_low[s * long + RIM + rows : s * long + long] = high_rim[s]
        d_value[...] = jnp.zeros_like(d_value)
        d_rows[...] = jnp.zeros_like(d_rows)

        def turn(r, carry):
            top = pl.multiple_of(r * TILE, TILE)
            here = pl.ds(top, TILE)
            there = pl.ds(top, TILE + 2 * RIM)
            every = pl.ds(pl.multiple_of(s * rows + r * TILE, TILE), TILE)
            d_res = d_conv[s, here, :]
            values = value[s, there, :]
            softs = []
            d_kernels = []
            rim = jnp.zeros((RIM, width), F32)
            d_values = jnp.zeros((TILE + 2 * RIM, width), F32)
            total = jnp.zeros((TILE, width), F32)
            for tap in range(KERNEL):
                one = soft[s * (rows // TILE) + r, tap].astype(F32)
                softs.append(one)
                weighted = jnp.concatenate([rim, one * d_res, rim], axis=0)
                d_values = d_values + moved(weighted, KERNEL // 2 - tap)
                product = d_res * moved(values, tap - KERNEL // 2)[RIM : RIM + TILE]
                high = product.astype(BF)
                lower = (product - high.astype(F32)).astype(BF)
                sums = []
                for at in range(0, width, 2 * HEAD):
                    both = jnp.concatenate([high[:, at : at + 2 * HEAD], lower[:, at : at + 2 * HEAD]], axis=1)
                    sums.append(dot(both, group_sum, NN))
                d_kernel = jnp.concatenate(sums, axis=1)
                d_kernels.append(d_kernel)
                total = total + d_kernel * one
            d_value[there, :] += d_values
            slim = jnp.zeros((TILE, SMALL), F32)
            for tap in range(KERNEL):
                d_logits = (softs[tap] * (d_kernels[tap] - total)).astype(BF)
                slim = slim + dot(d_logits, head_columns(tap, False), NN)
            slim = slim.astype(BF)
            slim_all[every] = slim
            d_mix = dot(slim, span[...], NT)
            dq_conv[s, here, :] = d_mix * key_conv[s, here, :]
            d_key = (d_mix * q_out[s, here, :].astype(F32)).astype(BF)
            d_key_all[every] = d_key
            d_spread = dot(d_key, rest[:, point_at : point_at + width], NT)
            around = ext[there, :]
            wide_rim = jnp.zeros((RIM, model), F32)
            padded = jnp.concatenate([wide_rim, d_spread, wide_rim], axis=0)
            back = jnp.zeros((TILE + 2 * RIM, model), F32)
            for tap in range(KERNEL):
                depth_sums[tap] += fold(d_spread * moved(around, tap - KERNEL // 2)[RIM : RIM + TILE])
                back = back + moved(padded, KERNEL // 2 - tap) * depth[tap : tap + 1]
            d_rows[there, :] += back
            return carry

        lax.fori_loop(0, rows // TILE, turn, 0)
        value_low = d_value[...].astype(BF)
        value_part = dot(ext_low[s * long : s * long + long], value_low, TN)
        if s == 0:
            grad_value = value_part
        else:
            grad_value = grad_value + value_part
        all_rows = dot(value_low, rest[:, value_at : value_at + width], NT) + d_rows[...]
        grad_rows[s] = all_rows[RIM : RIM + rows] + d_first[s]
        low_edge[s] = all_rows[0:RIM].astype(BF)
        high_edge[s] = all_rows[RIM + rows :].astype(BF)

    grad_point = dot(spread[...].reshape(seqs * rows, model), d_key_all[...], TN)
    grad_span = dot(mix[...].reshape(seqs * rows, width), slim_all[...], TN)
    lines = [jnp.zeros((64, model), F32)]
    lines += [jnp.sum(depth_sums[tap], axis=0, keepdims=True) for tap in range(KERNEL)]
    lines += [jnp.sum(norm_sums[j], axis=0, keepdims=True) for j in range(4)]
    lines += [jnp.zeros((SMALL - 64 - KERNEL - 4, model), F32)]
    block, head_block = model // shards, width // shards
    slots = []
    for z in range(shards):
        slots += [grad_span[z * head_block : z * head_block + head_block], jnp.zeros((block - head_block, SMALL), F32)]
    small = jnp.concatenate(lines, axis=0).T + jnp.concatenate(slots, axis=0)
    whole = jnp.concatenate([grad_value, grad_point, small, jnp.zeros((model, SMALL), F32)], axis=1).astype(BF)
    if by_kernel:
        piece = block // QUADS
        wide = whole.shape[1] // members
        for z in range(shards):
            for q in range(QUADS):
                row = z * block + q * piece
                for c in range(members):
                    part_out[c, z, q] = whole[row : row + piece, c * wide : c * wide + wide]
    else:
        part_out[...] = whole


def conv_back(by_kernel, shards, members, *arrays):
    hidden = arrays[0]
    seqs, rows, model = hidden.shape
    width = HEADS * HEAD
    long = rows + 2 * RIM
    columns = 2 * width + 2 * SMALL
    shape = jax.ShapeDtypeStruct
    if by_kernel:
        part = shape((members, shards, QUADS, model // shards // QUADS, columns // members), BF)
    else:
        part = shape((model, columns), BF)
    return pl.pallas_call(
        functools.partial(conv_back_kernel, by_kernel, shards, members),
        out_shape=[
            shape((seqs, rows, model), F32),
            shape((seqs, RIM, model), BF),
            shape((seqs, RIM, model), BF),
            shape((seqs, rows, width), F32),
            part,
        ],
        scratch_shapes=[
            pltpu.VMEM((long, model), F32),
            pltpu.VMEM((long, width), F32),
            pltpu.VMEM((long, model), F32),
            pltpu.VMEM((seqs * rows, SMALL), BF),
            pltpu.VMEM((seqs * rows, width), BF),
            pltpu.VMEM((KERNEL, 8, model), F32),
            pltpu.VMEM((seqs * long, model), BF),
        ],
        compiler_params=pltpu.CompilerParams(vmem_limit_bytes=60 * 2**20),
    )(*arrays)


def tail_kernel(by_kernel, shards, members, *refs):
    hidden, first, dq_in, dkv_in, dq_conv, grad_rows, low_edge, high_edge, grad_in, out, d_all, *scratch = refs
    seqs, rows, model = hidden.shape
    half = rows // 2
    width = HEADS * HEAD
    is_low = low_lanes()
    if by_kernel:
        part, *scratch = scratch
        place = Place(members, shards)
        place.greet(True)
        one = Reduce(place, part, out, 2, scratch)
    for s in range(seqs):
        for j in range(HEADS // 2):
            a = dq_in[s * 2 + 2 * j // TRIPLE, 2 * j % TRIPLE].astype(F32)
            b = dq_in[s * 2 + (2 * j + 1) // TRIPLE, (2 * j + 1) % TRIPLE].astype(F32)
            at = j * 2 * HEAD
            upper = jnp.where(is_low, a, swap_halves(b)) + dq_conv[s, 0:half, at : at + 2 * HEAD]
            lower = jnp.where(is_low, swap_halves(a), b) + dq_conv[s, half:rows, at : at + 2 * HEAD]
            d_all[s * rows : s * rows + half, at : at + 2 * HEAD] = upper.astype(BF)
            d_all[s * rows + half : s * rows + rows, at : at + 2 * HEAD] = lower.astype(BF)
        for h in range(HEADS):
            at = width + h * 2 * HEAD
            d_all[s * rows : s * rows + rows, at : at + 2 * HEAD] = dkv_in[s * 2 + h // TRIPLE, h % TRIPLE]
    tokens = hidden[...].reshape(seqs * rows, model)
    if by_kernel:
        block = model // shards
        piece = block // QUADS
        wide = part.shape[4]
        for c in range(members):
            left, right = c * wide, min(c * wide + wide, 3 * width)
            value = dot(tokens, d_all[:, left:right], TN).astype(BF)
            for z in range(shards):
                for q in range(QUADS):
                    row = z * block + q * piece
                    part[c, z, q, :, 0 : right - left] = value[row : row + piece]
                    if right - left < wide:
                        part[c, z, q, :, right - left : wide] = jnp.zeros((piece, wide - right + left), BF)
        one.start()
    else:
        out[:, : 3 * width] = dot(tokens, d_all[...], TN).astype(BF)
        out[:, 3 * width :] = jnp.zeros((model, out.shape[1] - 3 * width), BF)

    def rows_turn(s):
        total = grad_rows[s] + dot(d_all[s * rows : s * rows + rows], first[:, : 3 * width], NT)
        grad_in[s] = total
        grad_in[s, 0:RIM] = total[0:RIM] + low_edge[s].astype(F32)
        grad_in[s, rows - RIM : rows] = total[rows - RIM : rows] + high_edge[s].astype(F32)

    if by_kernel:
        one.to_quads()
    for s in range(seqs):
        rows_turn(s)
    if by_kernel:
        one.to_shards()
        one.give()
        one.share()
        one.end()


def tail(by_kernel, shards, members, *arrays):
    hidden = arrays[0]
    seqs, rows, model = hidden.shape
    width = HEADS * HEAD
    columns = 3 * width + SMALL
    shape = jax.ShapeDtypeStruct
    scratch = [pltpu.VMEM((seqs * rows, 3 * width), BF)]
    if by_kernel:
        piece = (model // shards // QUADS, columns // members)
        scratch += [pltpu.VMEM((members, shards, QUADS, *piece), BF)] + Reduce.scratch(members, shards, *piece)
        params = pltpu.CompilerParams(collective_id=4, has_side_effects=True, vmem_limit_bytes=56 * 2**20)
    else:
        params = pltpu.CompilerParams(vmem_limit_bytes=56 * 2**20)
    vm = pl.BlockSpec(memory_space=pltpu.VMEM)
    return pl.pallas_call(
        functools.partial(tail_kernel, by_kernel, shards, members),
        in_specs=[vm] * len(arrays),
        out_specs=[vm, pl.BlockSpec(memory_space=pl.ANY) if by_kernel else vm],
        out_shape=[
            shape((seqs, rows, model), F32),
            shape((model // shards if by_kernel else model, columns), BF),
        ],
        scratch_shapes=scratch,
        compiler_params=params,
    )(*arrays)


SPLITS = (2, 2, 4, 1)


def shards(
    hidden_in,
    cotangent,
    qkv_weight,
    conv_depth,
    conv_point,
    span_weight,
    conv_value,
    dense_attn,
    dense_conv,
    attn_norm_gain,
    attn_norm_bias,
    ffn_inner,
    ffn_outer,
    out_norm_gain,
    out_norm_bias,
):
    attn_width = HEADS * HEAD
    seq_count, local_rows, model_width = hidden_in.shape
    ctx_count = lax.axis_size("ctx")
    members = ctx_count // QUADS
    shard_count = lax.axis_size("shard")
    width_rows = model_width // shard_count
    head_rows = attn_width // shard_count
    forward = [(i, i + 1) for i in range(ctx_count - 1)]
    backward = [(i + 1, i) for i in range(ctx_count - 1)]
    small = jnp.concatenate(
        [
            jnp.pad(span_weight, ((0, width_rows - head_rows), (0, 64 - HEADS * KERNEL))),
            conv_depth.T,
            jnp.stack([attn_norm_gain, attn_norm_bias, out_norm_gain, out_norm_bias], axis=1),
            jnp.zeros((width_rows, SMALL - 64 - KERNEL - 4), BF),
        ],
        axis=1,
    )
    pairs = qkv_weight[:, attn_width:].reshape(width_rows, 2, HEADS, HEAD).transpose(0, 2, 1, 3)
    qkv_block = jnp.concatenate(
        [qkv_weight[:, :attn_width], pairs.reshape(width_rows, -1), jnp.zeros((width_rows, SMALL), BF)], axis=1
    )
    rest_block = jnp.concatenate([conv_value, conv_point, small, jnp.zeros((width_rows, SMALL), BF)], axis=1)
    second_block = jnp.concatenate([dense_attn, dense_conv, ffn_inner[0], ffn_inner[1]], axis=1)
    third_block = jnp.concatenate([ffn_outer[0], ffn_outer[1]], axis=1)
    blocks = (qkv_block, rest_block, second_block, third_block)
    by_kernel = members == 2 and all(fits(*one.shape, members, split) for one, split in zip(blocks, SPLITS))
    if by_kernel:
        arrays = blocks
    else:
        qkv, rest, second, third = (lax.all_gather(one, "shard", axis=0, tiled=True) for one in blocks)
        span = rest[:, 2 * attn_width : 2 * attn_width + SMALL].reshape(shard_count, width_rows, SMALL)
        span = span[:, :head_rows].reshape(attn_width, SMALL)
        arrays = (qkv, rest, span)
    (
        kv_all, q_all, out_all, lse, context, q_low, spread, key_conv, span_mix, kernel_soft, value_ext, conv_low,
        small_turned, low_rim, high_rim, *gathered,
    ) = front(by_kernel, members, shard_count, hidden_in, *arrays)
    if by_kernel:
        qkv, rest, span, second, third = gathered
    layer_out, d_first, d_context, d_conv, second_part, third_part, norm_sums = middle(
        context, conv_low, hidden_in, cotangent, second, third, small_turned, by_kernel, shard_count, members
    )
    grad_rows, low_edge, high_edge, dq_conv, middle_part = conv_back(
        by_kernel, shard_count, members,
        hidden_in, low_rim, high_rim, rest, span, small_turned, d_conv, q_low, spread, key_conv, span_mix,
        kernel_soft, value_ext, d_first, norm_sums,
    )
    forward = [(i, i + 1) for i in range(ctx_count - 1)]
    backward = [(i + 1, i) for i in range(ctx_count - 1)]
    low_in = lax.ppermute(high_edge, "ctx", forward)
    high_in = lax.ppermute(low_edge, "ctx", backward)
    parts = ()
    part_splits = ()
    middle_width = 2 * attn_width + 2 * SMALL
    if by_kernel:
        parts = (
            (third_part, third_block.shape),
            (second_part, second_block.shape),
            (middle_part, (width_rows, middle_width)),
        )
        part_splits = (SPLITS[3], SPLITS[2], SPLITS[1])
    dq_packed, dkv, *reduced = attend_backward(
        d_context, kv_all, q_all, out_all, lse, members, shard_count, parts, part_splits
    )
    grad_in, first_sum = tail(
        by_kernel, shard_count, members,
        hidden_in, qkv, dq_packed, dkv, dq_conv, grad_rows, low_in, high_in,
    )
    if by_kernel:
        third_sum, second_sum, middle_sum = reduced
    else:
        first_sum, second_sum, third_sum, middle_sum = (
            lax.psum(lax.psum_scatter(one, "shard", scatter_dimension=0, tiled=True), "ctx")
            for one in (first_sum, second_part, third_part, middle_part)
        )
    first_sum, second_sum, third_sum, middle_sum = (
        one.astype(F32) for one in (first_sum, second_sum, third_sum, middle_sum)
    )
    edge = 2 * attn_width
    norms = middle_sum[:, edge + 64 + KERNEL : edge + 68 + KERNEL].T
    pair_sum = first_sum[:, attn_width : 3 * attn_width].reshape(width_rows, HEADS, 2, HEAD).transpose(0, 2, 1, 3)
    result_grads = (
        jnp.concatenate([first_sum[:, :attn_width], pair_sum.reshape(width_rows, -1)], axis=1),
        middle_sum[:, edge + 64 : edge + 64 + KERNEL].T,
        middle_sum[:, attn_width:edge],
        middle_sum[:head_rows, edge : edge + HEADS * KERNEL],
        middle_sum[:, :attn_width],
        second_sum[:, :model_width],
        second_sum[:, model_width : 2 * model_width],
        norms[0],
        norms[1],
        second_sum[:, 2 * model_width :].reshape(head_rows, GROUPS, -1).transpose(1, 0, 2),
        third_sum.reshape(-1, GROUPS, D // GROUPS).transpose(1, 0, 2),
        norms[2],
        norms[3],
    )
    return (layer_out, grad_in) + result_grads


def solution(mesh):
    return jax.shard_map(
        shards,
        mesh=mesh,
        in_specs=(
            P("shard", "ctx", None),
            P("shard", "ctx", None),
            P("shard", None),
            P(None, "shard"),
            P("shard", None),
            P("shard", None),
            P("shard", None),
            P("shard", None),
            P("shard", None),
            P("shard"),
            P("shard"),
            P(None, "shard", None),
            P(None, "shard", None),
            P("shard"),
            P("shard"),
        ),
        out_specs=(
            P("shard", "ctx", None),
            P("shard", "ctx", None),
            P("shard", None),
            P(None, "shard"),
            P("shard", None),
            P("shard", None),
            P("shard", None),
            P("shard", None),
            P("shard", None),
            P("shard"),
            P("shard"),
            P(None, "shard", None),
            P(None, "shard", None),
            P("shard"),
            P("shard"),
        ),
        check_vma=False,
    )
```

```python
import functools
import math

import jax
import jax.numpy as jnp
from jax import lax
from jax.experimental import pallas as pl
from jax.experimental.pallas import tpu as pltpu
from jax.sharding import PartitionSpec as P

D = 768
HEADS = 6
HEAD = 64
GROUPS = 2
KERNEL = 9


norm_eps = 1e-12


BF = jnp.bfloat16
F32 = jnp.float32
MESH_ID = pl.DeviceIdType.MESH
NT = (((1,), (1,)), ((), ()))
NN = (((1,), (0,)), ((), ()))
EXP2_SCALE = math.log2(math.e) / math.sqrt(HEAD)
TRIPLE = 3
QUADS = 4
CHUNK = 128


def dot(a, b, dims):
    return lax.dot_general(a, b, dims, preferred_element_type=F32)


def swap_halves(packed):
    return jnp.concatenate([packed[:, HEAD:], packed[:, :HEAD]], axis=1)


def low_lanes():
    return lax.broadcasted_iota(jnp.int32, (1, 2 * HEAD), 1) < HEAD


def remote(src, dst, send, recv, target):
    return pltpu.make_async_remote_copy(
        src_ref=src, dst_ref=dst, send_sem=send, recv_sem=recv,
        device_id=target, device_id_type=MESH_ID,
    )


def greet(peers):
    barrier = pltpu.get_barrier_semaphore()
    for peer in peers:
        pl.semaphore_signal(barrier, inc=1, device_id=peer, device_id_type=MESH_ID)
    pl.semaphore_wait(barrier, len(peers))


class Place:
    def __init__(self, members, shards):
        self.members, self.shards = members, shards
        self.me = lax.axis_index("ctx")
        self.z = lax.axis_index("shard")
        self.quad, self.sub = self.me // members, self.me % members

    def peer(self, step):
        return ((self.quad + step) % QUADS * self.members + self.sub, self.z)

    def sibling(self, step):
        return (self.quad * self.members + (self.sub + step) % self.members, self.z)

    def cross(self, step, other):
        return (
            (self.quad + step) % QUADS * self.members + (self.sub + other) % self.members, self.z,
        )

    def behind(self, step):
        return (self.quad + QUADS - step) % QUADS

    def along(self, step):
        return (self.me, (self.z + step) % self.shards)

    def z_behind(self, step):
        return (self.z + self.shards - step) % self.shards

    def greet(self, with_shard, more=()):
        peers = [self.peer(k) for k in range(1, QUADS)]
        peers += [self.sibling(m) for m in range(1, self.members)]
        if with_shard:
            peers += [self.along(d) for d in range(1, self.shards)]
        greet(peers + list(more))


class Pieces:
    def __init__(self, place, rows, columns, col_split):
        count = QUADS * place.members
        self.place, self.rows, self.col_split = place, rows, col_split
        self.piece_rows = rows // (count // col_split)
        self.piece_cols = columns // col_split

    def at(self, ref, z, quad, sub):
        index = quad * self.place.members + sub
        top = pl.multiple_of(z * self.rows + index // self.col_split * self.piece_rows, 16)
        left = pl.multiple_of(index % self.col_split * self.piece_cols, 128)
        return ref.at[pl.ds(top, self.piece_rows), pl.ds(left, self.piece_cols)]


def fits(rows, columns, members, col_split):
    count = QUADS * members
    if count % col_split:
        return False
    row_split = count // col_split
    return rows % (16 * row_split) == 0 and columns % (128 * col_split) == 0


class Gather:
    def __init__(self, place, shard_ref, full_ref, col_split, sems):
        self.place, self.shard_ref, self.full_ref = place, shard_ref, full_ref
        rows, columns = shard_ref.shape
        self.rows = rows
        self.pieces = Pieces(place, rows, columns, col_split)
        self.z_s, self.z_r, self.q_s, self.q_r, self.f_s, self.f_r, self.local = sems

    @staticmethod
    def semaphores(members, shards):
        dma = pltpu.SemaphoreType.DMA
        return [
            dma((shards,)), dma((shards,)), dma((shards, QUADS)), dma((shards, QUADS)),
            dma((shards, QUADS, members)), dma((shards, QUADS, members)), dma((1,)),
        ]

    def z_copy(self, d):
        p = self.place
        return remote(
            self.pieces.at(self.shard_ref, 0, p.quad, p.sub), self.pieces.at(self.full_ref, p.z, p.quad, p.sub),
            self.z_s.at[d], self.z_r.at[d], p.along(d),
        )

    def q_copy(self, d, k):
        p = self.place
        block = self.pieces.at(self.full_ref, p.z_behind(d), p.quad, p.sub)
        return remote(block, block, self.q_s.at[d, k], self.q_r.at[d, k], p.peer(k))

    def f_copy(self, d, k, m):
        p = self.place
        block = self.pieces.at(self.full_ref, p.z_behind(d), p.behind(k), p.sub)
        return remote(block, block, self.f_s.at[d, k, m], self.f_r.at[d, k, m], p.sibling(m))

    def own_copy(self):
        top = pl.multiple_of(self.place.z * self.rows, 16)
        return pltpu.make_async_copy(
            self.shard_ref, self.full_ref.at[pl.ds(top, self.rows), :], self.local.at[0]
        )

    def start(self):
        for d in range(1, self.place.shards):
            self.z_copy(d).start()
        self.own_copy().start()

    def relay(self):
        for d in range(1, self.place.shards):
            self.z_copy(d).wait_recv()
            for k in range(1, QUADS):
                self.q_copy(d, k).start()
            for m in range(1, self.place.members):
                self.f_copy(d, 0, m).start()

    def share(self):
        for d in range(1, self.place.shards):
            for k in range(1, QUADS):
                self.q_copy(d, k).wait_recv()
                for m in range(1, self.place.members):
                    self.f_copy(d, k, m).start()

    def end(self):
        for d in range(1, self.place.shards):
            self.z_copy(d).wait_send()
            for k in range(QUADS):
                if k:
                    self.q_copy(d, k).wait_send()
                for m in range(1, self.place.members):
                    self.f_copy(d, k, m).wait()
        self.own_copy().wait()


class Reduce:
    def __init__(self, place, part, block, out, col_split, head=None, tail=None):
        self.place, self.part, self.block, self.out, self.col_split = place, part, block, out, col_split
        self.straight = out is not None and len(out.shape) == 3
        if head is not None:
            self.half, self.half_in, self.quad_in, self.h_s, self.h_r, self.q_s, self.q_r = head
        if tail is not None:
            self.z_in, self.last, self.z_s, self.z_r, self.a_s, self.a_r, self.f_s, self.f_r, self.local = tail

    @staticmethod
    def head_scratch(members, shards, rows, columns):
        dma = pltpu.SemaphoreType.DMA
        return [
            pltpu.VMEM((shards, QUADS, rows, columns), BF),
            pltpu.VMEM((members - 1, shards, QUADS, rows, columns), BF),
            pltpu.VMEM((QUADS - 1, shards, rows, columns), BF),
            dma((members,)), dma((members,)), dma((QUADS,)), dma((QUADS,)),
        ]

    @staticmethod
    def tail_scratch(members, shards, rows, columns):
        dma = pltpu.SemaphoreType.DMA
        return [
            pltpu.VMEM((shards - 1, rows, columns), BF),
            pltpu.VMEM((rows, columns), BF),
            dma((shards,)), dma((shards,)), dma((QUADS,)), dma((QUADS,)),
            dma((QUADS, members)), dma((QUADS, members)), dma((1,)),
        ]

    def piece(self, quad, sub):
        rows, columns = self.last.shape
        if len(self.out.shape) == 3:
            return self.out.at[sub, pl.ds(pl.multiple_of(quad * rows, 16), rows), :]
        index = quad * self.place.members + sub
        top = pl.multiple_of(index // self.col_split * rows, 16)
        left = pl.multiple_of(index % self.col_split * columns, 128)
        return self.out.at[pl.ds(top, rows), pl.ds(left, columns)]

    def h_copy(self, m):
        p = self.place
        return remote(
            self.part.at[(p.sub + m) % p.members], self.half_in.at[m - 1], self.h_s.at[m], self.h_r.at[m], p.sibling(m)
        )

    def q_copy(self, k):
        p = self.place
        return remote(
            self.half.at[:, (p.quad + k) % QUADS], self.quad_in.at[k - 1], self.q_s.at[k], self.q_r.at[k], p.peer(k)
        )

    def z_copy(self, d):
        p = self.place
        return remote(
            self.block.at[(p.z + d) % p.shards], self.z_in.at[d - 1], self.z_s.at[d], self.z_r.at[d], p.along(d)
        )

    def a_copy(self, k):
        p = self.place
        return remote(self.last, self.piece(p.quad, p.sub), self.a_s.at[k], self.a_r.at[k], p.peer(k))

    def f_copy(self, k, m):
        p = self.place
        block = self.piece(p.behind(k), p.sub)
        return remote(block, block, self.f_s.at[k, m], self.f_r.at[k, m], p.sibling(m))

    def s_copy(self, k, m):
        p = self.place
        return remote(
            self.last, self.piece(p.quad, p.sub), self.f_s.at[k, m], self.f_r.at[k, m], p.cross(k, m)
        )

    def start(self):
        for m in range(1, self.place.members):
            self.h_copy(m).start()

    def to_quads(self):
        for m in range(1, self.place.members):
            self.h_copy(m).wait_recv()

        def turn(i, carry):
            z, q = i // QUADS, i % QUADS
            total = self.part[self.place.sub, z, q].astype(F32)
            for m in range(1, self.place.members):
                total = total + self.half_in[m - 1, z, q].astype(F32)
            self.half[z, q] = total.astype(BF)
            return carry

        lax.fori_loop(0, self.place.shards * QUADS, turn, 0)
        for k in range(1, QUADS):
            self.q_copy(k).start()

    def to_block(self):
        for k in range(1, QUADS):
            self.q_copy(k).wait_recv()

        def turn(z, carry):
            total = self.half[z, self.place.quad].astype(F32)
            for k in range(1, QUADS):
                total = total + self.quad_in[k - 1, z].astype(F32)
            self.block[z] = total.astype(BF)
            return carry

        lax.fori_loop(0, self.place.shards, turn, 0)

    def to_shards(self):
        for d in range(1, self.place.shards):
            self.z_copy(d).start()

    def block_to_shards(self):
        self.to_block()
        self.to_shards()

    def give(self):
        total = self.block[self.place.z].astype(F32)
        for d in range(1, self.place.shards):
            self.z_copy(d).wait_recv()
            total = total + self.z_in[d - 1].astype(F32)
        self.last[...] = total.astype(BF)
        for k in range(1, QUADS):
            self.a_copy(k).start()
            if self.straight:
                for m in range(1, self.place.members):
                    self.s_copy(k, m).start()
        own = pltpu.make_async_copy(self.last, self.piece(self.place.quad, self.place.sub), self.local.at[0])
        own.start()
        own.wait()
        for m in range(1, self.place.members):
            self.f_copy(0, m).start()

    def share(self):
        for k in range(1, QUADS):
            self.a_copy(k).wait_recv()
            if not self.straight:
                for m in range(1, self.place.members):
                    self.f_copy(k, m).start()

    def end_head(self):
        for m in range(1, self.place.members):
            self.h_copy(m).wait_send()
        for k in range(1, QUADS):
            self.q_copy(k).wait_send()

    def end_tail(self):
        for d in range(1, self.place.shards):
            self.z_copy(d).wait_send()
        for k in range(QUADS):
            if k:
                self.a_copy(k).wait_send()
            for m in range(1, self.place.members):
                if k and self.straight:
                    self.s_copy(k, m).wait()
                else:
                    self.f_copy(k, m).wait()


RIM = 16
TILE = 128
SMALL = 128
TN = (((0,), (0,)), ((), ()))


def moved(value, by):
    rows = value.shape[0]
    return value if by % rows == 0 else pltpu.roll(value, (-by) % rows, 0)


def head_columns(tap, wide_first):
    shape = (SMALL, HEADS * HEAD) if wide_first else (HEADS * HEAD, SMALL)
    narrow = lax.broadcasted_iota(jnp.int32, shape, 0 if wide_first else 1)
    wide = lax.broadcasted_iota(jnp.int32, shape, 1 if wide_first else 0)
    if wide_first:
        same = narrow == wide // HEAD * KERNEL + tap
    else:
        same = (narrow * HEAD == (wide * KERNEL + tap * HEAD)) & (wide % HEAD == 0)
    return jnp.where(same, 1.0, 0.0).astype(BF)


def norm_rows(value):
    center = value - jnp.mean(value, axis=-1, keepdims=True)
    inv_std = lax.rsqrt(jnp.mean(center * center, axis=-1, keepdims=True) + norm_eps)
    return center * inv_std, inv_std


def norm_rows_back(normed, inv_std, d_scaled):
    return inv_std * (
        d_scaled
        - jnp.mean(d_scaled, axis=-1, keepdims=True)
        - normed * jnp.mean(d_scaled * normed, axis=-1, keepdims=True)
    )


def fold(value):
    return jnp.sum(value.reshape(value.shape[0] // 8, 8, value.shape[1]), axis=0)


def gelu_both(value):
    size = jnp.abs(value)
    turn = 1.0 / (1.0 + (0.3275911 / math.sqrt(2.0)) * size)
    bell = jnp.exp2(value * value * (-0.5 * math.log2(math.e)))
    poly = ((((1.061405429 * turn - 1.453152027) * turn + 1.421413741) * turn - 0.284496736) * turn + 0.254829592) * turn
    tail = 0.5 * poly * bell
    below = jnp.where(value < 0.0, tail, 1.0 - tail)
    return value * below, below + value * bell * (1.0 / math.sqrt(2.0 * math.pi))


def project_body(hidden, qkv, kv_out, q_packed, q_out):
    seqs, rows, _ = hidden.shape
    half = rows // 2
    width = HEADS * HEAD
    is_low = low_lanes()

    def turn(step, carry):
        s, r = step // (half // TILE), step % (half // TILE)
        tops = (pl.multiple_of(r * TILE, TILE), pl.multiple_of(half + r * TILE, TILE))
        rows_in = jnp.concatenate([hidden[s, pl.ds(top, TILE), :] for top in tops], axis=0)
        mixed = dot(rows_in, qkv[:, : 3 * width], NN).astype(BF)
        blocks = [
            [mixed[part * TILE : part * TILE + TILE, h * width : h * width + 2 * HEAD] for h in range(TRIPLE)]
            for part in range(2)
        ]

        def placed(part, head, low):
            block = blocks[part][head % TRIPLE]
            return block if (head < TRIPLE) == low else swap_halves(block)

        for part, top in enumerate(tops):
            for j in range(HEADS // 2):
                q_out[s, pl.ds(top, TILE), j * 2 * HEAD : j * 2 * HEAD + 2 * HEAD] = jnp.where(
                    is_low, placed(part, 2 * j, True), placed(part, 2 * j + 1, False)
                )
            for h in range(HEADS):
                at = h % TRIPLE * width + 2 * HEAD + h // TRIPLE * 2 * HEAD
                kv_out[s * 2 + h // TRIPLE, h % TRIPLE, pl.ds(top, TILE), :] = mixed[
                    part * TILE : part * TILE + TILE, at : at + 2 * HEAD
                ]
        for h in range(HEADS):
            q_packed[s * 2 + h // TRIPLE, h % TRIPLE, pl.ds(tops[0], TILE), :] = jnp.where(
                is_low, placed(0, h, True), placed(1, h, False)
            )
        return carry

    lax.fori_loop(0, seqs * half // TILE, turn, 0)


def conv_forward_body(
    s, hidden, low_rim, high_rim, rest, q_out, spread_out, key_out, mix_out, soft_out, value_out, conv_out,
    small_turned, span_wide, ext, soft_tile, soft_sem,
):
    seqs, rows, model = hidden.shape
    width = HEADS * HEAD
    tiles = rows // TILE
    depth = small_turned[64 : 64 + 16, :]
    low, high = low_rim[s], high_rim[s]
    ext[0:RIM] = low.astype(F32)
    ext[RIM : RIM + rows] = hidden[s].astype(F32)
    ext[RIM + rows : rows + 2 * RIM] = high.astype(F32)
    value = rest[:, 0:width]
    value_out[s, 0:RIM] = dot(low, value, NN)
    value_out[s, RIM : RIM + rows] = dot(hidden[s], value, NN)
    value_out[s, RIM + rows : rows + 2 * RIM] = dot(high, value, NN)

    def soft_copy(number):
        return pltpu.make_async_copy(soft_tile.at[number % 2], soft_out.at[number], soft_sem.at[number % 2])

    def turn(r, carry):
        number = s * tiles + r
        top = pl.multiple_of(r * TILE, TILE)
        around = ext[pl.ds(top, TILE + 2 * RIM), :]
        spread = jnp.zeros((TILE, model), F32)
        for tap in range(KERNEL):
            spread = spread + moved(around, tap - KERNEL // 2)[RIM : RIM + TILE] * depth[tap : tap + 1]
        spread_low = spread.astype(BF)
        spread_out[s, pl.ds(top, TILE), :] = spread_low
        key_conv = dot(spread_low, rest[:, width : 2 * width], NN)
        key_out[s, pl.ds(top, TILE), :] = key_conv
        mix = (key_conv * q_out[s, pl.ds(top, TILE), :].astype(F32)).astype(BF)
        mix_out[s, pl.ds(top, TILE), :] = mix
        logits = [dot(mix, span_wide[:, tap * width : tap * width + width], NN) for tap in range(KERNEL)]
        peak = functools.reduce(jnp.maximum, logits)
        powers = [jnp.exp(one - peak) for one in logits]
        scale = 1.0 / sum(powers[1:], powers[0])
        values = value_out[s, pl.ds(top, TILE + 2 * RIM), :]

        @pl.when(number > 1)
        def _():
            soft_copy(number - 2).wait()

        result = jnp.zeros((TILE, width), F32)
        for tap in range(KERNEL):
            soft = powers[tap] * scale
            soft_tile[number % 2, tap] = soft.astype(BF)
            result = result + soft * moved(values, tap - KERNEL // 2)[RIM : RIM + TILE]
        conv_out[s, pl.ds(top, TILE), :] = result.astype(BF)
        soft_copy(number).start()
        return carry

    lax.fori_loop(0, tiles, turn, 0)
    if s == seqs - 1:
        soft_copy(seqs * tiles - 2).wait()
        soft_copy(seqs * tiles - 1).wait()


OUTS = 13


def pack_first(qkv_weight, span_weight, conv_depth, norms, qkv_block, rest_block):
    rows = qkv_weight.shape[0]
    width = HEADS * HEAD
    is_low = low_lanes()

    def pair(left, right):
        a, b = (qkv_weight[:, x // 2 * 2 * HEAD : x // 2 * 2 * HEAD + 2 * HEAD] for x in (left, right))
        return jnp.where(is_low, swap_halves(a) if left % 2 else a, b if right % 2 else swap_halves(b))

    for h in range(TRIPLE):
        for j, (left, right) in enumerate(
            ((h, h + TRIPLE), (HEADS + h, 2 * HEADS + h), (HEADS + TRIPLE + h, 2 * HEADS + TRIPLE + h))
        ):
            at = h * width + j * 2 * HEAD
            qkv_block[:, at : at + 2 * HEAD] = pair(left, right)
    qkv_block[:, 3 * width :] = jnp.zeros((rows, SMALL), BF)
    lines = [jnp.zeros((64, rows), F32), conv_depth[...].astype(F32), norms[...].astype(F32)]
    lines += [jnp.zeros((SMALL - 64 - KERNEL - 4, rows), F32)]
    span = span_weight[...].astype(F32)
    span = jnp.concatenate([span, jnp.zeros((span.shape[0], SMALL - span.shape[1]), F32)], axis=1)
    span = jnp.concatenate([span, jnp.zeros((rows - span.shape[0], SMALL), F32)], axis=0)
    rest_block[:, 2 * width : 2 * width + SMALL] = (jnp.concatenate(lines, axis=0).T + span).astype(BF)
    rest_block[:, 2 * width + SMALL :] = jnp.zeros((rows, SMALL), BF)


def front_kernel(by_kernel, members, shards, splits, *refs):
    if by_kernel:
        (
            hidden, qkv_weight, conv_value, conv_point, span_weight, conv_depth, norms,
            dense_attn, dense_conv, ffn_inner, ffn_outer, *refs,
        ) = refs
    else:
        hidden, qkv, rest, span, *refs = refs
    ctx_out, soft_out, *refs = refs
    outs, refs = refs[:OUTS], refs[OUTS:]
    if by_kernel:
        qkv_out, rest_out, span_out, second, third, *refs = refs
    (
        kv_all, q_all, out_all, lse, q_out, spread_out, key_out, mix_out, value_out, conv_out,
        small_turned, low_rim, high_rim,
        kv_in, q_in, out_send, ext, span_wide, soft_tile,
        kv_s, kv_r, q_s, q_r, f_s, f_r, o_s, o_r, e_s, e_r, soft_sem, local, out_sem, *refs,
    ) = refs
    held = (
        kv_all, q_all, out_all, lse, q_out, spread_out, key_out, mix_out, value_out, conv_out,
        small_turned, low_rim, high_rim,
    )
    if by_kernel:
        qkv, rest, span, qkv_block, rest_block, second_block, third_block, load_sem, *sems = refs
        held += (qkv, rest, span)
        outs = (*outs, qkv_out, rest_out, span_out)
        blocks = (qkv_block, rest_block, second_block, third_block)

    def leave(j):
        return pltpu.make_async_copy(held[j], outs[j], out_sem.at[j])

    early = [j for j in range(len(held)) if j not in (0, 1, 2, 3)]
    seqs, rows, model = hidden.shape
    half = rows // 2
    width = HEADS * HEAD
    place = Place(members, shards)
    quad, sub, peer, sibling = place.quad, place.sub, place.peer, place.sibling
    count = QUADS * members
    after = ((place.me + 1) % count, place.z)
    before = ((place.me + count - 1) % count, place.z)
    loads = []
    if by_kernel:
        units = ffn_inner.shape[2]
        group = model // GROUPS
        plan = [(conv_value, rest_block, 0, width), (conv_point, rest_block, width, width)]
        plan += [(dense_attn, second_block, 0, model), (dense_conv, second_block, model, model)]
        for g in range(GROUPS):
            plan += [(ffn_inner.at[g], second_block, 2 * model + g * units, units)]
            plan += [(ffn_outer.at[g], third_block, g * group, group)]
        loads = [
            pltpu.make_async_copy(source, block.at[:, at : at + size], load_sem.at[j])
            for j, (source, block, at, size) in enumerate(plan)
        ]
        for load in loads:
            load.start()
        pack_first(qkv_weight, span_weight, conv_depth, norms, qkv_block, rest_block)
    place.greet(by_kernel, [after, before])
    gathers = []
    if by_kernel:
        gathers = [
            Gather(place, block, full, split, sems[7 * j : 7 * j + 7])
            for j, (block, full, split) in enumerate(zip(blocks, (qkv, rest, second, third), splits))
        ]
        gathers[0].start()
    rims = (
        remote(hidden.at[:, rows - RIM : rows, :], low_rim, e_s.at[0], e_r.at[0], after),
        remote(hidden.at[:, 0:RIM, :], high_rim, e_s.at[1], e_r.at[1], before),
    )
    for rim in rims:
        rim.start()
    for load in loads:
        load.wait()
    if by_kernel:
        gathers[0].relay()
        gathers[1].start()
        gathers[0].share()
        gathers[1].relay()
        gathers[2].start()
        gathers[3].start()
        gathers[0].end()
    project_body(hidden, qkv, kv_in, q_in, q_out)

    def kv_copy(h, k):
        return remote(
            kv_in.at[(quad + k) % QUADS, h], kv_all.at[h, quad, sub], kv_s.at[h, k], kv_r.at[h, k], peer(k)
        )

    def q_copy(h, k):
        return remote(
            q_in.at[(quad + k) % QUADS, h], q_all.at[h, quad], q_s.at[h, k], q_r.at[h, k], peer(k)
        )

    def forward_copy(h, m):
        return remote(
            kv_all.at[h, :, sub], kv_all.at[h, :, sub], f_s.at[h, m], f_r.at[h, m], sibling(m)
        )

    def out_copy(h, i, k):
        return remote(
            out_send.at[h, i], ctx_out.at[quad, h], o_s.at[h, i], o_r.at[h, i], peer(k)
        )

    def receive(h):
        for k in range(1, QUADS):
            kv_copy(h, k).wait_recv()
            q_copy(h, k).wait_recv()
        for m in range(1, members):
            forward_copy(h, m).start()

    own_kv = pltpu.make_async_copy(kv_in.at[quad], kv_all.at[:, quad, sub], local.at[0])
    own_q = pltpu.make_async_copy(q_in.at[quad], q_all.at[:, quad], local.at[1])
    own_kv.start()
    own_q.start()
    for h in range(TRIPLE):
        for k in range(1, QUADS):
            kv_copy(h, k).start()
            q_copy(h, k).start()
    for rim in rims:
        rim.wait()

    @pl.when(place.me == 0)
    def _():
        low_rim[...] = jnp.zeros_like(low_rim)

    @pl.when(place.me == count - 1)
    def _():
        high_rim[...] = jnp.zeros_like(high_rim)

    if by_kernel:
        gathers[1].share()
        gathers[1].end()
        block, head_block = model // shards, width // shards
        for z in range(shards):
            span[z * head_block : z * head_block + head_block] = rest[
                z * block : z * block + head_block, 2 * width : 2 * width + SMALL
            ]
    small_turned[...] = rest[:, 2 * width : 2 * width + SMALL].astype(F32).T
    for tap in range(KERNEL):
        span_wide[:, tap * width : tap * width + width] = dot(span[...], head_columns(tap, True), NN).astype(BF)
    own_kv.wait()
    own_q.wait()
    for s in range(seqs):
        conv_forward_body(
            s, hidden, low_rim, high_rim, rest, q_out, spread_out, key_out, mix_out, soft_out, value_out, conv_out,
            small_turned, span_wide, ext, soft_tile, soft_sem,
        )
        receive(s)
    for j in early:
        leave(j).start()
    is_low = low_lanes()

    def block(step, carry):
        h, i = step // QUADS, step % QUADS
        k = (i + 1) % QUADS
        source = (quad + k) % QUADS

        @pl.when(i == 0)
        def _():
            for m in range(1, members):
                forward_copy(h, m).wait_recv()

        keys = kv_all[h].reshape(QUADS * members * rows, 2 * HEAD)

        def rows_turn(r, inner):
            at = pl.multiple_of(r * CHUNK, CHUNK)
            packed = q_all[h, source, pl.ds(at, CHUNK), :]
            outs = []
            stats = []
            for part in range(2):
                q = jnp.where(is_low, packed if part == 0 else swap_halves(packed), jnp.zeros_like(packed))
                scores = dot(q, keys, NT)
                top = jnp.max(scores, axis=1, keepdims=True)
                probs = jnp.exp2((scores - top) * EXP2_SCALE)
                total = jnp.sum(probs, axis=1, keepdims=True)
                outs.append(dot(probs.astype(BF), keys, NN) / total)
                stats.append(top * EXP2_SCALE + jnp.log2(total))
            both = jnp.where(is_low, swap_halves(outs[0]), outs[1])
            out_all[h, source, pl.ds(at, CHUNK), :] = both
            out_send[h, i, pl.ds(at, CHUNK), :] = both.astype(BF)
            for part in range(2):
                lse[h, source, part, r] = jnp.broadcast_to(stats[part], (CHUNK, CHUNK)).T[0:8, :]
            return inner

        lax.fori_loop(0, half // CHUNK, rows_turn, 0)

        @pl.when(k != 0)
        def _():
            out_copy(h, i, k).start()

        @pl.when(k == 0)
        def _():
            own = pltpu.make_async_copy(out_send.at[h, i], ctx_out.at[quad, h], local.at[0])
            own.start()
            own.wait()

        for j in range(seqs, TRIPLE):

            @pl.when(step == (j - seqs) * QUADS + 2)
            def _(j=j):
                receive(j)

        if by_kernel:

            @pl.when(step == 1)
            def _():
                for gather in gathers[2:]:
                    gather.relay()

            @pl.when(step == TRIPLE * QUADS - 2)
            def _():
                for gather in gathers[2:]:
                    gather.share()

        return carry

    lax.fori_loop(0, TRIPLE * QUADS, block, 0)
    for j in (0, 1, 2, 3):
        leave(j).start()
    for gather in gathers[2:]:
        gather.end()
    for h in range(TRIPLE):
        for k in range(1, QUADS):
            out_copy(h, k - 1, k).wait()
            kv_copy(h, k).wait_send()
            q_copy(h, k).wait_send()
        for m in range(1, members):
            forward_copy(h, m).wait_send()
    for j in range(len(held)):
        leave(j).wait()


def front(by_kernel, members, shards, hidden, *arrays):
    seqs, rows, model = hidden.shape
    half = rows // 2
    width = HEADS * HEAD
    vm = pl.BlockSpec(memory_space=pltpu.VMEM)
    anywhere = pl.BlockSpec(memory_space=pl.ANY)
    dma = pltpu.SemaphoreType.DMA
    shape = jax.ShapeDtypeStruct
    splits = SPLITS if by_kernel else ()
    held = [
        shape((TRIPLE, QUADS, members, rows, 2 * HEAD), BF),
        shape((TRIPLE, QUADS, half, 2 * HEAD), BF),
        shape((TRIPLE, QUADS, half, 2 * HEAD), F32),
        shape((TRIPLE, QUADS, 2, half // CHUNK, 8, CHUNK), F32),
        shape((seqs, rows, width), BF),
        shape((seqs, rows, model), BF),
        shape((seqs, rows, width), F32),
        shape((seqs, rows, width), BF),
        shape((seqs, rows + 2 * RIM, width), F32),
        shape((seqs, rows, width), BF),
        shape((SMALL, model), F32),
        shape((seqs, RIM, model), BF),
        shape((seqs, RIM, model), BF),
    ]
    gathered = []
    scratch = []
    in_specs = [vm] * (1 + len(arrays))
    if by_kernel:
        block, head_block = model // shards, width // shards
        units = arrays[8].shape[2]
        gathered = [
            shape((model, 3 * width + SMALL), BF), shape((model, 2 * width + 2 * SMALL), BF), shape((width, SMALL), BF),
            shape((width, 2 * model + GROUPS * units), BF), shape((units, model), BF),
        ]
        scratch = [pltpu.VMEM(one.shape, BF) for one in gathered[:3]]
        scratch += [
            pltpu.VMEM((block, 3 * width + SMALL), BF),
            pltpu.VMEM((block, 2 * width + 2 * SMALL), BF),
            pltpu.VMEM((head_block, 2 * model + GROUPS * units), BF),
            pltpu.VMEM((units // shards, model), BF),
            dma((4 + 2 * GROUPS,)),
        ]
        in_specs = [vm, vm, anywhere, anywhere, vm, vm, vm, anywhere, anywhere, anywhere, anywhere]
    total = TRIPLE * QUADS * rows * QUADS * members * rows
    result = [
        shape((QUADS, TRIPLE, half, 2 * HEAD), BF),
        shape((seqs * rows // TILE, KERNEL, TILE, width), BF),
        *held,
        *gathered,
    ]
    return pl.pallas_call(
        functools.partial(front_kernel, by_kernel, members, shards, splits),
        in_specs=in_specs,
        out_specs=[anywhere] * len(result),
        out_shape=result,
        scratch_shapes=[pltpu.VMEM(one.shape, one.dtype) for one in held]
        + [
            pltpu.VMEM((QUADS, TRIPLE, rows, 2 * HEAD), BF),
            pltpu.VMEM((QUADS, TRIPLE, half, 2 * HEAD), BF),
            pltpu.VMEM((TRIPLE, QUADS, half, 2 * HEAD), BF),
            pltpu.VMEM((rows + 2 * RIM, model), F32),
            pltpu.VMEM((width, KERNEL * width), BF),
            pltpu.VMEM((2, KERNEL, TILE, width), BF),
            dma((TRIPLE, QUADS)), dma((TRIPLE, QUADS)), dma((TRIPLE, QUADS)), dma((TRIPLE, QUADS)),
            dma((TRIPLE, members)), dma((TRIPLE, members)), dma((TRIPLE, QUADS)), dma((TRIPLE, QUADS)),
            dma((2,)), dma((2,)), dma((2,)), dma((2,)), dma((OUTS + 3,)),
        ]
        + scratch
        + Gather.semaphores(members, shards) * len(splits),
        compiler_params=pltpu.CompilerParams(
            collective_id=1, has_side_effects=True, vmem_limit_bytes=62 * 2**20
        ),
        cost_estimate=pl.CostEstimate(flops=total * 256, bytes_accessed=8 * 2**20, transcendentals=total),
    )(hidden, *arrays)


def middle_kernel(
    by_kernel, shards, members,
    context, conv, hidden, cotangent, second, third, small_turned,
    layer_out, d_first_out, d_context_out, d_conv_out, dense_part, inner_part, third_part, norm_sums,
    context_low, hidden_low, active_all, d_outer_all, d_inner_all, d_dense_all, d_context_all,
):
    seqs, rows, model = hidden.shape
    half = rows // 2
    width = HEADS * HEAD
    group = model // GROUPS
    units = third.shape[0]
    is_low = low_lanes()
    gains = small_turned[64 + KERNEL : 64 + KERNEL + 4, :]
    attn_gain, attn_bias, out_gain, out_bias = (gains[j : j + 1] for j in range(4))
    norm_sums[...] = jnp.zeros_like(norm_sums)

    def turn(step, carry):
        s, p = step // 2, step % 2
        top = pl.multiple_of(p * half, half)
        at = pl.ds(top, half)
        every = pl.ds(pl.multiple_of(step * half, half), half)
        pairs = []
        for j in range(HEADS // 2):
            a = context[s * 2 + 2 * j // TRIPLE, 2 * j % TRIPLE]
            b = context[s * 2 + (2 * j + 1) // TRIPLE, (2 * j + 1) % TRIPLE]
            upper = jnp.where(is_low, a, swap_halves(b))
            lower = jnp.where(is_low, swap_halves(a), b)
            pairs.append(jnp.where(p == 0, upper, lower))
        low = jnp.concatenate(pairs, axis=1)
        context_low[every] = low
        dense = dot(low, second[:, :model], NN) + dot(conv[s, at], second[:, model : 2 * model], NN)
        normed_one, inv_one = norm_rows(dense + hidden[s, at].astype(F32))
        hidden_one = normed_one * attn_gain + attn_bias
        one_low = hidden_one.astype(BF)
        hidden_low[every] = one_low
        outers = []
        slopes = []
        for g in range(GROUPS):
            edge = 2 * model + g * units
            inner = dot(one_low[:, g * group : g * group + group], second[:, edge : edge + units], NN)
            active, slope = gelu_both(inner)
            active = active.astype(BF)
            active_all[every, g * units : g * units + units] = active
            slopes.append(slope)
            outers.append(dot(active, third[:, g * group : g * group + group], NN))
        normed_two, inv_two = norm_rows(jnp.concatenate(outers, axis=1) + hidden_one)
        layer_out[s, at] = (normed_two * out_gain + out_bias).astype(BF)
        d_result = cotangent[s, at].astype(F32)
        norm_sums[2] += fold(d_result * normed_two)
        norm_sums[3] += fold(d_result)
        d_second = norm_rows_back(normed_two, inv_two, d_result * out_gain)
        d_outer = d_second.astype(BF)
        d_outer_all[every] = d_outer
        backs = []
        for g in range(GROUPS):
            edge = 2 * model + g * units
            d_active = dot(d_outer[:, g * group : g * group + group], third[:, g * group : g * group + group], NT)
            d_inner = (d_active * slopes[g]).astype(BF)
            d_inner_all[every, g * units : g * units + units] = d_inner
            backs.append(dot(d_inner, second[:, edge : edge + units], NT))
        d_hidden = jnp.concatenate(backs, axis=1) + d_second
        norm_sums[0] += fold(d_hidden * normed_one)
        norm_sums[1] += fold(d_hidden)
        d_first = norm_rows_back(normed_one, inv_one, d_hidden * attn_gain)
        d_first_out[s, at] = d_first
        d_dense = d_first.astype(BF)
        d_dense_all[every] = d_dense
        d_context_all[every] = dot(d_dense, second[:, :model], NT).astype(BF)
        d_conv_out[s, at] = dot(d_dense, second[:, model : 2 * model], NT)
        return carry

    lax.fori_loop(0, seqs * 2, turn, 0)
    for s in range(seqs):
        for h in range(HEADS):
            at = h // 2 * 2 * HEAD
            upper = d_context_all[s * rows : s * rows + half, at : at + 2 * HEAD]
            lower = d_context_all[s * rows + half : s * rows + rows, at : at + 2 * HEAD]
            if h % 2:
                packed = jnp.where(is_low, swap_halves(upper), lower)
            else:
                packed = jnp.where(is_low, upper, swap_halves(lower))
            d_context_out[s * 2 + h // TRIPLE, h % TRIPLE] = packed
    for g in range(GROUPS):
        for z in range(shards):
            block = units // shards
            part = dot(
                active_all[:, g * units + z * block : g * units + z * block + block],
                d_outer_all[:, g * group : g * group + group], TN,
            ).astype(BF)
            if by_kernel:
                piece = block // (QUADS * members)
                for q in range(QUADS):
                    for c in range(members):
                        row = (q * members + c) * piece
                        third_part[c, z, q, :, g * group : g * group + group] = part[row : row + piece]
            else:
                third_part[z * block : z * block + block, g * group : g * group + group] = part

    def columns(left, right):
        found = []
        for start, size, rows_in, columns_in in (
            (0, model, context_low[...], d_dense_all),
            (model, model, None, d_dense_all),
            (2 * model, units, hidden_low[:, :group], d_inner_all.at[:, :units]),
            (2 * model + units, units, hidden_low[:, group:], d_inner_all.at[:, units:]),
        ):
            a, b = max(left, start), min(right, start + size)
            if a < b:
                if rows_in is None:
                    rows_in = conv[...].reshape(seqs * rows, width)
                found.append(dot(rows_in, columns_in[:, a - start : b - start], TN).astype(BF))
        return jnp.concatenate(found, axis=1) if len(found) > 1 else found[0]

    for part_out, start, size in ((dense_part, 0, 2 * model), (inner_part, 2 * model, GROUPS * units)):
        wide = size // 4
        for j in range(4):
            part = columns(start + j * wide, start + j * wide + wide)
            if by_kernel:
                block = width // shards
                piece = block // 2
                for z in range(shards):
                    for r in range(2):
                        row = z * block + r * piece
                        part_out[j % members, z, r * 2 + j // members] = part[row : row + piece]
            else:
                part_out[:, j * wide : j * wide + wide] = part


def middle(context, conv, hidden, cotangent, second, third, small_turned, by_kernel, shards, members):
    seqs, rows, model = hidden.shape
    width = HEADS * HEAD
    units = third.shape[0]
    tokens = seqs * rows
    shape = jax.ShapeDtypeStruct
    if by_kernel:
        parts = [
            shape((members, shards, QUADS, width // shards // 2, 2 * model // 4), BF),
            shape((members, shards, QUADS, width // shards // 2, GROUPS * units // 4), BF),
            shape((members, shards, QUADS, units // shards // (QUADS * members), model), BF),
        ]
    else:
        parts = [shape((width, 2 * model), BF), shape((width, GROUPS * units), BF), shape(third.shape, BF)]
    return pl.pallas_call(
        functools.partial(middle_kernel, by_kernel, shards, members),
        out_shape=[
            shape((seqs, rows, model), BF),
            shape((seqs, rows, model), F32),
            shape((QUADS, TRIPLE, rows // 2, 2 * HEAD), BF),
            shape((seqs, rows, width), F32),
            *parts,
            shape((4, 8, model), F32),
        ],
        scratch_shapes=[
            pltpu.VMEM((tokens, width), BF),
            pltpu.VMEM((tokens, model), BF),
            pltpu.VMEM((tokens, GROUPS * units), BF),
            pltpu.VMEM((tokens, model), BF),
            pltpu.VMEM((tokens, GROUPS * units), BF),
            pltpu.VMEM((tokens, model), BF),
            pltpu.VMEM((tokens, width), BF),
        ],
        compiler_params=pltpu.CompilerParams(vmem_limit_bytes=60 * 2**20),
    )(context, conv, hidden, cotangent, second, third, small_turned)


def conv_back_kernel(by_kernel, shards, members, *refs):
    (
        hidden, low_rim, high_rim, rest, span, small_turned, d_conv, q_out, spread, key_conv, mix, soft, value, d_first,
        norm_sums, d_in, *refs,
    ) = refs
    if by_kernel:
        third_part, dense_part, *refs = refs
    grad_rows, low_edge, high_edge, dq_conv, part_out, d_all, *refs = refs
    if by_kernel:
        third_block, dense_block, *refs = refs
    (
        ext, d_value, d_rows, slim_all, d_key_all, depth_sums, ext_low, soft_tile,
        d_s, d_r, soft_sem, local, *scratch,
    ) = refs
    seqs, rows, model = hidden.shape
    width = HEADS * HEAD
    value_at, point_at = 0, width
    tiles = rows // TILE
    place = Place(members, shards)
    quad, peer = place.quad, place.peer
    place.greet(False)

    def d_copy(h, k):
        return remote(
            d_in.at[(quad + k) % QUADS, h], d_all.at[h, quad], d_s.at[h, k], d_r.at[h, k], peer(k)
        )

    def soft_copy(number):
        return pltpu.make_async_copy(soft.at[number], soft_tile.at[number % 2], soft_sem.at[number % 2])

    soft_copy(0).start()
    base = pltpu.make_async_copy(d_first, grad_rows, local.at[0])
    base.start()
    own = pltpu.make_async_copy(d_in.at[quad], d_all.at[:, quad], local.at[1])
    own.start()
    for h in range(TRIPLE):
        for k in range(1, QUADS):
            d_copy(h, k).start()
    if by_kernel:
        third = Reduce(place, third_part, third_block, None, 1, head=scratch[0:7])
        dense = Reduce(place, dense_part, dense_block, None, 4, head=scratch[7:14])
        third.start()
        dense.start()
    is_low = low_lanes()
    depth = small_turned[64 : 64 + 16, :]
    pair = lax.broadcasted_iota(jnp.int32, (4 * HEAD, 2 * HEAD), 0) // HEAD % 2
    same = pair == lax.broadcasted_iota(jnp.int32, (4 * HEAD, 2 * HEAD), 1) // HEAD
    group_sum = jnp.where(same, 1.0, 0.0).astype(BF)
    depth_sums[...] = jnp.zeros_like(depth_sums)
    long = rows + 2 * RIM
    for s in range(seqs):
        ext[0:RIM] = low_rim[s].astype(F32)
        ext[RIM : RIM + rows] = hidden[s].astype(F32)
        ext[RIM + rows : long] = high_rim[s].astype(F32)
        ext_low[s * long : s * long + RIM] = low_rim[s]
        ext_low[s * long + RIM : s * long + RIM + rows] = hidden[s]
        ext_low[s * long + RIM + rows : s * long + long] = high_rim[s]
        d_value[...] = jnp.zeros_like(d_value)
        d_rows[...] = jnp.zeros_like(d_rows)

        def turn(r, carry):
            number = s * tiles + r

            @pl.when(number + 1 < seqs * tiles)
            def _():
                soft_copy(number + 1).start()

            top = pl.multiple_of(r * TILE, TILE)
            here = pl.ds(top, TILE)
            there = pl.ds(top, TILE + 2 * RIM)
            every = pl.ds(pl.multiple_of(s * rows + r * TILE, TILE), TILE)
            d_res = d_conv[s, here, :]
            values = value[s, there, :]
            softs = []
            d_kernels = []
            soft_copy(number).wait()
            rim = jnp.zeros((RIM, width), F32)
            d_values = jnp.zeros((TILE + 2 * RIM, width), F32)
            total = jnp.zeros((TILE, width), F32)
            for tap in range(KERNEL):
                one = soft_tile[number % 2, tap].astype(F32)
                softs.append(one)
                weighted = jnp.concatenate([rim, one * d_res, rim], axis=0)
                d_values = d_values + moved(weighted, KERNEL // 2 - tap)
                product = d_res * moved(values, tap - KERNEL // 2)[RIM : RIM + TILE]
                high = product.astype(BF)
                lower = (product - high.astype(F32)).astype(BF)
                sums = []
                for at in range(0, width, 2 * HEAD):
                    both = jnp.concatenate([high[:, at : at + 2 * HEAD], lower[:, at : at + 2 * HEAD]], axis=1)
                    sums.append(dot(both, group_sum, NN))
                d_kernel = jnp.concatenate(sums, axis=1)
                d_kernels.append(d_kernel)
                total = total + d_kernel * one
            d_value[there, :] += d_values
            slim = jnp.zeros((TILE, SMALL), F32)
            for tap in range(KERNEL):
                d_logits = (softs[tap] * (d_kernels[tap] - total)).astype(BF)
                slim = slim + dot(d_logits, head_columns(tap, False), NN)
            slim = slim.astype(BF)
            slim_all[every] = slim
            d_mix = dot(slim, span[...], NT)
            d_query = d_mix * key_conv[s, here, :]
            for h in range(TRIPLE):
                a, b = (d_query[:, x // 2 * 2 * HEAD : x // 2 * 2 * HEAD + 2 * HEAD] for x in (h, h + TRIPLE))
                a = swap_halves(a) if h % 2 else a
                b = b if (h + TRIPLE) % 2 else swap_halves(b)
                dq_conv[h, s, here, :] = jnp.where(is_low, a, b)
            d_key = (d_mix * q_out[s, here, :].astype(F32)).astype(BF)
            d_key_all[every] = d_key
            d_spread = dot(d_key, rest[:, point_at : point_at + width], NT)
            around = ext[there, :]
            wide_rim = jnp.zeros((RIM, model), F32)
            padded = jnp.concatenate([wide_rim, d_spread, wide_rim], axis=0)
            back = jnp.zeros((TILE + 2 * RIM, model), F32)
            for tap in range(KERNEL):
                depth_sums[tap] += fold(d_spread * moved(around, tap - KERNEL // 2)[RIM : RIM + TILE])
                back = back + moved(padded, KERNEL // 2 - tap) * depth[tap : tap + 1]
            d_rows[there, :] += back
            if by_kernel:

                @pl.when(number == 1)
                def _():
                    third.to_quads()

                @pl.when(number == 2)
                def _():
                    dense.to_quads()

            return carry

        lax.fori_loop(0, tiles, turn, 0)
        if s == 0:
            base.wait()
        value_low = d_value[...].astype(BF)
        value_part = dot(ext_low[s * long : s * long + long], value_low, TN)
        if s == 0:
            grad_value = value_part
        else:
            grad_value = grad_value + value_part
        all_rows = dot(value_low, rest[:, value_at : value_at + width], NT) + d_rows[...]
        grad_rows[s] += all_rows[RIM : RIM + rows]
        low_edge[s] = all_rows[0:RIM].astype(BF)
        high_edge[s] = all_rows[RIM + rows :].astype(BF)

    grad_point = dot(spread[...].reshape(seqs * rows, model), d_key_all[...], TN)
    grad_span = dot(mix[...].reshape(seqs * rows, width), slim_all[...], TN)
    lines = [jnp.zeros((64, model), F32)]
    lines += [jnp.sum(depth_sums[tap], axis=0, keepdims=True) for tap in range(KERNEL)]
    lines += [jnp.sum(norm_sums[j], axis=0, keepdims=True) for j in range(4)]
    lines += [jnp.zeros((SMALL - 64 - KERNEL - 4, model), F32)]
    block, head_block = model // shards, width // shards
    slots = []
    for z in range(shards):
        slots += [grad_span[z * head_block : z * head_block + head_block], jnp.zeros((block - head_block, SMALL), F32)]
    small = jnp.concatenate(lines, axis=0).T + jnp.concatenate(slots, axis=0)
    whole = jnp.concatenate([grad_value, grad_point, small, jnp.zeros((model, SMALL), F32)], axis=1).astype(BF)
    if by_kernel:
        piece = block // QUADS
        wide = whole.shape[1] // members
        for z in range(shards):
            for q in range(QUADS):
                row = z * block + q * piece
                for c in range(members):
                    part_out[c, z, q] = whole[row : row + piece, c * wide : c * wide + wide]
    else:
        part_out[...] = whole
    own.wait()
    for h in range(TRIPLE):
        for k in range(1, QUADS):
            d_copy(h, k).wait()
    if by_kernel:
        for one in (third, dense):
            one.to_block()
            one.end_head()


def conv_back(by_kernel, shards, members, *arrays):
    hidden = arrays[0]
    seqs, rows, model = hidden.shape
    width = HEADS * HEAD
    long = rows + 2 * RIM
    columns = 2 * width + 2 * SMALL
    shape = jax.ShapeDtypeStruct
    if by_kernel:
        part = shape((members, shards, QUADS, model // shards // QUADS, columns // members), BF)
    else:
        part = shape((model, columns), BF)
    vm = pl.BlockSpec(memory_space=pltpu.VMEM)
    anywhere = pl.BlockSpec(memory_space=pl.ANY)
    dma = pltpu.SemaphoreType.DMA
    blocks = [one.shape[1:2] + one.shape[3:] for one in arrays[16:]]
    return pl.pallas_call(
        functools.partial(conv_back_kernel, by_kernel, shards, members),
        in_specs=[vm] * 11 + [anywhere, vm, anywhere, vm, anywhere] + [vm] * len(blocks),
        out_specs=[vm] * (6 + len(blocks)),
        out_shape=[
            shape((seqs, rows, model), F32),
            shape((seqs, RIM, model), BF),
            shape((seqs, RIM, model), BF),
            shape((TRIPLE, seqs, rows, 2 * HEAD), F32),
            part,
            shape((TRIPLE, QUADS, rows // 2, 2 * HEAD), BF),
        ]
        + [shape(one, BF) for one in blocks],
        scratch_shapes=[
            pltpu.VMEM((long, model), F32),
            pltpu.VMEM((long, width), F32),
            pltpu.VMEM((long, model), F32),
            pltpu.VMEM((seqs * rows, SMALL), BF),
            pltpu.VMEM((seqs * rows, width), BF),
            pltpu.VMEM((KERNEL, 8, model), F32),
            pltpu.VMEM((seqs * long, model), BF),
            pltpu.VMEM((2, KERNEL, TILE, width), BF),
            dma((TRIPLE, QUADS)), dma((TRIPLE, QUADS)), dma((2,)), dma((2,)),
        ]
        + sum((Reduce.head_scratch(members, shards, *one[1:]) for one in blocks), []),
        compiler_params=pltpu.CompilerParams(
            collective_id=3, has_side_effects=True, vmem_limit_bytes=60 * 2**20
        ),
    )(*arrays)


def back_kernel(by_kernel, shards, members, *refs):
    d_all, kv_all, q_all, out_all, lse, hidden, qkv, dq_conv, grad_rows, low_edge, high_edge, *refs = refs
    if by_kernel:
        third_block, dense_block, inner_part, middle_part, *refs = refs
        grad_in, third_sum, dense_sum, inner_sum, middle_sum, *refs = refs
        sums, refs = refs[:TRIPLE], refs[TRIPLE:]
    else:
        grad_in, whole, *refs = refs
    (
        q_zero, d_zero, stat, delta, dq_sum, dkv_sum, own_part, sib_send, sib_recv, dkv_send, dq_send,
        dq_out, dkv_out, d_columns, low_in, high_in,
        p_s, p_r, k_s, k_r, g_s, g_r, e_s, e_r, local, *scratch,
    ) = refs
    rows = kv_all.shape[3]
    half = rows // 2
    seqs, _, model = hidden.shape
    width = HEADS * HEAD
    steps = TRIPLE * QUADS
    place = Place(members, shards)
    quad, sub, peer, sibling = place.quad, place.sub, place.peer, place.sibling
    count = QUADS * members
    after = ((place.me + 1) % count, place.z)
    before = ((place.me + count - 1) % count, place.z)
    more = [place.cross(k, m) for k in range(1, QUADS) for m in range(1, members)] if by_kernel else []
    place.greet(by_kernel, [after, before, *more])
    is_low = low_lanes()
    third = dense = inner = middle = None
    chunks = []
    if by_kernel:
        third = Reduce(place, None, third_block, third_sum, 1, tail=scratch[0:9])
        dense = Reduce(place, None, dense_block, dense_sum, 4, tail=scratch[9:18])
        inner_block, middle_block, *scratch = scratch[18:]
        inner = Reduce(place, inner_part, inner_block, inner_sum, 4, head=scratch[0:7], tail=scratch[7:16])
        middle = Reduce(place, middle_part, middle_block, middle_sum, 2, head=scratch[16:23], tail=scratch[23:32])
        scratch = scratch[32:]
        for h in range(TRIPLE):
            part, block, *scratch = scratch
            chunks.append(Reduce(place, part, block, sums[h], 1, head=scratch[0:7], tail=scratch[7:16]))
            scratch = scratch[16:]
    edges = (
        remote(high_edge, low_in, e_s.at[0], e_r.at[0], after),
        remote(low_edge, high_in, e_s.at[1], e_r.at[1], before),
    )
    for edge in edges:
        edge.start()
    if by_kernel:
        third.to_shards()
        dense.to_shards()
        inner.start()
        middle.start()
    base = pltpu.make_async_copy(grad_rows, grad_in, local.at[1])
    base.start()
    base.wait()

    def part_copy(step, m):
        return remote(
            sib_send.at[step % 2, m - 1], sib_recv.at[step, m - 1], p_s.at[step, m], p_r.at[step, m], sibling(m)
        )

    def dkv_copy(h, i, k):
        return remote(
            dkv_send.at[h, i], dkv_out.at[quad, h], k_s.at[h, i], k_r.at[h, i], peer(k)
        )

    def dq_copy(h, k):
        return remote(
            dq_send.at[h, (quad + k) % QUADS], dq_out.at[quad, h], g_s.at[h, k], g_r.at[h, k], peer(k)
        )

    def finish(step):
        h, i = step // QUADS, step % QUADS
        k = (i + 1) % QUADS
        total = own_part[step % 2]
        for m in range(1, members):
            part_copy(step, m).wait_recv()
            total = total + sib_recv[step, m - 1].astype(F32)
        dkv_send[h, i] = total.astype(BF)

        @pl.when(k != 0)
        def _():
            dkv_copy(h, i, k).start()

        @pl.when(k == 0)
        def _():
            own = pltpu.make_async_copy(dkv_send.at[h, i], dkv_out.at[quad, h], local.at[0])
            own.start()
            own.wait()

    def columns_of(h):
        for k in range(1, QUADS):
            dkv_copy(h, k - 1, k).wait_recv()
            dq_copy(h, k).wait_recv()
        for s in range(seqs):
            a = dq_out[s * 2, h].astype(F32)
            b = dq_out[s * 2 + 1, h].astype(F32)
            top = s * rows
            upper = jnp.where(is_low, a, swap_halves(b)) + dq_conv[h, s, 0:half, :]
            lower = jnp.where(is_low, swap_halves(a), b) + dq_conv[h, s, half:rows, :]
            d_columns[top : top + half, 0 : 2 * HEAD] = upper.astype(BF)
            d_columns[top + half : top + rows, 0 : 2 * HEAD] = lower.astype(BF)
            d_columns[top : top + rows, 2 * HEAD : 4 * HEAD] = dkv_out[s * 2, h]
            d_columns[top : top + rows, 4 * HEAD : 6 * HEAD] = dkv_out[s * 2 + 1, h]
        value = dot(hidden[...].reshape(seqs * rows, model), d_columns[...], TN).astype(BF)
        if by_kernel:
            part = chunks[h].part
            block = model // shards
            piece = block // QUADS
            wide = part.shape[4]
            for z in range(shards):
                for q in range(QUADS):
                    row = z * block + q * piece
                    for c in range(members):
                        part[c, z, q] = value[row : row + piece, c * wide : c * wide + wide]
            chunks[h].start()
        else:
            whole[:, h * width : h * width + width] = value

    def rows_of(h):
        for s in range(seqs):
            grad_in[s] += dot(d_columns[s * rows : s * rows + rows, :], qkv[:, h * width : h * width + width], NT)

    def block(step, carry):
        h, i = step // QUADS, step % QUADS
        k = (i + 1) % QUADS
        source = (quad + k) % QUADS

        @pl.when(i == 0)
        def _():
            def prepare(b, inner):
                q = q_all[h, b]
                d = d_all[h, b]
                zero = jnp.zeros_like(q)
                q_zero[b, 0:half] = jnp.where(is_low, q, zero)
                q_zero[b, half:rows] = jnp.where(is_low, swap_halves(q), zero)
                d_zero[b, 0:half] = jnp.where(is_low, zero, swap_halves(d))
                d_zero[b, half:rows] = jnp.where(is_low, zero, d)
                both = (out_all[h, b] * d.astype(F32)).T
                delta[b, :, 0:half] = jnp.broadcast_to(jnp.sum(both[0:HEAD], axis=0, keepdims=True), (8, half))
                delta[b, :, half:rows] = jnp.broadcast_to(jnp.sum(both[HEAD:], axis=0, keepdims=True), (8, half))
                for part in range(2):
                    for r in range(half // CHUNK):
                        at = part * half + r * CHUNK
                        stat[b, :, at : at + CHUNK] = lse[h, b, part, r]
                dq_sum[b] = jnp.zeros((HEAD, rows), F32)
                return inner

            lax.fori_loop(0, QUADS, prepare, 0)

        keys = kv_all[h, source].reshape(members * rows, 2 * HEAD)
        keys_turned = keys.T[0:HEAD]
        dkv_sum[...] = jnp.zeros_like(dkv_sum)

        def queries_turn(b, inner):
            qz = q_zero[b]
            dz = d_zero[b]
            probs = jnp.exp2(dot(keys, qz, NT) * EXP2_SCALE - stat[b, 0:1, :])
            d_probs = dot(keys, dz, NT)
            d_scores = (probs * (d_probs - delta[b, 0:1, :])).astype(BF)
            dkv_sum[...] += dot(d_scores, qz, NN) * (1.0 / math.sqrt(HEAD)) + dot(probs.astype(BF), dz, NN)
            dq_sum[b] += dot(keys_turned, d_scores, NN)
            return inner

        lax.fori_loop(0, QUADS, queries_turn, 0)

        @pl.when(step > 0)
        def _():
            finish(step - 1)

        own_part[step % 2] = dkv_sum[pl.ds(pl.multiple_of(sub * rows, rows), rows), :]
        for m in range(1, members):

            @pl.when(step > 1)
            def _():
                part_copy(step - 2, m).wait_send()

            target = (sub + m) % members
            sib_send[step % 2, m - 1] = dkv_sum[pl.ds(pl.multiple_of(target * rows, rows), rows), :].astype(BF)
            part_copy(step, m).start()

        @pl.when(i == QUADS - 1)
        def _():
            def give(b, inner):
                turned = dq_sum[b] * (1.0 / math.sqrt(HEAD))
                dq_send[h, b] = jnp.concatenate([turned[:, 0:half], turned[:, half:rows]], axis=0).T.astype(BF)
                return inner

            lax.fori_loop(0, QUADS, give, 0)
            for j in range(1, QUADS):
                dq_copy(h, j).start()
            mine = pltpu.make_async_copy(dq_send.at[h, quad], dq_out.at[quad, h], local.at[0])
            mine.start()
            mine.wait()

        plan = [(5, lambda: columns_of(0)), (5, lambda: rows_of(0)), (9, lambda: columns_of(1)), (9, lambda: rows_of(1))]
        if by_kernel:
            plan += [
                (0, inner.to_quads), (1, middle.to_quads),
                (2, third.give), (2, dense.give), (4, third.share), (4, dense.share),
                (4, inner.block_to_shards), (6, inner.give), (8, inner.share),
                (5, middle.block_to_shards), (7, middle.give), (9, middle.share),
                (6, chunks[0].to_quads), (8, chunks[0].block_to_shards), (9, chunks[0].give), (10, chunks[0].share),
                (10, chunks[1].to_quads), (11, chunks[1].block_to_shards),
            ]
        for at in range(steps):
            stages = [stage for when, stage in plan if when == at]
            if stages:

                @pl.when(step == at)
                def _(stages=stages):
                    for stage in stages:
                        stage()

        return carry

    lax.fori_loop(0, steps, block, 0)
    finish(steps - 1)
    columns_of(TRIPLE - 1)
    if by_kernel:
        chunks[1].give()
        chunks[2].to_quads()
    rows_of(TRIPLE - 1)
    for edge in edges:
        edge.wait()

    @pl.when(place.me > 0)
    def _():
        grad_in[:, 0:RIM, :] += low_in[...].astype(F32)

    @pl.when(place.me < count - 1)
    def _():
        grad_in[:, rows - RIM : rows, :] += high_in[...].astype(F32)

    if by_kernel:
        chunks[1].share()
        third.end_tail()
        dense.end_tail()
        inner.end_tail()
        middle.end_tail()
        inner.end_head()
        middle.end_head()
        chunks[2].block_to_shards()
        chunks[2].give()
        chunks[2].share()
        for h in range(TRIPLE):
            chunks[h].end_head()
            chunks[h].end_tail()
    for m in range(1, members):
        part_copy(steps - 2, m).wait_send()
        part_copy(steps - 1, m).wait_send()
    for h in range(TRIPLE):
        for k in range(1, QUADS):
            dkv_copy(h, k - 1, k).wait_send()
            dq_copy(h, k).wait_send()


def back(by_kernel, shards, members, *arrays):
    kv_all, hidden = arrays[1], arrays[5]
    rows = kv_all.shape[3]
    half = rows // 2
    seqs, _, model = hidden.shape
    width = HEADS * HEAD
    units = 2 * model
    steps = TRIPLE * QUADS
    vm = pl.BlockSpec(memory_space=pltpu.VMEM)
    dma = pltpu.SemaphoreType.DMA
    shape = jax.ShapeDtypeStruct
    outs = [shape((seqs, rows, model), F32)]
    reducing = []
    if by_kernel:
        block, head_block = model // shards, width // shards
        outs += [
            shape((units // shards, model), BF),
            shape((head_block, 2 * model), BF),
            shape((head_block, GROUPS * units), BF),
            shape((block, 2 * width + 2 * SMALL), BF),
        ]
        outs += [shape((members, block, width // members), BF)] * TRIPLE
        third, dense, inner, middle = (one.shape[-2:] for one in arrays[11:])
        chunk = (block // QUADS, width // members)
        reducing = [
            *Reduce.tail_scratch(members, shards, *third),
            *Reduce.tail_scratch(members, shards, *dense),
            pltpu.VMEM((shards, *inner), BF),
            pltpu.VMEM((shards, *middle), BF),
            *Reduce.head_scratch(members, shards, *inner),
            *Reduce.tail_scratch(members, shards, *inner),
            *Reduce.head_scratch(members, shards, *middle),
            *Reduce.tail_scratch(members, shards, *middle),
        ]
        for _ in range(TRIPLE):
            reducing += [
                pltpu.VMEM((members, shards, QUADS, *chunk), BF),
                pltpu.VMEM((shards, *chunk), BF),
                *Reduce.head_scratch(members, shards, *chunk),
                *Reduce.tail_scratch(members, shards, *chunk),
            ]
    else:
        outs += [shape((model, 3 * width), BF)]
    total = TRIPLE * QUADS * rows * QUADS * members * rows
    return pl.pallas_call(
        functools.partial(back_kernel, by_kernel, shards, members),
        in_specs=[vm] * 8 + [pl.BlockSpec(memory_space=pl.ANY)] + [vm] * (len(arrays) - 9),
        out_specs=[vm] * len(outs),
        out_shape=outs,
        scratch_shapes=[
            pltpu.VMEM((QUADS, rows, 2 * HEAD), BF),
            pltpu.VMEM((QUADS, rows, 2 * HEAD), BF),
            pltpu.VMEM((QUADS, 8, rows), F32),
            pltpu.VMEM((QUADS, 8, rows), F32),
            pltpu.VMEM((QUADS, HEAD, rows), F32),
            pltpu.VMEM((members * rows, 2 * HEAD), F32),
            pltpu.VMEM((2, rows, 2 * HEAD), F32),
            pltpu.VMEM((2, members - 1, rows, 2 * HEAD), BF),
            pltpu.VMEM((steps, members - 1, rows, 2 * HEAD), BF),
            pltpu.VMEM((TRIPLE, QUADS, rows, 2 * HEAD), BF),
            pltpu.VMEM((TRIPLE, QUADS, half, 2 * HEAD), BF),
            pltpu.VMEM((QUADS, TRIPLE, half, 2 * HEAD), BF),
            pltpu.VMEM((QUADS, TRIPLE, rows, 2 * HEAD), BF),
            pltpu.VMEM((seqs * rows, width), BF),
            pltpu.VMEM((seqs, RIM, model), BF),
            pltpu.VMEM((seqs, RIM, model), BF),
            dma((steps, members)), dma((steps, members)),
            dma((TRIPLE, QUADS)), dma((TRIPLE, QUADS)), dma((TRIPLE, QUADS)), dma((TRIPLE, QUADS)),
            dma((2,)), dma((2,)), dma((2,)),
        ]
        + reducing,
        compiler_params=pltpu.CompilerParams(
            collective_id=2, has_side_effects=True, vmem_limit_bytes=62 * 2**20
        ),
        cost_estimate=pl.CostEstimate(flops=total * 640, bytes_accessed=8 * 2**20, transcendentals=total),
    )(*arrays)


def finish_kernel(rows_in, third_sum, dense_sum, inner_sum, middle_sum, *refs):
    sums, refs = refs[:TRIPLE], refs[TRIPLE:]
    rows_out, g_qkv, g_depth, g_point, g_span, g_value, g_attn, g_conv, g_norms, g_inner, g_outer = refs
    rows_out[...] = rows_in[...]
    width = HEADS * HEAD
    model = third_sum.shape[1]
    group, units = model // GROUPS, g_inner.shape[2]
    for g in range(GROUPS):
        g_outer[g] = third_sum[:, g * group : g * group + group].astype(F32)
        g_inner[g] = inner_sum[:, g * units : g * units + units].astype(F32)
    g_attn[...] = dense_sum[:, :model].astype(F32)
    g_conv[...] = dense_sum[:, model:].astype(F32)
    g_value[...] = middle_sum[:, :width].astype(F32)
    g_point[...] = middle_sum[:, width : 2 * width].astype(F32)
    small = middle_sum[:, 2 * width : 2 * width + SMALL].astype(F32)
    g_span[...] = small[: g_span.shape[0], : HEADS * KERNEL]
    turned = small.T
    g_depth[...] = turned[64 : 64 + KERNEL]
    g_norms[...] = turned[64 + KERNEL : 68 + KERNEL]
    found = {}
    for h in range(TRIPLE):
        both = jnp.concatenate([sums[h][c].astype(F32) for c in range(sums[h].shape[0])], axis=1)
        for t in range(2):
            head = TRIPLE * t + h
            found[head] = both[:, t * HEAD : t * HEAD + HEAD]
            at = 2 * HEAD + t * 2 * HEAD
            found[HEADS + head] = both[:, at : at + HEAD]
            found[2 * HEADS + head] = both[:, at + HEAD : at + 2 * HEAD]
    for j in range(3 * HEADS // 2):
        g_qkv[:, j * 2 * HEAD : j * 2 * HEAD + 2 * HEAD] = jnp.concatenate([found[2 * j], found[2 * j + 1]], axis=1)


def finish_all(shards, rows_in, *arrays):
    vm = pl.BlockSpec(memory_space=pltpu.VMEM)
    width, model = HEADS * HEAD, rows_in.shape[2]
    units = 2 * model
    block, head_block = model // shards, width // shards
    shape = jax.ShapeDtypeStruct
    outs = [
        shape(rows_in.shape, F32),
        shape((block, 3 * width), F32),
        shape((KERNEL, block), F32),
        shape((block, width), F32),
        shape((head_block, HEADS * KERNEL), F32),
        shape((block, width), F32),
        shape((head_block, model), F32),
        shape((head_block, model), F32),
        shape((4, block), F32),
        shape((GROUPS, head_block, units), F32),
        shape((GROUPS, units // shards, model // GROUPS), F32),
    ]
    return pl.pallas_call(
        finish_kernel,
        in_specs=[vm] * (1 + len(arrays)),
        out_specs=[vm] * len(outs),
        out_shape=outs,
        compiler_params=pltpu.CompilerParams(vmem_limit_bytes=62 * 2**20),
    )(rows_in, *arrays)


SPLITS = (2, 2, 4, 1)


def shards(
    hidden_in,
    cotangent,
    qkv_weight,
    conv_depth,
    conv_point,
    span_weight,
    conv_value,
    dense_attn,
    dense_conv,
    attn_norm_gain,
    attn_norm_bias,
    ffn_inner,
    ffn_outer,
    out_norm_gain,
    out_norm_bias,
):
    attn_width = HEADS * HEAD
    seq_count, local_rows, model_width = hidden_in.shape
    ctx_count = lax.axis_size("ctx")
    members = ctx_count // QUADS
    shard_count = lax.axis_size("shard")
    width_rows = model_width // shard_count
    head_rows = attn_width // shard_count
    forward = [(i, i + 1) for i in range(ctx_count - 1)]
    backward = [(i + 1, i) for i in range(ctx_count - 1)]
    units = ffn_inner.shape[2]
    block_shapes = (
        (width_rows, 3 * attn_width + SMALL), (width_rows, 2 * attn_width + 2 * SMALL),
        (head_rows, 2 * model_width + GROUPS * units), (units // shard_count, model_width),
    )
    by_kernel = members == 2 and all(fits(*one, members, split) for one, split in zip(block_shapes, SPLITS))
    norm_rows_in = jnp.stack([attn_norm_gain, attn_norm_bias, out_norm_gain, out_norm_bias])
    if by_kernel:
        arrays = (
            qkv_weight, conv_value, conv_point, span_weight, conv_depth, norm_rows_in,
            dense_attn, dense_conv, ffn_inner, ffn_outer,
        )
    else:
        small = jnp.concatenate(
            [
                jnp.pad(span_weight, ((0, width_rows - head_rows), (0, 64 - HEADS * KERNEL))),
                conv_depth.T,
                norm_rows_in.T,
                jnp.zeros((width_rows, SMALL - 64 - KERNEL - 4), BF),
            ],
            axis=1,
        )
        by_head = qkv_weight.reshape(width_rows, 3, 2, TRIPLE, HEAD)
        q_block = by_head[:, 0].transpose(0, 2, 1, 3).reshape(width_rows, TRIPLE, 2 * HEAD)
        pair_block = by_head[:, 1:].transpose(0, 3, 2, 1, 4).reshape(width_rows, TRIPLE, 4 * HEAD)
        qkv_block = jnp.concatenate([q_block, pair_block], axis=2).reshape(width_rows, 3 * attn_width)
        qkv_block = jnp.pad(qkv_block, ((0, 0), (0, SMALL)))
        rest_block = jnp.concatenate([conv_value, conv_point, small, jnp.zeros((width_rows, SMALL), BF)], axis=1)
        second_block = jnp.concatenate([dense_attn, dense_conv, ffn_inner[0], ffn_inner[1]], axis=1)
        third_block = jnp.concatenate([ffn_outer[0], ffn_outer[1]], axis=1)
        qkv, rest, second, third = (
            lax.all_gather(one, "shard", axis=0, tiled=True)
            for one in (qkv_block, rest_block, second_block, third_block)
        )
        span = rest[:, 2 * attn_width : 2 * attn_width + SMALL].reshape(shard_count, width_rows, SMALL)
        span = span[:, :head_rows].reshape(attn_width, SMALL)
        arrays = (qkv, rest, span)
    (
        context, kernel_soft, kv_all, q_all, out_all, lse, q_low, spread, key_conv, span_mix, value_ext, conv_low,
        small_turned, low_rim, high_rim, *gathered,
    ) = front(by_kernel, members, shard_count, hidden_in, *arrays)
    if by_kernel:
        qkv, rest, span, second, third = gathered
    layer_out, d_first, d_context, d_conv, dense_part, inner_part, third_part, norm_sums = middle(
        context, conv_low, hidden_in, cotangent, second, third, small_turned, by_kernel, shard_count, members
    )
    grad_rows, low_edge, high_edge, dq_conv, middle_part, d_all, *sums = conv_back(
        by_kernel, shard_count, members,
        hidden_in, low_rim, high_rim, rest, span, small_turned, d_conv, q_low, spread, key_conv, span_mix,
        kernel_soft, value_ext, d_first, norm_sums, d_context, *((third_part, dense_part) if by_kernel else ()),
    )
    grad_in, *results = back(
        by_kernel, shard_count, members,
        d_all, kv_all, q_all, out_all, lse, hidden_in, qkv, dq_conv, grad_rows, low_edge, high_edge,
        *((*sums, inner_part, middle_part) if by_kernel else ()),
    )
    if by_kernel:
        grad_in, g_qkv, g_depth, g_point, g_span, g_value, g_attn, g_conv, norms, g_inner, g_outer = finish_all(
            shard_count, grad_in, *results
        )
    else:
        qkv_sum, dense_sum, inner_sum, third_sum, middle_sum = (
            lax.psum(lax.psum_scatter(one, "shard", scatter_dimension=0, tiled=True), "ctx").astype(F32)
            for one in (results[0], dense_part, inner_part, third_part, middle_part)
        )
        by_head = qkv_sum.reshape(width_rows, TRIPLE, attn_width)
        g_q = by_head[:, :, : 2 * HEAD].reshape(width_rows, TRIPLE, 2, HEAD).transpose(0, 2, 1, 3)
        g_pair = by_head[:, :, 2 * HEAD :].reshape(width_rows, TRIPLE, 2, 2, HEAD).transpose(0, 3, 2, 1, 4)
        g_qkv = jnp.concatenate([g_q.reshape(width_rows, -1), g_pair.reshape(width_rows, -1)], axis=1)
        small_sum = middle_sum[:, 2 * attn_width : 2 * attn_width + SMALL]
        g_depth = small_sum[:, 64 : 64 + KERNEL].T
        norms = small_sum[:, 64 + KERNEL : 68 + KERNEL].T
        g_span = small_sum[:head_rows, : HEADS * KERNEL]
        g_value, g_point = middle_sum[:, :attn_width], middle_sum[:, attn_width : 2 * attn_width]
        g_attn, g_conv = dense_sum[:, :model_width], dense_sum[:, model_width:]
        g_inner = inner_sum.reshape(head_rows, GROUPS, -1).transpose(1, 0, 2)
        g_outer = third_sum.reshape(-1, GROUPS, D // GROUPS).transpose(1, 0, 2)
    return (
        layer_out, grad_in, g_qkv, g_depth, g_point, g_span, g_value, g_attn, g_conv,
        norms[0], norms[1], g_inner, g_outer, norms[2], norms[3],
    )


def solution(mesh):
    return jax.shard_map(
        shards,
        mesh=mesh,
        in_specs=(
            P("shard", "ctx", None),
            P("shard", "ctx", None),
            P("shard", None),
            P(None, "shard"),
            P("shard", None),
            P("shard", None),
            P("shard", None),
            P("shard", None),
            P("shard", None),
            P("shard"),
            P("shard"),
            P(None, "shard", None),
            P(None, "shard", None),
            P("shard"),
            P("shard"),
        ),
        out_specs=(
            P("shard", "ctx", None),
            P("shard", "ctx", None),
            P("shard", None),
            P(None, "shard"),
            P("shard", None),
            P("shard", None),
            P("shard", None),
            P("shard", None),
            P("shard", None),
            P("shard"),
            P("shard"),
            P(None, "shard", None),
            P(None, "shard", None),
            P("shard"),
            P("shard"),
        ),
        check_vma=False,
    )
```

```python
import functools
import math

import jax
import jax.numpy as jnp
from jax import lax
from jax.experimental import pallas as pl
from jax.experimental.pallas import tpu as pltpu
from jax.sharding import PartitionSpec as P

D = 768
HEADS = 6
HEAD = 64
GROUPS = 2
KERNEL = 9


norm_eps = 1e-12


BF = jnp.bfloat16
F32 = jnp.float32
MESH_ID = pl.DeviceIdType.MESH
NT = (((1,), (1,)), ((), ()))
NN = (((1,), (0,)), ((), ()))
EXP2_SCALE = math.log2(math.e) / math.sqrt(HEAD)
TRIPLE = 3
QUADS = 4
CHUNK = 128


def dot(a, b, dims):
    return lax.dot_general(a, b, dims, preferred_element_type=F32)


def swap_halves(packed):
    return jnp.concatenate([packed[:, HEAD:], packed[:, :HEAD]], axis=1)


def low_lanes():
    return lax.broadcasted_iota(jnp.int32, (1, 2 * HEAD), 1) < HEAD


def remote(src, dst, send, recv, target):
    return pltpu.make_async_remote_copy(
        src_ref=src, dst_ref=dst, send_sem=send, recv_sem=recv,
        device_id=target, device_id_type=MESH_ID,
    )


def greet(peers):
    barrier = pltpu.get_barrier_semaphore()
    for peer in peers:
        pl.semaphore_signal(barrier, inc=1, device_id=peer, device_id_type=MESH_ID)
    pl.semaphore_wait(barrier, len(peers))


class Place:
    def __init__(self, members, shards):
        self.members, self.shards = members, shards
        self.me = lax.axis_index("ctx")
        self.z = lax.axis_index("shard")
        self.quad, self.sub = self.me // members, self.me % members

    def peer(self, step):
        return ((self.quad + step) % QUADS * self.members + self.sub, self.z)

    def sibling(self, step):
        return (self.quad * self.members + (self.sub + step) % self.members, self.z)

    def cross(self, step, other):
        return (
            (self.quad + step) % QUADS * self.members + (self.sub + other) % self.members, self.z,
        )

    def behind(self, step):
        return (self.quad + QUADS - step) % QUADS

    def along(self, step):
        return (self.me, (self.z + step) % self.shards)

    def z_behind(self, step):
        return (self.z + self.shards - step) % self.shards

    def greet(self, with_shard, more=()):
        peers = [self.peer(k) for k in range(1, QUADS)]
        peers += [self.sibling(m) for m in range(1, self.members)]
        if with_shard:
            peers += [self.along(d) for d in range(1, self.shards)]
        greet(peers + list(more))


class Pieces:
    def __init__(self, place, rows, columns, col_split):
        count = QUADS * place.members
        self.place, self.rows, self.col_split = place, rows, col_split
        self.piece_rows = rows // (count // col_split)
        self.piece_cols = columns // col_split

    def at(self, ref, z, quad, sub):
        index = quad * self.place.members + sub
        top = pl.multiple_of(z * self.rows + index // self.col_split * self.piece_rows, 16)
        left = pl.multiple_of(index % self.col_split * self.piece_cols, 128)
        return ref.at[pl.ds(top, self.piece_rows), pl.ds(left, self.piece_cols)]


def fits(rows, columns, members, col_split):
    count = QUADS * members
    if count % col_split:
        return False
    row_split = count // col_split
    return rows % (16 * row_split) == 0 and columns % (128 * col_split) == 0


class Gather:
    def __init__(self, place, shard_ref, full_ref, col_split, sems):
        self.place, self.shard_ref, self.full_ref = place, shard_ref, full_ref
        rows, columns = shard_ref.shape
        self.rows = rows
        self.pieces = Pieces(place, rows, columns, col_split)
        self.z_s, self.z_r, self.q_s, self.q_r, self.f_s, self.f_r, self.local = sems

    @staticmethod
    def semaphores(members, shards):
        dma = pltpu.SemaphoreType.DMA
        return [
            dma((shards,)), dma((shards,)), dma((shards, QUADS)), dma((shards, QUADS)),
            dma((shards, QUADS, members)), dma((shards, QUADS, members)), dma((1,)),
        ]

    def z_copy(self, d):
        p = self.place
        return remote(
            self.pieces.at(self.shard_ref, 0, p.quad, p.sub), self.pieces.at(self.full_ref, p.z, p.quad, p.sub),
            self.z_s.at[d], self.z_r.at[d], p.along(d),
        )

    def q_copy(self, d, k):
        p = self.place
        block = self.pieces.at(self.full_ref, p.z_behind(d), p.quad, p.sub)
        return remote(block, block, self.q_s.at[d, k], self.q_r.at[d, k], p.peer(k))

    def f_copy(self, d, k, m):
        p = self.place
        block = self.pieces.at(self.full_ref, p.z_behind(d), p.behind(k), p.sub)
        return remote(block, block, self.f_s.at[d, k, m], self.f_r.at[d, k, m], p.sibling(m))

    def own_copy(self):
        top = pl.multiple_of(self.place.z * self.rows, 16)
        return pltpu.make_async_copy(
            self.shard_ref, self.full_ref.at[pl.ds(top, self.rows), :], self.local.at[0]
        )

    def start(self):
        for d in range(1, self.place.shards):
            self.z_copy(d).start()
        self.own_copy().start()

    def relay(self):
        for d in range(1, self.place.shards):
            self.z_copy(d).wait_recv()
            for k in range(1, QUADS):
                self.q_copy(d, k).start()
            for m in range(1, self.place.members):
                self.f_copy(d, 0, m).start()

    def share(self):
        for d in range(1, self.place.shards):
            for k in range(1, QUADS):
                self.q_copy(d, k).wait_recv()
                for m in range(1, self.place.members):
                    self.f_copy(d, k, m).start()

    def end(self):
        for d in range(1, self.place.shards):
            self.z_copy(d).wait_send()
            for k in range(QUADS):
                if k:
                    self.q_copy(d, k).wait_send()
                for m in range(1, self.place.members):
                    self.f_copy(d, k, m).wait()
        self.own_copy().wait()


class Reduce:
    def __init__(self, place, part, block, out, col_split, head=None, tail=None):
        self.place, self.part, self.block, self.out, self.col_split = place, part, block, out, col_split
        self.straight = out is not None and len(out.shape) == 3
        if head is not None:
            self.half, self.half_in, self.quad_in, self.h_s, self.h_r, self.q_s, self.q_r = head
        if tail is not None:
            self.z_in, self.last, self.z_s, self.z_r, self.a_s, self.a_r, self.f_s, self.f_r, self.local = tail

    @staticmethod
    def head_scratch(members, shards, rows, columns):
        dma = pltpu.SemaphoreType.DMA
        return [
            pltpu.VMEM((shards, QUADS, rows, columns), BF),
            pltpu.VMEM((members - 1, shards, QUADS, rows, columns), BF),
            pltpu.VMEM((QUADS - 1, shards, rows, columns), BF),
            dma((members,)), dma((members,)), dma((QUADS,)), dma((QUADS,)),
        ]

    @staticmethod
    def tail_scratch(members, shards, rows, columns):
        dma = pltpu.SemaphoreType.DMA
        return [
            pltpu.VMEM((shards - 1, rows, columns), BF),
            pltpu.VMEM((rows, columns), BF),
            dma((shards,)), dma((shards,)), dma((QUADS,)), dma((QUADS,)),
            dma((QUADS, members)), dma((QUADS, members)), dma((1,)),
        ]

    def piece(self, quad, sub):
        rows, columns = self.last.shape
        if len(self.out.shape) == 3:
            return self.out.at[sub, pl.ds(pl.multiple_of(quad * rows, 16), rows), :]
        index = quad * self.place.members + sub
        top = pl.multiple_of(index // self.col_split * rows, 16)
        left = pl.multiple_of(index % self.col_split * columns, 128)
        return self.out.at[pl.ds(top, rows), pl.ds(left, columns)]

    def h_copy(self, m):
        p = self.place
        return remote(
            self.part.at[(p.sub + m) % p.members], self.half_in.at[m - 1], self.h_s.at[m], self.h_r.at[m], p.sibling(m)
        )

    def q_copy(self, k):
        p = self.place
        return remote(
            self.half.at[:, (p.quad + k) % QUADS], self.quad_in.at[k - 1], self.q_s.at[k], self.q_r.at[k], p.peer(k)
        )

    def z_copy(self, d):
        p = self.place
        return remote(
            self.block.at[(p.z + d) % p.shards], self.z_in.at[d - 1], self.z_s.at[d], self.z_r.at[d], p.along(d)
        )

    def a_copy(self, k):
        p = self.place
        return remote(self.last, self.piece(p.quad, p.sub), self.a_s.at[k], self.a_r.at[k], p.peer(k))

    def f_copy(self, k, m):
        p = self.place
        block = self.piece(p.behind(k), p.sub)
        return remote(block, block, self.f_s.at[k, m], self.f_r.at[k, m], p.sibling(m))

    def s_copy(self, k, m):
        p = self.place
        return remote(
            self.last, self.piece(p.quad, p.sub), self.f_s.at[k, m], self.f_r.at[k, m], p.cross(k, m)
        )

    def start(self):
        for m in range(1, self.place.members):
            self.h_copy(m).start()

    def to_quads(self):
        for m in range(1, self.place.members):
            self.h_copy(m).wait_recv()

        def turn(i, carry):
            z, q = i // QUADS, i % QUADS
            total = self.part[self.place.sub, z, q].astype(F32)
            for m in range(1, self.place.members):
                total = total + self.half_in[m - 1, z, q].astype(F32)
            self.half[z, q] = total.astype(BF)
            return carry

        lax.fori_loop(0, self.place.shards * QUADS, turn, 0)
        for k in range(1, QUADS):
            self.q_copy(k).start()

    def to_block(self):
        for k in range(1, QUADS):
            self.q_copy(k).wait_recv()

        def turn(z, carry):
            total = self.half[z, self.place.quad].astype(F32)
            for k in range(1, QUADS):
                total = total + self.quad_in[k - 1, z].astype(F32)
            self.block[z] = total.astype(BF)
            return carry

        lax.fori_loop(0, self.place.shards, turn, 0)

    def to_shards(self):
        for d in range(1, self.place.shards):
            self.z_copy(d).start()

    def block_to_shards(self):
        self.to_block()
        self.to_shards()

    def give(self):
        total = self.block[self.place.z].astype(F32)
        for d in range(1, self.place.shards):
            self.z_copy(d).wait_recv()
            total = total + self.z_in[d - 1].astype(F32)
        self.last[...] = total.astype(BF)
        for k in range(1, QUADS):
            self.a_copy(k).start()
            if self.straight:
                for m in range(1, self.place.members):
                    self.s_copy(k, m).start()
        own = pltpu.make_async_copy(self.last, self.piece(self.place.quad, self.place.sub), self.local.at[0])
        own.start()
        own.wait()
        for m in range(1, self.place.members):
            self.f_copy(0, m).start()

    def share(self):
        for k in range(1, QUADS):
            self.a_copy(k).wait_recv()
            if not self.straight:
                for m in range(1, self.place.members):
                    self.f_copy(k, m).start()

    def end_head(self):
        for m in range(1, self.place.members):
            self.h_copy(m).wait_send()
        for k in range(1, QUADS):
            self.q_copy(k).wait_send()

    def end_tail(self):
        for d in range(1, self.place.shards):
            self.z_copy(d).wait_send()
        for k in range(QUADS):
            if k:
                self.a_copy(k).wait_send()
            for m in range(1, self.place.members):
                if k and self.straight:
                    self.s_copy(k, m).wait()
                else:
                    self.f_copy(k, m).wait()


RIM = 16
TILE = 128
SMALL = 128
TN = (((0,), (0,)), ((), ()))


def moved(value, by):
    rows = value.shape[0]
    return value if by % rows == 0 else pltpu.roll(value, (-by) % rows, 0)


def head_columns(tap, wide_first):
    shape = (SMALL, HEADS * HEAD) if wide_first else (HEADS * HEAD, SMALL)
    narrow = lax.broadcasted_iota(jnp.int32, shape, 0 if wide_first else 1)
    wide = lax.broadcasted_iota(jnp.int32, shape, 1 if wide_first else 0)
    if wide_first:
        same = narrow == wide // HEAD * KERNEL + tap
    else:
        same = (narrow * HEAD == (wide * KERNEL + tap * HEAD)) & (wide % HEAD == 0)
    return jnp.where(same, 1.0, 0.0).astype(BF)


def norm_rows(value):
    center = value - jnp.mean(value, axis=-1, keepdims=True)
    inv_std = lax.rsqrt(jnp.mean(center * center, axis=-1, keepdims=True) + norm_eps)
    return center * inv_std, inv_std


def norm_rows_back(normed, inv_std, d_scaled):
    return inv_std * (
        d_scaled
        - jnp.mean(d_scaled, axis=-1, keepdims=True)
        - normed * jnp.mean(d_scaled * normed, axis=-1, keepdims=True)
    )


def fold(value):
    return jnp.sum(value.reshape(value.shape[0] // 8, 8, value.shape[1]), axis=0)


def gelu_both(value):
    size = jnp.abs(value)
    turn = 1.0 / (1.0 + (0.3275911 / math.sqrt(2.0)) * size)
    bell = jnp.exp2(value * value * (-0.5 * math.log2(math.e)))
    poly = ((((1.061405429 * turn - 1.453152027) * turn + 1.421413741) * turn - 0.284496736) * turn + 0.254829592) * turn
    tail = 0.5 * poly * bell
    below = jnp.where(value < 0.0, tail, 1.0 - tail)
    return value * below, below + value * bell * (1.0 / math.sqrt(2.0 * math.pi))


def project_body(hidden, qkv, kv_out, q_packed, q_out):
    seqs, rows, _ = hidden.shape
    half = rows // 2
    width = HEADS * HEAD
    is_low = low_lanes()

    def turn(step, carry):
        s, r = step // (half // TILE), step % (half // TILE)
        tops = (pl.multiple_of(r * TILE, TILE), pl.multiple_of(half + r * TILE, TILE))
        rows_in = jnp.concatenate([hidden[s, pl.ds(top, TILE), :] for top in tops], axis=0)
        mixed = dot(rows_in, qkv[:, : 3 * width], NN).astype(BF)
        blocks = [
            [mixed[part * TILE : part * TILE + TILE, h * width : h * width + 2 * HEAD] for h in range(TRIPLE)]
            for part in range(2)
        ]

        def placed(part, head, low):
            block = blocks[part][head % TRIPLE]
            return block if (head < TRIPLE) == low else swap_halves(block)

        for part, top in enumerate(tops):
            for j in range(HEADS // 2):
                q_out[s, pl.ds(top, TILE), j * 2 * HEAD : j * 2 * HEAD + 2 * HEAD] = jnp.where(
                    is_low, placed(part, 2 * j, True), placed(part, 2 * j + 1, False)
                )
            for h in range(HEADS):
                at = h % TRIPLE * width + 2 * HEAD + h // TRIPLE * 2 * HEAD
                kv_out[s * 2 + h // TRIPLE, h % TRIPLE, pl.ds(top, TILE), :] = mixed[
                    part * TILE : part * TILE + TILE, at : at + 2 * HEAD
                ]
        for h in range(HEADS):
            q_packed[s * 2 + h // TRIPLE, h % TRIPLE, pl.ds(tops[0], TILE), :] = jnp.where(
                is_low, placed(0, h, True), placed(1, h, False)
            )
        return carry

    lax.fori_loop(0, seqs * half // TILE, turn, 0)


def conv_forward_body(
    s, hidden, low_rim, high_rim, rest, q_out, spread_out, key_out, mix_out, soft_out, value_out, conv_out,
    small_turned, span_wide, ext, soft_tile, soft_sem,
):
    seqs, rows, model = hidden.shape
    width = HEADS * HEAD
    tiles = rows // TILE
    depth = small_turned[64 : 64 + 16, :]
    low, high = low_rim[s], high_rim[s]
    ext[0:RIM] = low.astype(F32)
    ext[RIM : RIM + rows] = hidden[s].astype(F32)
    ext[RIM + rows : rows + 2 * RIM] = high.astype(F32)
    value = rest[:, 0:width]
    value_out[s, 0:RIM] = dot(low, value, NN)
    value_out[s, RIM : RIM + rows] = dot(hidden[s], value, NN)
    value_out[s, RIM + rows : rows + 2 * RIM] = dot(high, value, NN)

    def soft_copy(number):
        return pltpu.make_async_copy(soft_tile.at[number % 2], soft_out.at[number], soft_sem.at[number % 2])

    def turn(r, carry):
        number = s * tiles + r
        top = pl.multiple_of(r * TILE, TILE)
        around = ext[pl.ds(top, TILE + 2 * RIM), :]
        spread = jnp.zeros((TILE, model), F32)
        for tap in range(KERNEL):
            spread = spread + moved(around, tap - KERNEL // 2)[RIM : RIM + TILE] * depth[tap : tap + 1]
        spread_low = spread.astype(BF)
        spread_out[s, pl.ds(top, TILE), :] = spread_low
        key_conv = dot(spread_low, rest[:, width : 2 * width], NN)
        key_out[s, pl.ds(top, TILE), :] = key_conv
        mix = (key_conv * q_out[s, pl.ds(top, TILE), :].astype(F32)).astype(BF)
        mix_out[s, pl.ds(top, TILE), :] = mix
        logits = [dot(mix, span_wide[:, tap * width : tap * width + width], NN) for tap in range(KERNEL)]
        peak = functools.reduce(jnp.maximum, logits)
        powers = [jnp.exp(one - peak) for one in logits]
        scale = 1.0 / sum(powers[1:], powers[0])
        values = value_out[s, pl.ds(top, TILE + 2 * RIM), :]

        @pl.when(number > 1)
        def _():
            soft_copy(number - 2).wait()

        result = jnp.zeros((TILE, width), F32)
        for tap in range(KERNEL):
            soft = powers[tap] * scale
            soft_tile[number % 2, tap] = soft.astype(BF)
            result = result + soft * moved(values, tap - KERNEL // 2)[RIM : RIM + TILE]
        conv_out[s, pl.ds(top, TILE), :] = result.astype(BF)
        soft_copy(number).start()
        return carry

    lax.fori_loop(0, tiles, turn, 0)
    if s == seqs - 1:
        soft_copy(seqs * tiles - 2).wait()
        soft_copy(seqs * tiles - 1).wait()


OUTS = 13


def pack_first(qkv_weight, span_weight, conv_depth, norms, qkv_block, rest_block):
    rows = qkv_weight.shape[0]
    width = HEADS * HEAD
    is_low = low_lanes()

    def pair(left, right):
        a, b = (qkv_weight[:, x // 2 * 2 * HEAD : x // 2 * 2 * HEAD + 2 * HEAD] for x in (left, right))
        return jnp.where(is_low, swap_halves(a) if left % 2 else a, b if right % 2 else swap_halves(b))

    for h in range(TRIPLE):
        for j, (left, right) in enumerate(
            ((h, h + TRIPLE), (HEADS + h, 2 * HEADS + h), (HEADS + TRIPLE + h, 2 * HEADS + TRIPLE + h))
        ):
            at = h * width + j * 2 * HEAD
            qkv_block[:, at : at + 2 * HEAD] = pair(left, right)
    qkv_block[:, 3 * width :] = jnp.zeros((rows, SMALL), BF)
    lines = [jnp.zeros((64, rows), F32), conv_depth[...].astype(F32), norms[...].astype(F32)]
    lines += [jnp.zeros((SMALL - 64 - KERNEL - 4, rows), F32)]
    span = span_weight[...].astype(F32)
    span = jnp.concatenate([span, jnp.zeros((span.shape[0], SMALL - span.shape[1]), F32)], axis=1)
    span = jnp.concatenate([span, jnp.zeros((rows - span.shape[0], SMALL), F32)], axis=0)
    rest_block[:, 2 * width : 2 * width + SMALL] = (jnp.concatenate(lines, axis=0).T + span).astype(BF)
    rest_block[:, 2 * width + SMALL :] = jnp.zeros((rows, SMALL), BF)


def front_kernel(by_kernel, members, shards, splits, *refs):
    if by_kernel:
        (
            hidden, qkv_weight, conv_value, conv_point, span_weight, conv_depth, norms,
            dense_attn, dense_conv, ffn_inner, ffn_outer, *refs,
        ) = refs
    else:
        hidden, qkv, rest, span, *refs = refs
    ctx_out, soft_out, *refs = refs
    outs, refs = refs[:OUTS], refs[OUTS:]
    if by_kernel:
        qkv_out, rest_out, span_out, second, third, *refs = refs
    (
        kv_all, q_all, out_all, lse, q_out, spread_out, key_out, mix_out, value_out, conv_out,
        small_turned, low_rim, high_rim,
        kv_in, q_in, out_send, ext, span_wide, soft_tile,
        kv_s, kv_r, q_s, q_r, f_s, f_r, o_s, o_r, e_s, e_r, soft_sem, local, out_sem, *refs,
    ) = refs
    held = (
        kv_all, q_all, out_all, lse, q_out, spread_out, key_out, mix_out, value_out, conv_out,
        small_turned, low_rim, high_rim,
    )
    if by_kernel:
        qkv, rest, span, qkv_block, rest_block, second_block, third_block, load_sem, *sems = refs
        held += (qkv, rest, span)
        outs = (*outs, qkv_out, rest_out, span_out)
        blocks = (qkv_block, rest_block, second_block, third_block)

    def leave(j):
        return pltpu.make_async_copy(held[j], outs[j], out_sem.at[j])

    early = [j for j in range(len(held)) if j not in (0, 1, 2, 3)]
    seqs, rows, model = hidden.shape
    half = rows // 2
    width = HEADS * HEAD
    place = Place(members, shards)
    quad, sub, peer, sibling = place.quad, place.sub, place.peer, place.sibling
    count = QUADS * members
    after = ((place.me + 1) % count, place.z)
    before = ((place.me + count - 1) % count, place.z)
    loads = []
    if by_kernel:
        units = ffn_inner.shape[2]
        group = model // GROUPS
        plan = [(conv_value, rest_block, 0, width), (conv_point, rest_block, width, width)]
        plan += [(dense_attn, second_block, 0, model), (dense_conv, second_block, model, model)]
        for g in range(GROUPS):
            plan += [(ffn_inner.at[g], second_block, 2 * model + g * units, units)]
            plan += [(ffn_outer.at[g], third_block, g * group, group)]
        loads = [
            pltpu.make_async_copy(source, block.at[:, at : at + size], load_sem.at[j])
            for j, (source, block, at, size) in enumerate(plan)
        ]
        for load in loads:
            load.start()
        pack_first(qkv_weight, span_weight, conv_depth, norms, qkv_block, rest_block)
    place.greet(by_kernel, [after, before])
    gathers = []
    if by_kernel:
        gathers = [
            Gather(place, block, full, split, sems[7 * j : 7 * j + 7])
            for j, (block, full, split) in enumerate(zip(blocks, (qkv, rest, second, third), splits))
        ]
        gathers[0].start()
    rims = (
        remote(hidden.at[:, rows - RIM : rows, :], low_rim, e_s.at[0], e_r.at[0], after),
        remote(hidden.at[:, 0:RIM, :], high_rim, e_s.at[1], e_r.at[1], before),
    )
    for rim in rims:
        rim.start()
    for load in loads:
        load.wait()
    if by_kernel:
        gathers[0].relay()
        gathers[1].start()
        gathers[0].share()
        gathers[1].relay()
        gathers[2].start()
        gathers[3].start()
        gathers[0].end()
    project_body(hidden, qkv, kv_in, q_in, q_out)

    def kv_copy(h, k):
        return remote(
            kv_in.at[(quad + k) % QUADS, h], kv_all.at[h, quad, sub], kv_s.at[h, k], kv_r.at[h, k], peer(k)
        )

    def q_copy(h, k):
        return remote(
            q_in.at[(quad + k) % QUADS, h], q_all.at[h, quad], q_s.at[h, k], q_r.at[h, k], peer(k)
        )

    def forward_copy(h, m):
        return remote(
            kv_all.at[h, :, sub], kv_all.at[h, :, sub], f_s.at[h, m], f_r.at[h, m], sibling(m)
        )

    def out_copy(h, i, k):
        return remote(
            out_send.at[h, i], ctx_out.at[quad, h], o_s.at[h, i], o_r.at[h, i], peer(k)
        )

    def receive(h):
        for k in range(1, QUADS):
            kv_copy(h, k).wait_recv()
            q_copy(h, k).wait_recv()
        for m in range(1, members):
            forward_copy(h, m).start()

    own_kv = pltpu.make_async_copy(kv_in.at[quad], kv_all.at[:, quad, sub], local.at[0])
    own_q = pltpu.make_async_copy(q_in.at[quad], q_all.at[:, quad], local.at[1])
    own_kv.start()
    own_q.start()
    for h in range(TRIPLE):
        for k in range(1, QUADS):
            kv_copy(h, k).start()
            q_copy(h, k).start()
    for rim in rims:
        rim.wait()

    @pl.when(place.me == 0)
    def _():
        low_rim[...] = jnp.zeros_like(low_rim)

    @pl.when(place.me == count - 1)
    def _():
        high_rim[...] = jnp.zeros_like(high_rim)

    if by_kernel:
        gathers[1].share()
        gathers[1].end()
        block, head_block = model // shards, width // shards
        for z in range(shards):
            span[z * head_block : z * head_block + head_block] = rest[
                z * block : z * block + head_block, 2 * width : 2 * width + SMALL
            ]
    small_turned[...] = rest[:, 2 * width : 2 * width + SMALL].astype(F32).T
    for tap in range(KERNEL):
        span_wide[:, tap * width : tap * width + width] = dot(span[...], head_columns(tap, True), NN).astype(BF)
    own_kv.wait()
    own_q.wait()
    for s in range(seqs):
        conv_forward_body(
            s, hidden, low_rim, high_rim, rest, q_out, spread_out, key_out, mix_out, soft_out, value_out, conv_out,
            small_turned, span_wide, ext, soft_tile, soft_sem,
        )
        receive(s)
    for j in early:
        leave(j).start()
    is_low = low_lanes()
    tiles = 2 if half % (2 * CHUNK) == 0 else 1

    def block(step, carry):
        h, i = step // QUADS, step % QUADS
        k = (i + 1) % QUADS
        source = (quad + k) % QUADS

        @pl.when(i == 0)
        def _():
            for m in range(1, members):
                forward_copy(h, m).wait_recv()

        keys = kv_all[h].reshape(QUADS * members * rows, 2 * HEAD)

        def rows_turn(r, inner):
            parts = []
            for tile in range(tiles):
                at = pl.multiple_of((r * tiles + tile) * CHUNK, CHUNK)
                packed = q_all[h, source, pl.ds(at, CHUNK), :]
                for part in range(2):
                    q = jnp.where(is_low, packed if part == 0 else swap_halves(packed), jnp.zeros_like(packed))
                    parts.append((tile, part, q))
            outs = []
            following = dot(parts[0][2], keys, NT)
            for number, (tile, part, _) in enumerate(parts):
                scores = following
                if number + 1 < len(parts):
                    following = dot(parts[number + 1][2], keys, NT)
                top = jnp.max(scores, axis=1, keepdims=True)
                probs = jnp.exp2((scores - top) * EXP2_SCALE)
                total = jnp.sum(probs, axis=1, keepdims=True)
                outs.append(dot(probs.astype(BF), keys, NN) / total)
                stat = top * EXP2_SCALE + jnp.log2(total)
                lse[h, source, part, r * tiles + tile] = jnp.broadcast_to(stat, (CHUNK, CHUNK)).T[0:8, :]
                if part == 1:
                    at = pl.multiple_of((r * tiles + tile) * CHUNK, CHUNK)
                    both = jnp.where(is_low, swap_halves(outs[-2]), outs[-1])
                    out_all[h, source, pl.ds(at, CHUNK), :] = both
                    out_send[h, i, pl.ds(at, CHUNK), :] = both.astype(BF)
            return inner

        lax.fori_loop(0, half // (CHUNK * tiles), rows_turn, 0)

        @pl.when(k != 0)
        def _():
            out_copy(h, i, k).start()

        @pl.when(k == 0)
        def _():
            own = pltpu.make_async_copy(out_send.at[h, i], ctx_out.at[quad, h], local.at[0])
            own.start()
            own.wait()

        for j in range(seqs, TRIPLE):

            @pl.when(step == (j - seqs) * QUADS + 2)
            def _(j=j):
                receive(j)

        if by_kernel:

            @pl.when(step == 1)
            def _():
                for gather in gathers[2:]:
                    gather.relay()

            @pl.when(step == TRIPLE * QUADS - 2)
            def _():
                for gather in gathers[2:]:
                    gather.share()

        return carry

    lax.fori_loop(0, TRIPLE * QUADS, block, 0)
    for j in (0, 1, 2, 3):
        leave(j).start()
    for gather in gathers[2:]:
        gather.end()
    for h in range(TRIPLE):
        for k in range(1, QUADS):
            out_copy(h, k - 1, k).wait()
            kv_copy(h, k).wait_send()
            q_copy(h, k).wait_send()
        for m in range(1, members):
            forward_copy(h, m).wait_send()
    for j in range(len(held)):
        leave(j).wait()


def front(by_kernel, members, shards, hidden, *arrays):
    seqs, rows, model = hidden.shape
    half = rows // 2
    width = HEADS * HEAD
    vm = pl.BlockSpec(memory_space=pltpu.VMEM)
    anywhere = pl.BlockSpec(memory_space=pl.ANY)
    dma = pltpu.SemaphoreType.DMA
    shape = jax.ShapeDtypeStruct
    splits = SPLITS if by_kernel else ()
    held = [
        shape((TRIPLE, QUADS, members, rows, 2 * HEAD), BF),
        shape((TRIPLE, QUADS, half, 2 * HEAD), BF),
        shape((TRIPLE, QUADS, half, 2 * HEAD), F32),
        shape((TRIPLE, QUADS, 2, half // CHUNK, 8, CHUNK), F32),
        shape((seqs, rows, width), BF),
        shape((seqs, rows, model), BF),
        shape((seqs, rows, width), F32),
        shape((seqs, rows, width), BF),
        shape((seqs, rows + 2 * RIM, width), F32),
        shape((seqs, rows, width), BF),
        shape((SMALL, model), F32),
        shape((seqs, RIM, model), BF),
        shape((seqs, RIM, model), BF),
    ]
    gathered = []
    scratch = []
    in_specs = [vm] * (1 + len(arrays))
    if by_kernel:
        block, head_block = model // shards, width // shards
        units = arrays[8].shape[2]
        gathered = [
            shape((model, 3 * width + SMALL), BF), shape((model, 2 * width + 2 * SMALL), BF), shape((width, SMALL), BF),
            shape((width, 2 * model + GROUPS * units), BF), shape((units, model), BF),
        ]
        scratch = [pltpu.VMEM(one.shape, BF) for one in gathered[:3]]
        scratch += [
            pltpu.VMEM((block, 3 * width + SMALL), BF),
            pltpu.VMEM((block, 2 * width + 2 * SMALL), BF),
            pltpu.VMEM((head_block, 2 * model + GROUPS * units), BF),
            pltpu.VMEM((units // shards, model), BF),
            dma((4 + 2 * GROUPS,)),
        ]
        in_specs = [vm, vm, anywhere, anywhere, vm, vm, vm, anywhere, anywhere, anywhere, anywhere]
    total = TRIPLE * QUADS * rows * QUADS * members * rows
    result = [
        shape((QUADS, TRIPLE, half, 2 * HEAD), BF),
        shape((seqs * rows // TILE, KERNEL, TILE, width), BF),
        *held,
        *gathered,
    ]
    return pl.pallas_call(
        functools.partial(front_kernel, by_kernel, members, shards, splits),
        in_specs=in_specs,
        out_specs=[anywhere] * len(result),
        out_shape=result,
        scratch_shapes=[pltpu.VMEM(one.shape, one.dtype) for one in held]
        + [
            pltpu.VMEM((QUADS, TRIPLE, rows, 2 * HEAD), BF),
            pltpu.VMEM((QUADS, TRIPLE, half, 2 * HEAD), BF),
            pltpu.VMEM((TRIPLE, QUADS, half, 2 * HEAD), BF),
            pltpu.VMEM((rows + 2 * RIM, model), F32),
            pltpu.VMEM((width, KERNEL * width), BF),
            pltpu.VMEM((2, KERNEL, TILE, width), BF),
            dma((TRIPLE, QUADS)), dma((TRIPLE, QUADS)), dma((TRIPLE, QUADS)), dma((TRIPLE, QUADS)),
            dma((TRIPLE, members)), dma((TRIPLE, members)), dma((TRIPLE, QUADS)), dma((TRIPLE, QUADS)),
            dma((2,)), dma((2,)), dma((2,)), dma((2,)), dma((OUTS + 3,)),
        ]
        + scratch
        + Gather.semaphores(members, shards) * len(splits),
        compiler_params=pltpu.CompilerParams(
            collective_id=1, has_side_effects=True, vmem_limit_bytes=62 * 2**20
        ),
        cost_estimate=pl.CostEstimate(flops=total * 256, bytes_accessed=8 * 2**20, transcendentals=total),
    )(hidden, *arrays)


def middle_kernel(
    by_kernel, shards, members,
    context, conv, hidden, cotangent, second, third, small_turned,
    layer_out, d_first_out, d_context_out, d_conv_out, dense_part, inner_part, third_part, norm_sums,
    context_low, hidden_low, active_all, d_outer_all, d_inner_all, d_dense_all, d_context_all,
):
    seqs, rows, model = hidden.shape
    half = rows // 2
    width = HEADS * HEAD
    group = model // GROUPS
    units = third.shape[0]
    is_low = low_lanes()
    gains = small_turned[64 + KERNEL : 64 + KERNEL + 4, :]
    attn_gain, attn_bias, out_gain, out_bias = (gains[j : j + 1] for j in range(4))
    norm_sums[...] = jnp.zeros_like(norm_sums)

    def turn(step, carry):
        s, p = step // 2, step % 2
        top = pl.multiple_of(p * half, half)
        at = pl.ds(top, half)
        every = pl.ds(pl.multiple_of(step * half, half), half)
        pairs = []
        for j in range(HEADS // 2):
            a = context[s * 2 + 2 * j // TRIPLE, 2 * j % TRIPLE]
            b = context[s * 2 + (2 * j + 1) // TRIPLE, (2 * j + 1) % TRIPLE]
            upper = jnp.where(is_low, a, swap_halves(b))
            lower = jnp.where(is_low, swap_halves(a), b)
            pairs.append(jnp.where(p == 0, upper, lower))
        low = jnp.concatenate(pairs, axis=1)
        context_low[every] = low
        dense = dot(low, second[:, :model], NN) + dot(conv[s, at], second[:, model : 2 * model], NN)
        normed_one, inv_one = norm_rows(dense + hidden[s, at].astype(F32))
        hidden_one = normed_one * attn_gain + attn_bias
        one_low = hidden_one.astype(BF)
        hidden_low[every] = one_low
        slopes = []
        wide = units // 3
        plan = [(g, g * units + j * wide, j * wide) for g in range(GROUPS) for j in range(3)]

        def enter(g, at):
            return dot(one_low[:, g * group : g * group + group], second[:, 2 * model + at : 2 * model + at + wide], NN)

        outers = [jnp.zeros((half, group), F32)] * GROUPS
        following = enter(*plan[0][:2])
        for number, (g, column, row) in enumerate(plan):
            inner = following
            if number + 1 < len(plan):
                following = enter(*plan[number + 1][:2])
            active, slope = gelu_both(inner)
            active = active.astype(BF)
            active_all[every, column : column + wide] = active
            slopes.append(slope)
            outers[g] = outers[g] + dot(active, third[row : row + wide, g * group : g * group + group], NN)
        normed_two, inv_two = norm_rows(jnp.concatenate(outers, axis=1) + hidden_one)
        layer_out[s, at] = (normed_two * out_gain + out_bias).astype(BF)
        d_result = cotangent[s, at].astype(F32)
        norm_sums[2] += fold(d_result * normed_two)
        norm_sums[3] += fold(d_result)
        d_second = norm_rows_back(normed_two, inv_two, d_result * out_gain)
        d_outer = d_second.astype(BF)
        d_outer_all[every] = d_outer
        backs = [jnp.zeros((half, group), F32)] * GROUPS

        def leave(g, row):
            return dot(d_outer[:, g * group : g * group + group], third[row : row + wide, g * group : g * group + group], NT)

        following = leave(plan[0][0], plan[0][2])
        for number, (g, column, row) in enumerate(plan):
            d_active = following
            if number + 1 < len(plan):
                following = leave(plan[number + 1][0], plan[number + 1][2])
            d_inner = (d_active * slopes[number]).astype(BF)
            d_inner_all[every, column : column + wide] = d_inner
            backs[g] = backs[g] + dot(d_inner, second[:, 2 * model + column : 2 * model + column + wide], NT)
        d_hidden = jnp.concatenate(backs, axis=1) + d_second
        norm_sums[0] += fold(d_hidden * normed_one)
        norm_sums[1] += fold(d_hidden)
        d_first = norm_rows_back(normed_one, inv_one, d_hidden * attn_gain)
        d_first_out[s, at] = d_first
        d_dense = d_first.astype(BF)
        d_dense_all[every] = d_dense
        d_context_all[every] = dot(d_dense, second[:, :model], NT).astype(BF)
        d_conv_out[s, at] = dot(d_dense, second[:, model : 2 * model], NT)
        return carry

    lax.fori_loop(0, seqs * 2, turn, 0)
    for s in range(seqs):
        for h in range(HEADS):
            at = h // 2 * 2 * HEAD
            upper = d_context_all[s * rows : s * rows + half, at : at + 2 * HEAD]
            lower = d_context_all[s * rows + half : s * rows + rows, at : at + 2 * HEAD]
            if h % 2:
                packed = jnp.where(is_low, swap_halves(upper), lower)
            else:
                packed = jnp.where(is_low, upper, swap_halves(lower))
            d_context_out[s * 2 + h // TRIPLE, h % TRIPLE] = packed
    for g in range(GROUPS):
        for z in range(shards):
            block = units // shards
            part = dot(
                active_all[:, g * units + z * block : g * units + z * block + block],
                d_outer_all[:, g * group : g * group + group], TN,
            ).astype(BF)
            if by_kernel:
                piece = block // (QUADS * members)
                for q in range(QUADS):
                    for c in range(members):
                        row = (q * members + c) * piece
                        third_part[c, z, q, :, g * group : g * group + group] = part[row : row + piece]
            else:
                third_part[z * block : z * block + block, g * group : g * group + group] = part

    def columns(left, right):
        found = []
        for start, size, rows_in, columns_in in (
            (0, model, context_low[...], d_dense_all),
            (model, model, None, d_dense_all),
            (2 * model, units, hidden_low[:, :group], d_inner_all.at[:, :units]),
            (2 * model + units, units, hidden_low[:, group:], d_inner_all.at[:, units:]),
        ):
            a, b = max(left, start), min(right, start + size)
            if a < b:
                if rows_in is None:
                    rows_in = conv[...].reshape(seqs * rows, width)
                found.append(dot(rows_in, columns_in[:, a - start : b - start], TN).astype(BF))
        return jnp.concatenate(found, axis=1) if len(found) > 1 else found[0]

    for part_out, start, size in ((dense_part, 0, 2 * model), (inner_part, 2 * model, GROUPS * units)):
        wide = size // 4
        for j in range(4):
            part = columns(start + j * wide, start + j * wide + wide)
            if by_kernel:
                block = width // shards
                piece = block // 2
                for z in range(shards):
                    for r in range(2):
                        row = z * block + r * piece
                        part_out[j % members, z, r * 2 + j // members] = part[row : row + piece]
            else:
                part_out[:, j * wide : j * wide + wide] = part


def middle(context, conv, hidden, cotangent, second, third, small_turned, by_kernel, shards, members):
    seqs, rows, model = hidden.shape
    width = HEADS * HEAD
    units = third.shape[0]
    tokens = seqs * rows
    shape = jax.ShapeDtypeStruct
    if by_kernel:
        parts = [
            shape((members, shards, QUADS, width // shards // 2, 2 * model // 4), BF),
            shape((members, shards, QUADS, width // shards // 2, GROUPS * units // 4), BF),
            shape((members, shards, QUADS, units // shards // (QUADS * members), model), BF),
        ]
    else:
        parts = [shape((width, 2 * model), BF), shape((width, GROUPS * units), BF), shape(third.shape, BF)]
    return pl.pallas_call(
        functools.partial(middle_kernel, by_kernel, shards, members),
        out_shape=[
            shape((seqs, rows, model), BF),
            shape((seqs, rows, model), F32),
            shape((QUADS, TRIPLE, rows // 2, 2 * HEAD), BF),
            shape((seqs, rows, width), F32),
            *parts,
            shape((4, 8, model), F32),
        ],
        scratch_shapes=[
            pltpu.VMEM((tokens, width), BF),
            pltpu.VMEM((tokens, model), BF),
            pltpu.VMEM((tokens, GROUPS * units), BF),
            pltpu.VMEM((tokens, model), BF),
            pltpu.VMEM((tokens, GROUPS * units), BF),
            pltpu.VMEM((tokens, model), BF),
            pltpu.VMEM((tokens, width), BF),
        ],
        compiler_params=pltpu.CompilerParams(vmem_limit_bytes=60 * 2**20),
    )(context, conv, hidden, cotangent, second, third, small_turned)


def conv_back_kernel(by_kernel, shards, members, *refs):
    (
        hidden, low_rim, high_rim, rest, span, small_turned, d_conv, q_out, spread, key_conv, mix, soft, value, d_first,
        norm_sums, d_in, *refs,
    ) = refs
    if by_kernel:
        third_part, dense_part, *refs = refs
    grad_rows, low_edge, high_edge, dq_conv, part_out, d_all, *refs = refs
    if by_kernel:
        third_block, dense_block, *refs = refs
    (
        ext, d_value, d_rows, slim_all, d_key_all, depth_sums, ext_low, soft_tile,
        d_s, d_r, soft_sem, local, *scratch,
    ) = refs
    seqs, rows, model = hidden.shape
    width = HEADS * HEAD
    value_at, point_at = 0, width
    tiles = rows // TILE
    place = Place(members, shards)
    quad, peer = place.quad, place.peer
    place.greet(False)

    def d_copy(h, k):
        return remote(
            d_in.at[(quad + k) % QUADS, h], d_all.at[h, quad], d_s.at[h, k], d_r.at[h, k], peer(k)
        )

    def soft_copy(number):
        return pltpu.make_async_copy(soft.at[number], soft_tile.at[number % 2], soft_sem.at[number % 2])

    soft_copy(0).start()
    base = pltpu.make_async_copy(d_first, grad_rows, local.at[0])
    base.start()
    own = pltpu.make_async_copy(d_in.at[quad], d_all.at[:, quad], local.at[1])
    own.start()
    for h in range(TRIPLE):
        for k in range(1, QUADS):
            d_copy(h, k).start()
    if by_kernel:
        third = Reduce(place, third_part, third_block, None, 1, head=scratch[0:7])
        dense = Reduce(place, dense_part, dense_block, None, 4, head=scratch[7:14])
        third.start()
        dense.start()
    is_low = low_lanes()
    depth = small_turned[64 : 64 + 16, :]
    pair = lax.broadcasted_iota(jnp.int32, (4 * HEAD, 2 * HEAD), 0) // HEAD % 2
    same = pair == lax.broadcasted_iota(jnp.int32, (4 * HEAD, 2 * HEAD), 1) // HEAD
    group_sum = jnp.where(same, 1.0, 0.0).astype(BF)
    depth_sums[...] = jnp.zeros_like(depth_sums)
    long = rows + 2 * RIM
    for s in range(seqs):
        ext[0:RIM] = low_rim[s].astype(F32)
        ext[RIM : RIM + rows] = hidden[s].astype(F32)
        ext[RIM + rows : long] = high_rim[s].astype(F32)
        ext_low[s * long : s * long + RIM] = low_rim[s]
        ext_low[s * long + RIM : s * long + RIM + rows] = hidden[s]
        ext_low[s * long + RIM + rows : s * long + long] = high_rim[s]
        d_value[...] = jnp.zeros_like(d_value)
        d_rows[...] = jnp.zeros_like(d_rows)

        def turn(r, carry):
            number = s * tiles + r

            @pl.when(number + 1 < seqs * tiles)
            def _():
                soft_copy(number + 1).start()

            top = pl.multiple_of(r * TILE, TILE)
            here = pl.ds(top, TILE)
            there = pl.ds(top, TILE + 2 * RIM)
            every = pl.ds(pl.multiple_of(s * rows + r * TILE, TILE), TILE)
            d_res = d_conv[s, here, :]
            values = value[s, there, :]
            softs = []
            d_kernels = []
            soft_copy(number).wait()
            rim = jnp.zeros((RIM, width), F32)
            d_values = jnp.zeros((TILE + 2 * RIM, width), F32)
            total = jnp.zeros((TILE, width), F32)
            for tap in range(KERNEL):
                one = soft_tile[number % 2, tap].astype(F32)
                softs.append(one)
                weighted = jnp.concatenate([rim, one * d_res, rim], axis=0)
                d_values = d_values + moved(weighted, KERNEL // 2 - tap)
                product = d_res * moved(values, tap - KERNEL // 2)[RIM : RIM + TILE]
                high = product.astype(BF)
                lower = (product - high.astype(F32)).astype(BF)
                sums = []
                for at in range(0, width, 2 * HEAD):
                    both = jnp.concatenate([high[:, at : at + 2 * HEAD], lower[:, at : at + 2 * HEAD]], axis=1)
                    sums.append(dot(both, group_sum, NN))
                d_kernel = jnp.concatenate(sums, axis=1)
                d_kernels.append(d_kernel)
                total = total + d_kernel * one
            d_value[there, :] += d_values
            slim = jnp.zeros((TILE, SMALL), F32)
            for tap in range(KERNEL):
                d_logits = (softs[tap] * (d_kernels[tap] - total)).astype(BF)
                slim = slim + dot(d_logits, head_columns(tap, False), NN)
            slim = slim.astype(BF)
            slim_all[every] = slim
            d_mix = dot(slim, span[...], NT)
            d_query = d_mix * key_conv[s, here, :]
            for h in range(TRIPLE):
                a, b = (d_query[:, x // 2 * 2 * HEAD : x // 2 * 2 * HEAD + 2 * HEAD] for x in (h, h + TRIPLE))
                a = swap_halves(a) if h % 2 else a
                b = b if (h + TRIPLE) % 2 else swap_halves(b)
                dq_conv[h, s, here, :] = jnp.where(is_low, a, b)
            d_key = (d_mix * q_out[s, here, :].astype(F32)).astype(BF)
            d_key_all[every] = d_key
            d_spread = dot(d_key, rest[:, point_at : point_at + width], NT)
            around = ext[there, :]
            wide_rim = jnp.zeros((RIM, model), F32)
            padded = jnp.concatenate([wide_rim, d_spread, wide_rim], axis=0)
            back = jnp.zeros((TILE + 2 * RIM, model), F32)
            for tap in range(KERNEL):
                depth_sums[tap] += fold(d_spread * moved(around, tap - KERNEL // 2)[RIM : RIM + TILE])
                back = back + moved(padded, KERNEL // 2 - tap) * depth[tap : tap + 1]
            d_rows[there, :] += back
            if by_kernel:

                @pl.when(number == 1)
                def _():
                    third.to_quads()

                @pl.when(number == 2)
                def _():
                    dense.to_quads()

            return carry

        lax.fori_loop(0, tiles, turn, 0)
        if s == 0:
            base.wait()
        value_low = d_value[...].astype(BF)
        value_part = dot(ext_low[s * long : s * long + long], value_low, TN)
        if s == 0:
            grad_value = value_part
        else:
            grad_value = grad_value + value_part
        all_rows = dot(value_low, rest[:, value_at : value_at + width], NT) + d_rows[...]
        grad_rows[s] += all_rows[RIM : RIM + rows]
        low_edge[s] = all_rows[0:RIM].astype(BF)
        high_edge[s] = all_rows[RIM + rows :].astype(BF)

    grad_point = dot(spread[...].reshape(seqs * rows, model), d_key_all[...], TN)
    grad_span = dot(mix[...].reshape(seqs * rows, width), slim_all[...], TN)
    lines = [jnp.zeros((64, model), F32)]
    lines += [jnp.sum(depth_sums[tap], axis=0, keepdims=True) for tap in range(KERNEL)]
    lines += [jnp.sum(norm_sums[j], axis=0, keepdims=True) for j in range(4)]
    lines += [jnp.zeros((SMALL - 64 - KERNEL - 4, model), F32)]
    block, head_block = model // shards, width // shards
    slots = []
    for z in range(shards):
        slots += [grad_span[z * head_block : z * head_block + head_block], jnp.zeros((block - head_block, SMALL), F32)]
    small = jnp.concatenate(lines, axis=0).T + jnp.concatenate(slots, axis=0)
    whole = jnp.concatenate([grad_value, grad_point, small, jnp.zeros((model, SMALL), F32)], axis=1).astype(BF)
    if by_kernel:
        piece = block // QUADS
        wide = whole.shape[1] // members
        for z in range(shards):
            for q in range(QUADS):
                row = z * block + q * piece
                for c in range(members):
                    part_out[c, z, q] = whole[row : row + piece, c * wide : c * wide + wide]
    else:
        part_out[...] = whole
    own.wait()
    for h in range(TRIPLE):
        for k in range(1, QUADS):
            d_copy(h, k).wait()
    if by_kernel:
        for one in (third, dense):
            one.to_block()
            one.end_head()


def conv_back(by_kernel, shards, members, *arrays):
    hidden = arrays[0]
    seqs, rows, model = hidden.shape
    width = HEADS * HEAD
    long = rows + 2 * RIM
    columns = 2 * width + 2 * SMALL
    shape = jax.ShapeDtypeStruct
    if by_kernel:
        part = shape((members, shards, QUADS, model // shards // QUADS, columns // members), BF)
    else:
        part = shape((model, columns), BF)
    vm = pl.BlockSpec(memory_space=pltpu.VMEM)
    anywhere = pl.BlockSpec(memory_space=pl.ANY)
    dma = pltpu.SemaphoreType.DMA
    blocks = [one.shape[1:2] + one.shape[3:] for one in arrays[16:]]
    return pl.pallas_call(
        functools.partial(conv_back_kernel, by_kernel, shards, members),
        in_specs=[vm] * 11 + [anywhere, vm, anywhere, vm, anywhere] + [vm] * len(blocks),
        out_specs=[vm] * (6 + len(blocks)),
        out_shape=[
            shape((seqs, rows, model), F32),
            shape((seqs, RIM, model), BF),
            shape((seqs, RIM, model), BF),
            shape((TRIPLE, seqs, rows, 2 * HEAD), F32),
            part,
            shape((TRIPLE, QUADS, rows // 2, 2 * HEAD), BF),
        ]
        + [shape(one, BF) for one in blocks],
        scratch_shapes=[
            pltpu.VMEM((long, model), F32),
            pltpu.VMEM((long, width), F32),
            pltpu.VMEM((long, model), F32),
            pltpu.VMEM((seqs * rows, SMALL), BF),
            pltpu.VMEM((seqs * rows, width), BF),
            pltpu.VMEM((KERNEL, 8, model), F32),
            pltpu.VMEM((seqs * long, model), BF),
            pltpu.VMEM((2, KERNEL, TILE, width), BF),
            dma((TRIPLE, QUADS)), dma((TRIPLE, QUADS)), dma((2,)), dma((2,)),
        ]
        + sum((Reduce.head_scratch(members, shards, *one[1:]) for one in blocks), []),
        compiler_params=pltpu.CompilerParams(
            collective_id=3, has_side_effects=True, vmem_limit_bytes=60 * 2**20
        ),
    )(*arrays)


UNROLL = 4


def back_kernel(by_kernel, shards, members, *refs):
    d_all, kv_all, q_all, out_all, lse, *late, grad_rows, low_edge, high_edge = refs[:11]
    refs = refs[11:]
    if by_kernel:
        third_block, dense_block, inner_late, middle_late, *refs = refs
        late += [inner_late, middle_late]
        grad_in, third_sum, dense_sum, inner_sum, middle_sum, *refs = refs
        sums, refs = refs[:TRIPLE], refs[TRIPLE:]
    else:
        grad_in, whole, *refs = refs
    (
        q_zero, d_zero, stat, delta, dq_sum, dkv_sum, own_part, sib_send, sib_recv, dkv_send, dq_send,
        dq_out, dkv_out, d_columns, low_in, high_in, hidden, qkv, dq_conv, load_sem,
        p_s, p_r, k_s, k_r, g_s, g_r, e_s, e_r, local, *scratch,
    ) = refs
    rows = kv_all.shape[3]
    half = rows // 2
    seqs, _, model = hidden.shape
    width = HEADS * HEAD
    steps = TRIPLE * QUADS
    place = Place(members, shards)
    quad, sub, peer, sibling = place.quad, place.sub, place.peer, place.sibling
    count = QUADS * members
    after = ((place.me + 1) % count, place.z)
    before = ((place.me + count - 1) % count, place.z)
    more = [place.cross(k, m) for k in range(1, QUADS) for m in range(1, members)] if by_kernel else []
    held = [hidden, qkv, dq_conv]
    if by_kernel:
        inner_part, middle_part, *scratch = scratch
        held += [inner_part, middle_part]
    loads = [pltpu.make_async_copy(late[j], held[j], load_sem.at[j]) for j in range(len(held))]
    for load in loads[3:] + loads[:3]:
        load.start()

    def wait_loads():
        for load in loads[:3]:
            load.wait()

    place.greet(by_kernel, [after, before, *more])
    for load in loads[3:]:
        load.wait()
    is_low = low_lanes()
    third = dense = inner = middle = None
    chunks = []
    if by_kernel:
        third = Reduce(place, None, third_block, third_sum, 1, tail=scratch[0:9])
        dense = Reduce(place, None, dense_block, dense_sum, 4, tail=scratch[9:18])
        inner_block, middle_block, *scratch = scratch[18:]
        inner = Reduce(place, inner_part, inner_block, inner_sum, 4, head=scratch[0:7], tail=scratch[7:16])
        middle = Reduce(place, middle_part, middle_block, middle_sum, 2, head=scratch[16:23], tail=scratch[23:32])
        scratch = scratch[32:]
        for h in range(TRIPLE):
            part, block, *scratch = scratch
            chunks.append(Reduce(place, part, block, sums[h], 1, head=scratch[0:7], tail=scratch[7:16]))
            scratch = scratch[16:]
    edges = (
        remote(high_edge, low_in, e_s.at[0], e_r.at[0], after),
        remote(low_edge, high_in, e_s.at[1], e_r.at[1], before),
    )
    for edge in edges:
        edge.start()
    if by_kernel:
        third.to_shards()
        dense.to_shards()
        inner.start()
        middle.start()
    base = pltpu.make_async_copy(grad_rows, grad_in, local.at[1])
    base.start()
    base.wait()

    def part_copy(step, m):
        return remote(
            sib_send.at[step % 2, m - 1], sib_recv.at[step, m - 1], p_s.at[step, m], p_r.at[step, m], sibling(m)
        )

    def dkv_copy(h, i, k):
        return remote(
            dkv_send.at[h, i], dkv_out.at[quad, h], k_s.at[h, i], k_r.at[h, i], peer(k)
        )

    def dq_copy(h, k):
        return remote(
            dq_send.at[h, (quad + k) % QUADS], dq_out.at[quad, h], g_s.at[h, k], g_r.at[h, k], peer(k)
        )

    def finish(step):
        h, i = step // QUADS, step % QUADS
        k = (i + 1) % QUADS
        total = own_part[step % 2]
        for m in range(1, members):
            part_copy(step, m).wait_recv()
            total = total + sib_recv[step, m - 1].astype(F32)
        dkv_send[h, i] = total.astype(BF)

        @pl.when(k != 0)
        def _():
            dkv_copy(h, i, k).start()

        @pl.when(k == 0)
        def _():
            own = pltpu.make_async_copy(dkv_send.at[h, i], dkv_out.at[quad, h], local.at[0])
            own.start()
            own.wait()

    def columns_of(h):
        for k in range(1, QUADS):
            dkv_copy(h, k - 1, k).wait_recv()
            dq_copy(h, k).wait_recv()
        for s in range(seqs):
            a = dq_out[s * 2, h].astype(F32)
            b = dq_out[s * 2 + 1, h].astype(F32)
            top = s * rows
            upper = jnp.where(is_low, a, swap_halves(b)) + dq_conv[h, s, 0:half, :]
            lower = jnp.where(is_low, swap_halves(a), b) + dq_conv[h, s, half:rows, :]
            d_columns[top : top + half, 0 : 2 * HEAD] = upper.astype(BF)
            d_columns[top + half : top + rows, 0 : 2 * HEAD] = lower.astype(BF)
            d_columns[top : top + rows, 2 * HEAD : 4 * HEAD] = dkv_out[s * 2, h]
            d_columns[top : top + rows, 4 * HEAD : 6 * HEAD] = dkv_out[s * 2 + 1, h]
        value = dot(hidden[...].reshape(seqs * rows, model), d_columns[...], TN).astype(BF)
        if by_kernel:
            part = chunks[h].part
            block = model // shards
            piece = block // QUADS
            wide = part.shape[4]
            for z in range(shards):
                for q in range(QUADS):
                    row = z * block + q * piece
                    for c in range(members):
                        part[c, z, q] = value[row : row + piece, c * wide : c * wide + wide]
            chunks[h].start()
        else:
            whole[:, h * width : h * width + width] = value

    def rows_of(h):
        for s in range(seqs):
            grad_in[s] += dot(d_columns[s * rows : s * rows + rows, :], qkv[:, h * width : h * width + width], NT)

    def block(step, carry):
        h, i = step // QUADS, step % QUADS
        k = (i + 1) % QUADS
        source = (quad + k) % QUADS

        @pl.when(i == 0)
        def _():
            def prepare(b, inner):
                q = q_all[h, b]
                d = d_all[h, b]
                zero = jnp.zeros_like(q)
                q_zero[b, 0:half] = jnp.where(is_low, q, zero)
                q_zero[b, half:rows] = jnp.where(is_low, swap_halves(q), zero)
                d_zero[b, 0:half] = jnp.where(is_low, zero, swap_halves(d))
                d_zero[b, half:rows] = jnp.where(is_low, zero, d)
                both = (out_all[h, b] * d.astype(F32)).T
                delta[b, :, 0:half] = jnp.broadcast_to(jnp.sum(both[0:HEAD], axis=0, keepdims=True), (8, half))
                delta[b, :, half:rows] = jnp.broadcast_to(jnp.sum(both[HEAD:], axis=0, keepdims=True), (8, half))
                for part in range(2):
                    for r in range(half // CHUNK):
                        at = part * half + r * CHUNK
                        stat[b, :, at : at + CHUNK] = lse[h, b, part, r]
                dq_sum[b] = jnp.zeros((HEAD, rows), F32)
                return inner

            lax.fori_loop(0, QUADS, prepare, 0)

        keys = kv_all[h, source].reshape(members * rows, 2 * HEAD)
        keys_turned = keys.T[0:HEAD]
        dkv_sum[...] = jnp.zeros_like(dkv_sum)

        def queries_turn(turn, inner):
            def products(b):
                return dot(keys, q_zero[b], NT), dot(keys, d_zero[b], NT)

            following = products(turn * UNROLL)
            for number in range(UNROLL):
                b = turn * UNROLL + number
                scores, d_probs = following
                if number + 1 < UNROLL:
                    following = products(b + 1)
                probs = jnp.exp2(scores * EXP2_SCALE - stat[b, 0:1, :])
                d_scores = (probs * (d_probs - delta[b, 0:1, :])).astype(BF)
                both = jnp.concatenate([probs.astype(BF), d_scores], axis=1)
                dkv_sum[...] += dot(both, jnp.concatenate([d_zero[b], q_zero[b]], axis=0), NN)
                dq_sum[b] += dot(keys_turned, d_scores, NN)
            return inner

        lax.fori_loop(0, QUADS // UNROLL, queries_turn, 0)

        @pl.when(step > 0)
        def _():
            finish(step - 1)

        scale = jnp.where(is_low, 1.0 / math.sqrt(HEAD), 1.0)
        own_part[step % 2] = dkv_sum[pl.ds(pl.multiple_of(sub * rows, rows), rows), :] * scale
        for m in range(1, members):

            @pl.when(step > 1)
            def _():
                part_copy(step - 2, m).wait_send()

            target = (sub + m) % members
            theirs = dkv_sum[pl.ds(pl.multiple_of(target * rows, rows), rows), :] * scale
            sib_send[step % 2, m - 1] = theirs.astype(BF)
            part_copy(step, m).start()

        @pl.when(i == QUADS - 1)
        def _():
            def give(b, inner):
                turned = dq_sum[b] * (1.0 / math.sqrt(HEAD))
                dq_send[h, b] = jnp.concatenate([turned[:, 0:half], turned[:, half:rows]], axis=0).T.astype(BF)
                return inner

            lax.fori_loop(0, QUADS, give, 0)
            for j in range(1, QUADS):
                dq_copy(h, j).start()
            mine = pltpu.make_async_copy(dq_send.at[h, quad], dq_out.at[quad, h], local.at[0])
            mine.start()
            mine.wait()

        plan = [(5, wait_loads), (5, lambda: columns_of(0)), (5, lambda: rows_of(0)), (9, lambda: columns_of(1)), (9, lambda: rows_of(1))]
        if by_kernel:
            plan += [
                (0, inner.to_quads), (1, middle.to_quads),
                (2, third.give), (2, dense.give), (4, third.share), (4, dense.share),
                (4, inner.block_to_shards), (6, inner.give), (8, inner.share),
                (5, middle.block_to_shards), (7, middle.give), (9, middle.share),
                (6, chunks[0].to_quads), (8, chunks[0].block_to_shards), (9, chunks[0].give), (10, chunks[0].share),
                (10, chunks[1].to_quads), (11, chunks[1].block_to_shards),
            ]
        for at in range(steps):
            stages = [stage for when, stage in plan if when == at]
            if stages:

                @pl.when(step == at)
                def _(stages=stages):
                    for stage in stages:
                        stage()

        return carry

    lax.fori_loop(0, steps, block, 0)
    finish(steps - 1)
    columns_of(TRIPLE - 1)
    if by_kernel:
        chunks[1].give()
        chunks[2].to_quads()
    rows_of(TRIPLE - 1)
    for edge in edges:
        edge.wait()

    @pl.when(place.me > 0)
    def _():
        grad_in[:, 0:RIM, :] += low_in[...].astype(F32)

    @pl.when(place.me < count - 1)
    def _():
        grad_in[:, rows - RIM : rows, :] += high_in[...].astype(F32)

    if by_kernel:
        chunks[1].share()
        third.end_tail()
        dense.end_tail()
        inner.end_tail()
        middle.end_tail()
        inner.end_head()
        middle.end_head()
        chunks[2].block_to_shards()
        chunks[2].give()
        chunks[2].share()
        for h in range(TRIPLE):
            chunks[h].end_head()
            chunks[h].end_tail()
    for m in range(1, members):
        part_copy(steps - 2, m).wait_send()
        part_copy(steps - 1, m).wait_send()
    for h in range(TRIPLE):
        for k in range(1, QUADS):
            dkv_copy(h, k - 1, k).wait_send()
            dq_copy(h, k).wait_send()


def back(by_kernel, shards, members, *arrays):
    kv_all, hidden = arrays[1], arrays[5]
    rows = kv_all.shape[3]
    half = rows // 2
    seqs, _, model = hidden.shape
    width = HEADS * HEAD
    units = 2 * model
    steps = TRIPLE * QUADS
    vm = pl.BlockSpec(memory_space=pltpu.VMEM)
    anywhere = pl.BlockSpec(memory_space=pl.ANY)
    dma = pltpu.SemaphoreType.DMA
    shape = jax.ShapeDtypeStruct
    outs = [shape((seqs, rows, model), F32)]
    reducing = []
    if by_kernel:
        block, head_block = model // shards, width // shards
        outs += [
            shape((units // shards, model), BF),
            shape((head_block, 2 * model), BF),
            shape((head_block, GROUPS * units), BF),
            shape((block, 2 * width + 2 * SMALL), BF),
        ]
        outs += [shape((members, block, width // members), BF)] * TRIPLE
        third, dense, inner, middle = (one.shape[-2:] for one in arrays[11:])
        chunk = (block // QUADS, width // members)
        reducing = [
            pltpu.VMEM(arrays[13].shape, BF),
            pltpu.VMEM(arrays[14].shape, BF),
            *Reduce.tail_scratch(members, shards, *third),
            *Reduce.tail_scratch(members, shards, *dense),
            pltpu.VMEM((shards, *inner), BF),
            pltpu.VMEM((shards, *middle), BF),
            *Reduce.head_scratch(members, shards, *inner),
            *Reduce.tail_scratch(members, shards, *inner),
            *Reduce.head_scratch(members, shards, *middle),
            *Reduce.tail_scratch(members, shards, *middle),
        ]
        for _ in range(TRIPLE):
            reducing += [
                pltpu.VMEM((members, shards, QUADS, *chunk), BF),
                pltpu.VMEM((shards, *chunk), BF),
                *Reduce.head_scratch(members, shards, *chunk),
                *Reduce.tail_scratch(members, shards, *chunk),
            ]
    else:
        outs += [shape((model, 3 * width), BF)]
    total = TRIPLE * QUADS * rows * QUADS * members * rows
    return pl.pallas_call(
        functools.partial(back_kernel, by_kernel, shards, members),
        in_specs=[vm] * 5 + [anywhere] * 4 + [vm, vm] + ([vm, vm, anywhere, anywhere] if by_kernel else []),
        out_specs=[vm] * len(outs),
        out_shape=outs,
        scratch_shapes=[
            pltpu.VMEM((QUADS, rows, 2 * HEAD), BF),
            pltpu.VMEM((QUADS, rows, 2 * HEAD), BF),
            pltpu.VMEM((QUADS, 8, rows), F32),
            pltpu.VMEM((QUADS, 8, rows), F32),
            pltpu.VMEM((QUADS, HEAD, rows), F32),
            pltpu.VMEM((members * rows, 2 * HEAD), F32),
            pltpu.VMEM((2, rows, 2 * HEAD), F32),
            pltpu.VMEM((2, members - 1, rows, 2 * HEAD), BF),
            pltpu.VMEM((steps, members - 1, rows, 2 * HEAD), BF),
            pltpu.VMEM((TRIPLE, QUADS, rows, 2 * HEAD), BF),
            pltpu.VMEM((TRIPLE, QUADS, half, 2 * HEAD), BF),
            pltpu.VMEM((QUADS, TRIPLE, half, 2 * HEAD), BF),
            pltpu.VMEM((QUADS, TRIPLE, rows, 2 * HEAD), BF),
            pltpu.VMEM((seqs * rows, width), BF),
            pltpu.VMEM((seqs, RIM, model), BF),
            pltpu.VMEM((seqs, RIM, model), BF),
            *[pltpu.VMEM(one.shape, one.dtype) for one in arrays[5:8]],
            dma((5,)),
            dma((steps, members)), dma((steps, members)),
            dma((TRIPLE, QUADS)), dma((TRIPLE, QUADS)), dma((TRIPLE, QUADS)), dma((TRIPLE, QUADS)),
            dma((2,)), dma((2,)), dma((2,)),
        ]
        + reducing,
        compiler_params=pltpu.CompilerParams(
            collective_id=2, has_side_effects=True, vmem_limit_bytes=62 * 2**20
        ),
        cost_estimate=pl.CostEstimate(flops=total * 640, bytes_accessed=8 * 2**20, transcendentals=total),
    )(*arrays)


def finish_kernel(rows_in, third_sum, dense_sum, inner_sum, middle_sum, *refs):
    sums, refs = refs[:TRIPLE], refs[TRIPLE:]
    rows_out, g_qkv, g_depth, g_point, g_span, g_value, g_attn, g_conv, g_norms, g_inner, g_outer = refs
    rows_out[...] = rows_in[...]
    width = HEADS * HEAD
    model = third_sum.shape[1]
    group, units = model // GROUPS, g_inner.shape[2]
    for g in range(GROUPS):
        g_outer[g] = third_sum[:, g * group : g * group + group].astype(F32)
        g_inner[g] = inner_sum[:, g * units : g * units + units].astype(F32)
    g_attn[...] = dense_sum[:, :model].astype(F32)
    g_conv[...] = dense_sum[:, model:].astype(F32)
    g_value[...] = middle_sum[:, :width].astype(F32)
    g_point[...] = middle_sum[:, width : 2 * width].astype(F32)
    small = middle_sum[:, 2 * width : 2 * width + SMALL].astype(F32)
    g_span[...] = small[: g_span.shape[0], : HEADS * KERNEL]
    turned = small.T
    g_depth[...] = turned[64 : 64 + KERNEL]
    g_norms[...] = turned[64 + KERNEL : 68 + KERNEL]
    found = {}
    for h in range(TRIPLE):
        both = jnp.concatenate([sums[h][c].astype(F32) for c in range(sums[h].shape[0])], axis=1)
        for t in range(2):
            head = TRIPLE * t + h
            found[head] = both[:, t * HEAD : t * HEAD + HEAD]
            at = 2 * HEAD + t * 2 * HEAD
            found[HEADS + head] = both[:, at : at + HEAD]
            found[2 * HEADS + head] = both[:, at + HEAD : at + 2 * HEAD]
    for j in range(3 * HEADS // 2):
        g_qkv[:, j * 2 * HEAD : j * 2 * HEAD + 2 * HEAD] = jnp.concatenate([found[2 * j], found[2 * j + 1]], axis=1)


def finish_all(shards, rows_in, *arrays):
    vm = pl.BlockSpec(memory_space=pltpu.VMEM)
    width, model = HEADS * HEAD, rows_in.shape[2]
    units = 2 * model
    block, head_block = model // shards, width // shards
    shape = jax.ShapeDtypeStruct
    outs = [
        shape(rows_in.shape, F32),
        shape((block, 3 * width), F32),
        shape((KERNEL, block), F32),
        shape((block, width), F32),
        shape((head_block, HEADS * KERNEL), F32),
        shape((block, width), F32),
        shape((head_block, model), F32),
        shape((head_block, model), F32),
        shape((4, block), F32),
        shape((GROUPS, head_block, units), F32),
        shape((GROUPS, units // shards, model // GROUPS), F32),
    ]
    return pl.pallas_call(
        finish_kernel,
        in_specs=[vm] * (1 + len(arrays)),
        out_specs=[vm] * len(outs),
        out_shape=outs,
        compiler_params=pltpu.CompilerParams(vmem_limit_bytes=62 * 2**20),
    )(rows_in, *arrays)


SPLITS = (2, 2, 4, 1)


def shards(
    hidden_in,
    cotangent,
    qkv_weight,
    conv_depth,
    conv_point,
    span_weight,
    conv_value,
    dense_attn,
    dense_conv,
    attn_norm_gain,
    attn_norm_bias,
    ffn_inner,
    ffn_outer,
    out_norm_gain,
    out_norm_bias,
):
    attn_width = HEADS * HEAD
    seq_count, local_rows, model_width = hidden_in.shape
    ctx_count = lax.axis_size("ctx")
    members = ctx_count // QUADS
    shard_count = lax.axis_size("shard")
    width_rows = model_width // shard_count
    head_rows = attn_width // shard_count
    forward = [(i, i + 1) for i in range(ctx_count - 1)]
    backward = [(i + 1, i) for i in range(ctx_count - 1)]
    units = ffn_inner.shape[2]
    block_shapes = (
        (width_rows, 3 * attn_width + SMALL), (width_rows, 2 * attn_width + 2 * SMALL),
        (head_rows, 2 * model_width + GROUPS * units), (units // shard_count, model_width),
    )
    by_kernel = members == 2 and all(fits(*one, members, split) for one, split in zip(block_shapes, SPLITS))
    norm_rows_in = jnp.stack([attn_norm_gain, attn_norm_bias, out_norm_gain, out_norm_bias])
    if by_kernel:
        arrays = (
            qkv_weight, conv_value, conv_point, span_weight, conv_depth, norm_rows_in,
            dense_attn, dense_conv, ffn_inner, ffn_outer,
        )
    else:
        small = jnp.concatenate(
            [
                jnp.pad(span_weight, ((0, width_rows - head_rows), (0, 64 - HEADS * KERNEL))),
                conv_depth.T,
                norm_rows_in.T,
                jnp.zeros((width_rows, SMALL - 64 - KERNEL - 4), BF),
            ],
            axis=1,
        )
        by_head = qkv_weight.reshape(width_rows, 3, 2, TRIPLE, HEAD)
        q_block = by_head[:, 0].transpose(0, 2, 1, 3).reshape(width_rows, TRIPLE, 2 * HEAD)
        pair_block = by_head[:, 1:].transpose(0, 3, 2, 1, 4).reshape(width_rows, TRIPLE, 4 * HEAD)
        qkv_block = jnp.concatenate([q_block, pair_block], axis=2).reshape(width_rows, 3 * attn_width)
        qkv_block = jnp.pad(qkv_block, ((0, 0), (0, SMALL)))
        rest_block = jnp.concatenate([conv_value, conv_point, small, jnp.zeros((width_rows, SMALL), BF)], axis=1)
        second_block = jnp.concatenate([dense_attn, dense_conv, ffn_inner[0], ffn_inner[1]], axis=1)
        third_block = jnp.concatenate([ffn_outer[0], ffn_outer[1]], axis=1)
        qkv, rest, second, third = (
            lax.all_gather(one, "shard", axis=0, tiled=True)
            for one in (qkv_block, rest_block, second_block, third_block)
        )
        span = rest[:, 2 * attn_width : 2 * attn_width + SMALL].reshape(shard_count, width_rows, SMALL)
        span = span[:, :head_rows].reshape(attn_width, SMALL)
        arrays = (qkv, rest, span)
    (
        context, kernel_soft, kv_all, q_all, out_all, lse, q_low, spread, key_conv, span_mix, value_ext, conv_low,
        small_turned, low_rim, high_rim, *gathered,
    ) = front(by_kernel, members, shard_count, hidden_in, *arrays)
    if by_kernel:
        qkv, rest, span, second, third = gathered
    layer_out, d_first, d_context, d_conv, dense_part, inner_part, third_part, norm_sums = middle(
        context, conv_low, hidden_in, cotangent, second, third, small_turned, by_kernel, shard_count, members
    )
    grad_rows, low_edge, high_edge, dq_conv, middle_part, d_all, *sums = conv_back(
        by_kernel, shard_count, members,
        hidden_in, low_rim, high_rim, rest, span, small_turned, d_conv, q_low, spread, key_conv, span_mix,
        kernel_soft, value_ext, d_first, norm_sums, d_context, *((third_part, dense_part) if by_kernel else ()),
    )
    grad_in, *results = back(
        by_kernel, shard_count, members,
        d_all, kv_all, q_all, out_all, lse, hidden_in, qkv, dq_conv, grad_rows, low_edge, high_edge,
        *((*sums, inner_part, middle_part) if by_kernel else ()),
    )
    if by_kernel:
        grad_in, g_qkv, g_depth, g_point, g_span, g_value, g_attn, g_conv, norms, g_inner, g_outer = finish_all(
            shard_count, grad_in, *results
        )
    else:
        qkv_sum, dense_sum, inner_sum, third_sum, middle_sum = (
            lax.psum(lax.psum_scatter(one, "shard", scatter_dimension=0, tiled=True), "ctx").astype(F32)
            for one in (results[0], dense_part, inner_part, third_part, middle_part)
        )
        by_head = qkv_sum.reshape(width_rows, TRIPLE, attn_width)
        g_q = by_head[:, :, : 2 * HEAD].reshape(width_rows, TRIPLE, 2, HEAD).transpose(0, 2, 1, 3)
        g_pair = by_head[:, :, 2 * HEAD :].reshape(width_rows, TRIPLE, 2, 2, HEAD).transpose(0, 3, 2, 1, 4)
        g_qkv = jnp.concatenate([g_q.reshape(width_rows, -1), g_pair.reshape(width_rows, -1)], axis=1)
        small_sum = middle_sum[:, 2 * attn_width : 2 * attn_width + SMALL]
        g_depth = small_sum[:, 64 : 64 + KERNEL].T
        norms = small_sum[:, 64 + KERNEL : 68 + KERNEL].T
        g_span = small_sum[:head_rows, : HEADS * KERNEL]
        g_value, g_point = middle_sum[:, :attn_width], middle_sum[:, attn_width : 2 * attn_width]
        g_attn, g_conv = dense_sum[:, :model_width], dense_sum[:, model_width:]
        g_inner = inner_sum.reshape(head_rows, GROUPS, -1).transpose(1, 0, 2)
        g_outer = third_sum.reshape(-1, GROUPS, D // GROUPS).transpose(1, 0, 2)
    return (
        layer_out, grad_in, g_qkv, g_depth, g_point, g_span, g_value, g_attn, g_conv,
        norms[0], norms[1], g_inner, g_outer, norms[2], norms[3],
    )


def solution(mesh):
    return jax.shard_map(
        shards,
        mesh=mesh,
        in_specs=(
            P("shard", "ctx", None),
            P("shard", "ctx", None),
            P("shard", None),
            P(None, "shard"),
            P("shard", None),
            P("shard", None),
            P("shard", None),
            P("shard", None),
            P("shard", None),
            P("shard"),
            P("shard"),
            P(None, "shard", None),
            P(None, "shard", None),
            P("shard"),
            P("shard"),
        ),
        out_specs=(
            P("shard", "ctx", None),
            P("shard", "ctx", None),
            P("shard", None),
            P(None, "shard"),
            P("shard", None),
            P("shard", None),
            P("shard", None),
            P("shard", None),
            P("shard", None),
            P("shard"),
            P("shard"),
            P(None, "shard", None),
            P(None, "shard", None),
            P("shard"),
            P("shard"),
        ),
        check_vma=False,
    )
```

```python
import functools
import math

import jax
import jax.numpy as jnp
from jax import lax
from jax.experimental import pallas as pl
from jax.experimental.pallas import tpu as pltpu
from jax.sharding import PartitionSpec as P

D = 768
HEADS = 6
HEAD = 64
GROUPS = 2
KERNEL = 9


norm_eps = 1e-12


BF = jnp.bfloat16
F32 = jnp.float32
MESH_ID = pl.DeviceIdType.MESH
NT = (((1,), (1,)), ((), ()))
NN = (((1,), (0,)), ((), ()))
EXP2_SCALE = math.log2(math.e) / math.sqrt(HEAD)
TRIPLE = 3
QUADS = 4
CHUNK = 128


def dot(a, b, dims):
    return lax.dot_general(a, b, dims, preferred_element_type=F32)


def swap_halves(packed):
    return jnp.concatenate([packed[:, HEAD:], packed[:, :HEAD]], axis=1)


def low_lanes():
    return lax.broadcasted_iota(jnp.int32, (1, 2 * HEAD), 1) < HEAD


def remote(src, dst, send, recv, target):
    return pltpu.make_async_remote_copy(
        src_ref=src, dst_ref=dst, send_sem=send, recv_sem=recv,
        device_id=target, device_id_type=MESH_ID,
    )


def greet(peers):
    barrier = pltpu.get_barrier_semaphore()
    for peer in peers:
        pl.semaphore_signal(barrier, inc=1, device_id=peer, device_id_type=MESH_ID)
    pl.semaphore_wait(barrier, len(peers))


class Place:
    def __init__(self, members, shards):
        self.members, self.shards = members, shards
        self.me = lax.axis_index("ctx")
        self.z = lax.axis_index("shard")
        self.quad, self.sub = self.me // members, self.me % members

    def peer(self, step):
        return ((self.quad + step) % QUADS * self.members + self.sub, self.z)

    def sibling(self, step):
        return (self.quad * self.members + (self.sub + step) % self.members, self.z)

    def cross(self, step, other):
        return (
            (self.quad + step) % QUADS * self.members + (self.sub + other) % self.members, self.z,
        )

    def behind(self, step):
        return (self.quad + QUADS - step) % QUADS

    def along(self, step):
        return (self.me, (self.z + step) % self.shards)

    def z_behind(self, step):
        return (self.z + self.shards - step) % self.shards

    def greet(self, with_shard, more=()):
        peers = [self.peer(k) for k in range(1, QUADS)]
        peers += [self.sibling(m) for m in range(1, self.members)]
        if with_shard:
            peers += [self.along(d) for d in range(1, self.shards)]
        greet(peers + list(more))


class Pieces:
    def __init__(self, place, rows, columns, col_split):
        count = QUADS * place.members
        self.place, self.rows, self.col_split = place, rows, col_split
        self.piece_rows = rows // (count // col_split)
        self.piece_cols = columns // col_split

    def at(self, ref, z, quad, sub):
        index = quad * self.place.members + sub
        top = pl.multiple_of(z * self.rows + index // self.col_split * self.piece_rows, 16)
        left = pl.multiple_of(index % self.col_split * self.piece_cols, 128)
        return ref.at[pl.ds(top, self.piece_rows), pl.ds(left, self.piece_cols)]


def fits(rows, columns, members, col_split):
    count = QUADS * members
    if count % col_split:
        return False
    row_split = count // col_split
    return rows % (16 * row_split) == 0 and columns % (128 * col_split) == 0


class Gather:
    def __init__(self, place, shard_ref, full_ref, col_split, sems):
        self.place, self.shard_ref, self.full_ref = place, shard_ref, full_ref
        rows, columns = shard_ref.shape
        self.rows = rows
        self.pieces = Pieces(place, rows, columns, col_split)
        self.z_s, self.z_r, self.q_s, self.q_r, self.f_s, self.f_r, self.local = sems

    @staticmethod
    def semaphores(members, shards):
        dma = pltpu.SemaphoreType.DMA
        return [
            dma((shards,)), dma((shards,)), dma((shards, QUADS)), dma((shards, QUADS)),
            dma((shards, QUADS, members)), dma((shards, QUADS, members)), dma((1,)),
        ]

    def z_copy(self, d):
        p = self.place
        return remote(
            self.pieces.at(self.shard_ref, 0, p.quad, p.sub), self.pieces.at(self.full_ref, p.z, p.quad, p.sub),
            self.z_s.at[d], self.z_r.at[d], p.along(d),
        )

    def q_copy(self, d, k):
        p = self.place
        block = self.pieces.at(self.full_ref, p.z_behind(d), p.quad, p.sub)
        return remote(block, block, self.q_s.at[d, k], self.q_r.at[d, k], p.peer(k))

    def f_copy(self, d, k, m):
        p = self.place
        block = self.pieces.at(self.full_ref, p.z_behind(d), p.behind(k), p.sub)
        return remote(block, block, self.f_s.at[d, k, m], self.f_r.at[d, k, m], p.sibling(m))

    def own_copy(self):
        top = pl.multiple_of(self.place.z * self.rows, 16)
        return pltpu.make_async_copy(
            self.shard_ref, self.full_ref.at[pl.ds(top, self.rows), :], self.local.at[0]
        )

    def start(self):
        for d in range(1, self.place.shards):
            self.z_copy(d).start()
        self.own_copy().start()

    def relay(self):
        for d in range(1, self.place.shards):
            self.z_copy(d).wait_recv()
            for k in range(1, QUADS):
                self.q_copy(d, k).start()
            for m in range(1, self.place.members):
                self.f_copy(d, 0, m).start()

    def share(self):
        for d in range(1, self.place.shards):
            for k in range(1, QUADS):
                self.q_copy(d, k).wait_recv()
                for m in range(1, self.place.members):
                    self.f_copy(d, k, m).start()

    def end(self):
        for d in range(1, self.place.shards):
            self.z_copy(d).wait_send()
            for k in range(QUADS):
                if k:
                    self.q_copy(d, k).wait_send()
                for m in range(1, self.place.members):
                    self.f_copy(d, k, m).wait()
        self.own_copy().wait()


class Reduce:
    def __init__(self, place, part, block, out, col_split, head=None, tail=None):
        self.place, self.part, self.block, self.out, self.col_split = place, part, block, out, col_split
        self.straight = out is not None and len(out.shape) == 3
        if head is not None:
            self.half, self.half_in, self.quad_in, self.h_s, self.h_r, self.q_s, self.q_r = head
        if tail is not None:
            self.z_in, self.last, self.z_s, self.z_r, self.a_s, self.a_r, self.f_s, self.f_r, self.local = tail

    @staticmethod
    def head_scratch(members, shards, rows, columns):
        dma = pltpu.SemaphoreType.DMA
        return [
            pltpu.VMEM((shards, QUADS, rows, columns), BF),
            pltpu.VMEM((members - 1, shards, QUADS, rows, columns), BF),
            pltpu.VMEM((QUADS - 1, shards, rows, columns), BF),
            dma((members,)), dma((members,)), dma((QUADS,)), dma((QUADS,)),
        ]

    @staticmethod
    def tail_scratch(members, shards, rows, columns):
        dma = pltpu.SemaphoreType.DMA
        return [
            pltpu.VMEM((shards - 1, rows, columns), BF),
            pltpu.VMEM((rows, columns), BF),
            dma((shards,)), dma((shards,)), dma((QUADS,)), dma((QUADS,)),
            dma((QUADS, members)), dma((QUADS, members)), dma((1,)),
        ]

    def piece(self, quad, sub):
        rows, columns = self.last.shape
        if len(self.out.shape) == 3:
            return self.out.at[sub, pl.ds(pl.multiple_of(quad * rows, 16), rows), :]
        index = quad * self.place.members + sub
        top = pl.multiple_of(index // self.col_split * rows, 16)
        left = pl.multiple_of(index % self.col_split * columns, 128)
        return self.out.at[pl.ds(top, rows), pl.ds(left, columns)]

    def h_copy(self, m):
        p = self.place
        return remote(
            self.part.at[(p.sub + m) % p.members], self.half_in.at[m - 1], self.h_s.at[m], self.h_r.at[m], p.sibling(m)
        )

    def q_copy(self, k):
        p = self.place
        return remote(
            self.half.at[:, (p.quad + k) % QUADS], self.quad_in.at[k - 1], self.q_s.at[k], self.q_r.at[k], p.peer(k)
        )

    def z_copy(self, d):
        p = self.place
        return remote(
            self.block.at[(p.z + d) % p.shards], self.z_in.at[d - 1], self.z_s.at[d], self.z_r.at[d], p.along(d)
        )

    def a_copy(self, k):
        p = self.place
        return remote(self.last, self.piece(p.quad, p.sub), self.a_s.at[k], self.a_r.at[k], p.peer(k))

    def f_copy(self, k, m):
        p = self.place
        block = self.piece(p.behind(k), p.sub)
        return remote(block, block, self.f_s.at[k, m], self.f_r.at[k, m], p.sibling(m))

    def s_copy(self, k, m):
        p = self.place
        return remote(
            self.last, self.piece(p.quad, p.sub), self.f_s.at[k, m], self.f_r.at[k, m], p.cross(k, m)
        )

    def start(self):
        for m in range(1, self.place.members):
            self.h_copy(m).start()

    def to_quads(self):
        for m in range(1, self.place.members):
            self.h_copy(m).wait_recv()

        def turn(i, carry):
            z, q = i // QUADS, i % QUADS
            total = self.part[self.place.sub, z, q].astype(F32)
            for m in range(1, self.place.members):
                total = total + self.half_in[m - 1, z, q].astype(F32)
            self.half[z, q] = total.astype(BF)
            return carry

        lax.fori_loop(0, self.place.shards * QUADS, turn, 0)
        for k in range(1, QUADS):
            self.q_copy(k).start()

    def to_block(self):
        for k in range(1, QUADS):
            self.q_copy(k).wait_recv()

        def turn(z, carry):
            total = self.half[z, self.place.quad].astype(F32)
            for k in range(1, QUADS):
                total = total + self.quad_in[k - 1, z].astype(F32)
            self.block[z] = total.astype(BF)
            return carry

        lax.fori_loop(0, self.place.shards, turn, 0)

    def to_shards(self):
        for d in range(1, self.place.shards):
            self.z_copy(d).start()

    def block_to_shards(self):
        self.to_block()
        self.to_shards()

    def give(self):
        total = self.block[self.place.z].astype(F32)
        for d in range(1, self.place.shards):
            self.z_copy(d).wait_recv()
            total = total + self.z_in[d - 1].astype(F32)
        self.last[...] = total.astype(BF)
        for k in range(1, QUADS):
            self.a_copy(k).start()
            if self.straight:
                for m in range(1, self.place.members):
                    self.s_copy(k, m).start()
        own = pltpu.make_async_copy(self.last, self.piece(self.place.quad, self.place.sub), self.local.at[0])
        own.start()
        own.wait()
        for m in range(1, self.place.members):
            self.f_copy(0, m).start()

    def share(self):
        for k in range(1, QUADS):
            self.a_copy(k).wait_recv()
            if not self.straight:
                for m in range(1, self.place.members):
                    self.f_copy(k, m).start()

    def end_head(self):
        for m in range(1, self.place.members):
            self.h_copy(m).wait_send()
        for k in range(1, QUADS):
            self.q_copy(k).wait_send()

    def end_tail(self):
        for d in range(1, self.place.shards):
            self.z_copy(d).wait_send()
        for k in range(QUADS):
            if k:
                self.a_copy(k).wait_send()
            for m in range(1, self.place.members):
                if k and self.straight:
                    self.s_copy(k, m).wait()
                else:
                    self.f_copy(k, m).wait()


RIM = 16
TILE = 128
SMALL = 128
TN = (((0,), (0,)), ((), ()))


def moved(value, by):
    rows = value.shape[0]
    return value if by % rows == 0 else pltpu.roll(value, (-by) % rows, 0)


def head_columns(tap, wide_first):
    shape = (SMALL, HEADS * HEAD) if wide_first else (HEADS * HEAD, SMALL)
    narrow = lax.broadcasted_iota(jnp.int32, shape, 0 if wide_first else 1)
    wide = lax.broadcasted_iota(jnp.int32, shape, 1 if wide_first else 0)
    if wide_first:
        same = narrow == wide // HEAD * KERNEL + tap
    else:
        same = (narrow * HEAD == (wide * KERNEL + tap * HEAD)) & (wide % HEAD == 0)
    return jnp.where(same, 1.0, 0.0).astype(BF)


def norm_rows(value):
    center = value - jnp.mean(value, axis=-1, keepdims=True)
    inv_std = lax.rsqrt(jnp.mean(center * center, axis=-1, keepdims=True) + norm_eps)
    return center * inv_std, inv_std


def norm_rows_back(normed, inv_std, d_scaled):
    return inv_std * (
        d_scaled
        - jnp.mean(d_scaled, axis=-1, keepdims=True)
        - normed * jnp.mean(d_scaled * normed, axis=-1, keepdims=True)
    )


def fold(value):
    return jnp.sum(value.reshape(value.shape[0] // 8, 8, value.shape[1]), axis=0)


def gelu_both(value):
    size = jnp.abs(value)
    turn = 1.0 / (1.0 + (0.3275911 / math.sqrt(2.0)) * size)
    bell = jnp.exp2(value * value * (-0.5 * math.log2(math.e)))
    poly = ((((1.061405429 * turn - 1.453152027) * turn + 1.421413741) * turn - 0.284496736) * turn + 0.254829592) * turn
    tail = 0.5 * poly * bell
    below = jnp.where(value < 0.0, tail, 1.0 - tail)
    return value * below, below + value * bell * (1.0 / math.sqrt(2.0 * math.pi))


def project_body(hidden, qkv, kv_out, q_packed, q_out):
    seqs, rows, _ = hidden.shape
    half = rows // 2
    width = HEADS * HEAD
    is_low = low_lanes()

    def turn(step, carry):
        s, r = step // (half // TILE), step % (half // TILE)
        tops = (pl.multiple_of(r * TILE, TILE), pl.multiple_of(half + r * TILE, TILE))
        rows_in = jnp.concatenate([hidden[s, pl.ds(top, TILE), :] for top in tops], axis=0)
        mixed = dot(rows_in, qkv[:, : 3 * width], NN).astype(BF)
        blocks = [
            [mixed[part * TILE : part * TILE + TILE, h * width : h * width + 2 * HEAD] for h in range(TRIPLE)]
            for part in range(2)
        ]

        def placed(part, head, low):
            block = blocks[part][head % TRIPLE]
            return block if (head < TRIPLE) == low else swap_halves(block)

        for part, top in enumerate(tops):
            for j in range(HEADS // 2):
                q_out[s, pl.ds(top, TILE), j * 2 * HEAD : j * 2 * HEAD + 2 * HEAD] = jnp.where(
                    is_low, placed(part, 2 * j, True), placed(part, 2 * j + 1, False)
                )
            for h in range(HEADS):
                at = h % TRIPLE * width + 2 * HEAD + h // TRIPLE * 2 * HEAD
                kv_out[s * 2 + h // TRIPLE, h % TRIPLE, pl.ds(top, TILE), :] = mixed[
                    part * TILE : part * TILE + TILE, at : at + 2 * HEAD
                ]
        for h in range(HEADS):
            q_packed[s * 2 + h // TRIPLE, h % TRIPLE, pl.ds(tops[0], TILE), :] = jnp.where(
                is_low, placed(0, h, True), placed(1, h, False)
            )
        return carry

    lax.fori_loop(0, seqs * half // TILE, turn, 0)


def conv_forward_body(
    s, hidden, low_rim, high_rim, rest, q_out, spread_out, key_out, mix_out, soft_out, value_out, conv_out,
    small_turned, span_wide, ext, soft_tile, soft_sem,
):
    seqs, rows, model = hidden.shape
    width = HEADS * HEAD
    tiles = rows // TILE
    depth = small_turned[64 : 64 + 16, :]
    low, high = low_rim[s], high_rim[s]
    ext[0:RIM] = low.astype(F32)
    ext[RIM : RIM + rows] = hidden[s].astype(F32)
    ext[RIM + rows : rows + 2 * RIM] = high.astype(F32)
    value = rest[:, 0:width]
    value_out[s, 0:RIM] = dot(low, value, NN)
    value_out[s, RIM : RIM + rows] = dot(hidden[s], value, NN)
    value_out[s, RIM + rows : rows + 2 * RIM] = dot(high, value, NN)

    def soft_copy(number):
        return pltpu.make_async_copy(soft_tile.at[number % 2], soft_out.at[number], soft_sem.at[number % 2])

    def turn(r, carry):
        number = s * tiles + r
        top = pl.multiple_of(r * TILE, TILE)
        around = ext[pl.ds(top, TILE + 2 * RIM), :]
        spread = jnp.zeros((TILE, model), F32)
        for tap in range(KERNEL):
            spread = spread + moved(around, tap - KERNEL // 2)[RIM : RIM + TILE] * depth[tap : tap + 1]
        spread_low = spread.astype(BF)
        spread_out[s, pl.ds(top, TILE), :] = spread_low
        key_conv = dot(spread_low, rest[:, width : 2 * width], NN)
        key_out[s, pl.ds(top, TILE), :] = key_conv
        mix = (key_conv * q_out[s, pl.ds(top, TILE), :].astype(F32)).astype(BF)
        mix_out[s, pl.ds(top, TILE), :] = mix
        logits = [dot(mix, span_wide[:, tap * width : tap * width + width], NN) for tap in range(KERNEL)]
        peak = functools.reduce(jnp.maximum, logits)
        powers = [jnp.exp(one - peak) for one in logits]
        scale = 1.0 / sum(powers[1:], powers[0])
        values = value_out[s, pl.ds(top, TILE + 2 * RIM), :]

        @pl.when(number > 1)
        def _():
            soft_copy(number - 2).wait()

        result = jnp.zeros((TILE, width), F32)
        for tap in range(KERNEL):
            soft = powers[tap] * scale
            soft_tile[number % 2, tap] = soft.astype(BF)
            result = result + soft * moved(values, tap - KERNEL // 2)[RIM : RIM + TILE]
        conv_out[s, pl.ds(top, TILE), :] = result.astype(BF)
        soft_copy(number).start()
        return carry

    lax.fori_loop(0, tiles, turn, 0)
    if s == seqs - 1:
        soft_copy(seqs * tiles - 2).wait()
        soft_copy(seqs * tiles - 1).wait()


OUTS = 13


def pack_first(qkv_weight, span_weight, conv_depth, norms, qkv_block, rest_block):
    rows = qkv_weight.shape[0]
    width = HEADS * HEAD
    is_low = low_lanes()

    def pair(left, right):
        a, b = (qkv_weight[:, x // 2 * 2 * HEAD : x // 2 * 2 * HEAD + 2 * HEAD] for x in (left, right))
        return jnp.where(is_low, swap_halves(a) if left % 2 else a, b if right % 2 else swap_halves(b))

    for h in range(TRIPLE):
        for j, (left, right) in enumerate(
            ((h, h + TRIPLE), (HEADS + h, 2 * HEADS + h), (HEADS + TRIPLE + h, 2 * HEADS + TRIPLE + h))
        ):
            at = h * width + j * 2 * HEAD
            qkv_block[:, at : at + 2 * HEAD] = pair(left, right)
    qkv_block[:, 3 * width :] = jnp.zeros((rows, SMALL), BF)
    lines = [jnp.zeros((64, rows), F32), conv_depth[...].astype(F32), norms[...].astype(F32)]
    lines += [jnp.zeros((SMALL - 64 - KERNEL - 4, rows), F32)]
    span = span_weight[...].astype(F32)
    span = jnp.concatenate([span, jnp.zeros((span.shape[0], SMALL - span.shape[1]), F32)], axis=1)
    span = jnp.concatenate([span, jnp.zeros((rows - span.shape[0], SMALL), F32)], axis=0)
    rest_block[:, 2 * width : 2 * width + SMALL] = (jnp.concatenate(lines, axis=0).T + span).astype(BF)
    rest_block[:, 2 * width + SMALL :] = jnp.zeros((rows, SMALL), BF)


def front_kernel(by_kernel, members, shards, splits, *refs):
    if by_kernel:
        (
            hidden, qkv_weight, conv_value, conv_point, span_weight, conv_depth, norms,
            dense_attn, dense_conv, ffn_inner, ffn_outer, *refs,
        ) = refs
    else:
        hidden, qkv, rest, span, *refs = refs
    ctx_out, soft_out, *refs = refs
    outs, refs = refs[:OUTS], refs[OUTS:]
    if by_kernel:
        qkv_out, rest_out, span_out, second, third, *refs = refs
    (
        kv_all, q_all, out_all, lse, q_out, spread_out, key_out, mix_out, value_out, conv_out,
        small_turned, low_rim, high_rim,
        kv_in, q_in, out_send, ext, span_wide, soft_tile,
        kv_s, kv_r, q_s, q_r, f_s, f_r, o_s, o_r, e_s, e_r, soft_sem, local, out_sem, *refs,
    ) = refs
    held = (
        kv_all, q_all, out_all, lse, q_out, spread_out, key_out, mix_out, value_out, conv_out,
        small_turned, low_rim, high_rim,
    )
    if by_kernel:
        qkv, rest, span, qkv_block, rest_block, second_block, third_block, load_sem, *sems = refs
        held += (qkv, rest, span)
        outs = (*outs, qkv_out, rest_out, span_out)
        blocks = (qkv_block, rest_block, second_block, third_block)

    def leave(j):
        return pltpu.make_async_copy(held[j], outs[j], out_sem.at[j])

    early = [j for j in range(len(held)) if j not in (0, 1, 2, 3)]
    seqs, rows, model = hidden.shape
    half = rows // 2
    width = HEADS * HEAD
    place = Place(members, shards)
    quad, sub, peer, sibling = place.quad, place.sub, place.peer, place.sibling
    count = QUADS * members
    after = ((place.me + 1) % count, place.z)
    before = ((place.me + count - 1) % count, place.z)
    loads = []
    if by_kernel:
        units = ffn_inner.shape[2]
        group = model // GROUPS
        plan = [(conv_value, rest_block, 0, width), (conv_point, rest_block, width, width)]
        plan += [(dense_attn, second_block, 0, model), (dense_conv, second_block, model, model)]
        for g in range(GROUPS):
            plan += [(ffn_inner.at[g], second_block, 2 * model + g * units, units)]
            plan += [(ffn_outer.at[g], third_block, g * group, group)]
        loads = [
            pltpu.make_async_copy(source, block.at[:, at : at + size], load_sem.at[j])
            for j, (source, block, at, size) in enumerate(plan)
        ]
        for load in loads:
            load.start()
        pack_first(qkv_weight, span_weight, conv_depth, norms, qkv_block, rest_block)
    place.greet(by_kernel, [after, before])
    gathers = []
    if by_kernel:
        gathers = [
            Gather(place, block, full, split, sems[7 * j : 7 * j + 7])
            for j, (block, full, split) in enumerate(zip(blocks, (qkv, rest, second, third), splits))
        ]
        gathers[0].start()
    rims = (
        remote(hidden.at[:, rows - RIM : rows, :], low_rim, e_s.at[0], e_r.at[0], after),
        remote(hidden.at[:, 0:RIM, :], high_rim, e_s.at[1], e_r.at[1], before),
    )
    for rim in rims:
        rim.start()
    for load in loads:
        load.wait()
    if by_kernel:
        gathers[0].relay()
        gathers[1].start()
        gathers[0].share()
        gathers[1].relay()
        gathers[2].start()
        gathers[3].start()
        gathers[0].end()
    project_body(hidden, qkv, kv_in, q_in, q_out)

    def kv_copy(h, k):
        return remote(
            kv_in.at[(quad + k) % QUADS, h], kv_all.at[h, quad, sub], kv_s.at[h, k], kv_r.at[h, k], peer(k)
        )

    def q_copy(h, k):
        return remote(
            q_in.at[(quad + k) % QUADS, h], q_all.at[h, quad], q_s.at[h, k], q_r.at[h, k], peer(k)
        )

    def forward_copy(h, m):
        return remote(
            kv_all.at[h, :, sub], kv_all.at[h, :, sub], f_s.at[h, m], f_r.at[h, m], sibling(m)
        )

    def out_copy(h, i, k):
        return remote(
            out_send.at[h, i], ctx_out.at[quad, h], o_s.at[h, i], o_r.at[h, i], peer(k)
        )

    def receive(h):
        for k in range(1, QUADS):
            kv_copy(h, k).wait_recv()
            q_copy(h, k).wait_recv()
        for m in range(1, members):
            forward_copy(h, m).start()

    own_kv = pltpu.make_async_copy(kv_in.at[quad], kv_all.at[:, quad, sub], local.at[0])
    own_q = pltpu.make_async_copy(q_in.at[quad], q_all.at[:, quad], local.at[1])
    own_kv.start()
    own_q.start()
    for h in range(TRIPLE):
        for k in range(1, QUADS):
            kv_copy(h, k).start()
            q_copy(h, k).start()
    for rim in rims:
        rim.wait()

    @pl.when(place.me == 0)
    def _():
        low_rim[...] = jnp.zeros_like(low_rim)

    @pl.when(place.me == count - 1)
    def _():
        high_rim[...] = jnp.zeros_like(high_rim)

    if by_kernel:
        gathers[1].share()
        gathers[1].end()
        block, head_block = model // shards, width // shards
        for z in range(shards):
            span[z * head_block : z * head_block + head_block] = rest[
                z * block : z * block + head_block, 2 * width : 2 * width + SMALL
            ]
    small_turned[...] = rest[:, 2 * width : 2 * width + SMALL].astype(F32).T
    for tap in range(KERNEL):
        span_wide[:, tap * width : tap * width + width] = dot(span[...], head_columns(tap, True), NN).astype(BF)
    own_kv.wait()
    own_q.wait()
    for s in range(seqs):
        conv_forward_body(
            s, hidden, low_rim, high_rim, rest, q_out, spread_out, key_out, mix_out, soft_out, value_out, conv_out,
            small_turned, span_wide, ext, soft_tile, soft_sem,
        )
        receive(s)
    for j in early:
        leave(j).start()
    is_low = low_lanes()
    tiles = 2 if half % (2 * CHUNK) == 0 else 1

    def block(step, carry):
        h, i = step // QUADS, step % QUADS
        k = (i + 1) % QUADS
        source = (quad + k) % QUADS

        @pl.when(i == 0)
        def _():
            for m in range(1, members):
                forward_copy(h, m).wait_recv()

        keys = kv_all[h].reshape(QUADS * members * rows, 2 * HEAD)

        def rows_turn(r, inner):
            parts = []
            for tile in range(tiles):
                at = pl.multiple_of((r * tiles + tile) * CHUNK, CHUNK)
                packed = q_all[h, source, pl.ds(at, CHUNK), :]
                for part in range(2):
                    q = jnp.where(is_low, packed if part == 0 else swap_halves(packed), jnp.zeros_like(packed))
                    parts.append((tile, part, q))
            outs = []
            following = dot(parts[0][2], keys, NT)
            for number, (tile, part, _) in enumerate(parts):
                scores = following
                if number + 1 < len(parts):
                    following = dot(parts[number + 1][2], keys, NT)
                top = jnp.max(scores, axis=1, keepdims=True)
                probs = jnp.exp2((scores - top) * EXP2_SCALE)
                total = jnp.sum(probs, axis=1, keepdims=True)
                outs.append(dot(probs.astype(BF), keys, NN) / total)
                stat = top * EXP2_SCALE + jnp.log2(total)
                lse[h, source, part, r * tiles + tile] = jnp.broadcast_to(stat, (CHUNK, CHUNK)).T[0:8, :]
                if part == 1:
                    at = pl.multiple_of((r * tiles + tile) * CHUNK, CHUNK)
                    both = jnp.where(is_low, swap_halves(outs[-2]), outs[-1])
                    out_all[h, source, pl.ds(at, CHUNK), :] = both
                    out_send[h, i, pl.ds(at, CHUNK), :] = both.astype(BF)
            return inner

        lax.fori_loop(0, half // (CHUNK * tiles), rows_turn, 0)

        @pl.when(k != 0)
        def _():
            out_copy(h, i, k).start()

        @pl.when(k == 0)
        def _():
            own = pltpu.make_async_copy(out_send.at[h, i], ctx_out.at[quad, h], local.at[0])
            own.start()
            own.wait()

        @pl.when(step == TRIPLE * QUADS - 3)
        def _():
            leave(0).start()
            leave(1).start()

        for j in range(seqs, TRIPLE):

            @pl.when(step == (j - seqs) * QUADS + 2)
            def _(j=j):
                receive(j)

        if by_kernel:

            @pl.when(step == 1)
            def _():
                for gather in gathers[2:]:
                    gather.relay()

            @pl.when(step == TRIPLE * QUADS - 2)
            def _():
                for gather in gathers[2:]:
                    gather.share()

        return carry

    lax.fori_loop(0, TRIPLE * QUADS, block, 0)
    for j in (2, 3):
        leave(j).start()
    for gather in gathers[2:]:
        gather.end()
    for h in range(TRIPLE):
        for k in range(1, QUADS):
            out_copy(h, k - 1, k).wait()
            kv_copy(h, k).wait_send()
            q_copy(h, k).wait_send()
        for m in range(1, members):
            forward_copy(h, m).wait_send()
    for j in range(len(held)):
        leave(j).wait()


def front(by_kernel, members, shards, hidden, *arrays):
    seqs, rows, model = hidden.shape
    half = rows // 2
    width = HEADS * HEAD
    vm = pl.BlockSpec(memory_space=pltpu.VMEM)
    anywhere = pl.BlockSpec(memory_space=pl.ANY)
    dma = pltpu.SemaphoreType.DMA
    shape = jax.ShapeDtypeStruct
    splits = SPLITS if by_kernel else ()
    held = [
        shape((TRIPLE, QUADS, members, rows, 2 * HEAD), BF),
        shape((TRIPLE, QUADS, half, 2 * HEAD), BF),
        shape((TRIPLE, QUADS, half, 2 * HEAD), F32),
        shape((TRIPLE, QUADS, 2, half // CHUNK, 8, CHUNK), F32),
        shape((seqs, rows, width), BF),
        shape((seqs, rows, model), BF),
        shape((seqs, rows, width), F32),
        shape((seqs, rows, width), BF),
        shape((seqs, rows + 2 * RIM, width), F32),
        shape((seqs, rows, width), BF),
        shape((SMALL, model), F32),
        shape((seqs, RIM, model), BF),
        shape((seqs, RIM, model), BF),
    ]
    gathered = []
    scratch = []
    in_specs = [vm] * (1 + len(arrays))
    if by_kernel:
        block, head_block = model // shards, width // shards
        units = arrays[8].shape[2]
        gathered = [
            shape((model, 3 * width + SMALL), BF), shape((model, 2 * width + 2 * SMALL), BF), shape((width, SMALL), BF),
            shape((width, 2 * model + GROUPS * units), BF), shape((units, model), BF),
        ]
        scratch = [pltpu.VMEM(one.shape, BF) for one in gathered[:3]]
        scratch += [
            pltpu.VMEM((block, 3 * width + SMALL), BF),
            pltpu.VMEM((block, 2 * width + 2 * SMALL), BF),
            pltpu.VMEM((head_block, 2 * model + GROUPS * units), BF),
            pltpu.VMEM((units // shards, model), BF),
            dma((4 + 2 * GROUPS,)),
        ]
        in_specs = [vm, vm, anywhere, anywhere, vm, vm, vm, anywhere, anywhere, anywhere, anywhere]
    total = TRIPLE * QUADS * rows * QUADS * members * rows
    result = [
        shape((QUADS, TRIPLE, half, 2 * HEAD), BF),
        shape((seqs * rows // TILE, KERNEL, TILE, width), BF),
        *held,
        *gathered,
    ]
    return pl.pallas_call(
        functools.partial(front_kernel, by_kernel, members, shards, splits),
        in_specs=in_specs,
        out_specs=[anywhere] * len(result),
        out_shape=result,
        scratch_shapes=[pltpu.VMEM(one.shape, one.dtype) for one in held]
        + [
            pltpu.VMEM((QUADS, TRIPLE, rows, 2 * HEAD), BF),
            pltpu.VMEM((QUADS, TRIPLE, half, 2 * HEAD), BF),
            pltpu.VMEM((TRIPLE, QUADS, half, 2 * HEAD), BF),
            pltpu.VMEM((rows + 2 * RIM, model), F32),
            pltpu.VMEM((width, KERNEL * width), BF),
            pltpu.VMEM((2, KERNEL, TILE, width), BF),
            dma((TRIPLE, QUADS)), dma((TRIPLE, QUADS)), dma((TRIPLE, QUADS)), dma((TRIPLE, QUADS)),
            dma((TRIPLE, members)), dma((TRIPLE, members)), dma((TRIPLE, QUADS)), dma((TRIPLE, QUADS)),
            dma((2,)), dma((2,)), dma((2,)), dma((2,)), dma((OUTS + 3,)),
        ]
        + scratch
        + Gather.semaphores(members, shards) * len(splits),
        compiler_params=pltpu.CompilerParams(
            collective_id=1, has_side_effects=True, vmem_limit_bytes=62 * 2**20
        ),
        cost_estimate=pl.CostEstimate(flops=total * 256, bytes_accessed=8 * 2**20, transcendentals=total),
    )(hidden, *arrays)


def middle_kernel(
    by_kernel, shards, members,
    context, conv, hidden, cotangent, second, third, small_turned,
    layer_out, d_first_out, d_context_out, d_conv_out, dense_part, inner_part, third_part, norm_sums,
    context_low, hidden_low, active_all, d_outer_all, d_inner_all, d_dense_all, d_context_all,
):
    seqs, rows, model = hidden.shape
    half = rows // 2
    width = HEADS * HEAD
    group = model // GROUPS
    units = third.shape[0]
    is_low = low_lanes()
    gains = small_turned[64 + KERNEL : 64 + KERNEL + 4, :]
    attn_gain, attn_bias, out_gain, out_bias = (gains[j : j + 1] for j in range(4))
    norm_sums[...] = jnp.zeros_like(norm_sums)

    def turn(step, carry):
        s, p = step // 2, step % 2
        top = pl.multiple_of(p * half, half)
        at = pl.ds(top, half)
        every = pl.ds(pl.multiple_of(step * half, half), half)
        pairs = []
        for j in range(HEADS // 2):
            a = context[s * 2 + 2 * j // TRIPLE, 2 * j % TRIPLE]
            b = context[s * 2 + (2 * j + 1) // TRIPLE, (2 * j + 1) % TRIPLE]
            upper = jnp.where(is_low, a, swap_halves(b))
            lower = jnp.where(is_low, swap_halves(a), b)
            pairs.append(jnp.where(p == 0, upper, lower))
        low = jnp.concatenate(pairs, axis=1)
        context_low[every] = low
        dense = dot(low, second[:, :model], NN) + dot(conv[s, at], second[:, model : 2 * model], NN)
        normed_one, inv_one = norm_rows(dense + hidden[s, at].astype(F32))
        hidden_one = normed_one * attn_gain + attn_bias
        one_low = hidden_one.astype(BF)
        hidden_low[every] = one_low
        slopes = []
        wide = units // 3
        plan = [(g, g * units + j * wide, j * wide) for g in range(GROUPS) for j in range(3)]

        def enter(g, at):
            return dot(one_low[:, g * group : g * group + group], second[:, 2 * model + at : 2 * model + at + wide], NN)

        outers = [jnp.zeros((half, group), F32)] * GROUPS
        following = enter(*plan[0][:2])
        for number, (g, column, row) in enumerate(plan):
            inner = following
            if number + 1 < len(plan):
                following = enter(*plan[number + 1][:2])
            active, slope = gelu_both(inner)
            active = active.astype(BF)
            active_all[every, column : column + wide] = active
            slopes.append(slope)
            outers[g] = outers[g] + dot(active, third[row : row + wide, g * group : g * group + group], NN)
        normed_two, inv_two = norm_rows(jnp.concatenate(outers, axis=1) + hidden_one)
        layer_out[s, at] = (normed_two * out_gain + out_bias).astype(BF)
        d_result = cotangent[s, at].astype(F32)
        norm_sums[2] += fold(d_result * normed_two)
        norm_sums[3] += fold(d_result)
        d_second = norm_rows_back(normed_two, inv_two, d_result * out_gain)
        d_outer = d_second.astype(BF)
        d_outer_all[every] = d_outer
        backs = [jnp.zeros((half, group), F32)] * GROUPS

        def leave(g, row):
            return dot(d_outer[:, g * group : g * group + group], third[row : row + wide, g * group : g * group + group], NT)

        following = leave(plan[0][0], plan[0][2])
        for number, (g, column, row) in enumerate(plan):
            d_active = following
            if number + 1 < len(plan):
                following = leave(plan[number + 1][0], plan[number + 1][2])
            d_inner = (d_active * slopes[number]).astype(BF)
            d_inner_all[every, column : column + wide] = d_inner
            backs[g] = backs[g] + dot(d_inner, second[:, 2 * model + column : 2 * model + column + wide], NT)
        d_hidden = jnp.concatenate(backs, axis=1) + d_second
        norm_sums[0] += fold(d_hidden * normed_one)
        norm_sums[1] += fold(d_hidden)
        d_first = norm_rows_back(normed_one, inv_one, d_hidden * attn_gain)
        d_first_out[s, at] = d_first
        d_dense = d_first.astype(BF)
        d_dense_all[every] = d_dense
        d_context_all[every] = dot(d_dense, second[:, :model], NT).astype(BF)
        d_conv_out[s, at] = dot(d_dense, second[:, model : 2 * model], NT)
        return carry

    lax.fori_loop(0, seqs * 2, turn, 0)
    for s in range(seqs):
        for h in range(HEADS):
            at = h // 2 * 2 * HEAD
            upper = d_context_all[s * rows : s * rows + half, at : at + 2 * HEAD]
            lower = d_context_all[s * rows + half : s * rows + rows, at : at + 2 * HEAD]
            if h % 2:
                packed = jnp.where(is_low, swap_halves(upper), lower)
            else:
                packed = jnp.where(is_low, upper, swap_halves(lower))
            d_context_out[s * 2 + h // TRIPLE, h % TRIPLE] = packed
    for g in range(GROUPS):
        for z in range(shards):
            block = units // shards
            part = dot(
                active_all[:, g * units + z * block : g * units + z * block + block],
                d_outer_all[:, g * group : g * group + group], TN,
            ).astype(BF)
            if by_kernel:
                piece = block // (QUADS * members)
                for q in range(QUADS):
                    for c in range(members):
                        row = (q * members + c) * piece
                        third_part[c, z, q, :, g * group : g * group + group] = part[row : row + piece]
            else:
                third_part[z * block : z * block + block, g * group : g * group + group] = part

    def columns(left, right):
        found = []
        for start, size, rows_in, columns_in in (
            (0, model, context_low[...], d_dense_all),
            (model, model, None, d_dense_all),
            (2 * model, units, hidden_low[:, :group], d_inner_all.at[:, :units]),
            (2 * model + units, units, hidden_low[:, group:], d_inner_all.at[:, units:]),
        ):
            a, b = max(left, start), min(right, start + size)
            if a < b:
                if rows_in is None:
                    rows_in = conv[...].reshape(seqs * rows, width)
                found.append(dot(rows_in, columns_in[:, a - start : b - start], TN).astype(BF))
        return jnp.concatenate(found, axis=1) if len(found) > 1 else found[0]

    for part_out, start, size in ((dense_part, 0, 2 * model), (inner_part, 2 * model, GROUPS * units)):
        wide = size // 4
        for j in range(4):
            part = columns(start + j * wide, start + j * wide + wide)
            if by_kernel:
                block = width // shards
                piece = block // 2
                for z in range(shards):
                    for r in range(2):
                        row = z * block + r * piece
                        part_out[j % members, z, r * 2 + j // members] = part[row : row + piece]
            else:
                part_out[:, j * wide : j * wide + wide] = part


def middle(context, conv, hidden, cotangent, second, third, small_turned, by_kernel, shards, members):
    seqs, rows, model = hidden.shape
    width = HEADS * HEAD
    units = third.shape[0]
    tokens = seqs * rows
    shape = jax.ShapeDtypeStruct
    if by_kernel:
        parts = [
            shape((members, shards, QUADS, width // shards // 2, 2 * model // 4), BF),
            shape((members, shards, QUADS, width // shards // 2, GROUPS * units // 4), BF),
            shape((members, shards, QUADS, units // shards // (QUADS * members), model), BF),
        ]
    else:
        parts = [shape((width, 2 * model), BF), shape((width, GROUPS * units), BF), shape(third.shape, BF)]
    return pl.pallas_call(
        functools.partial(middle_kernel, by_kernel, shards, members),
        out_shape=[
            shape((seqs, rows, model), BF),
            shape((seqs, rows, model), F32),
            shape((QUADS, TRIPLE, rows // 2, 2 * HEAD), BF),
            shape((seqs, rows, width), F32),
            *parts,
            shape((4, 8, model), F32),
        ],
        scratch_shapes=[
            pltpu.VMEM((tokens, width), BF),
            pltpu.VMEM((tokens, model), BF),
            pltpu.VMEM((tokens, GROUPS * units), BF),
            pltpu.VMEM((tokens, model), BF),
            pltpu.VMEM((tokens, GROUPS * units), BF),
            pltpu.VMEM((tokens, model), BF),
            pltpu.VMEM((tokens, width), BF),
        ],
        compiler_params=pltpu.CompilerParams(vmem_limit_bytes=60 * 2**20),
    )(context, conv, hidden, cotangent, second, third, small_turned)


def conv_back_kernel(by_kernel, shards, members, *refs):
    (
        hidden, low_rim, high_rim, rest, span, small_turned, d_conv, q_out, spread, key_conv, mix, soft, value, d_first,
        norm_sums, d_in, *refs,
    ) = refs
    if by_kernel:
        third_part, dense_part, *refs = refs
    grad_rows, low_edge, high_edge, dq_conv, part_out, d_all, *refs = refs
    if by_kernel:
        third_block, dense_block, *refs = refs
    (
        ext, d_value, d_rows, slim_all, d_key_all, depth_sums, ext_low, soft_tile,
        d_s, d_r, soft_sem, local, *scratch,
    ) = refs
    seqs, rows, model = hidden.shape
    width = HEADS * HEAD
    value_at, point_at = 0, width
    tiles = rows // TILE
    place = Place(members, shards)
    quad, peer = place.quad, place.peer
    place.greet(False)

    def d_copy(h, k):
        return remote(
            d_in.at[(quad + k) % QUADS, h], d_all.at[h, quad], d_s.at[h, k], d_r.at[h, k], peer(k)
        )

    def soft_copy(number):
        return pltpu.make_async_copy(soft.at[number], soft_tile.at[number % 2], soft_sem.at[number % 2])

    soft_copy(0).start()
    base = pltpu.make_async_copy(d_first, grad_rows, local.at[0])
    base.start()
    own = pltpu.make_async_copy(d_in.at[quad], d_all.at[:, quad], local.at[1])
    own.start()
    for h in range(TRIPLE):
        for k in range(1, QUADS):
            d_copy(h, k).start()
    if by_kernel:
        third = Reduce(place, third_part, third_block, None, 1, head=scratch[0:7])
        dense = Reduce(place, dense_part, dense_block, None, 4, head=scratch[7:14])
        third.start()
        dense.start()
    is_low = low_lanes()
    depth = small_turned[64 : 64 + 16, :]
    pair = lax.broadcasted_iota(jnp.int32, (4 * HEAD, 2 * HEAD), 0) // HEAD % 2
    same = pair == lax.broadcasted_iota(jnp.int32, (4 * HEAD, 2 * HEAD), 1) // HEAD
    group_sum = jnp.where(same, 1.0, 0.0).astype(BF)
    depth_sums[...] = jnp.zeros_like(depth_sums)
    long = rows + 2 * RIM
    for s in range(seqs):
        ext[0:RIM] = low_rim[s].astype(F32)
        ext[RIM : RIM + rows] = hidden[s].astype(F32)
        ext[RIM + rows : long] = high_rim[s].astype(F32)
        ext_low[s * long : s * long + RIM] = low_rim[s]
        ext_low[s * long + RIM : s * long + RIM + rows] = hidden[s]
        ext_low[s * long + RIM + rows : s * long + long] = high_rim[s]
        d_value[...] = jnp.zeros_like(d_value)
        d_rows[...] = jnp.zeros_like(d_rows)

        def turn(r, carry):
            number = s * tiles + r

            @pl.when(number + 1 < seqs * tiles)
            def _():
                soft_copy(number + 1).start()

            top = pl.multiple_of(r * TILE, TILE)
            here = pl.ds(top, TILE)
            there = pl.ds(top, TILE + 2 * RIM)
            every = pl.ds(pl.multiple_of(s * rows + r * TILE, TILE), TILE)
            d_res = d_conv[s, here, :]
            values = value[s, there, :]
            softs = []
            d_kernels = []
            soft_copy(number).wait()
            rim = jnp.zeros((RIM, width), F32)
            d_values = jnp.zeros((TILE + 2 * RIM, width), F32)
            total = jnp.zeros((TILE, width), F32)
            for tap in range(KERNEL):
                one = soft_tile[number % 2, tap].astype(F32)
                softs.append(one)
                weighted = jnp.concatenate([rim, one * d_res, rim], axis=0)
                d_values = d_values + moved(weighted, KERNEL // 2 - tap)
                product = d_res * moved(values, tap - KERNEL // 2)[RIM : RIM + TILE]
                high = product.astype(BF)
                lower = (product - high.astype(F32)).astype(BF)
                sums = []
                for at in range(0, width, 2 * HEAD):
                    both = jnp.concatenate([high[:, at : at + 2 * HEAD], lower[:, at : at + 2 * HEAD]], axis=1)
                    sums.append(dot(both, group_sum, NN))
                d_kernel = jnp.concatenate(sums, axis=1)
                d_kernels.append(d_kernel)
                total = total + d_kernel * one
            d_value[there, :] += d_values
            slim = jnp.zeros((TILE, SMALL), F32)
            for tap in range(KERNEL):
                d_logits = (softs[tap] * (d_kernels[tap] - total)).astype(BF)
                slim = slim + dot(d_logits, head_columns(tap, False), NN)
            slim = slim.astype(BF)
            slim_all[every] = slim
            d_mix = dot(slim, span[...], NT)
            d_query = d_mix * key_conv[s, here, :]
            for h in range(TRIPLE):
                a, b = (d_query[:, x // 2 * 2 * HEAD : x // 2 * 2 * HEAD + 2 * HEAD] for x in (h, h + TRIPLE))
                a = swap_halves(a) if h % 2 else a
                b = b if (h + TRIPLE) % 2 else swap_halves(b)
                dq_conv[h, s, here, :] = jnp.where(is_low, a, b)
            d_key = (d_mix * q_out[s, here, :].astype(F32)).astype(BF)
            d_key_all[every] = d_key
            d_spread = dot(d_key, rest[:, point_at : point_at + width], NT)
            around = ext[there, :]
            wide_rim = jnp.zeros((RIM, model), F32)
            padded = jnp.concatenate([wide_rim, d_spread, wide_rim], axis=0)
            back = jnp.zeros((TILE + 2 * RIM, model), F32)
            for tap in range(KERNEL):
                depth_sums[tap] += fold(d_spread * moved(around, tap - KERNEL // 2)[RIM : RIM + TILE])
                back = back + moved(padded, KERNEL // 2 - tap) * depth[tap : tap + 1]
            d_rows[there, :] += back
            if by_kernel:

                @pl.when(number == 1)
                def _():
                    third.to_quads()

                @pl.when(number == 2)
                def _():
                    dense.to_quads()

            return carry

        lax.fori_loop(0, tiles, turn, 0)
        if s == 0:
            base.wait()
        value_low = d_value[...].astype(BF)
        value_part = dot(ext_low[s * long : s * long + long], value_low, TN)
        if s == 0:
            grad_value = value_part
        else:
            grad_value = grad_value + value_part
        all_rows = dot(value_low, rest[:, value_at : value_at + width], NT) + d_rows[...]
        grad_rows[s] += all_rows[RIM : RIM + rows]
        low_edge[s] = all_rows[0:RIM].astype(BF)
        high_edge[s] = all_rows[RIM + rows :].astype(BF)

    grad_point = dot(spread[...].reshape(seqs * rows, model), d_key_all[...], TN)
    grad_span = dot(mix[...].reshape(seqs * rows, width), slim_all[...], TN)
    lines = [jnp.zeros((64, model), F32)]
    lines += [jnp.sum(depth_sums[tap], axis=0, keepdims=True) for tap in range(KERNEL)]
    lines += [jnp.sum(norm_sums[j], axis=0, keepdims=True) for j in range(4)]
    lines += [jnp.zeros((SMALL - 64 - KERNEL - 4, model), F32)]
    block, head_block = model // shards, width // shards
    slots = []
    for z in range(shards):
        slots += [grad_span[z * head_block : z * head_block + head_block], jnp.zeros((block - head_block, SMALL), F32)]
    small = jnp.concatenate(lines, axis=0).T + jnp.concatenate(slots, axis=0)
    whole = jnp.concatenate([grad_value, grad_point, small, jnp.zeros((model, SMALL), F32)], axis=1).astype(BF)
    if by_kernel:
        piece = block // QUADS
        wide = whole.shape[1] // members
        for z in range(shards):
            for q in range(QUADS):
                row = z * block + q * piece
                for c in range(members):
                    part_out[c, z, q] = whole[row : row + piece, c * wide : c * wide + wide]
    else:
        part_out[...] = whole
    own.wait()
    for h in range(TRIPLE):
        for k in range(1, QUADS):
            d_copy(h, k).wait()
    if by_kernel:
        for one in (third, dense):
            one.to_block()
            one.end_head()


def conv_back(by_kernel, shards, members, *arrays):
    hidden = arrays[0]
    seqs, rows, model = hidden.shape
    width = HEADS * HEAD
    long = rows + 2 * RIM
    columns = 2 * width + 2 * SMALL
    shape = jax.ShapeDtypeStruct
    if by_kernel:
        part = shape((members, shards, QUADS, model // shards // QUADS, columns // members), BF)
    else:
        part = shape((model, columns), BF)
    vm = pl.BlockSpec(memory_space=pltpu.VMEM)
    anywhere = pl.BlockSpec(memory_space=pl.ANY)
    dma = pltpu.SemaphoreType.DMA
    blocks = [one.shape[1:2] + one.shape[3:] for one in arrays[16:]]
    return pl.pallas_call(
        functools.partial(conv_back_kernel, by_kernel, shards, members),
        in_specs=[vm] * 11 + [anywhere, vm, anywhere, vm, anywhere] + [vm] * len(blocks),
        out_specs=[vm] * (6 + len(blocks)),
        out_shape=[
            shape((seqs, rows, model), F32),
            shape((seqs, RIM, model), BF),
            shape((seqs, RIM, model), BF),
            shape((TRIPLE, seqs, rows, 2 * HEAD), F32),
            part,
            shape((TRIPLE, QUADS, rows // 2, 2 * HEAD), BF),
        ]
        + [shape(one, BF) for one in blocks],
        scratch_shapes=[
            pltpu.VMEM((long, model), F32),
            pltpu.VMEM((long, width), F32),
            pltpu.VMEM((long, model), F32),
            pltpu.VMEM((seqs * rows, SMALL), BF),
            pltpu.VMEM((seqs * rows, width), BF),
            pltpu.VMEM((KERNEL, 8, model), F32),
            pltpu.VMEM((seqs * long, model), BF),
            pltpu.VMEM((2, KERNEL, TILE, width), BF),
            dma((TRIPLE, QUADS)), dma((TRIPLE, QUADS)), dma((2,)), dma((2,)),
        ]
        + sum((Reduce.head_scratch(members, shards, *one[1:]) for one in blocks), []),
        compiler_params=pltpu.CompilerParams(
            collective_id=3, has_side_effects=True, vmem_limit_bytes=60 * 2**20
        ),
    )(*arrays)


UNROLL = 4


def back_kernel(by_kernel, shards, members, *refs):
    d_all, kv_all, q_all, out_all, lse, *late, grad_rows, low_edge, high_edge = refs[:11]
    refs = refs[11:]
    if by_kernel:
        third_block, dense_block, inner_late, middle_late, *refs = refs
        late += [inner_late, middle_late]
        grad_in, third_sum, dense_sum, inner_sum, middle_sum, *refs = refs
        sums, refs = refs[:TRIPLE], refs[TRIPLE:]
    else:
        grad_in, whole, *refs = refs
    (
        q_zero, d_zero, stat, delta, dq_sum, dkv_sum, own_part, sib_send, sib_recv, dkv_send, dq_send,
        dq_out, dkv_out, d_columns, low_in, high_in, hidden, qkv, dq_conv, load_sem,
        p_s, p_r, k_s, k_r, g_s, g_r, e_s, e_r, local, *scratch,
    ) = refs
    rows = kv_all.shape[3]
    half = rows // 2
    seqs, _, model = hidden.shape
    width = HEADS * HEAD
    steps = TRIPLE * QUADS
    place = Place(members, shards)
    quad, sub, peer, sibling = place.quad, place.sub, place.peer, place.sibling
    count = QUADS * members
    after = ((place.me + 1) % count, place.z)
    before = ((place.me + count - 1) % count, place.z)
    more = [place.cross(k, m) for k in range(1, QUADS) for m in range(1, members)] if by_kernel else []
    held = [hidden, qkv, dq_conv]
    if by_kernel:
        inner_part, middle_part, *scratch = scratch
        held += [inner_part, middle_part]
    loads = [pltpu.make_async_copy(late[j], held[j], load_sem.at[j]) for j in range(len(held))]
    for load in loads[3:] + loads[:3]:
        load.start()

    def wait_loads():
        for load in loads[:3]:
            load.wait()

    place.greet(by_kernel, [after, before, *more])
    for load in loads[3:]:
        load.wait()
    is_low = low_lanes()
    third = dense = inner = middle = None
    chunks = []
    if by_kernel:
        third = Reduce(place, None, third_block, third_sum, 1, tail=scratch[0:9])
        dense = Reduce(place, None, dense_block, dense_sum, 4, tail=scratch[9:18])
        inner_block, middle_block, *scratch = scratch[18:]
        inner = Reduce(place, inner_part, inner_block, inner_sum, 4, head=scratch[0:7], tail=scratch[7:16])
        middle = Reduce(place, middle_part, middle_block, middle_sum, 2, head=scratch[16:23], tail=scratch[23:32])
        scratch = scratch[32:]
        for h in range(TRIPLE):
            part, block, *scratch = scratch
            chunks.append(Reduce(place, part, block, sums[h], 1, head=scratch[0:7], tail=scratch[7:16]))
            scratch = scratch[16:]
    edges = (
        remote(high_edge, low_in, e_s.at[0], e_r.at[0], after),
        remote(low_edge, high_in, e_s.at[1], e_r.at[1], before),
    )
    for edge in edges:
        edge.start()
    if by_kernel:
        third.to_shards()
        dense.to_shards()
        inner.start()
        middle.start()
    base = pltpu.make_async_copy(grad_rows, grad_in, local.at[1])
    base.start()
    base.wait()

    def part_copy(step, m):
        return remote(
            sib_send.at[step % 2, m - 1], sib_recv.at[step, m - 1], p_s.at[step, m], p_r.at[step, m], sibling(m)
        )

    def dkv_copy(h, i, k):
        return remote(
            dkv_send.at[h, i], dkv_out.at[quad, h], k_s.at[h, i], k_r.at[h, i], peer(k)
        )

    def dq_copy(h, k):
        return remote(
            dq_send.at[h, (quad + k) % QUADS], dq_out.at[quad, h], g_s.at[h, k], g_r.at[h, k], peer(k)
        )

    def finish(step):
        h, i = step // QUADS, step % QUADS
        k = (i + 1) % QUADS
        total = own_part[step % 2]
        for m in range(1, members):
            part_copy(step, m).wait_recv()
            total = total + sib_recv[step, m - 1].astype(F32)
        dkv_send[h, i] = total.astype(BF)

        @pl.when(k != 0)
        def _():
            dkv_copy(h, i, k).start()

        @pl.when(k == 0)
        def _():
            own = pltpu.make_async_copy(dkv_send.at[h, i], dkv_out.at[quad, h], local.at[0])
            own.start()
            own.wait()

    def columns_of(h):
        for k in range(1, QUADS):
            dkv_copy(h, k - 1, k).wait_recv()
            dq_copy(h, k).wait_recv()
        for s in range(seqs):
            a = dq_out[s * 2, h].astype(F32)
            b = dq_out[s * 2 + 1, h].astype(F32)
            top = s * rows
            upper = jnp.where(is_low, a, swap_halves(b)) + dq_conv[h, s, 0:half, :]
            lower = jnp.where(is_low, swap_halves(a), b) + dq_conv[h, s, half:rows, :]
            d_columns[top : top + half, 0 : 2 * HEAD] = upper.astype(BF)
            d_columns[top + half : top + rows, 0 : 2 * HEAD] = lower.astype(BF)
            d_columns[top : top + rows, 2 * HEAD : 4 * HEAD] = dkv_out[s * 2, h]
            d_columns[top : top + rows, 4 * HEAD : 6 * HEAD] = dkv_out[s * 2 + 1, h]
        value = dot(hidden[...].reshape(seqs * rows, model), d_columns[...], TN).astype(BF)
        if by_kernel:
            part = chunks[h].part
            block = model // shards
            piece = block // QUADS
            wide = part.shape[4]
            for z in range(shards):
                for q in range(QUADS):
                    row = z * block + q * piece
                    for c in range(members):
                        part[c, z, q] = value[row : row + piece, c * wide : c * wide + wide]
            chunks[h].start()
        else:
            whole[:, h * width : h * width + width] = value

    def rows_of(h):
        for s in range(seqs):
            grad_in[s] += dot(d_columns[s * rows : s * rows + rows, :], qkv[:, h * width : h * width + width], NT)

    def block(step, carry):
        h, i = step // QUADS, step % QUADS
        k = (i + 1) % QUADS
        source = (quad + k) % QUADS

        @pl.when(i == 0)
        def _():
            def prepare(b, inner):
                q = q_all[h, b]
                d = d_all[h, b]
                zero = jnp.zeros_like(q)
                q_zero[b, 0:half] = jnp.where(is_low, q, zero)
                q_zero[b, half:rows] = jnp.where(is_low, swap_halves(q), zero)
                d_zero[b, 0:half] = jnp.where(is_low, zero, swap_halves(d))
                d_zero[b, half:rows] = jnp.where(is_low, zero, d)
                both = (out_all[h, b] * d.astype(F32)).T
                delta[b, :, 0:half] = jnp.broadcast_to(jnp.sum(both[0:HEAD], axis=0, keepdims=True), (8, half))
                delta[b, :, half:rows] = jnp.broadcast_to(jnp.sum(both[HEAD:], axis=0, keepdims=True), (8, half))
                for part in range(2):
                    for r in range(half // CHUNK):
                        at = part * half + r * CHUNK
                        stat[b, :, at : at + CHUNK] = lse[h, b, part, r]
                dq_sum[b] = jnp.zeros((HEAD, rows), F32)
                return inner

            lax.fori_loop(0, QUADS, prepare, 0)

        keys = kv_all[h, source].reshape(members * rows, 2 * HEAD)
        keys_turned = keys.T[0:HEAD]
        dkv_sum[...] = jnp.zeros_like(dkv_sum)

        def queries_turn(turn, inner):
            def products(b):
                return dot(keys, q_zero[b], NT), dot(keys, d_zero[b], NT)

            following = products(turn * UNROLL)
            for number in range(UNROLL):
                b = turn * UNROLL + number
                scores, d_probs = following
                if number + 1 < UNROLL:
                    following = products(b + 1)
                probs = jnp.exp2(scores * EXP2_SCALE - stat[b, 0:1, :])
                d_scores = (probs * (d_probs - delta[b, 0:1, :])).astype(BF)
                both = jnp.concatenate([probs.astype(BF), d_scores], axis=1)
                dkv_sum[...] += dot(both, jnp.concatenate([d_zero[b], q_zero[b]], axis=0), NN)
                dq_sum[b] += dot(keys_turned, d_scores, NN)
            return inner

        lax.fori_loop(0, QUADS // UNROLL, queries_turn, 0)

        @pl.when(step > 0)
        def _():
            finish(step - 1)

        scale = jnp.where(is_low, 1.0 / math.sqrt(HEAD), 1.0)
        own_part[step % 2] = dkv_sum[pl.ds(pl.multiple_of(sub * rows, rows), rows), :] * scale
        for m in range(1, members):

            @pl.when(step > 1)
            def _():
                part_copy(step - 2, m).wait_send()

            target = (sub + m) % members
            theirs = dkv_sum[pl.ds(pl.multiple_of(target * rows, rows), rows), :] * scale
            sib_send[step % 2, m - 1] = theirs.astype(BF)
            part_copy(step, m).start()

        @pl.when(i == QUADS - 1)
        def _():
            def give(b, inner):
                turned = dq_sum[b] * (1.0 / math.sqrt(HEAD))
                dq_send[h, b] = jnp.concatenate([turned[:, 0:half], turned[:, half:rows]], axis=0).T.astype(BF)
                return inner

            lax.fori_loop(0, QUADS, give, 0)
            for j in range(1, QUADS):
                dq_copy(h, j).start()
            mine = pltpu.make_async_copy(dq_send.at[h, quad], dq_out.at[quad, h], local.at[0])
            mine.start()
            mine.wait()

        plan = [(5, wait_loads), (5, lambda: columns_of(0)), (5, lambda: rows_of(0)), (9, lambda: columns_of(1)), (9, lambda: rows_of(1))]
        if by_kernel:
            plan += [
                (0, inner.to_quads), (1, middle.to_quads),
                (2, third.give), (2, dense.give), (4, third.share), (4, dense.share),
                (4, inner.block_to_shards), (6, inner.give), (8, inner.share),
                (5, middle.block_to_shards), (7, middle.give), (9, middle.share),
                (6, chunks[0].to_quads), (8, chunks[0].block_to_shards), (9, chunks[0].give), (10, chunks[0].share),
                (10, chunks[1].to_quads), (11, chunks[1].block_to_shards),
            ]
        for at in range(steps):
            stages = [stage for when, stage in plan if when == at]
            if stages:

                @pl.when(step == at)
                def _(stages=stages):
                    for stage in stages:
                        stage()

        return carry

    lax.fori_loop(0, steps, block, 0)
    finish(steps - 1)
    columns_of(TRIPLE - 1)
    if by_kernel:
        chunks[1].give()
        chunks[2].to_quads()
    rows_of(TRIPLE - 1)
    for edge in edges:
        edge.wait()

    @pl.when(place.me > 0)
    def _():
        grad_in[:, 0:RIM, :] += low_in[...].astype(F32)

    @pl.when(place.me < count - 1)
    def _():
        grad_in[:, rows - RIM : rows, :] += high_in[...].astype(F32)

    if by_kernel:
        chunks[1].share()
        third.end_tail()
        dense.end_tail()
        inner.end_tail()
        middle.end_tail()
        inner.end_head()
        middle.end_head()
        chunks[2].block_to_shards()
        chunks[2].give()
        chunks[2].share()
        for h in range(TRIPLE):
            chunks[h].end_head()
            chunks[h].end_tail()
    for m in range(1, members):
        part_copy(steps - 2, m).wait_send()
        part_copy(steps - 1, m).wait_send()
    for h in range(TRIPLE):
        for k in range(1, QUADS):
            dkv_copy(h, k - 1, k).wait_send()
            dq_copy(h, k).wait_send()


def back(by_kernel, shards, members, *arrays):
    kv_all, hidden = arrays[1], arrays[5]
    rows = kv_all.shape[3]
    half = rows // 2
    seqs, _, model = hidden.shape
    width = HEADS * HEAD
    units = 2 * model
    steps = TRIPLE * QUADS
    vm = pl.BlockSpec(memory_space=pltpu.VMEM)
    anywhere = pl.BlockSpec(memory_space=pl.ANY)
    dma = pltpu.SemaphoreType.DMA
    shape = jax.ShapeDtypeStruct
    outs = [shape((seqs, rows, model), F32)]
    reducing = []
    if by_kernel:
        block, head_block = model // shards, width // shards
        outs += [
            shape((units // shards, model), BF),
            shape((head_block, 2 * model), BF),
            shape((head_block, GROUPS * units), BF),
            shape((block, 2 * width + 2 * SMALL), BF),
        ]
        outs += [shape((members, block, width // members), BF)] * TRIPLE
        third, dense, inner, middle = (one.shape[-2:] for one in arrays[11:])
        chunk = (block // QUADS, width // members)
        reducing = [
            pltpu.VMEM(arrays[13].shape, BF),
            pltpu.VMEM(arrays[14].shape, BF),
            *Reduce.tail_scratch(members, shards, *third),
            *Reduce.tail_scratch(members, shards, *dense),
            pltpu.VMEM((shards, *inner), BF),
            pltpu.VMEM((shards, *middle), BF),
            *Reduce.head_scratch(members, shards, *inner),
            *Reduce.tail_scratch(members, shards, *inner),
            *Reduce.head_scratch(members, shards, *middle),
            *Reduce.tail_scratch(members, shards, *middle),
        ]
        for _ in range(TRIPLE):
            reducing += [
                pltpu.VMEM((members, shards, QUADS, *chunk), BF),
                pltpu.VMEM((shards, *chunk), BF),
                *Reduce.head_scratch(members, shards, *chunk),
                *Reduce.tail_scratch(members, shards, *chunk),
            ]
    else:
        outs += [shape((model, 3 * width), BF)]
    total = TRIPLE * QUADS * rows * QUADS * members * rows
    return pl.pallas_call(
        functools.partial(back_kernel, by_kernel, shards, members),
        in_specs=[vm] * 5 + [anywhere] * 4 + [vm, vm] + ([vm, vm, anywhere, anywhere] if by_kernel else []),
        out_specs=[vm] * len(outs),
        out_shape=outs,
        scratch_shapes=[
            pltpu.VMEM((QUADS, rows, 2 * HEAD), BF),
            pltpu.VMEM((QUADS, rows, 2 * HEAD), BF),
            pltpu.VMEM((QUADS, 8, rows), F32),
            pltpu.VMEM((QUADS, 8, rows), F32),
            pltpu.VMEM((QUADS, HEAD, rows), F32),
            pltpu.VMEM((members * rows, 2 * HEAD), F32),
            pltpu.VMEM((2, rows, 2 * HEAD), F32),
            pltpu.VMEM((2, members - 1, rows, 2 * HEAD), BF),
            pltpu.VMEM((steps, members - 1, rows, 2 * HEAD), BF),
            pltpu.VMEM((TRIPLE, QUADS, rows, 2 * HEAD), BF),
            pltpu.VMEM((TRIPLE, QUADS, half, 2 * HEAD), BF),
            pltpu.VMEM((QUADS, TRIPLE, half, 2 * HEAD), BF),
            pltpu.VMEM((QUADS, TRIPLE, rows, 2 * HEAD), BF),
            pltpu.VMEM((seqs * rows, width), BF),
            pltpu.VMEM((seqs, RIM, model), BF),
            pltpu.VMEM((seqs, RIM, model), BF),
            *[pltpu.VMEM(one.shape, one.dtype) for one in arrays[5:8]],
            dma((5,)),
            dma((steps, members)), dma((steps, members)),
            dma((TRIPLE, QUADS)), dma((TRIPLE, QUADS)), dma((TRIPLE, QUADS)), dma((TRIPLE, QUADS)),
            dma((2,)), dma((2,)), dma((2,)),
        ]
        + reducing,
        compiler_params=pltpu.CompilerParams(
            collective_id=2, has_side_effects=True, vmem_limit_bytes=62 * 2**20
        ),
        cost_estimate=pl.CostEstimate(flops=total * 640, bytes_accessed=8 * 2**20, transcendentals=total),
    )(*arrays)


def finish_kernel(rows_in, third_sum, dense_sum, inner_sum, middle_sum, *refs):
    sums, refs = refs[:TRIPLE], refs[TRIPLE:]
    rows_out, g_qkv, g_depth, g_point, g_span, g_value, g_attn, g_conv, g_norms, g_inner, g_outer = refs
    rows_out[...] = rows_in[...]
    width = HEADS * HEAD
    model = third_sum.shape[1]
    group, units = model // GROUPS, g_inner.shape[2]
    for g in range(GROUPS):
        g_outer[g] = third_sum[:, g * group : g * group + group].astype(F32)
        g_inner[g] = inner_sum[:, g * units : g * units + units].astype(F32)
    g_attn[...] = dense_sum[:, :model].astype(F32)
    g_conv[...] = dense_sum[:, model:].astype(F32)
    g_value[...] = middle_sum[:, :width].astype(F32)
    g_point[...] = middle_sum[:, width : 2 * width].astype(F32)
    small = middle_sum[:, 2 * width : 2 * width + SMALL].astype(F32)
    g_span[...] = small[: g_span.shape[0], : HEADS * KERNEL]
    turned = small.T
    g_depth[...] = turned[64 : 64 + KERNEL]
    g_norms[...] = turned[64 + KERNEL : 68 + KERNEL]
    found = {}
    for h in range(TRIPLE):
        both = jnp.concatenate([sums[h][c].astype(F32) for c in range(sums[h].shape[0])], axis=1)
        for t in range(2):
            head = TRIPLE * t + h
            found[head] = both[:, t * HEAD : t * HEAD + HEAD]
            at = 2 * HEAD + t * 2 * HEAD
            found[HEADS + head] = both[:, at : at + HEAD]
            found[2 * HEADS + head] = both[:, at + HEAD : at + 2 * HEAD]
    for j in range(3 * HEADS // 2):
        g_qkv[:, j * 2 * HEAD : j * 2 * HEAD + 2 * HEAD] = jnp.concatenate([found[2 * j], found[2 * j + 1]], axis=1)


def finish_all(shards, rows_in, *arrays):
    vm = pl.BlockSpec(memory_space=pltpu.VMEM)
    width, model = HEADS * HEAD, rows_in.shape[2]
    units = 2 * model
    block, head_block = model // shards, width // shards
    shape = jax.ShapeDtypeStruct
    outs = [
        shape(rows_in.shape, F32),
        shape((block, 3 * width), F32),
        shape((KERNEL, block), F32),
        shape((block, width), F32),
        shape((head_block, HEADS * KERNEL), F32),
        shape((block, width), F32),
        shape((head_block, model), F32),
        shape((head_block, model), F32),
        shape((4, block), F32),
        shape((GROUPS, head_block, units), F32),
        shape((GROUPS, units // shards, model // GROUPS), F32),
    ]
    return pl.pallas_call(
        finish_kernel,
        in_specs=[vm] * (1 + len(arrays)),
        out_specs=[vm] * len(outs),
        out_shape=outs,
        compiler_params=pltpu.CompilerParams(vmem_limit_bytes=62 * 2**20),
    )(rows_in, *arrays)


SPLITS = (2, 2, 4, 1)


def shards(
    hidden_in,
    cotangent,
    qkv_weight,
    conv_depth,
    conv_point,
    span_weight,
    conv_value,
    dense_attn,
    dense_conv,
    attn_norm_gain,
    attn_norm_bias,
    ffn_inner,
    ffn_outer,
    out_norm_gain,
    out_norm_bias,
):
    attn_width = HEADS * HEAD
    seq_count, local_rows, model_width = hidden_in.shape
    ctx_count = lax.axis_size("ctx")
    members = ctx_count // QUADS
    shard_count = lax.axis_size("shard")
    width_rows = model_width // shard_count
    head_rows = attn_width // shard_count
    forward = [(i, i + 1) for i in range(ctx_count - 1)]
    backward = [(i + 1, i) for i in range(ctx_count - 1)]
    units = ffn_inner.shape[2]
    block_shapes = (
        (width_rows, 3 * attn_width + SMALL), (width_rows, 2 * attn_width + 2 * SMALL),
        (head_rows, 2 * model_width + GROUPS * units), (units // shard_count, model_width),
    )
    by_kernel = members == 2 and all(fits(*one, members, split) for one, split in zip(block_shapes, SPLITS))
    norm_rows_in = jnp.stack([attn_norm_gain, attn_norm_bias, out_norm_gain, out_norm_bias])
    if by_kernel:
        arrays = (
            qkv_weight, conv_value, conv_point, span_weight, conv_depth, norm_rows_in,
            dense_attn, dense_conv, ffn_inner, ffn_outer,
        )
    else:
        small = jnp.concatenate(
            [
                jnp.pad(span_weight, ((0, width_rows - head_rows), (0, 64 - HEADS * KERNEL))),
                conv_depth.T,
                norm_rows_in.T,
                jnp.zeros((width_rows, SMALL - 64 - KERNEL - 4), BF),
            ],
            axis=1,
        )
        by_head = qkv_weight.reshape(width_rows, 3, 2, TRIPLE, HEAD)
        q_block = by_head[:, 0].transpose(0, 2, 1, 3).reshape(width_rows, TRIPLE, 2 * HEAD)
        pair_block = by_head[:, 1:].transpose(0, 3, 2, 1, 4).reshape(width_rows, TRIPLE, 4 * HEAD)
        qkv_block = jnp.concatenate([q_block, pair_block], axis=2).reshape(width_rows, 3 * attn_width)
        qkv_block = jnp.pad(qkv_block, ((0, 0), (0, SMALL)))
        rest_block = jnp.concatenate([conv_value, conv_point, small, jnp.zeros((width_rows, SMALL), BF)], axis=1)
        second_block = jnp.concatenate([dense_attn, dense_conv, ffn_inner[0], ffn_inner[1]], axis=1)
        third_block = jnp.concatenate([ffn_outer[0], ffn_outer[1]], axis=1)
        qkv, rest, second, third = (
            lax.all_gather(one, "shard", axis=0, tiled=True)
            for one in (qkv_block, rest_block, second_block, third_block)
        )
        span = rest[:, 2 * attn_width : 2 * attn_width + SMALL].reshape(shard_count, width_rows, SMALL)
        span = span[:, :head_rows].reshape(attn_width, SMALL)
        arrays = (qkv, rest, span)
    (
        context, kernel_soft, kv_all, q_all, out_all, lse, q_low, spread, key_conv, span_mix, value_ext, conv_low,
        small_turned, low_rim, high_rim, *gathered,
    ) = front(by_kernel, members, shard_count, hidden_in, *arrays)
    if by_kernel:
        qkv, rest, span, second, third = gathered
    layer_out, d_first, d_context, d_conv, dense_part, inner_part, third_part, norm_sums = middle(
        context, conv_low, hidden_in, cotangent, second, third, small_turned, by_kernel, shard_count, members
    )
    grad_rows, low_edge, high_edge, dq_conv, middle_part, d_all, *sums = conv_back(
        by_kernel, shard_count, members,
        hidden_in, low_rim, high_rim, rest, span, small_turned, d_conv, q_low, spread, key_conv, span_mix,
        kernel_soft, value_ext, d_first, norm_sums, d_context, *((third_part, dense_part) if by_kernel else ()),
    )
    grad_in, *results = back(
        by_kernel, shard_count, members,
        d_all, kv_all, q_all, out_all, lse, hidden_in, qkv, dq_conv, grad_rows, low_edge, high_edge,
        *((*sums, inner_part, middle_part) if by_kernel else ()),
    )
    if by_kernel:
        grad_in, g_qkv, g_depth, g_point, g_span, g_value, g_attn, g_conv, norms, g_inner, g_outer = finish_all(
            shard_count, grad_in, *results
        )
    else:
        qkv_sum, dense_sum, inner_sum, third_sum, middle_sum = (
            lax.psum(lax.psum_scatter(one, "shard", scatter_dimension=0, tiled=True), "ctx").astype(F32)
            for one in (results[0], dense_part, inner_part, third_part, middle_part)
        )
        by_head = qkv_sum.reshape(width_rows, TRIPLE, attn_width)
        g_q = by_head[:, :, : 2 * HEAD].reshape(width_rows, TRIPLE, 2, HEAD).transpose(0, 2, 1, 3)
        g_pair = by_head[:, :, 2 * HEAD :].reshape(width_rows, TRIPLE, 2, 2, HEAD).transpose(0, 3, 2, 1, 4)
        g_qkv = jnp.concatenate([g_q.reshape(width_rows, -1), g_pair.reshape(width_rows, -1)], axis=1)
        small_sum = middle_sum[:, 2 * attn_width : 2 * attn_width + SMALL]
        g_depth = small_sum[:, 64 : 64 + KERNEL].T
        norms = small_sum[:, 64 + KERNEL : 68 + KERNEL].T
        g_span = small_sum[:head_rows, : HEADS * KERNEL]
        g_value, g_point = middle_sum[:, :attn_width], middle_sum[:, attn_width : 2 * attn_width]
        g_attn, g_conv = dense_sum[:, :model_width], dense_sum[:, model_width:]
        g_inner = inner_sum.reshape(head_rows, GROUPS, -1).transpose(1, 0, 2)
        g_outer = third_sum.reshape(-1, GROUPS, D // GROUPS).transpose(1, 0, 2)
    return (
        layer_out, grad_in, g_qkv, g_depth, g_point, g_span, g_value, g_attn, g_conv,
        norms[0], norms[1], g_inner, g_outer, norms[2], norms[3],
    )


def solution(mesh):
    return jax.shard_map(
        shards,
        mesh=mesh,
        in_specs=(
            P("shard", "ctx", None),
            P("shard", "ctx", None),
            P("shard", None),
            P(None, "shard"),
            P("shard", None),
            P("shard", None),
            P("shard", None),
            P("shard", None),
            P("shard", None),
            P("shard"),
            P("shard"),
            P(None, "shard", None),
            P(None, "shard", None),
            P("shard"),
            P("shard"),
        ),
        out_specs=(
            P("shard", "ctx", None),
            P("shard", "ctx", None),
            P("shard", None),
            P(None, "shard"),
            P("shard", None),
            P("shard", None),
            P("shard", None),
            P("shard", None),
            P("shard", None),
            P("shard"),
            P("shard"),
            P(None, "shard", None),
            P(None, "shard", None),
            P("shard"),
            P("shard"),
        ),
        check_vma=False,
    )
```
